32 devices in a mesh: src: 8 (over y, x, core), tm: 4 (over z).
Axes of the slice: x: 2, y: 2, z: 4, core: 2. Of those that a mesh axis runs over, the one named last changes fastest.
Arguments:
- observed: float32 [4, 8192], P(None, ('src', 'tm')), may hold values from -8 to 8
- weight_obs: float32 [4, 8192], P(None, ('src', 'tm')), may hold values from 0.25 to 4
- present: int32 [4, 8192], P(None, ('src', 'tm')), may hold values 0 or 1
- source_partials: float32 [5, 4, 8192], P(None, None, ('src', 'tm')), may hold values from -6 to 6
- attitude_partials: float32 [4, 4, 8192], P(None, None, ('src', 'tm')), may hold values from -6 to 6
- phase: float32 [4, 8192], P(None, ('src', 'tm')), may hold values from 0 to 1
- knot_base: int32 [4, 8192], P(None, ('src', 'tm')), may hold values from 0 to 28
- source_id: int32 [4, 8192], P(None, ('src', 'tm')), may hold values from 0 to 127, as said below
- cal_id: int32 [4, 8192], P(None, ('src', 'tm')), may hold values from 0 to 32767
- attitude: float32 [512], P('tm'), may hold values from -4 to 4
- calibration: float32 [32768], replicated, may hold values from -4 to 4
Outputs:
- source_params: float32 [5, 4096], P(None, ('src', 'tm'))
- attitude_out: float32 [512], P('tm')
- calibration_out: float32 [32768], replicated
- residual: float32 [4, 8192], P(None, ('src', 'tm'))
The draws below stay inside these ranges and needn't reach their ends.
Inputs may be any that keep to these rules, and one draw needn't show every extreme that they name: `source_id`: within each device's block of 256 columns the ids name that device's 128 sources, each of them at least once.
All inputs are finite; a program needn't handle non-finite values. No bound on the sum of `present` on one device may be relied on, other than what follows from the above.
Results may differ from the reference program's by a relative error of at most 0.0003.
Values sent between devices are 32-bit elements; how exact they have to be, the bound alone decides.
No kernel may reach another device: no remote copies, remote signals or barrier semaphores. Data moves between devices by JAX's collectives and lax.ppermute only.
A program may use at most 64 MiB of HBM per device.

```python
import math
import jax
import jax.numpy as jnp
from jax import lax

KNOTS_DEV = 32
SRC_DEV = 128
SLOT = 256
CAL = 32768
ITERS = 2
SOURCES = 4096
OBS_COLS = 8192
ATT = 512
N_TM = 4


def draw_source_id(key, part):
    key = jax.random.fold_in(key, 11)
    holders = SOURCES // SRC_DEV
    per_holder = N_TM * SLOT
    perm_keys = jax.random.split(jax.random.fold_in(key, 1), holders)
    orders = jax.vmap(lambda single: jax.random.permutation(single, SRC_DEV))(perm_keys)
    rest = jax.random.randint(jax.random.fold_in(key, 2), (holders, per_holder - SRC_DEV), 0, SRC_DEV)
    joined = jnp.concatenate([orders.astype(jnp.int32), rest.astype(jnp.int32)], axis=1)
    shuffle_keys = jax.random.split(jax.random.fold_in(key, 3), holders)
    mixed = jax.vmap(lambda single, values: jax.random.permutation(single, values))(shuffle_keys, joined)
    mixed = mixed.reshape(holders, N_TM, SLOT)
    return jnp.transpose(mixed, (1, 0, 2)).reshape(N_TM, holders * SLOT).astype(jnp.int32)


def touch_ends(values, own_key, smallest, top_value):
    place = [jax.random.randint(jax.random.fold_in(own_key, axis), (), 0, length) for axis, length in enumerate(values.shape)]
    longest = values.shape.index(max(values.shape))
    neighbour = place[:longest] + [(place[longest] + 1) % values.shape[longest]] + place[longest + 1:]
    return values.at[tuple(place)].set(smallest).at[tuple(neighbour)].set(top_value)


def with_spikes(values, key, source, target, blocks, factor):
    owner, partner = [(jnp.arange(values.shape[axis_at]) // (values.shape[axis_at] // blocks)).reshape([-1 if axis == axis_at else 1 for axis in range(values.ndim)]) for axis_at in (source, target)]
    chosen = jax.random.permutation(key, blocks)[partner]
    strong = (owner == chosen) | (owner == (partner + blocks // 2) % blocks)
    return jnp.where(strong, factor * values, values)


def steps_of(stream_key, shape, shards, smallest, largest):
    level, own = 1.0, jax.random.fold_in(stream_key, 6)
    for dim, parts in shards:
        heights = jnp.exp(jax.random.uniform(jax.random.fold_in(own, dim), (parts,), jnp.float32, smallest / len(shards), largest / len(shards)))
        level = level * jnp.repeat(heights, shape[dim] // parts).reshape([-1 if axis == dim else 1 for axis in range(len(shape))])
    return level


def bell_draw(rng, dims, spread, limit, pieces=(), kind=jnp.bfloat16):
    drawn = jax.random.normal(rng, dims, jnp.float32) * spread
    if len(pieces) > 0:
        drawn = steps_of(rng, dims, pieces, -0.22, 0.18) * drawn
    return jnp.clip(drawn, min=-limit, max=limit).astype(kind)


def noise_with(key, dims, deviation, bound, shards, heavy, kind=jnp.bfloat16):
    values = deviation * jax.random.normal(key, dims, jnp.float32)
    if shards:
        values = values * steps_of(key, dims, shards, -0.22, 0.18)
    return jnp.clip(with_spikes(values, jax.random.fold_in(key, 3), *heavy), -bound, bound).astype(kind)


def setup_inputs(seed: int = 0) -> dict:
    arg_keys = jax.random.split(jax.random.key(seed), 12)
    return {
        "observed": noise_with(arg_keys[0], (N_TM, OBS_COLS), 1.0, 8.0, ((1, 32),), (1, 0, 4, 2.0), jnp.float32),
        "weight_obs": jnp.clip(jnp.exp(math.log(4.0) - 2.7725887 * jax.random.uniform(arg_keys[1], (N_TM, OBS_COLS), jnp.float32) ** steps_of(arg_keys[1], (N_TM, OBS_COLS), ((1, 32),), -0.2, 0.2)), 0.25, 4.0),
        "present": touch_ends((jax.random.randint(arg_keys[2], (N_TM, OBS_COLS), 0, 4) < 3).astype(jnp.int32), jax.random.fold_in(arg_keys[2], 1), 0, 1),
        "source_partials": bell_draw(arg_keys[3], (5, N_TM, OBS_COLS), 1.0, 6.0, ((2, 32),), jnp.float32),
        "attitude_partials": bell_draw(arg_keys[4], (4, N_TM, OBS_COLS), 1.0, 6.0, ((2, 32),), jnp.float32),
        "phase": jnp.clip(1.0 * jax.random.uniform(arg_keys[5], (N_TM, OBS_COLS), jnp.float32) ** steps_of(arg_keys[5], (N_TM, OBS_COLS), ((1, 32),), -0.2, 0.2), 0.0, 1.0),
        "knot_base": touch_ends(jax.random.randint(arg_keys[6], (N_TM, OBS_COLS), 0, KNOTS_DEV - 3), jax.random.fold_in(arg_keys[6], 1), 0, (KNOTS_DEV - 3) - 1).astype(jnp.int32),
        "source_id": draw_source_id(jax.random.fold_in(arg_keys[11], 71), 0),
        "cal_id": touch_ends(jax.random.randint(arg_keys[8], (N_TM, OBS_COLS), 0, CAL), jax.random.fold_in(arg_keys[8], 1), 0, CAL - 1).astype(jnp.int32),
        "attitude": bell_draw(arg_keys[9], (ATT,), 0.5, 4.0, ((0, 4),), jnp.float32),
        "calibration": bell_draw(arg_keys[10], (CAL,), 0.5, 4.0, (), jnp.float32),
    }


PAIRS = [(row_id, col_id) for row_id in range(5) for col_id in range(row_id + 1)]

def spline_terms(phase, attitude_partials):
    other = 1.0 - phase
    square = phase * phase
    cube = square * phase
    basis = [other * other * other / 6.0, (3.0 * cube - 6.0 * square + 4.0) / 6.0, (-3.0 * cube + 3.0 * square + 3.0 * phase + 1.0) / 6.0, cube / 6.0]
    return jnp.stack([basis[knot_step] * attitude_partials[channel] for knot_step in range(4) for channel in range(4)])

def attitude_model(coefficients, terms, knot_base):
    table = coefficients.reshape(knot_base.shape[0], -1, 4)
    running = jnp.zeros(knot_base.shape, jnp.float32)
    for knot_step in range(4):
        for channel in range(4):
            picked = jnp.take_along_axis(table[:, :, channel], knot_base + knot_step, axis=1)
            running = running + terms[4 * knot_step + channel] * picked
    return running

def small_solve(matrix, right_side):
    extent = len(right_side)
    factor = {}
    for member in range(extent):
        for column in range(member + 1):
            running = matrix[member][column]
            for offset in range(column):
                running = running - factor[member, offset] * factor[column, offset]
            if member == column:
                factor[member, member] = jnp.sqrt(running)
            else:
                factor[member, column] = running / factor[column, column]
    forward = []
    for member in range(extent):
        running = right_side[member]
        for offset in range(member):
            running = running - factor[member, offset] * forward[offset]
        forward.append(running / factor[member, member])
    result = [None] * extent
    for member in reversed(range(extent)):
        running = forward[member]
        for offset in range(member + 1, extent):
            running = running - factor[offset, member] * result[offset]
        result[member] = running / factor[member, member]
    return jnp.stack(result)

def source_solve(ids, count, weighted, source_partials, target):
    products = [weighted * source_partials[row_id] * source_partials[col_id] for row_id, col_id in PAIRS]
    products = products + [weighted * source_partials[row_id] * target for row_id in range(5)]
    stacked = jnp.stack(products).reshape(len(products), -1).T
    sums = jax.ops.segment_sum(stacked, ids.reshape(-1), num_segments=count).T
    entries = {}
    for position, pair in enumerate(PAIRS):
        entry_value = sums[position] + (1.0 if pair[0] == pair[1] else 0.0)
        entries[pair[0], pair[1]] = entry_value
        entries[pair[1], pair[0]] = entry_value
    matrix = [[entries[row_id, col_id] for col_id in range(5)] for row_id in range(5)]
    return small_solve(matrix, [sums[15 + row_id] for row_id in range(5)])

def spd_solve(matrix, right_side):
    eye = jnp.eye(matrix.shape[-1], dtype=jnp.float32)
    lower = jnp.linalg.cholesky(matrix + eye)
    middle = lax.linalg.triangular_solve(lower, right_side[..., None], left_side=True, lower=True)
    result = lax.linalg.triangular_solve(lower, middle, left_side=True, lower=True, transpose_a=True)
    return result[..., 0]

def band_normals(terms, knot_base, weighted, resid):
    windows = KNOTS_DEV - 3
    width = 4 * KNOTS_DEV

    def single(item):
        part, base, weights, values = item
        outer = (part[:, None, :] * (weights[None, None, :] * part[None, :, :])).reshape(256, -1).T
        band = jax.ops.segment_sum(outer, base, num_segments=windows).reshape(windows, 16, 16)
        side = jax.ops.segment_sum((part * (weights * values)[None, :]).T, base, num_segments=windows)
        normal = jnp.zeros((width, width), jnp.float32)
        right = jnp.zeros((width,), jnp.float32)
        for start in range(windows):
            normal = normal.at[4 * start:4 * start + 16, 4 * start:4 * start + 16].add(band[start])
            right = right.at[4 * start:4 * start + 16].add(side[start])
        return (normal, right)
    return lax.map(single, (jnp.moveaxis(terms, 1, 0), knot_base, weighted, resid))

def reference(observed, weight_obs, present, source_partials, attitude_partials, phase, knot_base, source_id, cal_id, attitude, calibration):
    weighted = present.astype(jnp.float32) * weight_obs
    terms = spline_terms(phase, attitude_partials)
    holders = lax.broadcasted_iota(jnp.int32, source_id.shape, 1) // SLOT
    global_ids = (source_id + holders * SRC_DEV).astype(jnp.int32)
    current = attitude
    cal_now = calibration
    flat_cal = cal_id.reshape(-1)
    params = jnp.zeros((5, SOURCES), jnp.float32)
    for sweep in range(ITERS):
        target = observed - attitude_model(current, terms, knot_base) - cal_now[cal_id]
        params = source_solve(global_ids, SOURCES, weighted, source_partials, target)
        resid = target - lax.optimization_barrier(jnp.sum(source_partials * params[:, global_ids], axis=0))
        normals, rights = band_normals(terms, knot_base, weighted, resid)
        current = current + spd_solve(normals, rights).reshape(-1)
        numer = jax.ops.segment_sum((weighted * resid).reshape(-1), flat_cal, num_segments=CAL)
        denom = jax.ops.segment_sum(weighted.reshape(-1), flat_cal, num_segments=CAL)
        cal_now = cal_now + numer / (denom + 1.0)
    final = observed - attitude_model(current, terms, knot_base) - cal_now[cal_id]
    final = final - lax.optimization_barrier(jnp.sum(source_partials * params[:, global_ids], axis=0))
    return (params, current, cal_now, final)
```

```python
import functools

import jax
import jax.numpy as jnp
from jax import lax
from jax.experimental import pallas as pl
from jax.experimental.pallas import tpu as pltpu
from jax.sharding import PartitionSpec as P

KNOTS_DEV = 32
WIDTH = 4 * KNOTS_DEV
SRC_DEV = 128
CAL = 32768
LANES = 128
HIGH = CAL // LANES
SUB = 8
VMEM_BYTES = 48 * 1024 * 1024

F32 = jnp.float32
BF16 = jnp.bfloat16
EXACT = lax.Precision.HIGHEST


def iota(shape, dim):
    return lax.broadcasted_iota(jnp.int32, shape, dim)


def split3(value):
    first = value.astype(BF16)
    rest = value - first.astype(F32)
    second = rest.astype(BF16)
    third = (rest - second.astype(F32)).astype(BF16)
    return first, second, third


def dot(left, right):
    return lax.dot_general(left, right, (((1,), (0,)), ((), ())), preferred_element_type=F32)


def dot_t(left, right):
    return lax.dot_general(left, right, (((1,), (1,)), ((), ())), preferred_element_type=F32)


def exact_dot(left, right):
    return lax.dot_general(
        left, right, (((1,), (0,)), ((), ())), precision=EXACT, preferred_element_type=F32
    )


def exact_dot_t(left, right):
    return lax.dot_general(
        left, right, (((1,), (1,)), ((), ())), precision=EXACT, preferred_element_type=F32
    )


def one_hot(ids, count):
    return jnp.where(iota((count, ids.shape[1]), 0) == ids, 1.0, 0.0).astype(BF16)


def flat(value):
    return jnp.concatenate([value[row : row + 1] for row in range(value.shape[0])], axis=1)


def unflat(value, rows):
    slots = value.shape[1] // rows
    return [value[:, row * slots : (row + 1) * slots] for row in range(rows)]


def cal_pick(table, ids):
    parts = jnp.concatenate(split3(table.T), axis=0)
    high = ids // LANES
    low = ids % LANES
    found = dot(parts, one_hot(high, HIGH))
    found = found[:LANES] + found[LANES : 2 * LANES] + found[2 * LANES :]
    return jnp.sum(jnp.where(iota(found.shape, 0) == low, found, 0.0), axis=0, keepdims=True)


def cal_sums(values, ids):
    high = one_hot(ids // LANES, HIGH)
    low = iota((LANES, ids.shape[1]), 0) == ids % LANES
    total = None
    for part in split3(values):
        spread = jnp.where(low, part.astype(F32), 0.0).astype(BF16)
        added = dot_t(high, spread)
        total = added if total is None else total + added
    return total


def design_of(base, basis, partials):
    slots = base.shape[1]
    knot = iota((WIDTH, slots), 0) // 4
    step = knot - base
    spread = jnp.zeros((WIDTH, slots), F32)
    for index in range(4):
        spread = jnp.where(step == index, basis[index], spread)
    return spread * jnp.concatenate([partials] * (WIDTH // 8), axis=0)


def band_shift(tile, knot):
    return ((tile % 8) * 16 - (8 * tile + 4 * knot - 12)) % WIDTH


def pack_band(normal):
    place = iota((8, WIDTH), 1) // 16
    upper = iota((8, WIDTH), 0) < 4
    groups = []
    for group in range(2):
        packed = jnp.zeros((8, WIDTH), F32)
        for tile in range(8 * group, 8 * group + 8):
            rows = normal[8 * tile : 8 * tile + 8]
            rolled = jnp.where(
                upper,
                pltpu.roll(rows, band_shift(tile, 0), 1),
                pltpu.roll(rows, band_shift(tile, 1), 1),
            )
            packed = jnp.where(place == tile % 8, rolled, packed)
        groups.append(packed)
    return jnp.concatenate(groups, axis=0)


def unpack_band(packed):
    place = iota((8, WIDTH), 1) // 16
    upper = iota((8, WIDTH), 0) < 4
    tiles = []
    for tile in range(16):
        group = tile // 8
        rows = jnp.where(place == tile % 8, packed[8 * group : 8 * group + 8], 0.0)
        tiles.append(
            jnp.where(
                upper,
                pltpu.roll(rows, (-band_shift(tile, 0)) % WIDTH, 1),
                pltpu.roll(rows, (-band_shift(tile, 1)) % WIDTH, 1),
            )
        )
    full = jnp.concatenate(tiles, axis=0)
    return jnp.where(iota(full.shape, 0) >= iota(full.shape, 1), full, 0.0)


def coefs(first, last):
    return list(range(4 * first, 4 * last + 4))


STAGES = (
    ((coefs(0, 4), (0, 3)), (coefs(8, 13), (2, 8)), (coefs(17, 22), (7, 12)), (coefs(26, 31), (11, 15))),
    ((coefs(5, 7), (0, 8)), (coefs(23, 25), (7, 15))),
    ((coefs(14, 16), (0, 15)),),
)


def spd_inverse(matrix):
    tiles = [matrix[8 * tile : 8 * tile + 8] for tile in range(WIDTH // 8)]
    lane = iota((8, WIDTH), 1)
    lane_row = iota((1, WIDTH), 1)
    row = iota((8, 1), 0)
    for stage in STAGES:
        for step in range(max(len(chain) for chain, reach in stage)):
            pivots = [(chain[step], reach) for chain, reach in stage if step < len(chain)]
            held = list(tiles)
            for pivot, (low, high) in pivots:
                at, sub = pivot // 8, pivot % 8
                line = held[at][sub : sub + 1]
                scale = 1.0 / line[:, pivot : pivot + 1]
                line = jnp.where(lane_row == pivot, -1.0, line) * scale
                for tile in range(low, high + 1):
                    column = held[tile][:, pivot : pivot + 1]
                    drop = lane == pivot
                    if tile == at:
                        column = jnp.where(row == sub, -1.0, column)
                        drop = drop | (iota((8, WIDTH), 0) == sub)
                    tiles[tile] = jnp.where(drop, 0.0, tiles[tile]) - column * line
    return -jnp.concatenate(tiles, axis=0)


def small_factor(sums):
    factor = {}
    for member in range(5):
        for column in range(member + 1):
            running = sums[8 * member + column : 8 * member + column + 1]
            if member == column:
                running = running + 1.0
            for offset in range(column):
                running = running - factor[member, offset] * factor[column, offset]
            if member == column:
                factor[member, member] = jnp.sqrt(running)
            else:
                factor[member, column] = running * inverse_of[column]
        inverse_of = {} if member == 0 else inverse_of
        inverse_of[member] = 1.0 / factor[member, member]
    inverse = {}
    for column in range(5):
        inverse[column, column] = inverse_of[column]
        for member in range(column + 1, 5):
            running = factor[member, column] * inverse[column, column]
            for offset in range(column + 1, member):
                running = running + factor[member, offset] * inverse[offset, column]
            inverse[member, column] = -running * inverse_of[member]
    return inverse


PLACES = [(row_id, col_id) for row_id in range(5) for col_id in range(row_id + 1)]


def small_apply(inverse, sides):
    forward = []
    for member in range(5):
        running = inverse[member, 0] * sides[0]
        for column in range(1, member + 1):
            running = running + inverse[member, column] * sides[column]
        forward.append(running)
    result = []
    for column in range(5):
        running = inverse[column, column] * forward[column]
        for member in range(column + 1, 5):
            running = running + inverse[member, column] * forward[member]
        result.append(running)
    return result


PAIRS = [(row_id, col_id) for row_id in range(5) for col_id in range(row_id + 1)]


def spline_terms(phase, attitude_partials):
    other = 1.0 - phase
    square = phase * phase
    cube = square * phase
    basis = [
        other * other * other / 6.0,
        (3.0 * cube - 6.0 * square + 4.0) / 6.0,
        (-3.0 * cube + 3.0 * square + 3.0 * phase + 1.0) / 6.0,
        cube / 6.0,
    ]
    return jnp.stack(
        [
            basis[knot_step] * attitude_partials[channel]
            for knot_step in range(4)
            for channel in range(4)
        ]
    )


def attitude_model(local, terms, knot_base):
    coefficients = lax.all_gather(local, "tm", axis=0, tiled=True)
    blocks, slots = knot_base.shape
    table = coefficients.reshape(blocks, -1, 4)
    knots_count = table.shape[1]
    grid = lax.broadcasted_iota(jnp.int32, (1, knots_count, 1), 1)
    running = jnp.zeros(knot_base.shape, jnp.float32)
    for knot_step in range(4):
        hit = (grid == (knot_base + knot_step)[:, None, :]).astype(jnp.float32)
        picked = jnp.einsum(
            "bkc,bks->bcs",
            table,
            hit,
            precision=lax.Precision.HIGHEST,
            preferred_element_type=jnp.float32,
        )
        for channel in range(4):
            running = running + terms[4 * knot_step + channel] * picked[:, channel, :]
    return running


def small_solve(matrix, right_side):
    extent = len(right_side)
    factor = {}
    for member in range(extent):
        for column in range(member + 1):
            running = matrix[member][column]
            for offset in range(column):
                running = running - factor[member, offset] * factor[column, offset]
            if member == column:
                factor[member, member] = jnp.sqrt(running)
            else:
                factor[member, column] = running / factor[column, column]
    forward = []
    for member in range(extent):
        running = right_side[member]
        for offset in range(member):
            running = running - factor[member, offset] * forward[offset]
        forward.append(running / factor[member, member])
    result = [None] * extent
    for member in reversed(range(extent)):
        running = forward[member]
        for offset in range(member + 1, extent):
            running = running - factor[offset, member] * result[offset]
        result[member] = running / factor[member, member]
    return jnp.stack(result)


def source_solve(ids, count, weighted, source_partials, target):
    products = [
        weighted * source_partials[row_id] * source_partials[col_id] for row_id, col_id in PAIRS
    ]
    products = products + [weighted * source_partials[row_id] * target for row_id in range(5)]
    stacked = jnp.moveaxis(jnp.stack(products), 1, 0)
    owners = lax.broadcasted_iota(jnp.int32, (count, 1), 0)

    def accumulate(total, item):
        values, block_ids = item
        hit = (block_ids[None, :] == owners).astype(jnp.float32)
        added = lax.dot_general(
            values,
            hit,
            (((1,), (1,)), ((), ())),
            precision=lax.Precision.HIGHEST,
            preferred_element_type=jnp.float32,
        )
        return (total + added, None)

    sums, unused = lax.scan(
        accumulate, jnp.zeros((len(products), count), jnp.float32), (stacked, ids)
    )
    entries = {}
    for position, pair in enumerate(PAIRS):
        entry_value = sums[position] + (1.0 if pair[0] == pair[1] else 0.0)
        entries[pair[0], pair[1]] = entry_value
        entries[pair[1], pair[0]] = entry_value
    matrix = [[entries[row_id, col_id] for col_id in range(5)] for row_id in range(5)]
    return small_solve(matrix, [sums[15 + row_id] for row_id in range(5)])


def pick_params(params, ids):
    count = params.shape[1]
    owners = lax.broadcasted_iota(jnp.int32, (count, 1), 0)

    def pick_single(carry, block_ids):
        hit = (block_ids[None, :] == owners).astype(jnp.float32)
        return (
            carry,
            jnp.dot(
                params, hit, precision=lax.Precision.HIGHEST, preferred_element_type=jnp.float32
            ),
        )

    unused, picked = lax.scan(pick_single, 0, ids)
    return jnp.moveaxis(picked, 1, 0)


def spd_solve(matrix, right_side):
    eye = jnp.eye(matrix.shape[-1], dtype=jnp.float32)
    lower = jnp.linalg.cholesky(matrix + eye)
    middle = lax.linalg.triangular_solve(lower, right_side[..., None], left_side=True, lower=True)
    result = lax.linalg.triangular_solve(
        lower, middle, left_side=True, lower=True, transpose_a=True
    )
    return result[..., 0]


def block_normals(terms, knot_base, weighted, resid):
    blocks, slots = knot_base.shape
    spread = jnp.moveaxis(terms.reshape(4, 4, blocks, slots), 2, 0)

    def block_single(item):
        part, base, weights, values = item
        grid = lax.broadcasted_iota(jnp.int32, (KNOTS_DEV, slots), 0)
        design = jnp.zeros((KNOTS_DEV, 4, slots), jnp.float32)
        for knot_step in range(4):
            hit = (grid == base[None, :] + knot_step).astype(jnp.float32)
            design = design + hit[:, None, :] * part[knot_step][None, :, :]
        design = design.reshape(KNOTS_DEV * 4, slots)
        normal = lax.dot_general(
            design * weights[None, :],
            design,
            (((1,), (1,)), ((), ())),
            precision=lax.Precision.HIGHEST,
            preferred_element_type=jnp.float32,
        )
        right = jnp.dot(
            design,
            weights * values,
            precision=lax.Precision.HIGHEST,
            preferred_element_type=jnp.float32,
        )
        return (normal, right)

    return lax.map(block_single, (spread, knot_base, weighted, resid))


def plain_body(
    observed,
    weight_obs,
    present,
    source_partials,
    attitude_partials,
    phase,
    knot_base,
    source_id,
    cal_id,
    attitude,
    calibration,
):
    weighted = present.astype(jnp.float32) * weight_obs
    terms = spline_terms(phase, attitude_partials)
    flat_cal = cal_id.reshape(-1)
    local = attitude
    cal_now = calibration
    params = jnp.zeros((5, SRC_DEV), jnp.float32)
    for sweep in range(2):
        target = observed - attitude_model(local, terms, knot_base) - cal_now[cal_id]
        params = source_solve(source_id, SRC_DEV, weighted, source_partials, target)
        resid = target - jnp.sum(source_partials * pick_params(params, source_id), axis=0)
        normals, rights = block_normals(terms, knot_base, weighted, resid)
        normal, right = (
            lax.psum_scatter(normals, "tm", scatter_dimension=0, tiled=True),
            lax.psum_scatter(rights, "tm", scatter_dimension=0, tiled=True),
        )
        normal, right = lax.psum((normal[0], right[0]), "src")
        local = local + spd_solve(normal, right)
        numer = jax.ops.segment_sum((weighted * resid).reshape(-1), flat_cal, num_segments=CAL)
        denom = jax.ops.segment_sum(weighted.reshape(-1), flat_cal, num_segments=CAL)
        numer, denom = lax.psum((numer, denom), ("src", "tm"))
        cal_now = cal_now + numer / (denom + 1.0)
    final = observed - attitude_model(local, terms, knot_base) - cal_now[cal_id]
    final = final - jnp.sum(source_partials * pick_params(params, source_id), axis=0)
    return (params, local, cal_now, final)


BAND = 16


def fetch(pairs, sems):
    copies = [
        pltpu.make_async_copy(origin, held, sems.at[place])
        for place, (origin, held) in enumerate(pairs)
    ]
    for copy in copies:
        copy.start()
    for copy in copies:
        copy.wait()


def lines_of(value):
    rows, slots = value.shape
    return [
        value[row : row + 1, at : at + LANES] for row in range(rows) for at in range(0, slots, LANES)
    ]


def pick_from(table_t, ids):
    rows = ids.shape[0]
    ids = flat(ids)
    found = dot(jnp.concatenate(split3(table_t), axis=0), one_hot(ids // LANES, HIGH))
    found = found[:LANES] + found[LANES : 2 * LANES] + found[2 * LANES :]
    hit = iota(found.shape, 0) == ids % LANES
    return unflat(jnp.sum(jnp.where(hit, found, 0.0), axis=0, keepdims=True), rows)


def normals_kernel(
    observed_in, weight_in, present_in, source_in, attitude_in, phase_in, knot_in, id_in, cal_in,
    start_in,
    send_out, design_out, weighted_out, observed, source_id, cal_id, source_partials, start,
    weight_obs, present, attitude_partials, phase, knot_base, stacked, sems,
):
    fetch(
        [
            (observed_in, observed), (weight_in, weight_obs), (present_in, present),
            (source_in, source_partials), (attitude_in, attitude_partials), (phase_in, phase),
            (knot_in, knot_base), (id_in, source_id), (cal_in, cal_id), (start_in, start),
        ],
        sems,
    )
    rows, slots = observed.shape
    weighted = present[...].astype(F32) * weight_obs[...]
    weighted_out[...] = weighted
    u = phase[...]
    other = 1.0 - u
    square = u * u
    cube = square * u
    basis = [
        other * other * other / 6.0,
        (3.0 * cube - 6.0 * square + 4.0) / 6.0,
        (-3.0 * cube + 3.0 * square + 3.0 * u + 1.0) / 6.0,
        cube / 6.0,
    ]
    common = lines_of(cal_id[...].astype(F32)) + lines_of(weighted) + [start[...]]
    for row in range(rows):
        at = slice(row, row + 1)
        for channel in range(4):
            lines = attitude_partials[channel, at]
            stacked[row, channel : channel + 1] = lines
            stacked[row, channel + 4 : channel + 5] = lines
        design = design_of(knot_base[at], [part[at] for part in basis], stacked[row])
        design_out[row] = design
        band = pack_band(exact_dot_t(design * weighted[at], design))
        for index in range(BAND):
            send_out[row, index] = band[index : index + 1]
        for index, line in enumerate(common):
            send_out[row, BAND + index] = line


def sources_kernel(
    observed, source_partials, source_id, cal_id, weighted, calibration,
    partials_out, factor_out, target_out, table_out, table, sem,
):
    copy = pltpu.make_async_copy(calibration, table, sem)
    copy.start()
    rows, slots = observed.shape
    matrix = jnp.zeros((40, SRC_DEV), F32)
    for row in range(rows):
        at = slice(row, row + 1)
        for index in range(5):
            partials_out[row, index : index + 1] = source_partials[index, at]
        partials_out[row, 5:] = jnp.zeros((SUB - 5, slots), F32)
        partials = partials_out[row]
        products = jnp.concatenate(
            [partials * (weighted[at] * partials[index : index + 1]) for index in range(5)], axis=0
        )
        found = dot_t(jnp.concatenate(split3(products), axis=0), one_hot(source_id[at], SRC_DEV))
        matrix = matrix + found[:40] + found[40:80] + found[80:]
    inverse = small_factor(matrix)
    for place, pair in enumerate(PLACES):
        factor_out[place : place + 1] = inverse[pair]
    factor_out[15:16] = jnp.zeros((1, SRC_DEV), F32)
    copy.wait()
    table_t = table[...].T
    table_out[...] = table_t
    for row, picked in enumerate(pick_from(table_t, cal_id[...])):
        target_out[row : row + 1] = observed[row : row + 1] - picked


def relay_kernel(received, send_out):
    line = received.shape[0]
    count = received.shape[1] - BAND - 1
    for index in range(BAND):
        total = received[0, index]
        for device in range(1, line):
            total = total + received[device, index]
        for target in range(send_out.shape[0]):
            send_out[target, index] = total
    for device in range(line):
        for index in range(count):
            value = received[device, BAND + index]
            for target in range(send_out.shape[0]):
                send_out[target, BAND + device * count + index] = value


def residual_step(targets, design, partials, factor, weighted, source_id, send_out):
    rows = len(targets)
    hits = [one_hot(source_id[row : row + 1], SRC_DEV) for row in range(rows)]
    inverse = {pair: factor[place : place + 1] for place, pair in enumerate(PLACES)}
    sides = jnp.zeros((SUB, SRC_DEV), F32)
    for row in range(rows):
        products = partials[row] * (weighted[row : row + 1] * targets[row])
        found = dot_t(jnp.concatenate(split3(products), axis=0), hits[row])
        sides = sides + found[:SUB] + found[SUB : 2 * SUB] + found[2 * SUB :]
    params = small_apply(inverse, [sides[index : index + 1] for index in range(5)])
    table = jnp.concatenate(params + [jnp.zeros((3, SRC_DEV), F32)], axis=0)
    parts = jnp.concatenate(split3(table), axis=0)
    explained = []
    place = 0
    for row in range(rows):
        found = dot(parts, hits[row])
        found = found[:SUB] + found[SUB : 2 * SUB] + found[2 * SUB :]
        explained.append(jnp.sum(found * partials[row], axis=0, keepdims=True))
        scaled = weighted[row : row + 1] * (targets[row] - explained[row])
        for line in lines_of(scaled):
            for device in range(send_out.shape[0]):
                send_out[device, place] = line
            place += 1
        right = exact_dot_t(scaled, design[row])
        for device in range(row, send_out.shape[0], rows):
            send_out[device, send_out.shape[1] - 1] = right
    return params, explained


def first_kernel(received, target, design, partials, factor, weighted, source_id, send_out):
    last = received.shape[1] - 1
    targets = [
        target[row : row + 1] - exact_dot(received[row, last], design[row])
        for row in range(design.shape[0])
    ]
    residual_step(targets, design, partials, factor, weighted, source_id, send_out)


def second_kernel(
    pieces, picked, observed, design, partials, factor, weighted, source_id, send_out, params_out,
    explained_out,
):
    rows = design.shape[0]
    targets = [
        observed[row : row + 1] - exact_dot(pieces[row], design[row]) - picked[row : row + 1]
        for row in range(rows)
    ]
    params, explained = residual_step(
        targets, design, partials, factor, weighted, source_id, send_out
    )
    for index in range(5):
        params_out[index : index + 1] = params[index]
    for row in range(rows):
        explained_out[row : row + 1] = explained[row]


def inverse_kernel(relayed, inverse_out):
    rows = []
    for index in range(BAND):
        total = relayed[0, index]
        for device in range(1, relayed.shape[0]):
            total = total + relayed[device, index]
        rows.append(total)
    lower = unpack_band(jnp.concatenate(rows, axis=0))
    diagonal = iota(lower.shape, 0) == iota(lower.shape, 1)
    inverse_out[...] = spd_inverse(lower + jnp.where(diagonal, 1.0, lower.T))


def wide(row, count):
    tile = jnp.broadcast_to(row, (16, LANES)).astype(BF16)
    return jnp.concatenate([tile] * (count // 16), axis=0)


def unit_sums(relayed, line, value_of, total):
    groups = relayed.shape[0]
    count = (relayed.shape[1] - BAND) // (2 * line)
    low_row = iota((LANES, LANES), 0).astype(F32).astype(BF16)
    high_row = iota((HIGH, LANES), 0).astype(F32).astype(BF16)
    one, none = jnp.ones((), BF16), jnp.zeros((), BF16)
    for device in range(groups * line):
        group, member = device // line, device % line
        lefts, rights = [], []
        for index in range(count):
            unit = relayed[group, BAND + 2 * count * member + index]
            high = jnp.floor(unit * (1.0 / LANES))
            hit = low_row == wide(unit - LANES * high, LANES)
            value = value_of(group, member, index)
            first = value.astype(BF16).astype(F32)
            lefts.append(
                jnp.concatenate(
                    [
                        jnp.where(hit, wide(first, LANES), none),
                        jnp.where(hit, wide(value - first, LANES), none),
                    ],
                    axis=0,
                )
            )
            rights.append(jnp.where(high_row == wide(high, HIGH), one, none))
        found = dot_t(jnp.concatenate(lefts, axis=1), jnp.concatenate(rights, axis=1))
        if device == 0:
            total[...] = found[:LANES] + found[LANES:]
        else:
            total[...] += found[:LANES] + found[LANES:]


def scale_kernel(line, relayed, scale_out):
    count = (relayed.shape[1] - BAND) // (2 * line)
    unit_sums(
        relayed,
        line,
        lambda group, member, index: relayed[group, BAND + count * (2 * member + 1) + index],
        scale_out,
    )
    scale_out[...] = 1.0 / (scale_out[...] + 1.0)


def update_kernel(line, values, relayed, table, scale, cal_id, picked_out, table_out):
    unit_sums(
        relayed, line, lambda group, member, index: values[group * line + member, index], table_out
    )
    table_t = table[...] + table_out[...] * scale[...]
    table_out[...] = table_t
    for row, picked in enumerate(pick_from(table_t, cal_id[...])):
        picked_out[row : row + 1] = picked


def attitude_kernel(values, inverse, attitude, send_out, attitude_out):
    last = values.shape[1] - 1
    total = values[0, last]
    for device in range(1, values.shape[0]):
        total = total + values[device, last]
    line = attitude[...] + exact_dot(total, inverse[...])
    attitude_out[...] = line
    for target in range(send_out.shape[0]):
        send_out[target] = line


def final_kernel(pieces, picked, observed, design, explained, table, cal_out, resid_out):
    cal_out[...] = table[...].T
    for row in range(design.shape[0]):
        at = slice(row, row + 1)
        model = exact_dot(pieces[row], design[row])
        resid_out[at] = observed[at] - model - picked[at] - explained[at]


VMEM = pl.BlockSpec(memory_space=pltpu.VMEM)
ANY = pl.BlockSpec(memory_space=pltpu.HBM)


def call(kernel, outs, *args, away=0, scratch=()):
    near = args[: len(args) - away]
    far = [pltpu.with_memory_space_constraint(arg, pltpu.HBM) for arg in args[len(args) - away :]]
    return pl.pallas_call(
        kernel,
        out_shape=outs,
        in_specs=[VMEM] * len(near) + [ANY] * away,
        out_specs=[VMEM] * len(outs),
        scratch_shapes=scratch,
        compiler_params=pltpu.CompilerParams(vmem_limit_bytes=VMEM_BYTES),
    )(*near, *far)


def stay(*shape, dtype=F32):
    return pltpu.VMEM(shape, dtype)


def leave(*shape):
    return jax.ShapeDtypeStruct(shape, F32)


def exchange(value, axes):
    return lax.all_to_all(value, axes, 0, 0, tiled=True)


def body(
    observed, weight_obs, present, source_partials, attitude_partials, phase, knot_base, source_id,
    cal_id, attitude, calibration,
):
    rows, slots = observed.shape
    line, groups = lax.axis_size("tm"), lax.axis_size("src")
    devices = line * groups
    count = rows * slots // LANES
    everyone = ("src", "tm")
    first_q = attitude.reshape(1, WIDTH)
    held = [weight_obs, present, attitude_partials, phase, knot_base]
    send, design, weighted, seen, source_id, cal_id, source_partials, now = call(
        normals_kernel,
        [
            leave(rows, BAND + 2 * count + 1, 1, LANES), stay(rows, WIDTH, slots),
            stay(rows, slots), stay(rows, slots), stay(rows, slots, dtype=jnp.int32),
            stay(rows, slots, dtype=jnp.int32), stay(*source_partials.shape), stay(1, WIDTH),
        ],
        observed, weight_obs, present, source_partials, attitude_partials, phase, knot_base,
        source_id, cal_id, first_q,
        away=10,
        scratch=[pltpu.VMEM(each.shape, each.dtype) for each in held]
        + [pltpu.VMEM((rows, SUB, slots), F32), pltpu.SemaphoreType.DMA((10,))],
    )
    received = exchange(send, "tm")
    partials, factor, target, table = call(
        sources_kernel,
        [stay(rows, SUB, slots), stay(16, SRC_DEV), stay(rows, slots), stay(LANES, HIGH)],
        seen, source_partials, source_id, cal_id, weighted, calibration.reshape(HIGH, LANES),
        away=1,
        scratch=[pltpu.VMEM((HIGH, LANES), F32), pltpu.SemaphoreType.DMA],
    )
    (relayed,) = call(
        relay_kernel, [leave(groups, BAND + 2 * count * line, 1, LANES)], received
    )
    relayed, received = lax.optimization_barrier((relayed, received))
    relayed = exchange(relayed, "src")
    block = leave(devices, count + 1, 1, LANES)
    (values,) = call(
        first_kernel, [block], received, target, design, partials, factor, weighted, source_id
    )
    values = exchange(values, everyone)
    (inverse,) = call(inverse_kernel, [stay(WIDTH, WIDTH)], relayed)
    (scale,) = call(
        functools.partial(scale_kernel, line), [stay(LANES, HIGH)], relayed
    )

    def solve_attitude(values, now, out):
        return call(attitude_kernel, [leave(line, 1, WIDTH), out], values, inverse, now)

    def solve_units(values, table):
        return call(
            functools.partial(update_kernel, line),
            [stay(rows, slots), stay(LANES, HIGH)],
            values, relayed, table, scale, cal_id,
        )

    send, now = solve_attitude(values, now, stay(1, WIDTH))
    pieces = exchange(send, "tm")
    picked, table = solve_units(values, table)
    values, params, explained = call(
        second_kernel,
        [block, leave(5, SRC_DEV), stay(rows, slots)],
        pieces, picked, seen, design, partials, factor, weighted, source_id,
    )
    values = exchange(values, everyone)
    send, now = solve_attitude(values, now, leave(1, WIDTH))
    pieces = exchange(send, "tm")
    picked, table = solve_units(values, table)
    cal, final = call(
        final_kernel,
        [leave(HIGH, LANES), leave(rows, slots)],
        pieces, picked, seen, design, explained, table,
    )
    return (params, now.reshape(WIDTH), cal.reshape(CAL), final)


def solution(mesh):
    many = mesh.shape["src"] * mesh.shape["tm"]
    return jax.shard_map(
        body if many <= 64 else plain_body,
        mesh=mesh,
        in_specs=(
            P(None, ("src", "tm")),
            P(None, ("src", "tm")),
            P(None, ("src", "tm")),
            P(None, None, ("src", "tm")),
            P(None, None, ("src", "tm")),
            P(None, ("src", "tm")),
            P(None, ("src", "tm")),
            P(None, ("src", "tm")),
            P(None, ("src", "tm")),
            P("tm"),
            P(),
        ),
        out_specs=(P(None, ("src", "tm")), P("tm"), P(), P(None, ("src", "tm"))),
        check_vma=False,
    )
```

```python
import functools

import jax
import jax.numpy as jnp
from jax import lax
from jax.experimental import pallas as pl
from jax.experimental.pallas import tpu as pltpu
from jax.sharding import PartitionSpec as P

KNOTS_DEV = 32
WIDTH = 4 * KNOTS_DEV
SRC_DEV = 128
CAL = 32768
LANES = 128
HIGH = CAL // LANES
SUB = 8
VMEM_BYTES = 48 * 1024 * 1024

F32 = jnp.float32
BF16 = jnp.bfloat16
EXACT = lax.Precision.HIGHEST


def iota(shape, dim):
    return lax.broadcasted_iota(jnp.int32, shape, dim)


def split3(value):
    first = value.astype(BF16)
    rest = value - first.astype(F32)
    second = rest.astype(BF16)
    third = (rest - second.astype(F32)).astype(BF16)
    return first, second, third


def dot(left, right):
    return lax.dot_general(left, right, (((1,), (0,)), ((), ())), preferred_element_type=F32)


def dot_t(left, right):
    return lax.dot_general(left, right, (((1,), (1,)), ((), ())), preferred_element_type=F32)


def exact_dot(left, right):
    return lax.dot_general(
        left, right, (((1,), (0,)), ((), ())), precision=EXACT, preferred_element_type=F32
    )


def exact_dot_t(left, right):
    return lax.dot_general(
        left, right, (((1,), (1,)), ((), ())), precision=EXACT, preferred_element_type=F32
    )


def one_hot(ids, count):
    return jnp.where(iota((count, ids.shape[1]), 0) == ids, 1.0, 0.0).astype(BF16)


def flat(value):
    return jnp.concatenate([value[row : row + 1] for row in range(value.shape[0])], axis=1)


def unflat(value, rows):
    slots = value.shape[1] // rows
    return [value[:, row * slots : (row + 1) * slots] for row in range(rows)]


def cal_pick(table, ids):
    parts = jnp.concatenate(split3(table.T), axis=0)
    high = ids // LANES
    low = ids % LANES
    found = dot(parts, one_hot(high, HIGH))
    found = found[:LANES] + found[LANES : 2 * LANES] + found[2 * LANES :]
    return jnp.sum(jnp.where(iota(found.shape, 0) == low, found, 0.0), axis=0, keepdims=True)


def cal_sums(values, ids):
    high = one_hot(ids // LANES, HIGH)
    low = iota((LANES, ids.shape[1]), 0) == ids % LANES
    total = None
    for part in split3(values):
        spread = jnp.where(low, part.astype(F32), 0.0).astype(BF16)
        added = dot_t(high, spread)
        total = added if total is None else total + added
    return total


def design_of(base, basis, partials):
    slots = base.shape[1]
    knot = iota((WIDTH, slots), 0) // 4
    step = knot - base
    spread = jnp.zeros((WIDTH, slots), F32)
    for index in range(4):
        spread = jnp.where(step == index, basis[index], spread)
    return spread * jnp.concatenate([partials] * (WIDTH // 8), axis=0)


def band_shift(tile, knot):
    return ((tile % 8) * 16 - (8 * tile + 4 * knot - 12)) % WIDTH


def pack_band(normal):
    place = iota((8, WIDTH), 1) // 16
    upper = iota((8, WIDTH), 0) < 4
    groups = []
    for group in range(2):
        packed = jnp.zeros((8, WIDTH), F32)
        for tile in range(8 * group, 8 * group + 8):
            rows = normal[8 * tile : 8 * tile + 8]
            rolled = jnp.where(
                upper,
                pltpu.roll(rows, band_shift(tile, 0), 1),
                pltpu.roll(rows, band_shift(tile, 1), 1),
            )
            packed = jnp.where(place == tile % 8, rolled, packed)
        groups.append(packed)
    return jnp.concatenate(groups, axis=0)


def unpack_band(packed):
    place = iota((8, WIDTH), 1) // 16
    upper = iota((8, WIDTH), 0) < 4
    tiles = []
    for tile in range(16):
        group = tile // 8
        rows = jnp.where(place == tile % 8, packed[8 * group : 8 * group + 8], 0.0)
        tiles.append(
            jnp.where(
                upper,
                pltpu.roll(rows, (-band_shift(tile, 0)) % WIDTH, 1),
                pltpu.roll(rows, (-band_shift(tile, 1)) % WIDTH, 1),
            )
        )
    full = jnp.concatenate(tiles, axis=0)
    return jnp.where(iota(full.shape, 0) >= iota(full.shape, 1), full, 0.0)


def coefs(first, last):
    return list(range(4 * first, 4 * last + 4))


STAGES = (
    ((coefs(0, 4), (0, 3)), (coefs(8, 13), (2, 8)), (coefs(17, 22), (7, 12)), (coefs(26, 31), (11, 15))),
    ((coefs(5, 7), (0, 8)), (coefs(23, 25), (7, 15))),
    ((coefs(14, 16), (0, 15)),),
)


def spd_inverse(matrix, inverse_out):
    tiles = [matrix[8 * tile : 8 * tile + 8] for tile in range(WIDTH // 8)]
    lane = iota((8, WIDTH), 1)
    lane_row = iota((1, WIDTH), 1)
    row = iota((8, 1), 0)
    for stage in STAGES:
        for step in range(max(len(chain) for chain, reach in stage)):
            pivots = [(chain[step], reach) for chain, reach in stage if step < len(chain)]
            held = list(tiles)
            for pivot, (low, high) in pivots:
                at, sub = pivot // 8, pivot % 8
                line = held[at][sub : sub + 1]
                scale = 1.0 / line[:, pivot : pivot + 1]
                line = jnp.where(lane_row == pivot, -1.0, line) * scale
                for tile in range(low, high + 1):
                    column = held[tile][:, pivot : pivot + 1]
                    drop = lane == pivot
                    if tile == at:
                        column = jnp.where(row == sub, -1.0, column)
                        drop = drop | (iota((8, WIDTH), 0) == sub)
                    tiles[tile] = jnp.where(drop, 0.0, tiles[tile]) - column * line
            yield
    for tile, value in enumerate(tiles):
        inverse_out[8 * tile : 8 * tile + 8] = -value


def small_factor(sums):
    factor = {}
    for member in range(5):
        for column in range(member + 1):
            running = sums[8 * member + column : 8 * member + column + 1]
            if member == column:
                running = running + 1.0
            for offset in range(column):
                running = running - factor[member, offset] * factor[column, offset]
            if member == column:
                factor[member, member] = jnp.sqrt(running)
            else:
                factor[member, column] = running * inverse_of[column]
        inverse_of = {} if member == 0 else inverse_of
        inverse_of[member] = 1.0 / factor[member, member]
    inverse = {}
    for column in range(5):
        inverse[column, column] = inverse_of[column]
        for member in range(column + 1, 5):
            running = factor[member, column] * inverse[column, column]
            for offset in range(column + 1, member):
                running = running + factor[member, offset] * inverse[offset, column]
            inverse[member, column] = -running * inverse_of[member]
    return inverse


PLACES = [(row_id, col_id) for row_id in range(5) for col_id in range(row_id + 1)]


def small_apply(inverse, sides):
    forward = []
    for member in range(5):
        running = inverse[member, 0] * sides[0]
        for column in range(1, member + 1):
            running = running + inverse[member, column] * sides[column]
        forward.append(running)
    result = []
    for column in range(5):
        running = inverse[column, column] * forward[column]
        for member in range(column + 1, 5):
            running = running + inverse[member, column] * forward[member]
        result.append(running)
    return result


PAIRS = [(row_id, col_id) for row_id in range(5) for col_id in range(row_id + 1)]


def spline_terms(phase, attitude_partials):
    other = 1.0 - phase
    square = phase * phase
    cube = square * phase
    basis = [
        other * other * other / 6.0,
        (3.0 * cube - 6.0 * square + 4.0) / 6.0,
        (-3.0 * cube + 3.0 * square + 3.0 * phase + 1.0) / 6.0,
        cube / 6.0,
    ]
    return jnp.stack(
        [
            basis[knot_step] * attitude_partials[channel]
            for knot_step in range(4)
            for channel in range(4)
        ]
    )


def attitude_model(local, terms, knot_base):
    coefficients = lax.all_gather(local, "tm", axis=0, tiled=True)
    blocks, slots = knot_base.shape
    table = coefficients.reshape(blocks, -1, 4)
    knots_count = table.shape[1]
    grid = lax.broadcasted_iota(jnp.int32, (1, knots_count, 1), 1)
    running = jnp.zeros(knot_base.shape, jnp.float32)
    for knot_step in range(4):
        hit = (grid == (knot_base + knot_step)[:, None, :]).astype(jnp.float32)
        picked = jnp.einsum(
            "bkc,bks->bcs",
            table,
            hit,
            precision=lax.Precision.HIGHEST,
            preferred_element_type=jnp.float32,
        )
        for channel in range(4):
            running = running + terms[4 * knot_step + channel] * picked[:, channel, :]
    return running


def small_solve(matrix, right_side):
    extent = len(right_side)
    factor = {}
    for member in range(extent):
        for column in range(member + 1):
            running = matrix[member][column]
            for offset in range(column):
                running = running - factor[member, offset] * factor[column, offset]
            if member == column:
                factor[member, member] = jnp.sqrt(running)
            else:
                factor[member, column] = running / factor[column, column]
    forward = []
    for member in range(extent):
        running = right_side[member]
        for offset in range(member):
            running = running - factor[member, offset] * forward[offset]
        forward.append(running / factor[member, member])
    result = [None] * extent
    for member in reversed(range(extent)):
        running = forward[member]
        for offset in range(member + 1, extent):
            running = running - factor[offset, member] * result[offset]
        result[member] = running / factor[member, member]
    return jnp.stack(result)


def source_solve(ids, count, weighted, source_partials, target):
    products = [
        weighted * source_partials[row_id] * source_partials[col_id] for row_id, col_id in PAIRS
    ]
    products = products + [weighted * source_partials[row_id] * target for row_id in range(5)]
    stacked = jnp.moveaxis(jnp.stack(products), 1, 0)
    owners = lax.broadcasted_iota(jnp.int32, (count, 1), 0)

    def accumulate(total, item):
        values, block_ids = item
        hit = (block_ids[None, :] == owners).astype(jnp.float32)
        added = lax.dot_general(
            values,
            hit,
            (((1,), (1,)), ((), ())),
            precision=lax.Precision.HIGHEST,
            preferred_element_type=jnp.float32,
        )
        return (total + added, None)

    sums, unused = lax.scan(
        accumulate, jnp.zeros((len(products), count), jnp.float32), (stacked, ids)
    )
    entries = {}
    for position, pair in enumerate(PAIRS):
        entry_value = sums[position] + (1.0 if pair[0] == pair[1] else 0.0)
        entries[pair[0], pair[1]] = entry_value
        entries[pair[1], pair[0]] = entry_value
    matrix = [[entries[row_id, col_id] for col_id in range(5)] for row_id in range(5)]
    return small_solve(matrix, [sums[15 + row_id] for row_id in range(5)])


def pick_params(params, ids):
    count = params.shape[1]
    owners = lax.broadcasted_iota(jnp.int32, (count, 1), 0)

    def pick_single(carry, block_ids):
        hit = (block_ids[None, :] == owners).astype(jnp.float32)
        return (
            carry,
            jnp.dot(
                params, hit, precision=lax.Precision.HIGHEST, preferred_element_type=jnp.float32
            ),
        )

    unused, picked = lax.scan(pick_single, 0, ids)
    return jnp.moveaxis(picked, 1, 0)


def spd_solve(matrix, right_side):
    eye = jnp.eye(matrix.shape[-1], dtype=jnp.float32)
    lower = jnp.linalg.cholesky(matrix + eye)
    middle = lax.linalg.triangular_solve(lower, right_side[..., None], left_side=True, lower=True)
    result = lax.linalg.triangular_solve(
        lower, middle, left_side=True, lower=True, transpose_a=True
    )
    return result[..., 0]


def block_normals(terms, knot_base, weighted, resid):
    blocks, slots = knot_base.shape
    spread = jnp.moveaxis(terms.reshape(4, 4, blocks, slots), 2, 0)

    def block_single(item):
        part, base, weights, values = item
        grid = lax.broadcasted_iota(jnp.int32, (KNOTS_DEV, slots), 0)
        design = jnp.zeros((KNOTS_DEV, 4, slots), jnp.float32)
        for knot_step in range(4):
            hit = (grid == base[None, :] + knot_step).astype(jnp.float32)
            design = design + hit[:, None, :] * part[knot_step][None, :, :]
        design = design.reshape(KNOTS_DEV * 4, slots)
        normal = lax.dot_general(
            design * weights[None, :],
            design,
            (((1,), (1,)), ((), ())),
            precision=lax.Precision.HIGHEST,
            preferred_element_type=jnp.float32,
        )
        right = jnp.dot(
            design,
            weights * values,
            precision=lax.Precision.HIGHEST,
            preferred_element_type=jnp.float32,
        )
        return (normal, right)

    return lax.map(block_single, (spread, knot_base, weighted, resid))


def plain_body(
    observed,
    weight_obs,
    present,
    source_partials,
    attitude_partials,
    phase,
    knot_base,
    source_id,
    cal_id,
    attitude,
    calibration,
):
    weighted = present.astype(jnp.float32) * weight_obs
    terms = spline_terms(phase, attitude_partials)
    flat_cal = cal_id.reshape(-1)
    local = attitude
    cal_now = calibration
    params = jnp.zeros((5, SRC_DEV), jnp.float32)
    for sweep in range(2):
        target = observed - attitude_model(local, terms, knot_base) - cal_now[cal_id]
        params = source_solve(source_id, SRC_DEV, weighted, source_partials, target)
        resid = target - jnp.sum(source_partials * pick_params(params, source_id), axis=0)
        normals, rights = block_normals(terms, knot_base, weighted, resid)
        normal, right = (
            lax.psum_scatter(normals, "tm", scatter_dimension=0, tiled=True),
            lax.psum_scatter(rights, "tm", scatter_dimension=0, tiled=True),
        )
        normal, right = lax.psum((normal[0], right[0]), "src")
        local = local + spd_solve(normal, right)
        numer = jax.ops.segment_sum((weighted * resid).reshape(-1), flat_cal, num_segments=CAL)
        denom = jax.ops.segment_sum(weighted.reshape(-1), flat_cal, num_segments=CAL)
        numer, denom = lax.psum((numer, denom), ("src", "tm"))
        cal_now = cal_now + numer / (denom + 1.0)
    final = observed - attitude_model(local, terms, knot_base) - cal_now[cal_id]
    final = final - jnp.sum(source_partials * pick_params(params, source_id), axis=0)
    return (params, local, cal_now, final)


BAND = 16
PIECE = 2


def fetch(pairs, sems):
    copies = [
        pltpu.make_async_copy(origin, held, sems.at[place])
        for place, (origin, held) in enumerate(pairs)
    ]
    for copy in copies:
        copy.start()
    for copy in copies:
        copy.wait()


def tile_of(value):
    return jnp.concatenate(
        [value[:, at : at + LANES] for at in range(0, value.shape[1], LANES)], axis=0
    )


def pick_from(table_t, ids):
    rows = ids.shape[0]
    ids = flat(ids)
    found = dot(jnp.concatenate(split3(table_t), axis=0), one_hot(ids // LANES, HIGH))
    found = found[:LANES] + found[LANES : 2 * LANES] + found[2 * LANES :]
    hit = iota(found.shape, 0) == ids % LANES
    return unflat(jnp.sum(jnp.where(hit, found, 0.0), axis=0, keepdims=True), rows)


def normals_kernel(
    observed_in, weight_in, present_in, source_in, attitude_in, phase_in, knot_in, id_in, cal_in,
    start_in,
    send_out, design_out, weighted_out, observed, source_id, cal_id, source_partials,
    weight_obs, present, attitude_partials, phase, knot_base, start, stacked, sems,
):
    fetch(
        [
            (observed_in, observed), (weight_in, weight_obs), (present_in, present),
            (source_in, source_partials), (attitude_in, attitude_partials), (phase_in, phase),
            (knot_in, knot_base), (id_in, source_id), (cal_in, cal_id), (start_in, start),
        ],
        sems,
    )
    rows, slots = observed.shape
    weighted = present[...].astype(F32) * weight_obs[...]
    weighted_out[...] = weighted
    u = phase[...]
    other = 1.0 - u
    square = u * u
    cube = square * u
    basis = [
        other * other * other / 6.0,
        (3.0 * cube - 6.0 * square + 4.0) / 6.0,
        (-3.0 * cube + 3.0 * square + 3.0 * u + 1.0) / 6.0,
        cube / 6.0,
    ]
    first, second = tile_of(cal_id[...].astype(F32)), tile_of(weighted)
    count = first.shape[0]
    devices = send_out.shape[0]
    for index in range(count):
        for device in range(devices):
            send_out[device, PIECE + index] = first[index : index + 1]
            send_out[device, PIECE + count + index] = second[index : index + 1]
    for device in range(devices):
        send_out[device, PIECE + 2 * count] = start[...]
    for row in range(rows):
        at = slice(row, row + 1)
        for channel in range(4):
            lines = attitude_partials[channel, at]
            stacked[row, channel : channel + 1] = lines
            stacked[row, channel + 4 : channel + 5] = lines
        design = design_of(knot_base[at], [part[at] for part in basis], stacked[row])
        design_out[row] = design
        band = pack_band(exact_dot_t(design * weighted[at], design))
        for index in range(BAND):
            device, place = divmod(row * BAND + index, PIECE)
            send_out[device, place] = band[index : index + 1]


def sources_kernel(
    observed, source_partials, source_id, cal_id, weighted, calibration,
    partials_out, factor_out, target_out, table_out, table, sem,
):
    copy = pltpu.make_async_copy(calibration, table, sem)
    copy.start()
    rows, slots = observed.shape
    matrix = jnp.zeros((40, SRC_DEV), F32)
    for row in range(rows):
        at = slice(row, row + 1)
        for index in range(5):
            partials_out[row, index : index + 1] = source_partials[index, at]
        partials_out[row, 5:] = jnp.zeros((SUB - 5, slots), F32)
        partials = partials_out[row]
        products = jnp.concatenate(
            [partials * (weighted[at] * partials[index : index + 1]) for index in range(5)], axis=0
        )
        found = dot_t(jnp.concatenate(split3(products), axis=0), one_hot(source_id[at], SRC_DEV))
        matrix = matrix + found[:40] + found[40:80] + found[80:]
    inverse = small_factor(matrix)
    for place, pair in enumerate(PLACES):
        factor_out[place : place + 1] = inverse[pair]
    factor_out[15:16] = jnp.zeros((1, SRC_DEV), F32)
    copy.wait()
    table_t = table[...].T
    table_out[...] = table_t
    for row, picked in enumerate(pick_from(table_t, cal_id[...])):
        target_out[row : row + 1] = observed[row : row + 1] - picked


def residual_step(targets, design, partials, factor, weighted, source_id, send_out):
    rows, slots = len(targets), targets[0].shape[1]
    count = rows * slots // LANES
    hits = [one_hot(source_id[row : row + 1], SRC_DEV) for row in range(rows)]
    inverse = {pair: factor[place : place + 1] for place, pair in enumerate(PLACES)}
    sides = jnp.zeros((SUB, SRC_DEV), F32)
    for row in range(rows):
        products = partials[row] * (weighted[row : row + 1] * targets[row])
        found = dot_t(jnp.concatenate(split3(products), axis=0), hits[row])
        sides = sides + found[:SUB] + found[SUB : 2 * SUB] + found[2 * SUB :]
    params = small_apply(inverse, [sides[index : index + 1] for index in range(5)])
    table = jnp.concatenate(params + [jnp.zeros((3, SRC_DEV), F32)], axis=0)
    parts = jnp.concatenate(split3(table), axis=0)
    explained = []
    for row in range(rows):
        found = dot(parts, hits[row])
        found = found[:SUB] + found[SUB : 2 * SUB] + found[2 * SUB :]
        explained.append(jnp.sum(found * partials[row], axis=0, keepdims=True))
        scaled = weighted[row : row + 1] * (targets[row] - explained[row])
        for place in range(slots // LANES):
            for device in range(send_out.shape[0]):
                send_out[device, place * rows + row] = scaled[:, place * LANES : (place + 1) * LANES]
        right = exact_dot_t(scaled, design[row])
        for device in range(send_out.shape[0]):
            send_out[device, count + row] = right
    return params, explained


def first_kernel(received, target, design, partials, factor, weighted, source_id, send_out):
    rows = design.shape[0]
    last = received.shape[1] - 1
    targets = [
        target[row : row + 1] - exact_dot(received[row, last], design[row]) for row in range(rows)
    ]
    residual_step(targets, design, partials, factor, weighted, source_id, send_out)
    for place in range(PIECE):
        total = received[0, place]
        for device in range(1, received.shape[0]):
            total = total + received[device, place]
        for device in range(send_out.shape[0]):
            send_out[device, send_out.shape[1] - PIECE + place] = total


def wide(row, count):
    tile = jnp.broadcast_to(row, (16, LANES)).astype(BF16)
    return jnp.concatenate([tile] * (count // 16), axis=0)


def unit_sums(received, value_of, total):
    count = (received.shape[1] - PIECE - 1) // 2
    low_row = iota((LANES, LANES), 0).astype(F32).astype(BF16)
    high_row = iota((HIGH, LANES), 0).astype(F32).astype(BF16)
    one, none = jnp.ones((), BF16), jnp.zeros((), BF16)
    for device in range(received.shape[0]):
        lefts, rights = [], []
        for index in range(count):
            unit = received[device, PIECE + index]
            high = jnp.floor(unit * (1.0 / LANES))
            hit = low_row == wide(unit - LANES * high, LANES)
            value = value_of(device, index)
            first = value.astype(BF16).astype(F32)
            lefts.append(
                jnp.concatenate(
                    [
                        jnp.where(hit, wide(first, LANES), none),
                        jnp.where(hit, wide(value - first, LANES), none),
                    ],
                    axis=0,
                )
            )
            rights.append(jnp.where(high_row == wide(high, HIGH), one, none))
        found = dot_t(jnp.concatenate(lefts, axis=1), jnp.concatenate(rights, axis=1))
        if device == 0:
            total[...] = found[:LANES] + found[LANES:]
        else:
            total[...] += found[:LANES] + found[LANES:]
        yield


def matrix_of(band):
    lower = unpack_band(band)
    diagonal = iota(lower.shape, 0) == iota(lower.shape, 1)
    return lower + jnp.where(diagonal, 1.0, lower.T)


def together(works):
    works = list(works)
    while works:
        for work in list(works):
            if next(work, works) is works:
                works.remove(work)


def scale_kernel(received, scale_out):
    count = (received.shape[1] - PIECE - 1) // 2
    together(
        [
            unit_sums(
                received,
                lambda device, index: received[device, PIECE + count + index],
                scale_out,
            )
        ]
    )
    scale_out[...] = 1.0 / (scale_out[...] + 1.0)


def right_side(values, place):
    total = values[0, place]
    for device in range(1, values.shape[0]):
        total = total + values[device, place]
    return total


def second_kernel(
    values, received, table, scale, cal_id, observed, design, partials, factor, weighted, source_id,
    send_out, params_out, explained_out, table_out, attitude_out, inverses_out, bands,
):
    rows = design.shape[0]
    count = values.shape[1] - rows - PIECE
    for device in range(values.shape[0]):
        for place in range(PIECE):
            at = PIECE * device + place
            bands[at : at + 1] = values[device, count + rows + place]
    together(
        [unit_sums(received, lambda device, index: values[device, index], table_out)]
        + [
            spd_inverse(
                matrix_of(bands[BAND * row : BAND * (row + 1)]), inverses_out.at[row]
            )
            for row in range(rows)
        ]
    )
    table_t = table[...] + table_out[...] * scale[...]
    table_out[...] = table_t
    targets = []
    for row, picked in enumerate(pick_from(table_t, cal_id[...])):
        new = received[row, received.shape[1] - 1] + exact_dot(
            right_side(values, count + row), inverses_out[row]
        )
        attitude_out[row : row + 1] = new
        targets.append(observed[row : row + 1] - exact_dot(new, design[row]) - picked)
    params, explained = residual_step(
        targets, design, partials, factor, weighted, source_id, send_out
    )
    for index in range(5):
        params_out[index : index + 1] = params[index]
    for row in range(rows):
        explained_out[row : row + 1] = explained[row]


def final_kernel(
    axis, values, received, inverses, attitude, table, scale, cal_id, observed, design, explained,
    cal_out, attitude_out, resid_out, sums,
):
    rows = design.shape[0]
    count = values.shape[1] - rows
    me = lax.axis_index(axis)
    models = []
    for row in range(rows):
        new = attitude[row : row + 1] + exact_dot(right_side(values, count + row), inverses[row])
        models.append(exact_dot(new, design[row]))
        own = new if row == 0 else jnp.where(me == row, new, own)
    attitude_out[...] = own
    together([unit_sums(received, lambda device, index: values[device, index], sums)])
    table_t = table[...] + sums[...] * scale[...]
    cal_out[...] = table_t.T
    for row, picked in enumerate(pick_from(table_t, cal_id[...])):
        at = slice(row, row + 1)
        resid_out[at] = observed[at] - models[row] - picked - explained[at]


VMEM = pl.BlockSpec(memory_space=pltpu.VMEM)
ANY = pl.BlockSpec(memory_space=pltpu.HBM)


def call(kernel, outs, *args, away=0, scratch=()):
    near = args[: len(args) - away]
    far = [pltpu.with_memory_space_constraint(arg, pltpu.HBM) for arg in args[len(args) - away :]]
    return pl.pallas_call(
        kernel,
        out_shape=outs,
        in_specs=[VMEM] * len(near) + [ANY] * away,
        out_specs=[VMEM] * len(outs),
        scratch_shapes=scratch,
        compiler_params=pltpu.CompilerParams(vmem_limit_bytes=VMEM_BYTES),
    )(*near, *far)


def stay(*shape, dtype=F32):
    return pltpu.VMEM(shape, dtype)


def leave(*shape):
    return jax.ShapeDtypeStruct(shape, F32)


def exchange(value):
    return lax.all_to_all(value, ("src", "tm"), 0, 0, tiled=True)


def body(
    observed, weight_obs, present, source_partials, attitude_partials, phase, knot_base, source_id,
    cal_id, attitude, calibration,
):
    rows, slots = observed.shape
    devices = lax.axis_size("src") * lax.axis_size("tm")
    count = rows * slots // LANES
    first_q = attitude.reshape(1, WIDTH)
    held = [weight_obs, present, attitude_partials, phase, knot_base, first_q]
    received, design, weighted, seen, source_id, cal_id, source_partials = call(
        normals_kernel,
        [
            leave(devices, PIECE + 2 * count + 1, 1, LANES), stay(rows, WIDTH, slots),
            stay(rows, slots), stay(rows, slots), stay(rows, slots, dtype=jnp.int32),
            stay(rows, slots, dtype=jnp.int32), stay(*source_partials.shape),
        ],
        observed, weight_obs, present, source_partials, attitude_partials, phase, knot_base,
        source_id, cal_id, first_q,
        away=10,
        scratch=[pltpu.VMEM(each.shape, each.dtype) for each in held]
        + [pltpu.VMEM((rows, SUB, slots), F32), pltpu.SemaphoreType.DMA((10,))],
    )
    received = exchange(received)
    partials, factor, target, table = call(
        sources_kernel,
        [stay(rows, SUB, slots), stay(16, SRC_DEV), stay(rows, slots), stay(LANES, HIGH)],
        seen, source_partials, source_id, cal_id, weighted, calibration.reshape(HIGH, LANES),
        away=1,
        scratch=[pltpu.VMEM((HIGH, LANES), F32), pltpu.SemaphoreType.DMA],
    )
    received, factor = lax.optimization_barrier((received, factor))
    (values,) = call(
        first_kernel, [leave(devices, count + rows + PIECE, 1, LANES)],
        received, target, design, partials, factor, weighted, source_id,
    )
    values, received = lax.optimization_barrier((values, received))
    values = exchange(values)
    (scale,) = call(scale_kernel, [stay(LANES, HIGH)], received)
    values, params, explained, table, now, inverses = call(
        second_kernel,
        [
            leave(devices, count + rows, 1, LANES), leave(5, SRC_DEV), stay(rows, slots),
            stay(LANES, HIGH), stay(rows, WIDTH), stay(rows, WIDTH, WIDTH),
        ],
        values, received, table, scale, cal_id, seen, design, partials, factor, weighted, source_id,
        scratch=[pltpu.VMEM((rows * BAND, WIDTH), F32)],
    )
    values = exchange(values)
    cal, now, final = call(
        functools.partial(final_kernel, "tm"),
        [leave(HIGH, LANES), leave(1, WIDTH), leave(rows, slots)],
        values, received, inverses, now, table, scale, cal_id, seen, design, explained,
        scratch=[pltpu.VMEM((LANES, HIGH), F32)],
    )
    return (params, now.reshape(WIDTH), cal.reshape(CAL), final)


def solution(mesh):
    many = mesh.shape["src"] * mesh.shape["tm"]
    return jax.shard_map(
        body if many * PIECE == mesh.shape["tm"] * BAND else plain_body,
        mesh=mesh,
        in_specs=(
            P(None, ("src", "tm")),
            P(None, ("src", "tm")),
            P(None, ("src", "tm")),
            P(None, None, ("src", "tm")),
            P(None, None, ("src", "tm")),
            P(None, ("src", "tm")),
            P(None, ("src", "tm")),
            P(None, ("src", "tm")),
            P(None, ("src", "tm")),
            P("tm"),
            P(),
        ),
        out_specs=(P(None, ("src", "tm")), P("tm"), P(), P(None, ("src", "tm"))),
        check_vma=False,
    )
```

```python
import functools

import jax
import jax.numpy as jnp
from jax import lax
from jax.experimental import pallas as pl
from jax.experimental.pallas import tpu as pltpu
from jax.sharding import PartitionSpec as P

KNOTS_DEV = 32
WIDTH = 4 * KNOTS_DEV
SRC_DEV = 128
CAL = 32768
LANES = 128
HIGH = CAL // LANES
SUB = 8
VMEM_BYTES = 48 * 1024 * 1024

F32 = jnp.float32
BF16 = jnp.bfloat16
EXACT = lax.Precision.HIGHEST


def iota(shape, dim):
    return lax.broadcasted_iota(jnp.int32, shape, dim)


def split3(value):
    first = value.astype(BF16)
    rest = value - first.astype(F32)
    second = rest.astype(BF16)
    third = (rest - second.astype(F32)).astype(BF16)
    return first, second, third


def dot(left, right):
    return lax.dot_general(left, right, (((1,), (0,)), ((), ())), preferred_element_type=F32)


def dot_t(left, right):
    return lax.dot_general(left, right, (((1,), (1,)), ((), ())), preferred_element_type=F32)


def exact_dot(left, right):
    return lax.dot_general(
        left, right, (((1,), (0,)), ((), ())), precision=EXACT, preferred_element_type=F32
    )


def exact_dot_t(left, right):
    return lax.dot_general(
        left, right, (((1,), (1,)), ((), ())), precision=EXACT, preferred_element_type=F32
    )


def one_hot(ids, count):
    return jnp.where(iota((count, ids.shape[1]), 0) == ids, 1.0, 0.0).astype(BF16)


def flat(value):
    return jnp.concatenate([value[row : row + 1] for row in range(value.shape[0])], axis=1)


def unflat(value, rows):
    slots = value.shape[1] // rows
    return [value[:, row * slots : (row + 1) * slots] for row in range(rows)]


def cal_pick(table, ids):
    parts = jnp.concatenate(split3(table.T), axis=0)
    high = ids // LANES
    low = ids % LANES
    found = dot(parts, one_hot(high, HIGH))
    found = found[:LANES] + found[LANES : 2 * LANES] + found[2 * LANES :]
    return jnp.sum(jnp.where(iota(found.shape, 0) == low, found, 0.0), axis=0, keepdims=True)


def cal_sums(values, ids):
    high = one_hot(ids // LANES, HIGH)
    low = iota((LANES, ids.shape[1]), 0) == ids % LANES
    total = None
    for part in split3(values):
        spread = jnp.where(low, part.astype(F32), 0.0).astype(BF16)
        added = dot_t(high, spread)
        total = added if total is None else total + added
    return total


def design_of(base, basis, partials):
    slots = base.shape[1]
    knot = iota((WIDTH, slots), 0) // 4
    step = knot - base
    spread = jnp.zeros((WIDTH, slots), F32)
    for index in range(4):
        spread = jnp.where(step == index, basis[index], spread)
    return spread * jnp.concatenate([partials] * (WIDTH // 8), axis=0)


def band_shift(tile, knot):
    return ((tile % 8) * 16 - (8 * tile + 4 * knot - 12)) % WIDTH


def pack_band(normal):
    place = iota((8, WIDTH), 1) // 16
    upper = iota((8, WIDTH), 0) < 4
    groups = []
    for group in range(2):
        packed = jnp.zeros((8, WIDTH), F32)
        for tile in range(8 * group, 8 * group + 8):
            rows = normal[8 * tile : 8 * tile + 8]
            rolled = jnp.where(
                upper,
                pltpu.roll(rows, band_shift(tile, 0), 1),
                pltpu.roll(rows, band_shift(tile, 1), 1),
            )
            packed = jnp.where(place == tile % 8, rolled, packed)
        groups.append(packed)
    return jnp.concatenate(groups, axis=0)


def unpack_band(packed):
    place = iota((8, WIDTH), 1) // 16
    upper = iota((8, WIDTH), 0) < 4
    tiles = []
    for tile in range(16):
        group = tile // 8
        rows = jnp.where(place == tile % 8, packed[8 * group : 8 * group + 8], 0.0)
        tiles.append(
            jnp.where(
                upper,
                pltpu.roll(rows, (-band_shift(tile, 0)) % WIDTH, 1),
                pltpu.roll(rows, (-band_shift(tile, 1)) % WIDTH, 1),
            )
        )
    full = jnp.concatenate(tiles, axis=0)
    return jnp.where(iota(full.shape, 0) >= iota(full.shape, 1), full, 0.0)


def knots(first, last):
    return list(range(first, last + 1))


STAGES = (
    ((knots(0, 4), (0, 3)), (knots(8, 13), (2, 8)), (knots(17, 22), (7, 12)), (knots(26, 31), (11, 15))),
    ((knots(5, 7), (0, 8)), (knots(23, 25), (7, 15))),
    ((knots(14, 16), (0, 15)),),
)


def block_rows(entry, lines):
    scale = 1.0 / (entry[0, 0] * entry[1, 1] - entry[0, 1] * entry[0, 1])
    low, mid, high = entry[0, 0] * scale, entry[0, 1] * scale, entry[1, 1] * scale
    turned = {}
    for column in (2, 3):
        turned[0, column] = high * entry[0, column] - mid * entry[1, column]
        turned[1, column] = low * entry[1, column] - mid * entry[0, column]
    rest = {}
    for row, column in ((2, 2), (2, 3), (3, 3)):
        taken = entry[0, row] * turned[0, column] + entry[1, row] * turned[1, column]
        rest[row, column] = entry[row, column] - taken
    upper = [high * lines[0] - mid * lines[1], low * lines[1] - mid * lines[0]]
    lower = [
        lines[row] - (entry[0, row] * upper[0] + entry[1, row] * upper[1]) for row in (2, 3)
    ]
    scale = 1.0 / (rest[2, 2] * rest[3, 3] - rest[2, 3] * rest[2, 3])
    third = (rest[3, 3] * scale) * lower[0] - (rest[2, 3] * scale) * lower[1]
    fourth = (rest[2, 2] * scale) * lower[1] - (rest[2, 3] * scale) * lower[0]
    return [
        upper[0] - (turned[0, 2] * third + turned[0, 3] * fourth),
        upper[1] - (turned[1, 2] * third + turned[1, 3] * fourth),
        third,
        fourth,
    ]


def spd_inverse(matrix, inverse_out):
    shape = (8, WIDTH)
    tiles = [matrix[8 * tile : 8 * tile + 8] for tile in range(WIDTH // 8)]
    lane, row = iota(shape, 1), iota(shape, 0)
    for stage in STAGES:
        for step in range(max(len(chain) for chain, reach in stage)):
            pivots = [(chain[step], reach) for chain, reach in stage if step < len(chain)]
            held = list(tiles)
            for knot, (low, high) in pivots:
                at, sub, first = knot // 2, 4 * (knot % 2), 4 * knot
                inside = lane // 4 == knot
                columns = {
                    tile: [
                        jnp.broadcast_to(held[tile][:, first + index : first + index + 1], shape)
                        for index in range(4)
                    ]
                    for tile in range(low, high + 1)
                }
                entry = {
                    (one, two): jnp.broadcast_to(
                        columns[at][two][sub + one : sub + one + 1], shape
                    )
                    for one in range(4)
                    for two in range(one, 4)
                }
                lines = [
                    jnp.where(
                        inside,
                        jnp.where(lane == first + index, -1.0, 0.0),
                        jnp.broadcast_to(held[at][sub + index : sub + index + 1], shape),
                    )
                    for index in range(4)
                ]
                lines = block_rows(entry, lines)
                for tile in range(low, high + 1):
                    drop, factors = inside, columns[tile]
                    if tile == at:
                        drop = drop | (row // 4 == knot % 2)
                        factors = [
                            jnp.where(
                                row // 4 == knot % 2,
                                jnp.where(row == sub + index, -1.0, 0.0),
                                factors[index],
                            )
                            for index in range(4)
                        ]
                    taken = factors[0] * lines[0] + factors[1] * lines[1]
                    taken = taken + (factors[2] * lines[2] + factors[3] * lines[3])
                    tiles[tile] = jnp.where(drop, 0.0, tiles[tile]) - taken
            yield
    for tile, value in enumerate(tiles):
        inverse_out[8 * tile : 8 * tile + 8] = -value


def small_factor(sums):
    factor = {}
    for member in range(5):
        for column in range(member + 1):
            running = sums[8 * member + column : 8 * member + column + 1]
            if member == column:
                running = running + 1.0
            for offset in range(column):
                running = running - factor[member, offset] * factor[column, offset]
            if member == column:
                factor[member, member] = jnp.sqrt(running)
            else:
                factor[member, column] = running * inverse_of[column]
        inverse_of = {} if member == 0 else inverse_of
        inverse_of[member] = 1.0 / factor[member, member]
    inverse = {}
    for column in range(5):
        inverse[column, column] = inverse_of[column]
        for member in range(column + 1, 5):
            running = factor[member, column] * inverse[column, column]
            for offset in range(column + 1, member):
                running = running + factor[member, offset] * inverse[offset, column]
            inverse[member, column] = -running * inverse_of[member]
    return inverse


PLACES = [(row_id, col_id) for row_id in range(5) for col_id in range(row_id + 1)]


def small_apply(inverse, sides):
    forward = []
    for member in range(5):
        running = inverse[member, 0] * sides[0]
        for column in range(1, member + 1):
            running = running + inverse[member, column] * sides[column]
        forward.append(running)
    result = []
    for column in range(5):
        running = inverse[column, column] * forward[column]
        for member in range(column + 1, 5):
            running = running + inverse[member, column] * forward[member]
        result.append(running)
    return result


PAIRS = [(row_id, col_id) for row_id in range(5) for col_id in range(row_id + 1)]


def spline_terms(phase, attitude_partials):
    other = 1.0 - phase
    square = phase * phase
    cube = square * phase
    basis = [
        other * other * other / 6.0,
        (3.0 * cube - 6.0 * square + 4.0) / 6.0,
        (-3.0 * cube + 3.0 * square + 3.0 * phase + 1.0) / 6.0,
        cube / 6.0,
    ]
    return jnp.stack(
        [
            basis[knot_step] * attitude_partials[channel]
            for knot_step in range(4)
            for channel in range(4)
        ]
    )


def attitude_model(local, terms, knot_base):
    coefficients = lax.all_gather(local, "tm", axis=0, tiled=True)
    blocks, slots = knot_base.shape
    table = coefficients.reshape(blocks, -1, 4)
    knots_count = table.shape[1]
    grid = lax.broadcasted_iota(jnp.int32, (1, knots_count, 1), 1)
    running = jnp.zeros(knot_base.shape, jnp.float32)
    for knot_step in range(4):
        hit = (grid == (knot_base + knot_step)[:, None, :]).astype(jnp.float32)
        picked = jnp.einsum(
            "bkc,bks->bcs",
            table,
            hit,
            precision=lax.Precision.HIGHEST,
            preferred_element_type=jnp.float32,
        )
        for channel in range(4):
            running = running + terms[4 * knot_step + channel] * picked[:, channel, :]
    return running


def small_solve(matrix, right_side):
    extent = len(right_side)
    factor = {}
    for member in range(extent):
        for column in range(member + 1):
            running = matrix[member][column]
            for offset in range(column):
                running = running - factor[member, offset] * factor[column, offset]
            if member == column:
                factor[member, member] = jnp.sqrt(running)
            else:
                factor[member, column] = running / factor[column, column]
    forward = []
    for member in range(extent):
        running = right_side[member]
        for offset in range(member):
            running = running - factor[member, offset] * forward[offset]
        forward.append(running / factor[member, member])
    result = [None] * extent
    for member in reversed(range(extent)):
        running = forward[member]
        for offset in range(member + 1, extent):
            running = running - factor[offset, member] * result[offset]
        result[member] = running / factor[member, member]
    return jnp.stack(result)


def source_solve(ids, count, weighted, source_partials, target):
    products = [
        weighted * source_partials[row_id] * source_partials[col_id] for row_id, col_id in PAIRS
    ]
    products = products + [weighted * source_partials[row_id] * target for row_id in range(5)]
    stacked = jnp.moveaxis(jnp.stack(products), 1, 0)
    owners = lax.broadcasted_iota(jnp.int32, (count, 1), 0)

    def accumulate(total, item):
        values, block_ids = item
        hit = (block_ids[None, :] == owners).astype(jnp.float32)
        added = lax.dot_general(
            values,
            hit,
            (((1,), (1,)), ((), ())),
            precision=lax.Precision.HIGHEST,
            preferred_element_type=jnp.float32,
        )
        return (total + added, None)

    sums, unused = lax.scan(
        accumulate, jnp.zeros((len(products), count), jnp.float32), (stacked, ids)
    )
    entries = {}
    for position, pair in enumerate(PAIRS):
        entry_value = sums[position] + (1.0 if pair[0] == pair[1] else 0.0)
        entries[pair[0], pair[1]] = entry_value
        entries[pair[1], pair[0]] = entry_value
    matrix = [[entries[row_id, col_id] for col_id in range(5)] for row_id in range(5)]
    return small_solve(matrix, [sums[15 + row_id] for row_id in range(5)])


def pick_params(params, ids):
    count = params.shape[1]
    owners = lax.broadcasted_iota(jnp.int32, (count, 1), 0)

    def pick_single(carry, block_ids):
        hit = (block_ids[None, :] == owners).astype(jnp.float32)
        return (
            carry,
            jnp.dot(
                params, hit, precision=lax.Precision.HIGHEST, preferred_element_type=jnp.float32
            ),
        )

    unused, picked = lax.scan(pick_single, 0, ids)
    return jnp.moveaxis(picked, 1, 0)


def spd_solve(matrix, right_side):
    eye = jnp.eye(matrix.shape[-1], dtype=jnp.float32)
    lower = jnp.linalg.cholesky(matrix + eye)
    middle = lax.linalg.triangular_solve(lower, right_side[..., None], left_side=True, lower=True)
    result = lax.linalg.triangular_solve(
        lower, middle, left_side=True, lower=True, transpose_a=True
    )
    return result[..., 0]


def block_normals(terms, knot_base, weighted, resid):
    blocks, slots = knot_base.shape
    spread = jnp.moveaxis(terms.reshape(4, 4, blocks, slots), 2, 0)

    def block_single(item):
        part, base, weights, values = item
        grid = lax.broadcasted_iota(jnp.int32, (KNOTS_DEV, slots), 0)
        design = jnp.zeros((KNOTS_DEV, 4, slots), jnp.float32)
        for knot_step in range(4):
            hit = (grid == base[None, :] + knot_step).astype(jnp.float32)
            design = design + hit[:, None, :] * part[knot_step][None, :, :]
        design = design.reshape(KNOTS_DEV * 4, slots)
        normal = lax.dot_general(
            design * weights[None, :],
            design,
            (((1,), (1,)), ((), ())),
            precision=lax.Precision.HIGHEST,
            preferred_element_type=jnp.float32,
        )
        right = jnp.dot(
            design,
            weights * values,
            precision=lax.Precision.HIGHEST,
            preferred_element_type=jnp.float32,
        )
        return (normal, right)

    return lax.map(block_single, (spread, knot_base, weighted, resid))


def plain_body(
    observed,
    weight_obs,
    present,
    source_partials,
    attitude_partials,
    phase,
    knot_base,
    source_id,
    cal_id,
    attitude,
    calibration,
):
    weighted = present.astype(jnp.float32) * weight_obs
    terms = spline_terms(phase, attitude_partials)
    flat_cal = cal_id.reshape(-1)
    local = attitude
    cal_now = calibration
    params = jnp.zeros((5, SRC_DEV), jnp.float32)
    for sweep in range(2):
        target = observed - attitude_model(local, terms, knot_base) - cal_now[cal_id]
        params = source_solve(source_id, SRC_DEV, weighted, source_partials, target)
        resid = target - jnp.sum(source_partials * pick_params(params, source_id), axis=0)
        normals, rights = block_normals(terms, knot_base, weighted, resid)
        normal, right = (
            lax.psum_scatter(normals, "tm", scatter_dimension=0, tiled=True),
            lax.psum_scatter(rights, "tm", scatter_dimension=0, tiled=True),
        )
        normal, right = lax.psum((normal[0], right[0]), "src")
        local = local + spd_solve(normal, right)
        numer = jax.ops.segment_sum((weighted * resid).reshape(-1), flat_cal, num_segments=CAL)
        denom = jax.ops.segment_sum(weighted.reshape(-1), flat_cal, num_segments=CAL)
        numer, denom = lax.psum((numer, denom), ("src", "tm"))
        cal_now = cal_now + numer / (denom + 1.0)
    final = observed - attitude_model(local, terms, knot_base) - cal_now[cal_id]
    final = final - jnp.sum(source_partials * pick_params(params, source_id), axis=0)
    return (params, local, cal_now, final)


BAND = 16
PIECE = 2


def fetch(pairs, sems):
    copies = [
        pltpu.make_async_copy(origin, held, sems.at[place])
        for place, (origin, held) in enumerate(pairs)
    ]
    for copy in copies:
        copy.start()
    for copy in copies:
        copy.wait()


def tile_of(value):
    return jnp.concatenate(
        [value[:, at : at + LANES] for at in range(0, value.shape[1], LANES)], axis=0
    )


def pick_from(table_t, ids, units, rows):
    found = dot(jnp.concatenate(split3(table_t), axis=0), units)
    found = found[:LANES] + found[LANES : 2 * LANES] + found[2 * LANES :]
    hit = iota(found.shape, 0) == ids % LANES
    return unflat(jnp.sum(jnp.where(hit, found, 0.0), axis=0, keepdims=True), rows)


def two_parts(line):
    first = line.astype(BF16).astype(F32)
    return first, (line - first).astype(BF16).astype(F32)


def model_of(line, parts):
    first, second = two_parts(line)
    left = jnp.concatenate([first, first], axis=1)
    right = jnp.concatenate([second, jnp.zeros_like(second)], axis=1)
    row = iota((SUB, 2 * WIDTH), 0)
    both = jnp.where(row == 0, left, jnp.where(row == 1, right, 0.0)).astype(BF16)
    return jnp.sum(dot(both, parts), axis=0, keepdims=True)


def side_of(values, parts):
    first, second = two_parts(values)
    row = iota((SUB, values.shape[1]), 0)
    both = jnp.where(row == 0, first, jnp.where(row == 1, second, 0.0)).astype(BF16)
    found = dot_t(both, parts)
    return found[0:1, :WIDTH] + found[1:2, :WIDTH] + found[0:1, WIDTH:]


def normals_kernel(
    observed_in, weight_in, present_in, source_in, attitude_in, phase_in, knot_in, id_in, cal_in,
    start_in,
    send_out, design_out, weighted_out, observed, source_id, cal_id, source_partials,
    weight_obs, present, attitude_partials, phase, knot_base, start, stacked, sems,
):
    fetch(
        [
            (observed_in, observed), (weight_in, weight_obs), (present_in, present),
            (source_in, source_partials), (attitude_in, attitude_partials), (phase_in, phase),
            (knot_in, knot_base), (id_in, source_id), (cal_in, cal_id), (start_in, start),
        ],
        sems,
    )
    rows, slots = observed.shape
    weighted = present[...].astype(F32) * weight_obs[...]
    weighted_out[...] = weighted
    u = phase[...]
    other = 1.0 - u
    square = u * u
    cube = square * u
    basis = [
        other * other * other / 6.0,
        (3.0 * cube - 6.0 * square + 4.0) / 6.0,
        (-3.0 * cube + 3.0 * square + 3.0 * u + 1.0) / 6.0,
        cube / 6.0,
    ]
    first, second = tile_of(cal_id[...].astype(F32)), tile_of(weighted)
    count = first.shape[0]
    devices = send_out.shape[0]
    for index in range(count):
        for device in range(devices):
            send_out[device, PIECE + index] = first[index : index + 1]
            send_out[device, PIECE + count + index] = second[index : index + 1]
    for device in range(devices):
        send_out[device, PIECE + 2 * count] = start[...]
    for row in range(rows):
        at = slice(row, row + 1)
        for channel in range(4):
            lines = attitude_partials[channel, at]
            stacked[row, channel : channel + 1] = lines
            stacked[row, channel + 4 : channel + 5] = lines
        design = design_of(knot_base[at], [part[at] for part in basis], stacked[row])
        design_out[row] = design
        band = pack_band(exact_dot_t(design * weighted[at], design))
        for index in range(BAND):
            device, place = divmod(row * BAND + index, PIECE)
            send_out[device, place] = band[index : index + 1]


def sources_kernel(
    observed, source_partials, source_id, cal_id, weighted, design, calibration,
    partials_out, factor_out, target_out, table_out, hits_out, units_out, parts_out, table, sem,
):
    copy = pltpu.make_async_copy(calibration, table, sem)
    copy.start()
    rows, slots = observed.shape
    matrix = jnp.zeros((40, SRC_DEV), F32)
    for row in range(rows):
        at = slice(row, row + 1)
        for index in range(5):
            partials_out[row, index : index + 1] = source_partials[index, at]
        partials_out[row, 5:] = jnp.zeros((SUB - 5, slots), F32)
        partials = partials_out[row]
        products = jnp.concatenate(
            [partials * (weighted[at] * partials[index : index + 1]) for index in range(5)], axis=0
        )
        hits_out[row] = one_hot(source_id[at], SRC_DEV)
        found = dot_t(jnp.concatenate(split3(products), axis=0), hits_out[row])
        matrix = matrix + found[:40] + found[40:80] + found[80:]
        first, second, unused = split3(design[row])
        parts_out[row, :WIDTH] = first
        parts_out[row, WIDTH:] = second
    ids = flat(cal_id[...])
    units_out[...] = one_hot(ids // LANES, HIGH)
    inverse = small_factor(matrix)
    for place, pair in enumerate(PLACES):
        factor_out[place : place + 1] = inverse[pair]
    factor_out[15:16] = jnp.zeros((1, SRC_DEV), F32)
    copy.wait()
    table_t = table[...].T
    table_out[...] = table_t
    for row, picked in enumerate(pick_from(table_t, ids, units_out[...], rows)):
        target_out[row : row + 1] = observed[row : row + 1] - picked


def residual_step(targets, parts, partials, factor, weighted, hits, send_out):
    rows, slots = len(targets), targets[0].shape[1]
    count = rows * slots // LANES
    inverse = {pair: factor[place : place + 1] for place, pair in enumerate(PLACES)}
    sides = jnp.zeros((SUB, SRC_DEV), F32)
    for row in range(rows):
        products = partials[row] * (weighted[row : row + 1] * targets[row])
        found = dot_t(jnp.concatenate(split3(products), axis=0), hits[row])
        sides = sides + found[:SUB] + found[SUB : 2 * SUB] + found[2 * SUB :]
    params = small_apply(inverse, [sides[index : index + 1] for index in range(5)])
    table = jnp.concatenate(params + [jnp.zeros((3, SRC_DEV), F32)], axis=0)
    split = jnp.concatenate(split3(table), axis=0)
    explained = []
    for row in range(rows):
        found = dot(split, hits[row])
        found = found[:SUB] + found[SUB : 2 * SUB] + found[2 * SUB :]
        explained.append(jnp.sum(found * partials[row], axis=0, keepdims=True))
    for row in range(rows):
        scaled = weighted[row : row + 1] * (targets[row] - explained[row])
        right = side_of(scaled, parts[row])
        for place in range(slots // LANES):
            for device in range(send_out.shape[0]):
                send_out[device, place * rows + row] = scaled[:, place * LANES : (place + 1) * LANES]
        for device in range(send_out.shape[0]):
            send_out[device, count + row] = right
    return params, explained


def first_kernel(received, target, parts, partials, factor, weighted, hits, send_out):
    rows = parts.shape[0]
    last = received.shape[1] - 1
    targets = [
        target[row : row + 1] - model_of(received[row, last], parts[row]) for row in range(rows)
    ]
    residual_step(targets, parts, partials, factor, weighted, hits, send_out)
    for place in range(PIECE):
        total = received[0, place]
        for device in range(1, received.shape[0]):
            total = total + received[device, place]
        for device in range(send_out.shape[0]):
            send_out[device, send_out.shape[1] - PIECE + place] = total


def wide(row, count):
    tile = jnp.broadcast_to(row, (16, LANES)).astype(BF16)
    return jnp.concatenate([tile] * (count // 16), axis=0)


def unit_sums(received, value_of, total):
    count = (received.shape[1] - PIECE - 1) // 2
    low_row = iota((LANES, LANES), 0).astype(F32).astype(BF16)
    high_row = iota((HIGH, LANES), 0).astype(F32).astype(BF16)
    one, none = jnp.ones((), BF16), jnp.zeros((), BF16)
    for device in range(received.shape[0]):
        lefts, rights = [], []
        for index in range(count):
            unit = received[device, PIECE + index]
            high = jnp.floor(unit * (1.0 / LANES))
            hit = low_row == wide(unit - LANES * high, LANES)
            value = value_of(device, index)
            first = value.astype(BF16).astype(F32)
            lefts.append(
                jnp.concatenate(
                    [
                        jnp.where(hit, wide(first, LANES), none),
                        jnp.where(hit, wide(value - first, LANES), none),
                    ],
                    axis=0,
                )
            )
            rights.append(jnp.where(high_row == wide(high, HIGH), one, none))
        found = dot_t(jnp.concatenate(lefts, axis=1), jnp.concatenate(rights, axis=1))
        if device == 0:
            total[...] = found[:LANES] + found[LANES:]
        else:
            total[...] += found[:LANES] + found[LANES:]
        yield


def matrix_of(band):
    lower = unpack_band(band)
    diagonal = iota(lower.shape, 0) == iota(lower.shape, 1)
    return lower + jnp.where(diagonal, 1.0, lower.T)


def together(works):
    works = list(works)
    while works:
        for work in list(works):
            if next(work, works) is works:
                works.remove(work)


def scale_kernel(received, scale_out):
    count = (received.shape[1] - PIECE - 1) // 2
    together(
        [
            unit_sums(
                received,
                lambda device, index: received[device, PIECE + count + index],
                scale_out,
            )
        ]
    )
    scale_out[...] = 1.0 / (scale_out[...] + 1.0)


def right_side(values, place):
    total = values[0, place]
    for device in range(1, values.shape[0]):
        total = total + values[device, place]
    return total


def second_kernel(
    values, received, table, scale, cal_id, units, observed, parts, partials, factor, weighted, hits,
    send_out, params_out, explained_out, table_out, attitude_out, inverses_out, bands,
):
    rows = parts.shape[0]
    count = values.shape[1] - rows - PIECE
    for device in range(values.shape[0]):
        for place in range(PIECE):
            at = PIECE * device + place
            bands[at : at + 1] = values[device, count + rows + place]
    models = [None] * rows

    def attitude(row):
        yield from spd_inverse(
            matrix_of(bands[BAND * row : BAND * (row + 1)]), inverses_out.at[row]
        )
        change = exact_dot(right_side(values, count + row), inverses_out[row])
        yield
        new = received[row, received.shape[1] - 1] + change
        attitude_out[row : row + 1] = new
        models[row] = model_of(new, parts[row])
        yield

    together(
        [unit_sums(received, lambda device, index: values[device, index], table_out)]
        + [attitude(row) for row in range(rows)]
    )
    table_t = table[...] + table_out[...] * scale[...]
    table_out[...] = table_t
    picked = pick_from(table_t, flat(cal_id[...]), units[...], rows)
    targets = [observed[row : row + 1] - models[row] - picked[row] for row in range(rows)]
    params, explained = residual_step(targets, parts, partials, factor, weighted, hits, send_out)
    for index in range(5):
        params_out[index : index + 1] = params[index]
    for row in range(rows):
        explained_out[row : row + 1] = explained[row]


def final_kernel(
    axis, values, received, inverses, attitude, table, scale, cal_id, units, observed, parts,
    explained, cal_out, attitude_out, resid_out, sums,
):
    rows = parts.shape[0]
    count = values.shape[1] - rows
    me = lax.axis_index(axis)
    models, news = [None] * rows, [None] * rows

    def solve(row):
        change = exact_dot(right_side(values, count + row), inverses[row])
        yield
        news[row] = attitude[row : row + 1] + change
        models[row] = model_of(news[row], parts[row])
        yield

    together(
        [unit_sums(received, lambda device, index: values[device, index], sums)]
        + [solve(row) for row in range(rows)]
    )
    own = news[0]
    for row in range(1, rows):
        own = jnp.where(me == row, news[row], own)
    attitude_out[...] = own
    table_t = table[...] + sums[...] * scale[...]
    cal_out[...] = table_t.T
    for row, picked in enumerate(pick_from(table_t, flat(cal_id[...]), units[...], rows)):
        at = slice(row, row + 1)
        resid_out[at] = observed[at] - models[row] - picked - explained[at]


VMEM = pl.BlockSpec(memory_space=pltpu.VMEM)
ANY = pl.BlockSpec(memory_space=pltpu.HBM)


def call(kernel, outs, *args, away=0, scratch=()):
    near = args[: len(args) - away]
    far = [pltpu.with_memory_space_constraint(arg, pltpu.HBM) for arg in args[len(args) - away :]]
    return pl.pallas_call(
        kernel,
        out_shape=outs,
        in_specs=[VMEM] * len(near) + [ANY] * away,
        out_specs=[VMEM] * len(outs),
        scratch_shapes=scratch,
        compiler_params=pltpu.CompilerParams(vmem_limit_bytes=VMEM_BYTES),
    )(*near, *far)


def stay(*shape, dtype=F32):
    return pltpu.VMEM(shape, dtype)


def leave(*shape):
    return jax.ShapeDtypeStruct(shape, F32)


def exchange(value):
    return lax.all_to_all(value, ("src", "tm"), 0, 0, tiled=True)


def body(
    observed, weight_obs, present, source_partials, attitude_partials, phase, knot_base, source_id,
    cal_id, attitude, calibration,
):
    rows, slots = observed.shape
    devices = lax.axis_size("src") * lax.axis_size("tm")
    count = rows * slots // LANES
    first_q = attitude.reshape(1, WIDTH)
    held = [weight_obs, present, attitude_partials, phase, knot_base, first_q]
    received, design, weighted, seen, source_id, cal_id, source_partials = call(
        normals_kernel,
        [
            leave(devices, PIECE + 2 * count + 1, 1, LANES), stay(rows, WIDTH, slots),
            stay(rows, slots), stay(rows, slots), stay(rows, slots, dtype=jnp.int32),
            stay(rows, slots, dtype=jnp.int32), stay(*source_partials.shape),
        ],
        observed, weight_obs, present, source_partials, attitude_partials, phase, knot_base,
        source_id, cal_id, first_q,
        away=10,
        scratch=[pltpu.VMEM(each.shape, each.dtype) for each in held]
        + [pltpu.VMEM((rows, SUB, slots), F32), pltpu.SemaphoreType.DMA((10,))],
    )
    received = exchange(received)
    partials, factor, target, table, hits, units, parts = call(
        sources_kernel,
        [
            stay(rows, SUB, slots), stay(16, SRC_DEV), stay(rows, slots), stay(LANES, HIGH),
            stay(rows, SRC_DEV, slots, dtype=BF16), stay(HIGH, rows * slots, dtype=BF16),
            stay(rows, 2 * WIDTH, slots, dtype=BF16),
        ],
        seen, source_partials, source_id, cal_id, weighted, design, calibration.reshape(HIGH, LANES),
        away=1,
        scratch=[pltpu.VMEM((HIGH, LANES), F32), pltpu.SemaphoreType.DMA],
    )
    received, factor = lax.optimization_barrier((received, factor))
    (values,) = call(
        first_kernel, [leave(devices, count + rows + PIECE, 1, LANES)],
        received, target, parts, partials, factor, weighted, hits,
    )
    values, received = lax.optimization_barrier((values, received))
    values = exchange(values)
    (scale,) = call(scale_kernel, [stay(LANES, HIGH)], received)
    values, params, explained, table, now, inverses = call(
        second_kernel,
        [
            leave(devices, count + rows, 1, LANES), leave(5, SRC_DEV), stay(rows, slots),
            stay(LANES, HIGH), stay(rows, WIDTH), stay(rows, WIDTH, WIDTH),
        ],
        values, received, table, scale, cal_id, units, seen, parts, partials, factor, weighted, hits,
        scratch=[pltpu.VMEM((rows * BAND, WIDTH), F32)],
    )
    values = exchange(values)
    cal, now, final = call(
        functools.partial(final_kernel, "tm"),
        [leave(HIGH, LANES), leave(1, WIDTH), leave(rows, slots)],
        values, received, inverses, now, table, scale, cal_id, units, seen, parts, explained,
        scratch=[pltpu.VMEM((LANES, HIGH), F32)],
    )
    return (params, now.reshape(WIDTH), cal.reshape(CAL), final)


def solution(mesh):
    many = mesh.shape["src"] * mesh.shape["tm"]
    return jax.shard_map(
        body if many * PIECE == mesh.shape["tm"] * BAND else plain_body,
        mesh=mesh,
        in_specs=(
            P(None, ("src", "tm")),
            P(None, ("src", "tm")),
            P(None, ("src", "tm")),
            P(None, None, ("src", "tm")),
            P(None, None, ("src", "tm")),
            P(None, ("src", "tm")),
            P(None, ("src", "tm")),
            P(None, ("src", "tm")),
            P(None, ("src", "tm")),
            P("tm"),
            P(),
        ),
        out_specs=(P(None, ("src", "tm")), P("tm"), P(), P(None, ("src", "tm"))),
        check_vma=False,
    )
```

```python
import functools

import jax
import jax.numpy as jnp
from jax import lax
from jax.experimental import pallas as pl
from jax.experimental.pallas import tpu as pltpu
from jax.sharding import PartitionSpec as P

KNOTS_DEV = 32
WIDTH = 4 * KNOTS_DEV
SRC_DEV = 128
CAL = 32768
LANES = 128
HIGH = CAL // LANES
SUB = 8
VMEM_BYTES = 48 * 1024 * 1024

F32 = jnp.float32
BF16 = jnp.bfloat16
EXACT = lax.Precision.HIGHEST


def iota(shape, dim):
    return lax.broadcasted_iota(jnp.int32, shape, dim)


def split3(value):
    first = value.astype(BF16)
    rest = value - first.astype(F32)
    second = rest.astype(BF16)
    third = (rest - second.astype(F32)).astype(BF16)
    return first, second, third


def dot(left, right):
    return lax.dot_general(left, right, (((1,), (0,)), ((), ())), preferred_element_type=F32)


def dot_t(left, right):
    return lax.dot_general(left, right, (((1,), (1,)), ((), ())), preferred_element_type=F32)


def exact_dot(left, right):
    return lax.dot_general(
        left, right, (((1,), (0,)), ((), ())), precision=EXACT, preferred_element_type=F32
    )


def exact_dot_t(left, right):
    return lax.dot_general(
        left, right, (((1,), (1,)), ((), ())), precision=EXACT, preferred_element_type=F32
    )


def one_hot(ids, count):
    return jnp.where(iota((count, ids.shape[1]), 0) == ids, 1.0, 0.0).astype(BF16)


def flat(value):
    return jnp.concatenate([value[row : row + 1] for row in range(value.shape[0])], axis=1)


def unflat(value, rows):
    slots = value.shape[1] // rows
    return [value[:, row * slots : (row + 1) * slots] for row in range(rows)]


def cal_pick(table, ids):
    parts = jnp.concatenate(split3(table.T), axis=0)
    high = ids // LANES
    low = ids % LANES
    found = dot(parts, one_hot(high, HIGH))
    found = found[:LANES] + found[LANES : 2 * LANES] + found[2 * LANES :]
    return jnp.sum(jnp.where(iota(found.shape, 0) == low, found, 0.0), axis=0, keepdims=True)


def cal_sums(values, ids):
    high = one_hot(ids // LANES, HIGH)
    low = iota((LANES, ids.shape[1]), 0) == ids % LANES
    total = None
    for part in split3(values):
        spread = jnp.where(low, part.astype(F32), 0.0).astype(BF16)
        added = dot_t(high, spread)
        total = added if total is None else total + added
    return total


def design_of(base, basis, partials):
    slots = base.shape[1]
    knot = iota((WIDTH, slots), 0) // 4
    step = knot - base
    spread = jnp.zeros((WIDTH, slots), F32)
    for index in range(4):
        spread = jnp.where(step == index, basis[index], spread)
    return spread * jnp.concatenate([partials] * (WIDTH // 8), axis=0)


def band_shift(tile, knot):
    return ((tile % 8) * 16 - (8 * tile + 4 * knot - 12)) % WIDTH


def pack_band(normal):
    place = iota((8, WIDTH), 1) // 16
    upper = iota((8, WIDTH), 0) < 4
    groups = []
    for group in range(2):
        packed = jnp.zeros((8, WIDTH), F32)
        for tile in range(8 * group, 8 * group + 8):
            rows = normal[8 * tile : 8 * tile + 8]
            rolled = jnp.where(
                upper,
                pltpu.roll(rows, band_shift(tile, 0), 1),
                pltpu.roll(rows, band_shift(tile, 1), 1),
            )
            packed = jnp.where(place == tile % 8, rolled, packed)
        groups.append(packed)
    return jnp.concatenate(groups, axis=0)


def unpack_band(packed):
    place = iota((8, WIDTH), 1) // 16
    upper = iota((8, WIDTH), 0) < 4
    tiles = []
    for tile in range(16):
        group = tile // 8
        rows = jnp.where(place == tile % 8, packed[8 * group : 8 * group + 8], 0.0)
        tiles.append(
            jnp.where(
                upper,
                pltpu.roll(rows, (-band_shift(tile, 0)) % WIDTH, 1),
                pltpu.roll(rows, (-band_shift(tile, 1)) % WIDTH, 1),
            )
        )
    full = jnp.concatenate(tiles, axis=0)
    return jnp.where(iota(full.shape, 0) >= iota(full.shape, 1), full, 0.0)


ORDER = (
    (0, 8, 17, 31), (1, 9, 18, 30), (2, 10, 19, 29), (3, 11, 20, 28), (4, 12, 21, 27), (13, 22, 26),
    (5, 23), (6, 24), (7, 25), (14,), (15,), (16,),
)


def plan_of(order):
    near = {
        knot: {other for other in range(KNOTS_DEV) if 0 < abs(other - knot) <= 3}
        for knot in range(KNOTS_DEV)
    }
    plan = []
    for step in order:
        plan.append([(knot, sorted({other // 2 for other in near[knot]})) for knot in step])
        for knot in step:
            assert not near[knot] & set(step)
            for other in near[knot]:
                near[other] = (near[other] | near[knot]) - {other, knot}
    return plan


PLAN = plan_of(ORDER)


def block_rows(entry, lines):
    scale = 1.0 / (entry[0, 0] * entry[1, 1] - entry[0, 1] * entry[0, 1])
    low, mid, high = entry[0, 0] * scale, entry[0, 1] * scale, entry[1, 1] * scale
    turned = {}
    for column in (2, 3):
        turned[0, column] = high * entry[0, column] - mid * entry[1, column]
        turned[1, column] = low * entry[1, column] - mid * entry[0, column]
    rest = {}
    for row, column in ((2, 2), (2, 3), (3, 3)):
        taken = entry[0, row] * turned[0, column] + entry[1, row] * turned[1, column]
        rest[row, column] = entry[row, column] - taken
    upper = [high * lines[0] - mid * lines[1], low * lines[1] - mid * lines[0]]
    lower = [
        lines[row] - (entry[0, row] * upper[0] + entry[1, row] * upper[1]) for row in (2, 3)
    ]
    scale = 1.0 / (rest[2, 2] * rest[3, 3] - rest[2, 3] * rest[2, 3])
    third = (rest[3, 3] * scale) * lower[0] - (rest[2, 3] * scale) * lower[1]
    fourth = (rest[2, 2] * scale) * lower[1] - (rest[2, 3] * scale) * lower[0]
    return [
        upper[0] - (turned[0, 2] * third + turned[0, 3] * fourth),
        upper[1] - (turned[1, 2] * third + turned[1, 3] * fourth),
        third,
        fourth,
    ]


def eliminate(matrix, right, lines_out):
    shape = (8, WIDTH)
    tiles = [matrix[8 * tile : 8 * tile + 8] for tile in range(WIDTH // 8)]
    lane = iota(shape, 1)
    for step in PLAN:
        held = list(tiles)
        border = right
        for knot, reach in step:
            at, sub, first = knot // 2, 4 * (knot % 2), 4 * knot
            inside = lane // 4 == knot
            columns = {
                tile: [
                    jnp.broadcast_to(held[tile][:, first + index : first + index + 1], shape)
                    for index in range(4)
                ]
                for tile in sorted({at, *reach})
            }
            entry = {
                (one, two): jnp.broadcast_to(columns[at][two][sub + one : sub + one + 1], shape)
                for one in range(4)
                for two in range(one, 4)
            }
            lines = [
                jnp.where(
                    inside,
                    jnp.where(lane == first + index, -1.0, 0.0),
                    jnp.broadcast_to(held[at][sub + index : sub + index + 1], shape),
                )
                for index in range(4)
            ]
            lines = block_rows(entry, lines)
            for index in range(4):
                lines_out[first + index : first + index + 1] = lines[index][0:1]
            for tile in reach:
                factors = columns[tile]
                taken = factors[0] * lines[0] + factors[1] * lines[1]
                taken = taken + (factors[2] * lines[2] + factors[3] * lines[3])
                tiles[tile] = jnp.where(inside, 0.0, tiles[tile]) - taken
            right = swept(right, border, knot, [line[0:1] for line in lines])
        yield
    return right


def swept(right, border, knot, lines):
    first = 4 * knot
    right = jnp.where(iota(right.shape, 1) // 4 == knot, 0.0, right)
    factors = [border[:, first + index : first + index + 1] for index in range(4)]
    taken = factors[0] * lines[0] + factors[1] * lines[1]
    return right - (taken + (factors[2] * lines[2] + factors[3] * lines[3]))


def substitute(right, lines):
    for step in PLAN:
        border = right
        for knot, unused in step:
            kept = [lines[4 * knot + index : 4 * knot + index + 1] for index in range(4)]
            right = swept(right, border, knot, kept)
        yield
    return right


def small_factor(sums):
    factor = {}
    for member in range(5):
        for column in range(member + 1):
            running = sums[8 * member + column : 8 * member + column + 1]
            if member == column:
                running = running + 1.0
            for offset in range(column):
                running = running - factor[member, offset] * factor[column, offset]
            if member == column:
                factor[member, member] = jnp.sqrt(running)
            else:
                factor[member, column] = running * inverse_of[column]
        inverse_of = {} if member == 0 else inverse_of
        inverse_of[member] = 1.0 / factor[member, member]
    inverse = {}
    for column in range(5):
        inverse[column, column] = inverse_of[column]
        for member in range(column + 1, 5):
            running = factor[member, column] * inverse[column, column]
            for offset in range(column + 1, member):
                running = running + factor[member, offset] * inverse[offset, column]
            inverse[member, column] = -running * inverse_of[member]
    return inverse


PLACES = [(row_id, col_id) for row_id in range(5) for col_id in range(row_id + 1)]


def small_apply(inverse, sides):
    forward = []
    for member in range(5):
        running = inverse[member, 0] * sides[0]
        for column in range(1, member + 1):
            running = running + inverse[member, column] * sides[column]
        forward.append(running)
    result = []
    for column in range(5):
        running = inverse[column, column] * forward[column]
        for member in range(column + 1, 5):
            running = running + inverse[member, column] * forward[member]
        result.append(running)
    return result


PAIRS = [(row_id, col_id) for row_id in range(5) for col_id in range(row_id + 1)]


def spline_terms(phase, attitude_partials):
    other = 1.0 - phase
    square = phase * phase
    cube = square * phase
    basis = [
        other * other * other / 6.0,
        (3.0 * cube - 6.0 * square + 4.0) / 6.0,
        (-3.0 * cube + 3.0 * square + 3.0 * phase + 1.0) / 6.0,
        cube / 6.0,
    ]
    return jnp.stack(
        [
            basis[knot_step] * attitude_partials[channel]
            for knot_step in range(4)
            for channel in range(4)
        ]
    )


def attitude_model(local, terms, knot_base):
    coefficients = lax.all_gather(local, "tm", axis=0, tiled=True)
    blocks, slots = knot_base.shape
    table = coefficients.reshape(blocks, -1, 4)
    knots_count = table.shape[1]
    grid = lax.broadcasted_iota(jnp.int32, (1, knots_count, 1), 1)
    running = jnp.zeros(knot_base.shape, jnp.float32)
    for knot_step in range(4):
        hit = (grid == (knot_base + knot_step)[:, None, :]).astype(jnp.float32)
        picked = jnp.einsum(
            "bkc,bks->bcs",
            table,
            hit,
            precision=lax.Precision.HIGHEST,
            preferred_element_type=jnp.float32,
        )
        for channel in range(4):
            running = running + terms[4 * knot_step + channel] * picked[:, channel, :]
    return running


def small_solve(matrix, right_side):
    extent = len(right_side)
    factor = {}
    for member in range(extent):
        for column in range(member + 1):
            running = matrix[member][column]
            for offset in range(column):
                running = running - factor[member, offset] * factor[column, offset]
            if member == column:
                factor[member, member] = jnp.sqrt(running)
            else:
                factor[member, column] = running / factor[column, column]
    forward = []
    for member in range(extent):
        running = right_side[member]
        for offset in range(member):
            running = running - factor[member, offset] * forward[offset]
        forward.append(running / factor[member, member])
    result = [None] * extent
    for member in reversed(range(extent)):
        running = forward[member]
        for offset in range(member + 1, extent):
            running = running - factor[offset, member] * result[offset]
        result[member] = running / factor[member, member]
    return jnp.stack(result)


def source_solve(ids, count, weighted, source_partials, target):
    products = [
        weighted * source_partials[row_id] * source_partials[col_id] for row_id, col_id in PAIRS
    ]
    products = products + [weighted * source_partials[row_id] * target for row_id in range(5)]
    stacked = jnp.moveaxis(jnp.stack(products), 1, 0)
    owners = lax.broadcasted_iota(jnp.int32, (count, 1), 0)

    def accumulate(total, item):
        values, block_ids = item
        hit = (block_ids[None, :] == owners).astype(jnp.float32)
        added = lax.dot_general(
            values,
            hit,
            (((1,), (1,)), ((), ())),
            precision=lax.Precision.HIGHEST,
            preferred_element_type=jnp.float32,
        )
        return (total + added, None)

    sums, unused = lax.scan(
        accumulate, jnp.zeros((len(products), count), jnp.float32), (stacked, ids)
    )
    entries = {}
    for position, pair in enumerate(PAIRS):
        entry_value = sums[position] + (1.0 if pair[0] == pair[1] else 0.0)
        entries[pair[0], pair[1]] = entry_value
        entries[pair[1], pair[0]] = entry_value
    matrix = [[entries[row_id, col_id] for col_id in range(5)] for row_id in range(5)]
    return small_solve(matrix, [sums[15 + row_id] for row_id in range(5)])


def pick_params(params, ids):
    count = params.shape[1]
    owners = lax.broadcasted_iota(jnp.int32, (count, 1), 0)

    def pick_single(carry, block_ids):
        hit = (block_ids[None, :] == owners).astype(jnp.float32)
        return (
            carry,
            jnp.dot(
                params, hit, precision=lax.Precision.HIGHEST, preferred_element_type=jnp.float32
            ),
        )

    unused, picked = lax.scan(pick_single, 0, ids)
    return jnp.moveaxis(picked, 1, 0)


def spd_solve(matrix, right_side):
    eye = jnp.eye(matrix.shape[-1], dtype=jnp.float32)
    lower = jnp.linalg.cholesky(matrix + eye)
    middle = lax.linalg.triangular_solve(lower, right_side[..., None], left_side=True, lower=True)
    result = lax.linalg.triangular_solve(
        lower, middle, left_side=True, lower=True, transpose_a=True
    )
    return result[..., 0]


def block_normals(terms, knot_base, weighted, resid):
    blocks, slots = knot_base.shape
    spread = jnp.moveaxis(terms.reshape(4, 4, blocks, slots), 2, 0)

    def block_single(item):
        part, base, weights, values = item
        grid = lax.broadcasted_iota(jnp.int32, (KNOTS_DEV, slots), 0)
        design = jnp.zeros((KNOTS_DEV, 4, slots), jnp.float32)
        for knot_step in range(4):
            hit = (grid == base[None, :] + knot_step).astype(jnp.float32)
            design = design + hit[:, None, :] * part[knot_step][None, :, :]
        design = design.reshape(KNOTS_DEV * 4, slots)
        normal = lax.dot_general(
            design * weights[None, :],
            design,
            (((1,), (1,)), ((), ())),
            precision=lax.Precision.HIGHEST,
            preferred_element_type=jnp.float32,
        )
        right = jnp.dot(
            design,
            weights * values,
            precision=lax.Precision.HIGHEST,
            preferred_element_type=jnp.float32,
        )
        return (normal, right)

    return lax.map(block_single, (spread, knot_base, weighted, resid))


def plain_body(
    observed,
    weight_obs,
    present,
    source_partials,
    attitude_partials,
    phase,
    knot_base,
    source_id,
    cal_id,
    attitude,
    calibration,
):
    weighted = present.astype(jnp.float32) * weight_obs
    terms = spline_terms(phase, attitude_partials)
    flat_cal = cal_id.reshape(-1)
    local = attitude
    cal_now = calibration
    params = jnp.zeros((5, SRC_DEV), jnp.float32)
    for sweep in range(2):
        target = observed - attitude_model(local, terms, knot_base) - cal_now[cal_id]
        params = source_solve(source_id, SRC_DEV, weighted, source_partials, target)
        resid = target - jnp.sum(source_partials * pick_params(params, source_id), axis=0)
        normals, rights = block_normals(terms, knot_base, weighted, resid)
        normal, right = (
            lax.psum_scatter(normals, "tm", scatter_dimension=0, tiled=True),
            lax.psum_scatter(rights, "tm", scatter_dimension=0, tiled=True),
        )
        normal, right = lax.psum((normal[0], right[0]), "src")
        local = local + spd_solve(normal, right)
        numer = jax.ops.segment_sum((weighted * resid).reshape(-1), flat_cal, num_segments=CAL)
        denom = jax.ops.segment_sum(weighted.reshape(-1), flat_cal, num_segments=CAL)
        numer, denom = lax.psum((numer, denom), ("src", "tm"))
        cal_now = cal_now + numer / (denom + 1.0)
    final = observed - attitude_model(local, terms, knot_base) - cal_now[cal_id]
    final = final - jnp.sum(source_partials * pick_params(params, source_id), axis=0)
    return (params, local, cal_now, final)


BAND = 16
PIECE = 2


def fetch(pairs, sems):
    copies = [
        pltpu.make_async_copy(origin, held, sems.at[place])
        for place, (origin, held) in enumerate(pairs)
    ]
    for copy in copies:
        copy.start()
    for copy in copies:
        copy.wait()


def tile_of(value):
    return jnp.concatenate(
        [value[:, at : at + LANES] for at in range(0, value.shape[1], LANES)], axis=0
    )


def pick_from(table_t, ids, units, rows):
    found = dot(jnp.concatenate(split3(table_t), axis=0), units)
    found = found[:LANES] + found[LANES : 2 * LANES] + found[2 * LANES :]
    hit = iota(found.shape, 0) == ids % LANES
    return unflat(jnp.sum(jnp.where(hit, found, 0.0), axis=0, keepdims=True), rows)


def two_parts(line):
    first = line.astype(BF16).astype(F32)
    return first, (line - first).astype(BF16).astype(F32)


def model_of(line, parts):
    first, second = two_parts(line)
    left = jnp.concatenate([first, first], axis=1)
    right = jnp.concatenate([second, jnp.zeros_like(second)], axis=1)
    row = iota((SUB, 2 * WIDTH), 0)
    both = jnp.where(row == 0, left, jnp.where(row == 1, right, 0.0)).astype(BF16)
    return jnp.sum(dot(both, parts), axis=0, keepdims=True)


def side_of(values, parts):
    first, second = two_parts(values)
    row = iota((SUB, values.shape[1]), 0)
    both = jnp.where(row == 0, first, jnp.where(row == 1, second, 0.0)).astype(BF16)
    found = dot_t(both, parts)
    return found[0:1, :WIDTH] + found[1:2, :WIDTH] + found[0:1, WIDTH:]


def normals_kernel(
    observed_in, weight_in, present_in, source_in, attitude_in, phase_in, knot_in, id_in, cal_in,
    start_in,
    send_out, design_out, weighted_out, observed, source_id, cal_id, source_partials,
    weight_obs, present, attitude_partials, phase, knot_base, start, stacked, sems,
):
    fetch(
        [
            (observed_in, observed), (weight_in, weight_obs), (present_in, present),
            (source_in, source_partials), (attitude_in, attitude_partials), (phase_in, phase),
            (knot_in, knot_base), (id_in, source_id), (cal_in, cal_id), (start_in, start),
        ],
        sems,
    )
    rows, slots = observed.shape
    weighted = present[...].astype(F32) * weight_obs[...]
    weighted_out[...] = weighted
    u = phase[...]
    other = 1.0 - u
    square = u * u
    cube = square * u
    basis = [
        other * other * other / 6.0,
        (3.0 * cube - 6.0 * square + 4.0) / 6.0,
        (-3.0 * cube + 3.0 * square + 3.0 * u + 1.0) / 6.0,
        cube / 6.0,
    ]
    first, second = tile_of(cal_id[...].astype(F32)), tile_of(weighted)
    count = first.shape[0]
    devices = send_out.shape[0]
    for device in range(devices):
        part = second if device // rows % 2 else first
        for index in range(count):
            send_out[device, PIECE + index] = part[index : index + 1]
        send_out[device, PIECE + count] = start[...]
    for row in range(rows):
        at = slice(row, row + 1)
        for channel in range(4):
            lines = attitude_partials[channel, at]
            stacked[row, channel : channel + 1] = lines
            stacked[row, channel + 4 : channel + 5] = lines
        design = design_of(knot_base[at], [part[at] for part in basis], stacked[row])
        design_out[row] = design
        band = pack_band(exact_dot_t(design * weighted[at], design))
        for index in range(BAND):
            device, place = divmod(row * BAND + index, PIECE)
            send_out[device, place] = band[index : index + 1]


def sources_kernel(
    observed, source_partials, source_id, cal_id, weighted, design, calibration,
    partials_out, factor_out, target_out, table_out, hits_out, units_out, parts_out, table, sem,
):
    copy = pltpu.make_async_copy(calibration, table, sem)
    copy.start()
    rows, slots = observed.shape
    matrix = jnp.zeros((40, SRC_DEV), F32)
    for row in range(rows):
        at = slice(row, row + 1)
        for index in range(5):
            partials_out[row, index : index + 1] = source_partials[index, at]
        partials_out[row, 5:] = jnp.zeros((SUB - 5, slots), F32)
        partials = partials_out[row]
        products = jnp.concatenate(
            [partials * (weighted[at] * partials[index : index + 1]) for index in range(5)], axis=0
        )
        hits_out[row] = one_hot(source_id[at], SRC_DEV)
        found = dot_t(jnp.concatenate(split3(products), axis=0), hits_out[row])
        matrix = matrix + found[:40] + found[40:80] + found[80:]
        first, second, unused = split3(design[row])
        parts_out[row, :WIDTH] = first
        parts_out[row, WIDTH:] = second
    ids = flat(cal_id[...])
    units_out[...] = one_hot(ids // LANES, HIGH)
    inverse = small_factor(matrix)
    for place, pair in enumerate(PLACES):
        factor_out[place : place + 1] = inverse[pair]
    factor_out[15:16] = jnp.zeros((1, SRC_DEV), F32)
    copy.wait()
    table_t = table[...].T
    table_out[...] = table_t
    for row, picked in enumerate(pick_from(table_t, ids, units_out[...], rows)):
        target_out[row : row + 1] = observed[row : row + 1] - picked


def residual_step(targets, parts, partials, factor, weighted, hits, send_out):
    rows, slots = len(targets), targets[0].shape[1]
    count = rows * slots // LANES
    inverse = {pair: factor[place : place + 1] for place, pair in enumerate(PLACES)}
    sides = jnp.zeros((SUB, SRC_DEV), F32)
    for row in range(rows):
        products = partials[row] * (weighted[row : row + 1] * targets[row])
        found = dot_t(jnp.concatenate(split3(products), axis=0), hits[row])
        sides = sides + found[:SUB] + found[SUB : 2 * SUB] + found[2 * SUB :]
    params = small_apply(inverse, [sides[index : index + 1] for index in range(5)])
    table = jnp.concatenate(params + [jnp.zeros((3, SRC_DEV), F32)], axis=0)
    split = jnp.concatenate(split3(table), axis=0)
    explained = []
    for row in range(rows):
        found = dot(split, hits[row])
        found = found[:SUB] + found[SUB : 2 * SUB] + found[2 * SUB :]
        explained.append(jnp.sum(found * partials[row], axis=0, keepdims=True))
    for row in range(rows):
        scaled = weighted[row : row + 1] * (targets[row] - explained[row])
        right = side_of(scaled, parts[row])
        for place in range(slots // LANES):
            for device in range(send_out.shape[0]):
                send_out[device, place * rows + row] = scaled[:, place * LANES : (place + 1) * LANES]
        for device in range(send_out.shape[0]):
            send_out[device, count + row] = right
    return params, explained


def first_kernel(received, target, parts, partials, factor, weighted, hits, send_out):
    rows = parts.shape[0]
    last = received.shape[1] - 1
    targets = [
        target[row : row + 1] - model_of(received[row, last], parts[row]) for row in range(rows)
    ]
    residual_step(targets, parts, partials, factor, weighted, hits, send_out)
    for place in range(PIECE):
        total = received[0, place]
        for device in range(1, received.shape[0]):
            total = total + received[device, place]
        for device in range(send_out.shape[0]):
            send_out[device, send_out.shape[1] - PIECE + place] = total


def wide(row, count):
    tile = jnp.broadcast_to(row, (16, LANES)).astype(BF16)
    return jnp.concatenate([tile] * (count // 16), axis=0)


def unit_sums(units, value_of, total):
    low_row = iota((LANES, LANES), 0).astype(F32).astype(BF16)
    high_row = iota((HIGH, LANES), 0).astype(F32).astype(BF16)
    one, none = jnp.ones((), BF16), jnp.zeros((), BF16)
    for device in range(units.shape[0]):
        lefts, rights = [], []
        for index in range(units.shape[1]):
            unit = units[device, index]
            high = jnp.floor(unit * (1.0 / LANES))
            hit = low_row == wide(unit - LANES * high, LANES)
            value = value_of(device, index)
            first = value.astype(BF16).astype(F32)
            lefts.append(
                jnp.concatenate(
                    [
                        jnp.where(hit, wide(first, LANES), none),
                        jnp.where(hit, wide(value - first, LANES), none),
                    ],
                    axis=0,
                )
            )
            rights.append(jnp.where(high_row == wide(high, HIGH), one, none))
        found = dot_t(jnp.concatenate(lefts, axis=1), jnp.concatenate(rights, axis=1))
        if device == 0:
            total[...] = found[:LANES] + found[LANES:]
        else:
            total[...] += found[:LANES] + found[LANES:]
        yield


def matrix_of(band):
    lower = unpack_band(band)
    diagonal = iota(lower.shape, 0) == iota(lower.shape, 1)
    return lower + jnp.where(diagonal, 1.0, lower.T)


def together(works):
    works = list(works)
    while works:
        for work in list(works):
            if next(work, works) is works:
                works.remove(work)


def scale_kernel(axis, received, other, units_out, scale_out):
    first = lax.rem(lax.axis_index(axis), 2) == 0

    def weight(device, index):
        return jnp.where(first, other[device, PIECE + index], received[device, PIECE + index])

    for device in range(received.shape[0]):
        for index in range(units_out.shape[1]):
            units_out[device, index] = jnp.where(
                first, received[device, PIECE + index], other[device, PIECE + index]
            )
    together([unit_sums(units_out, weight, scale_out)])
    scale_out[...] = 1.0 / (scale_out[...] + 1.0)


def right_side(values, place):
    total = values[0, place]
    for device in range(1, values.shape[0]):
        total = total + values[device, place]
    return total


def second_kernel(
    values, received, owners, table, scale, cal_id, units, observed, parts, partials, factor, weighted,
    hits,
    send_out, params_out, explained_out, table_out, attitude_out, lines_out, bands,
):
    rows = parts.shape[0]
    count = values.shape[1] - rows - PIECE
    for device in range(values.shape[0]):
        for place in range(PIECE):
            at = PIECE * device + place
            bands[at : at + 1] = values[device, count + rows + place]
    models = [None] * rows

    def attitude(row):
        matrix = matrix_of(bands[BAND * row : BAND * (row + 1)])
        change = yield from eliminate(matrix, right_side(values, count + row), lines_out.at[row])
        new = received[row, received.shape[1] - 1] + change
        attitude_out[row : row + 1] = new
        models[row] = model_of(new, parts[row])
        yield

    def attitudes(first):
        for row in range(first, rows, 2):
            yield from attitude(row)

    together(
        [unit_sums(owners, lambda device, index: values[device, index], table_out)]
        + [attitudes(first) for first in range(2)]
    )
    table_t = table[...] + table_out[...] * scale[...]
    table_out[...] = table_t
    picked = pick_from(table_t, flat(cal_id[...]), units[...], rows)
    targets = [observed[row : row + 1] - models[row] - picked[row] for row in range(rows)]
    params, explained = residual_step(targets, parts, partials, factor, weighted, hits, send_out)
    for index in range(5):
        params_out[index : index + 1] = params[index]
    for row in range(rows):
        explained_out[row : row + 1] = explained[row]


def final_kernel(
    axis, values, owners, lines, attitude, table, scale, cal_id, units, observed, parts,
    explained, cal_out, attitude_out, resid_out, sums,
):
    rows = parts.shape[0]
    count = values.shape[1] - rows
    me = lax.axis_index(axis)
    models, news = [None] * rows, [None] * rows

    def solve(row):
        change = yield from substitute(right_side(values, count + row), lines.at[row])
        news[row] = attitude[row : row + 1] + change
        models[row] = model_of(news[row], parts[row])
        yield

    together(
        [unit_sums(owners, lambda device, index: values[device, index], sums)]
        + [solve(row) for row in range(rows)]
    )
    own = news[0]
    for row in range(1, rows):
        own = jnp.where(me == row, news[row], own)
    attitude_out[...] = own
    table_t = table[...] + sums[...] * scale[...]
    cal_out[...] = table_t.T
    for row, picked in enumerate(pick_from(table_t, flat(cal_id[...]), units[...], rows)):
        at = slice(row, row + 1)
        resid_out[at] = observed[at] - models[row] - picked - explained[at]


VMEM = pl.BlockSpec(memory_space=pltpu.VMEM)
ANY = pl.BlockSpec(memory_space=pltpu.HBM)


def call(kernel, outs, *args, away=0, scratch=()):
    near = args[: len(args) - away]
    far = [pltpu.with_memory_space_constraint(arg, pltpu.HBM) for arg in args[len(args) - away :]]
    return pl.pallas_call(
        kernel,
        out_shape=outs,
        in_specs=[VMEM] * len(near) + [ANY] * away,
        out_specs=[VMEM] * len(outs),
        scratch_shapes=scratch,
        compiler_params=pltpu.CompilerParams(vmem_limit_bytes=VMEM_BYTES),
    )(*near, *far)


def stay(*shape, dtype=F32):
    return pltpu.VMEM(shape, dtype)


def leave(*shape):
    return jax.ShapeDtypeStruct(shape, F32)


def exchange(value):
    return lax.all_to_all(value, ("src", "tm"), 0, 0, tiled=True)


def body(
    observed, weight_obs, present, source_partials, attitude_partials, phase, knot_base, source_id,
    cal_id, attitude, calibration,
):
    rows, slots = observed.shape
    devices = lax.axis_size("src") * lax.axis_size("tm")
    count = rows * slots // LANES
    first_q = attitude.reshape(1, WIDTH)
    held = [weight_obs, present, attitude_partials, phase, knot_base, first_q]
    received, design, weighted, seen, source_id, cal_id, source_partials = call(
        normals_kernel,
        [
            leave(devices, PIECE + count + 1, 1, LANES), stay(rows, WIDTH, slots),
            stay(rows, slots), stay(rows, slots), stay(rows, slots, dtype=jnp.int32),
            stay(rows, slots, dtype=jnp.int32), stay(*source_partials.shape),
        ],
        observed, weight_obs, present, source_partials, attitude_partials, phase, knot_base,
        source_id, cal_id, first_q,
        away=10,
        scratch=[pltpu.VMEM(each.shape, each.dtype) for each in held]
        + [pltpu.VMEM((rows, SUB, slots), F32), pltpu.SemaphoreType.DMA((10,))],
    )
    received = exchange(received)
    partials, factor, target, table, hits, units, parts = call(
        sources_kernel,
        [
            stay(rows, SUB, slots), stay(16, SRC_DEV), stay(rows, slots), stay(LANES, HIGH),
            stay(rows, SRC_DEV, slots, dtype=BF16), stay(HIGH, rows * slots, dtype=BF16),
            stay(rows, 2 * WIDTH, slots, dtype=BF16),
        ],
        seen, source_partials, source_id, cal_id, weighted, design, calibration.reshape(HIGH, LANES),
        away=1,
        scratch=[pltpu.VMEM((HIGH, LANES), F32), pltpu.SemaphoreType.DMA],
    )
    received, factor = lax.optimization_barrier((received, factor))
    (values,) = call(
        first_kernel, [leave(devices, count + rows + PIECE, 1, LANES)],
        received, target, parts, partials, factor, weighted, hits,
    )
    values, received = lax.optimization_barrier((values, received))
    values = exchange(values)
    sources = lax.axis_size("src")
    other = lax.ppermute(received, "src", [(at, at ^ 1) for at in range(sources)])
    owners, scale = call(
        functools.partial(scale_kernel, "src"),
        [stay(devices, count, 1, LANES), stay(LANES, HIGH)],
        received, other,
    )
    values, params, explained, table, now, lines = call(
        second_kernel,
        [
            leave(devices, count + rows, 1, LANES), leave(5, SRC_DEV), stay(rows, slots),
            stay(LANES, HIGH), stay(rows, WIDTH), stay(rows, WIDTH, WIDTH),
        ],
        values, received, owners, table, scale, cal_id, units, seen, parts, partials, factor, weighted,
        hits,
        scratch=[pltpu.VMEM((rows * BAND, WIDTH), F32)],
    )
    values = exchange(values)
    cal, now, final = call(
        functools.partial(final_kernel, "tm"),
        [leave(HIGH, LANES), leave(1, WIDTH), leave(rows, slots)],
        values, owners, lines, now, table, scale, cal_id, units, seen, parts, explained,
        scratch=[pltpu.VMEM((LANES, HIGH), F32)],
    )
    return (params, now.reshape(WIDTH), cal.reshape(CAL), final)


def solution(mesh):
    many = mesh.shape["src"] * mesh.shape["tm"]
    return jax.shard_map(
        body if many * PIECE == mesh.shape["tm"] * BAND else plain_body,
        mesh=mesh,
        in_specs=(
            P(None, ("src", "tm")),
            P(None, ("src", "tm")),
            P(None, ("src", "tm")),
            P(None, None, ("src", "tm")),
            P(None, None, ("src", "tm")),
            P(None, ("src", "tm")),
            P(None, ("src", "tm")),
            P(None, ("src", "tm")),
            P(None, ("src", "tm")),
            P("tm"),
            P(),
        ),
        out_specs=(P(None, ("src", "tm")), P("tm"), P(), P(None, ("src", "tm"))),
        check_vma=False,
    )
```

```python
import functools

import jax
import jax.numpy as jnp
from jax import lax
from jax.experimental import pallas as pl
from jax.experimental.pallas import tpu as pltpu
from jax.sharding import PartitionSpec as P

KNOTS_DEV = 32
WIDTH = 4 * KNOTS_DEV
SRC_DEV = 128
CAL = 32768
LANES = 128
HIGH = CAL // LANES
SUB = 8
VMEM_BYTES = 48 * 1024 * 1024

F32 = jnp.float32
BF16 = jnp.bfloat16
EXACT = lax.Precision.HIGHEST


def iota(shape, dim):
    return lax.broadcasted_iota(jnp.int32, shape, dim)


def split3(value):
    first = value.astype(BF16)
    rest = value - first.astype(F32)
    second = rest.astype(BF16)
    third = (rest - second.astype(F32)).astype(BF16)
    return first, second, third


def dot(left, right):
    return lax.dot_general(left, right, (((1,), (0,)), ((), ())), preferred_element_type=F32)


def dot_t(left, right):
    return lax.dot_general(left, right, (((1,), (1,)), ((), ())), preferred_element_type=F32)


def exact_dot(left, right):
    return lax.dot_general(
        left, right, (((1,), (0,)), ((), ())), precision=EXACT, preferred_element_type=F32
    )


def exact_dot_t(left, right):
    return lax.dot_general(
        left, right, (((1,), (1,)), ((), ())), precision=EXACT, preferred_element_type=F32
    )


def one_hot(ids, count):
    return jnp.where(iota((count, ids.shape[1]), 0) == ids, 1.0, 0.0).astype(BF16)


def flat(value):
    return jnp.concatenate([value[row : row + 1] for row in range(value.shape[0])], axis=1)


def unflat(value, rows):
    slots = value.shape[1] // rows
    return [value[:, row * slots : (row + 1) * slots] for row in range(rows)]


def cal_pick(table, ids):
    parts = jnp.concatenate(split3(table.T), axis=0)
    high = ids // LANES
    low = ids % LANES
    found = dot(parts, one_hot(high, HIGH))
    found = found[:LANES] + found[LANES : 2 * LANES] + found[2 * LANES :]
    return jnp.sum(jnp.where(iota(found.shape, 0) == low, found, 0.0), axis=0, keepdims=True)


def cal_sums(values, ids):
    high = one_hot(ids // LANES, HIGH)
    low = iota((LANES, ids.shape[1]), 0) == ids % LANES
    total = None
    for part in split3(values):
        spread = jnp.where(low, part.astype(F32), 0.0).astype(BF16)
        added = dot_t(high, spread)
        total = added if total is None else total + added
    return total


def design_of(base, basis, partials):
    slots = base.shape[1]
    knot = iota((WIDTH, slots), 0) // 4
    step = knot - base
    spread = jnp.zeros((WIDTH, slots), F32)
    for index in range(4):
        spread = jnp.where(step == index, basis[index], spread)
    return spread * jnp.concatenate([partials] * (WIDTH // 8), axis=0)


def band_shift(tile, knot):
    return ((tile % 8) * 16 - (8 * tile + 4 * knot - 12)) % WIDTH


def pack_band(normal):
    place = iota((8, WIDTH), 1) // 16
    upper = iota((8, WIDTH), 0) < 4
    groups = []
    for group in range(2):
        packed = jnp.zeros((8, WIDTH), F32)
        for tile in range(8 * group, 8 * group + 8):
            rows = normal[8 * tile : 8 * tile + 8]
            rolled = jnp.where(
                upper,
                pltpu.roll(rows, band_shift(tile, 0), 1),
                pltpu.roll(rows, band_shift(tile, 1), 1),
            )
            packed = jnp.where(place == tile % 8, rolled, packed)
        groups.append(packed)
    return jnp.concatenate(groups, axis=0)


def unpack_band(packed):
    place = iota((8, WIDTH), 1) // 16
    upper = iota((8, WIDTH), 0) < 4
    tiles = []
    for tile in range(16):
        group = tile // 8
        rows = jnp.where(place == tile % 8, packed[8 * group : 8 * group + 8], 0.0)
        tiles.append(
            jnp.where(
                upper,
                pltpu.roll(rows, (-band_shift(tile, 0)) % WIDTH, 1),
                pltpu.roll(rows, (-band_shift(tile, 1)) % WIDTH, 1),
            )
        )
    full = jnp.concatenate(tiles, axis=0)
    return jnp.where(iota(full.shape, 0) >= iota(full.shape, 1), full, 0.0)


ORDER = (
    (0, 8, 17, 31), (1, 9, 18, 30), (2, 10, 19, 29), (3, 11, 20, 28), (4, 12, 21, 27), (13, 22, 26),
    (5, 23), (6, 24), (7, 25), (14,), (15,), (16,),
)


def plan_of(order):
    near = {
        knot: {other for other in range(KNOTS_DEV) if 0 < abs(other - knot) <= 3}
        for knot in range(KNOTS_DEV)
    }
    plan = []
    for step in order:
        plan.append([(knot, sorted({other // 2 for other in near[knot]})) for knot in step])
        for knot in step:
            assert not near[knot] & set(step)
            for other in near[knot]:
                near[other] = (near[other] | near[knot]) - {other, knot}
    return plan


PLAN = plan_of(ORDER)


def block_rows(entry, lines):
    scale = 1.0 / (entry[0, 0] * entry[1, 1] - entry[0, 1] * entry[0, 1])
    low, mid, high = entry[0, 0] * scale, entry[0, 1] * scale, entry[1, 1] * scale
    turned = {}
    for column in (2, 3):
        turned[0, column] = high * entry[0, column] - mid * entry[1, column]
        turned[1, column] = low * entry[1, column] - mid * entry[0, column]
    rest = {}
    for row, column in ((2, 2), (2, 3), (3, 3)):
        taken = entry[0, row] * turned[0, column] + entry[1, row] * turned[1, column]
        rest[row, column] = entry[row, column] - taken
    upper = [high * lines[0] - mid * lines[1], low * lines[1] - mid * lines[0]]
    lower = [
        lines[row] - (entry[0, row] * upper[0] + entry[1, row] * upper[1]) for row in (2, 3)
    ]
    scale = 1.0 / (rest[2, 2] * rest[3, 3] - rest[2, 3] * rest[2, 3])
    third = (rest[3, 3] * scale) * lower[0] - (rest[2, 3] * scale) * lower[1]
    fourth = (rest[2, 2] * scale) * lower[1] - (rest[2, 3] * scale) * lower[0]
    return [
        upper[0] - (turned[0, 2] * third + turned[0, 3] * fourth),
        upper[1] - (turned[1, 2] * third + turned[1, 3] * fourth),
        third,
        fourth,
    ]


def eliminate(matrix, right, lines_out):
    shape = (8, WIDTH)
    tiles = [matrix[8 * tile : 8 * tile + 8] for tile in range(WIDTH // 8)]
    lane = iota(shape, 1)
    for step in PLAN:
        held = list(tiles)
        border = right
        for knot, reach in step:
            at, sub, first = knot // 2, 4 * (knot % 2), 4 * knot
            inside = lane // 4 == knot
            columns = {
                tile: [
                    jnp.broadcast_to(held[tile][:, first + index : first + index + 1], shape)
                    for index in range(4)
                ]
                for tile in sorted({at, *reach})
            }
            entry = {
                (one, two): jnp.broadcast_to(columns[at][two][sub + one : sub + one + 1], shape)
                for one in range(4)
                for two in range(one, 4)
            }
            lines = [
                jnp.where(
                    inside,
                    jnp.where(lane == first + index, -1.0, 0.0),
                    jnp.broadcast_to(held[at][sub + index : sub + index + 1], shape),
                )
                for index in range(4)
            ]
            lines = block_rows(entry, lines)
            for index in range(4):
                lines_out[first + index : first + index + 1] = lines[index][0:1]
            for tile in reach:
                factors = columns[tile]
                taken = factors[0] * lines[0] + factors[1] * lines[1]
                taken = taken + (factors[2] * lines[2] + factors[3] * lines[3])
                tiles[tile] = jnp.where(inside, 0.0, tiles[tile]) - taken
            right = swept(right, border, knot, [line[0:1] for line in lines])
        yield
    return right


def swept(right, border, knot, lines):
    first = 4 * knot
    right = jnp.where(iota(right.shape, 1) // 4 == knot, 0.0, right)
    factors = [border[:, first + index : first + index + 1] for index in range(4)]
    taken = factors[0] * lines[0] + factors[1] * lines[1]
    return right - (taken + (factors[2] * lines[2] + factors[3] * lines[3]))


def substitute(right, lines):
    for step in PLAN:
        border = right
        for knot, unused in step:
            kept = [lines[4 * knot + index : 4 * knot + index + 1] for index in range(4)]
            right = swept(right, border, knot, kept)
        yield
    return right


def small_factor(sums):
    factor = {}
    for member in range(5):
        for column in range(member + 1):
            running = sums[8 * member + column : 8 * member + column + 1]
            if member == column:
                running = running + 1.0
            for offset in range(column):
                running = running - factor[member, offset] * factor[column, offset]
            if member == column:
                factor[member, member] = jnp.sqrt(running)
            else:
                factor[member, column] = running * inverse_of[column]
        inverse_of = {} if member == 0 else inverse_of
        inverse_of[member] = 1.0 / factor[member, member]
    inverse = {}
    for column in range(5):
        inverse[column, column] = inverse_of[column]
        for member in range(column + 1, 5):
            running = factor[member, column] * inverse[column, column]
            for offset in range(column + 1, member):
                running = running + factor[member, offset] * inverse[offset, column]
            inverse[member, column] = -running * inverse_of[member]
    return inverse


PLACES = [(row_id, col_id) for row_id in range(5) for col_id in range(row_id + 1)]


def small_apply(inverse, sides):
    forward = []
    for member in range(5):
        running = inverse[member, 0] * sides[0]
        for column in range(1, member + 1):
            running = running + inverse[member, column] * sides[column]
        forward.append(running)
    result = []
    for column in range(5):
        running = inverse[column, column] * forward[column]
        for member in range(column + 1, 5):
            running = running + inverse[member, column] * forward[member]
        result.append(running)
    return result


PAIRS = [(row_id, col_id) for row_id in range(5) for col_id in range(row_id + 1)]


def spline_terms(phase, attitude_partials):
    other = 1.0 - phase
    square = phase * phase
    cube = square * phase
    basis = [
        other * other * other / 6.0,
        (3.0 * cube - 6.0 * square + 4.0) / 6.0,
        (-3.0 * cube + 3.0 * square + 3.0 * phase + 1.0) / 6.0,
        cube / 6.0,
    ]
    return jnp.stack(
        [
            basis[knot_step] * attitude_partials[channel]
            for knot_step in range(4)
            for channel in range(4)
        ]
    )


def attitude_model(local, terms, knot_base):
    coefficients = lax.all_gather(local, "tm", axis=0, tiled=True)
    blocks, slots = knot_base.shape
    table = coefficients.reshape(blocks, -1, 4)
    knots_count = table.shape[1]
    grid = lax.broadcasted_iota(jnp.int32, (1, knots_count, 1), 1)
    running = jnp.zeros(knot_base.shape, jnp.float32)
    for knot_step in range(4):
        hit = (grid == (knot_base + knot_step)[:, None, :]).astype(jnp.float32)
        picked = jnp.einsum(
            "bkc,bks->bcs",
            table,
            hit,
            precision=lax.Precision.HIGHEST,
            preferred_element_type=jnp.float32,
        )
        for channel in range(4):
            running = running + terms[4 * knot_step + channel] * picked[:, channel, :]
    return running


def small_solve(matrix, right_side):
    extent = len(right_side)
    factor = {}
    for member in range(extent):
        for column in range(member + 1):
            running = matrix[member][column]
            for offset in range(column):
                running = running - factor[member, offset] * factor[column, offset]
            if member == column:
                factor[member, member] = jnp.sqrt(running)
            else:
                factor[member, column] = running / factor[column, column]
    forward = []
    for member in range(extent):
        running = right_side[member]
        for offset in range(member):
            running = running - factor[member, offset] * forward[offset]
        forward.append(running / factor[member, member])
    result = [None] * extent
    for member in reversed(range(extent)):
        running = forward[member]
        for offset in range(member + 1, extent):
            running = running - factor[offset, member] * result[offset]
        result[member] = running / factor[member, member]
    return jnp.stack(result)


def source_solve(ids, count, weighted, source_partials, target):
    products = [
        weighted * source_partials[row_id] * source_partials[col_id] for row_id, col_id in PAIRS
    ]
    products = products + [weighted * source_partials[row_id] * target for row_id in range(5)]
    stacked = jnp.moveaxis(jnp.stack(products), 1, 0)
    owners = lax.broadcasted_iota(jnp.int32, (count, 1), 0)

    def accumulate(total, item):
        values, block_ids = item
        hit = (block_ids[None, :] == owners).astype(jnp.float32)
        added = lax.dot_general(
            values,
            hit,
            (((1,), (1,)), ((), ())),
            precision=lax.Precision.HIGHEST,
            preferred_element_type=jnp.float32,
        )
        return (total + added, None)

    sums, unused = lax.scan(
        accumulate, jnp.zeros((len(products), count), jnp.float32), (stacked, ids)
    )
    entries = {}
    for position, pair in enumerate(PAIRS):
        entry_value = sums[position] + (1.0 if pair[0] == pair[1] else 0.0)
        entries[pair[0], pair[1]] = entry_value
        entries[pair[1], pair[0]] = entry_value
    matrix = [[entries[row_id, col_id] for col_id in range(5)] for row_id in range(5)]
    return small_solve(matrix, [sums[15 + row_id] for row_id in range(5)])


def pick_params(params, ids):
    count = params.shape[1]
    owners = lax.broadcasted_iota(jnp.int32, (count, 1), 0)

    def pick_single(carry, block_ids):
        hit = (block_ids[None, :] == owners).astype(jnp.float32)
        return (
            carry,
            jnp.dot(
                params, hit, precision=lax.Precision.HIGHEST, preferred_element_type=jnp.float32
            ),
        )

    unused, picked = lax.scan(pick_single, 0, ids)
    return jnp.moveaxis(picked, 1, 0)


def spd_solve(matrix, right_side):
    eye = jnp.eye(matrix.shape[-1], dtype=jnp.float32)
    lower = jnp.linalg.cholesky(matrix + eye)
    middle = lax.linalg.triangular_solve(lower, right_side[..., None], left_side=True, lower=True)
    result = lax.linalg.triangular_solve(
        lower, middle, left_side=True, lower=True, transpose_a=True
    )
    return result[..., 0]


def block_normals(terms, knot_base, weighted, resid):
    blocks, slots = knot_base.shape
    spread = jnp.moveaxis(terms.reshape(4, 4, blocks, slots), 2, 0)

    def block_single(item):
        part, base, weights, values = item
        grid = lax.broadcasted_iota(jnp.int32, (KNOTS_DEV, slots), 0)
        design = jnp.zeros((KNOTS_DEV, 4, slots), jnp.float32)
        for knot_step in range(4):
            hit = (grid == base[None, :] + knot_step).astype(jnp.float32)
            design = design + hit[:, None, :] * part[knot_step][None, :, :]
        design = design.reshape(KNOTS_DEV * 4, slots)
        normal = lax.dot_general(
            design * weights[None, :],
            design,
            (((1,), (1,)), ((), ())),
            precision=lax.Precision.HIGHEST,
            preferred_element_type=jnp.float32,
        )
        right = jnp.dot(
            design,
            weights * values,
            precision=lax.Precision.HIGHEST,
            preferred_element_type=jnp.float32,
        )
        return (normal, right)

    return lax.map(block_single, (spread, knot_base, weighted, resid))


def plain_body(
    observed,
    weight_obs,
    present,
    source_partials,
    attitude_partials,
    phase,
    knot_base,
    source_id,
    cal_id,
    attitude,
    calibration,
):
    weighted = present.astype(jnp.float32) * weight_obs
    terms = spline_terms(phase, attitude_partials)
    flat_cal = cal_id.reshape(-1)
    local = attitude
    cal_now = calibration
    params = jnp.zeros((5, SRC_DEV), jnp.float32)
    for sweep in range(2):
        target = observed - attitude_model(local, terms, knot_base) - cal_now[cal_id]
        params = source_solve(source_id, SRC_DEV, weighted, source_partials, target)
        resid = target - jnp.sum(source_partials * pick_params(params, source_id), axis=0)
        normals, rights = block_normals(terms, knot_base, weighted, resid)
        normal, right = (
            lax.psum_scatter(normals, "tm", scatter_dimension=0, tiled=True),
            lax.psum_scatter(rights, "tm", scatter_dimension=0, tiled=True),
        )
        normal, right = lax.psum((normal[0], right[0]), "src")
        local = local + spd_solve(normal, right)
        numer = jax.ops.segment_sum((weighted * resid).reshape(-1), flat_cal, num_segments=CAL)
        denom = jax.ops.segment_sum(weighted.reshape(-1), flat_cal, num_segments=CAL)
        numer, denom = lax.psum((numer, denom), ("src", "tm"))
        cal_now = cal_now + numer / (denom + 1.0)
    final = observed - attitude_model(local, terms, knot_base) - cal_now[cal_id]
    final = final - jnp.sum(source_partials * pick_params(params, source_id), axis=0)
    return (params, local, cal_now, final)


BAND = 16
PIECE = 2
EARLY = 22


def fetch(pairs, sems):
    copies = [
        pltpu.make_async_copy(origin, held, sems.at[place])
        for place, (origin, held) in enumerate(pairs)
    ]
    for copy in copies:
        copy.start()
    for copy in copies:
        copy.wait()


def tile_of(value):
    return jnp.concatenate(
        [value[:, at : at + LANES] for at in range(0, value.shape[1], LANES)], axis=0
    )


def pick_from(table_t, ids, units, rows):
    found = dot(jnp.concatenate(split3(table_t), axis=0), units)
    found = found[:LANES] + found[LANES : 2 * LANES] + found[2 * LANES :]
    hit = iota(found.shape, 0) == ids % LANES
    return unflat(jnp.sum(jnp.where(hit, found, 0.0), axis=0, keepdims=True), rows)


def two_parts(line):
    first = line.astype(BF16).astype(F32)
    return first, (line - first).astype(BF16).astype(F32)


def model_of(line, parts):
    first, second = two_parts(line)
    left = jnp.concatenate([first, first], axis=1)
    right = jnp.concatenate([second, jnp.zeros_like(second)], axis=1)
    row = iota((SUB, 2 * WIDTH), 0)
    both = jnp.where(row == 0, left, jnp.where(row == 1, right, 0.0)).astype(BF16)
    return jnp.sum(dot(both, parts), axis=0, keepdims=True)


def side_of(values, parts):
    first, second = two_parts(values)
    row = iota((SUB, values.shape[1]), 0)
    both = jnp.where(row == 0, first, jnp.where(row == 1, second, 0.0)).astype(BF16)
    found = dot_t(both, parts)
    return found[0:1, :WIDTH] + found[1:2, :WIDTH] + found[0:1, WIDTH:]


def normals_kernel(
    observed_in, weight_in, present_in, source_in, attitude_in, phase_in, knot_in, id_in, cal_in,
    start_in,
    send_out, design_out, weighted_out, observed, source_id, cal_id, source_partials,
    weight_obs, present, attitude_partials, phase, knot_base, start, stacked, sems,
):
    fetch(
        [
            (observed_in, observed), (weight_in, weight_obs), (present_in, present),
            (source_in, source_partials), (attitude_in, attitude_partials), (phase_in, phase),
            (knot_in, knot_base), (id_in, source_id), (cal_in, cal_id), (start_in, start),
        ],
        sems,
    )
    rows, slots = observed.shape
    weighted = present[...].astype(F32) * weight_obs[...]
    weighted_out[...] = weighted
    u = phase[...]
    other = 1.0 - u
    square = u * u
    cube = square * u
    basis = [
        other * other * other / 6.0,
        (3.0 * cube - 6.0 * square + 4.0) / 6.0,
        (-3.0 * cube + 3.0 * square + 3.0 * u + 1.0) / 6.0,
        cube / 6.0,
    ]
    first, second = tile_of(cal_id[...].astype(F32)), tile_of(weighted)
    count = first.shape[0]
    devices = send_out.shape[0]
    for device in range(devices):
        part = second if core_of(device, rows) else first
        for index in range(count):
            send_out[device, PIECE + index] = part[index : index + 1]
        send_out[device, PIECE + count] = start[...]
    for row in range(rows):
        at = slice(row, row + 1)
        for channel in range(4):
            lines = attitude_partials[channel, at]
            stacked[row, channel : channel + 1] = lines
            stacked[row, channel + 4 : channel + 5] = lines
        design = design_of(knot_base[at], [part[at] for part in basis], stacked[row])
        design_out[row] = design
        band = pack_band(exact_dot_t(design * weighted[at], design))
        half, place = divmod(row, rows // PIECE)
        for index in range(BAND):
            send_out[place * BAND + index, half] = band[index : index + 1]


def sources_kernel(
    observed, source_partials, source_id, cal_id, weighted, design, calibration,
    partials_out, factor_out, target_out, table_out, hits_out, units_out, parts_out, table, sem,
):
    copy = pltpu.make_async_copy(calibration, table, sem)
    copy.start()
    rows, slots = observed.shape
    matrix = jnp.zeros((40, SRC_DEV), F32)
    for row in range(rows):
        at = slice(row, row + 1)
        for index in range(5):
            partials_out[row, index : index + 1] = source_partials[index, at]
        partials_out[row, 5:] = jnp.zeros((SUB - 5, slots), F32)
        partials = partials_out[row]
        products = jnp.concatenate(
            [partials * (weighted[at] * partials[index : index + 1]) for index in range(5)], axis=0
        )
        hits_out[row] = one_hot(source_id[at], SRC_DEV)
        found = dot_t(jnp.concatenate(split3(products), axis=0), hits_out[row])
        matrix = matrix + found[:40] + found[40:80] + found[80:]
        first, second, unused = split3(design[row])
        parts_out[row, :WIDTH] = first
        parts_out[row, WIDTH:] = second
    ids = flat(cal_id[...])
    units_out[...] = one_hot(ids // LANES, HIGH)
    inverse = small_factor(matrix)
    for place, pair in enumerate(PLACES):
        factor_out[place : place + 1] = inverse[pair]
    factor_out[15:16] = jnp.zeros((1, SRC_DEV), F32)
    copy.wait()
    table_t = table[...].T
    table_out[...] = table_t
    for row, picked in enumerate(pick_from(table_t, ids, units_out[...], rows)):
        target_out[row : row + 1] = observed[row : row + 1] - picked


def core_of(device, line):
    return device // line % 2


def residual_step(targets, parts, partials, factor, weighted, hits, send_out, shared):
    rows, slots = len(targets), targets[0].shape[1]
    inverse = {pair: factor[place : place + 1] for place, pair in enumerate(PLACES)}
    sides = jnp.zeros((SUB, SRC_DEV), F32)
    for row in range(rows):
        products = partials[row] * (weighted[row : row + 1] * targets[row])
        found = dot_t(jnp.concatenate(split3(products), axis=0), hits[row])
        sides = sides + found[:SUB] + found[SUB : 2 * SUB] + found[2 * SUB :]
    params = small_apply(inverse, [sides[index : index + 1] for index in range(5)])
    table = jnp.concatenate(params + [jnp.zeros((3, SRC_DEV), F32)], axis=0)
    split = jnp.concatenate(split3(table), axis=0)
    explained, scaled, rights = [], [], []
    for row in range(rows):
        found = dot(split, hits[row])
        found = found[:SUB] + found[SUB : 2 * SUB] + found[2 * SUB :]
        explained.append(jnp.sum(found * partials[row], axis=0, keepdims=True))
    for row in range(rows):
        scaled.append(weighted[row : row + 1] * (targets[row] - explained[row]))
        rights.append(side_of(scaled[row], parts[row]))
    half = rows // PIECE
    for device in range(send_out.shape[0]):
        core = core_of(device, rows)
        lines = [
            scaled[row][:, place * LANES : (place + 1) * LANES]
            for place in ((core,) if shared else range(slots // LANES))
            for row in range(rows)
        ]
        for index, line in enumerate(lines + rights[half * core : half * core + half]):
            send_out[device, index] = line
    return params, explained


def first_kernel(received, target, parts, partials, factor, weighted, hits, send_out):
    rows = parts.shape[0]
    last = received.shape[1] - 1
    targets = [
        target[row : row + 1] - model_of(received[row, last], parts[row]) for row in range(rows)
    ]
    residual_step(targets, parts, partials, factor, weighted, hits, send_out, False)
    totals = [right_side(received, place) for place in range(PIECE)]
    for device in range(send_out.shape[0]):
        send_out[device, send_out.shape[1] - 1] = totals[core_of(device, rows)]


def wide(row, count):
    tile = jnp.broadcast_to(row, (16, LANES)).astype(BF16)
    return jnp.concatenate([tile] * (count // 16), axis=0)


def unit_sums(units, devices, lines, value_of, total):
    low_row = iota((LANES, LANES), 0).astype(F32).astype(BF16)
    high_row = iota((HIGH, LANES), 0).astype(F32).astype(BF16)
    one, none = jnp.ones((), BF16), jnp.zeros((), BF16)
    for device in devices:
        lefts, rights = [], []
        for index, at in enumerate(lines):
            unit = units[device, at]
            high = jnp.floor(unit * (1.0 / LANES))
            hit = low_row == wide(unit - LANES * high, LANES)
            value = value_of(device, index)
            first = value.astype(BF16).astype(F32)
            lefts.append(
                jnp.concatenate(
                    [
                        jnp.where(hit, wide(first, LANES), none),
                        jnp.where(hit, wide(value - first, LANES), none),
                    ],
                    axis=0,
                )
            )
            rights.append(jnp.where(high_row == wide(high, HIGH), one, none))
        found = dot_t(jnp.concatenate(lefts, axis=1), jnp.concatenate(rights, axis=1))
        total[...] += found[:LANES] + found[LANES:]
        yield


def matrix_of(band):
    lower = unpack_band(band)
    diagonal = iota(lower.shape, 0) == iota(lower.shape, 1)
    return lower + jnp.where(diagonal, 1.0, lower.T)


def together(works):
    works = list(works)
    while works:
        for work in list(works):
            if next(work, works) is works:
                works.remove(work)


def scale_kernel(axis, received, other, units_out, scale_out):
    first = lax.rem(lax.axis_index(axis), 2) == 0

    def weight(device, index):
        return jnp.where(first, other[device, PIECE + index], received[device, PIECE + index])

    for device in range(received.shape[0]):
        for index in range(units_out.shape[1]):
            units_out[device, index] = jnp.where(
                first, received[device, PIECE + index], other[device, PIECE + index]
            )
    scale_out[...] = jnp.zeros_like(scale_out)
    devices, count = units_out.shape[:2]
    together([unit_sums(units_out, range(devices), range(count), weight, scale_out)])
    scale_out[...] = 1.0 / (scale_out[...] + 1.0)


def right_side(values, place):
    total = values[0, place]
    for device in range(1, values.shape[0]):
        total = total + values[device, place]
    return total


def core(axis):
    return lax.rem(lax.axis_index(axis), 2)


def solve_kernel(axis, values, received, units, news_out, lines_out, sums_out, bands):
    count = units.shape[1]
    half = news_out.shape[0]
    for device in range(values.shape[0]):
        bands[device : device + 1] = values[device, count + half]

    def attitude(place):
        matrix = matrix_of(bands[BAND * place : BAND * (place + 1)])
        change = yield from eliminate(matrix, right_side(values, count + place), lines_out.at[place])
        news_out[place] = received[half * core(axis) + place, received.shape[1] - 1] + change
        yield

    sums_out[...] = jnp.zeros_like(sums_out)
    together(
        [
            unit_sums(
                units, range(EARLY), range(count), lambda device, index: values[device, index], sums_out
            )
        ]
        + [attitude(place) for place in range(half)]
    )


def units_kernel(values, units, sums, table, scale, cal_id, hits, table_out, picked_out):
    rows = cal_id.shape[0]
    table_out[...] = sums[...]
    devices, count = units.shape[:2]
    together(
        [
            unit_sums(
                units,
                range(EARLY, devices),
                range(count),
                lambda device, index: values[device, index],
                table_out,
            )
        ]
    )
    table_t = table[...] + table_out[...] * scale[...]
    table_out[...] = table_t
    for row, picked in enumerate(pick_from(table_t, flat(cal_id[...]), hits[...], rows)):
        picked_out[row : row + 1] = picked


def both_halves(axis, own, other):
    half = own.shape[0]
    first = core(axis) == 0
    lines = [jnp.where(first, own[place], other[place]) for place in range(half)]
    return lines + [jnp.where(first, other[place], own[place]) for place in range(half)]


def second_kernel(
    axis, news, other, picked, observed, parts, partials, factor, weighted, hits,
    send_out, params_out, explained_out,
):
    rows = parts.shape[0]
    lines = both_halves(axis, news, other)
    targets = [
        observed[row : row + 1] - model_of(lines[row], parts[row]) - picked[row : row + 1]
        for row in range(rows)
    ]
    params, explained = residual_step(
        targets, parts, partials, factor, weighted, hits, send_out, True
    )
    for index in range(5):
        params_out[index : index + 1] = params[index]
    for row in range(rows):
        explained_out[row : row + 1] = explained[row]


def own_kernel(axis, values, units, lines, attitude, news_out, sums_out):
    half = attitude.shape[0]
    count = values.shape[1] - half

    def solve(place):
        change = yield from substitute(right_side(values, count + place), lines.at[place])
        news_out[place] = attitude[place] + change
        yield

    sums_out[...] = jnp.zeros_like(sums_out)
    together(
        [
            unit_sums(
                units,
                range(units.shape[0]),
                [count * core(axis) + index for index in range(count)],
                lambda device, index: values[device, index],
                sums_out,
            )
        ]
        + [solve(place) for place in range(half)]
    )


def other_kernel(
    axis, values, units, sums, table, scale, cal_id, hits, cal_out, picked_out, total
):
    count = units.shape[1] // 2
    total[...] = sums[...]
    together(
        [
            unit_sums(
                units,
                range(units.shape[0]),
                [count * (1 - core(axis)) + index for index in range(count)],
                lambda device, index: values[device, index],
                total,
            )
        ]
    )
    table_t = table[...] + total[...] * scale[...]
    cal_out[...] = table_t.T
    rows = cal_id.shape[0]
    for row, picked in enumerate(pick_from(table_t, flat(cal_id[...]), hits[...], rows)):
        picked_out[row : row + 1] = picked


def final_kernel(
    axis, line, news, other, picked, observed, parts, explained, attitude_out, resid_out
):
    me = lax.axis_index(line)
    lines = both_halves(axis, news, other)
    own = lines[0]
    for row in range(1, len(lines)):
        own = jnp.where(me == row, lines[row], own)
    attitude_out[...] = own
    for row, new in enumerate(lines):
        at = slice(row, row + 1)
        resid_out[at] = observed[at] - model_of(new, parts[row]) - picked[at] - explained[at]


VMEM = pl.BlockSpec(memory_space=pltpu.VMEM)
ANY = pl.BlockSpec(memory_space=pltpu.HBM)


def call(kernel, outs, *args, away=0, scratch=()):
    near = args[: len(args) - away]
    far = [pltpu.with_memory_space_constraint(arg, pltpu.HBM) for arg in args[len(args) - away :]]
    return pl.pallas_call(
        kernel,
        out_shape=outs,
        in_specs=[VMEM] * len(near) + [ANY] * away,
        out_specs=[VMEM] * len(outs),
        scratch_shapes=scratch,
        compiler_params=pltpu.CompilerParams(vmem_limit_bytes=VMEM_BYTES),
    )(*near, *far)


def stay(*shape, dtype=F32):
    return pltpu.VMEM(shape, dtype)


def leave(*shape):
    return jax.ShapeDtypeStruct(shape, F32)


def swap(value):
    return lax.ppermute(value, "src", [(at, at ^ 1) for at in range(lax.axis_size("src"))])


def exchange(value):
    return lax.all_to_all(value, ("src", "tm"), 0, 0, tiled=True)


def body(
    observed, weight_obs, present, source_partials, attitude_partials, phase, knot_base, source_id,
    cal_id, attitude, calibration,
):
    rows, slots = observed.shape
    devices = lax.axis_size("src") * lax.axis_size("tm")
    count = rows * slots // LANES
    half = rows // PIECE
    first_q = attitude.reshape(1, WIDTH)
    held = [weight_obs, present, attitude_partials, phase, knot_base, first_q]
    received, design, weighted, seen, source_id, cal_id, source_partials = call(
        normals_kernel,
        [
            leave(devices, PIECE + count + 1, 1, LANES), stay(rows, WIDTH, slots),
            stay(rows, slots), stay(rows, slots), stay(rows, slots, dtype=jnp.int32),
            stay(rows, slots, dtype=jnp.int32), stay(*source_partials.shape),
        ],
        observed, weight_obs, present, source_partials, attitude_partials, phase, knot_base,
        source_id, cal_id, first_q,
        away=10,
        scratch=[pltpu.VMEM(each.shape, each.dtype) for each in held]
        + [pltpu.VMEM((rows, SUB, slots), F32), pltpu.SemaphoreType.DMA((10,))],
    )
    received = exchange(received)
    partials, factor, target, table, hits, units, parts = call(
        sources_kernel,
        [
            stay(rows, SUB, slots), stay(16, SRC_DEV), stay(rows, slots), stay(LANES, HIGH),
            stay(rows, SRC_DEV, slots, dtype=BF16), stay(HIGH, rows * slots, dtype=BF16),
            stay(rows, 2 * WIDTH, slots, dtype=BF16),
        ],
        seen, source_partials, source_id, cal_id, weighted, design, calibration.reshape(HIGH, LANES),
        away=1,
        scratch=[pltpu.VMEM((HIGH, LANES), F32), pltpu.SemaphoreType.DMA],
    )
    received, factor = lax.optimization_barrier((received, factor))
    (values,) = call(
        first_kernel, [leave(devices, count + half + 1, 1, LANES)],
        received, target, parts, partials, factor, weighted, hits,
    )
    values, received = lax.optimization_barrier((values, received))
    values = exchange(values)
    other = swap(received)
    owners, scale = call(
        functools.partial(scale_kernel, "src"),
        [stay(devices, count, 1, LANES), stay(LANES, HIGH)],
        received, other,
    )
    news, lines, sums = call(
        functools.partial(solve_kernel, "src"),
        [leave(half, 1, WIDTH), stay(half, WIDTH, WIDTH), stay(LANES, HIGH)],
        values, received, owners,
        scratch=[pltpu.VMEM((half * BAND, WIDTH), F32)],
    )
    other = swap(news)
    table, picked = call(
        units_kernel, [stay(LANES, HIGH), stay(rows, slots)],
        values, owners, sums, table, scale, cal_id, units,
    )
    values, params, explained = call(
        functools.partial(second_kernel, "src"),
        [leave(devices, rows + half, 1, LANES), leave(5, SRC_DEV), stay(rows, slots)],
        news, other, picked, seen, parts, partials, factor, weighted, hits,
    )
    values = exchange(values)
    rest = swap(values)
    news, sums = call(
        functools.partial(own_kernel, "src"),
        [leave(half, 1, WIDTH), stay(LANES, HIGH)],
        values, owners, lines, news,
    )
    other = swap(news)
    cal, picked = call(
        functools.partial(other_kernel, "src"),
        [leave(HIGH, LANES), stay(rows, slots)],
        rest, owners, sums, table, scale, cal_id, units,
        scratch=[pltpu.VMEM((LANES, HIGH), F32)],
    )
    now, final = call(
        functools.partial(final_kernel, "src", "tm"),
        [leave(1, WIDTH), leave(rows, slots)],
        news, other, picked, seen, parts, explained,
    )
    return (params, now.reshape(WIDTH), cal.reshape(CAL), final)


def solution(mesh):
    many = mesh.shape["src"] * mesh.shape["tm"]
    return jax.shard_map(
        body if many * PIECE == mesh.shape["tm"] * BAND else plain_body,
        mesh=mesh,
        in_specs=(
            P(None, ("src", "tm")),
            P(None, ("src", "tm")),
            P(None, ("src", "tm")),
            P(None, None, ("src", "tm")),
            P(None, None, ("src", "tm")),
            P(None, ("src", "tm")),
            P(None, ("src", "tm")),
            P(None, ("src", "tm")),
            P(None, ("src", "tm")),
            P("tm"),
            P(),
        ),
        out_specs=(P(None, ("src", "tm")), P("tm"), P(), P(None, ("src", "tm"))),
        check_vma=False,
    )
```

```python
import functools

import jax
import jax.numpy as jnp
from jax import lax
from jax.experimental import pallas as pl
from jax.experimental.pallas import tpu as pltpu
from jax.sharding import PartitionSpec as P

KNOTS_DEV = 32
WIDTH = 4 * KNOTS_DEV
SRC_DEV = 128
CAL = 32768
LANES = 128
HIGH = CAL // LANES
SUB = 8
VMEM_BYTES = 48 * 1024 * 1024

F32 = jnp.float32
BF16 = jnp.bfloat16
EXACT = lax.Precision.HIGHEST


def iota(shape, dim):
    return lax.broadcasted_iota(jnp.int32, shape, dim)


def split3(value):
    first = value.astype(BF16)
    rest = value - first.astype(F32)
    second = rest.astype(BF16)
    third = (rest - second.astype(F32)).astype(BF16)
    return first, second, third


def dot(left, right):
    return lax.dot_general(left, right, (((1,), (0,)), ((), ())), preferred_element_type=F32)


def dot_t(left, right):
    return lax.dot_general(left, right, (((1,), (1,)), ((), ())), preferred_element_type=F32)


def exact_dot(left, right):
    return lax.dot_general(
        left, right, (((1,), (0,)), ((), ())), precision=EXACT, preferred_element_type=F32
    )


def exact_dot_t(left, right):
    return lax.dot_general(
        left, right, (((1,), (1,)), ((), ())), precision=EXACT, preferred_element_type=F32
    )


def one_hot(ids, count):
    return jnp.where(iota((count, ids.shape[1]), 0) == ids, 1.0, 0.0).astype(BF16)


def flat(value):
    return jnp.concatenate([value[row : row + 1] for row in range(value.shape[0])], axis=1)


def unflat(value, rows):
    slots = value.shape[1] // rows
    return [value[:, row * slots : (row + 1) * slots] for row in range(rows)]


def cal_pick(table, ids):
    parts = jnp.concatenate(split3(table.T), axis=0)
    high = ids // LANES
    low = ids % LANES
    found = dot(parts, one_hot(high, HIGH))
    found = found[:LANES] + found[LANES : 2 * LANES] + found[2 * LANES :]
    return jnp.sum(jnp.where(iota(found.shape, 0) == low, found, 0.0), axis=0, keepdims=True)


def cal_sums(values, ids):
    high = one_hot(ids // LANES, HIGH)
    low = iota((LANES, ids.shape[1]), 0) == ids % LANES
    total = None
    for part in split3(values):
        spread = jnp.where(low, part.astype(F32), 0.0).astype(BF16)
        added = dot_t(high, spread)
        total = added if total is None else total + added
    return total


def design_of(base, basis, partials):
    slots = base.shape[1]
    knot = iota((WIDTH, slots), 0) // 4
    step = knot - base
    spread = jnp.zeros((WIDTH, slots), F32)
    for index in range(4):
        spread = jnp.where(step == index, basis[index], spread)
    return spread * jnp.concatenate([partials] * (WIDTH // 8), axis=0)


def band_shift(tile, knot):
    return ((tile % 8) * 16 - (8 * tile + 4 * knot - 12)) % WIDTH


def pack_band(normal):
    place = iota((8, WIDTH), 1) // 16
    upper = iota((8, WIDTH), 0) < 4
    groups = []
    for group in range(2):
        packed = jnp.zeros((8, WIDTH), F32)
        for tile in range(8 * group, 8 * group + 8):
            rows = normal[8 * tile : 8 * tile + 8]
            rolled = jnp.where(
                upper,
                pltpu.roll(rows, band_shift(tile, 0), 1),
                pltpu.roll(rows, band_shift(tile, 1), 1),
            )
            packed = jnp.where(place == tile % 8, rolled, packed)
        groups.append(packed)
    return jnp.concatenate(groups, axis=0)


def unpack_band(packed):
    place = iota((8, WIDTH), 1) // 16
    upper = iota((8, WIDTH), 0) < 4
    tiles = []
    for tile in range(16):
        group = tile // 8
        rows = jnp.where(place == tile % 8, packed[8 * group : 8 * group + 8], 0.0)
        tiles.append(
            jnp.where(
                upper,
                pltpu.roll(rows, (-band_shift(tile, 0)) % WIDTH, 1),
                pltpu.roll(rows, (-band_shift(tile, 1)) % WIDTH, 1),
            )
        )
    full = jnp.concatenate(tiles, axis=0)
    return jnp.where(iota(full.shape, 0) >= iota(full.shape, 1), full, 0.0)


ORDER = (
    (0, 8, 17, 31), (1, 9, 18, 30), (2, 10, 19, 29), (3, 11, 20, 28), (4, 12, 21, 27), (13, 22, 26),
    (5, 23), (6, 24), (7, 25), (14,), (15,), (16,),
)


def plan_of(order):
    near = {
        knot: {other for other in range(KNOTS_DEV) if 0 < abs(other - knot) <= 3}
        for knot in range(KNOTS_DEV)
    }
    plan = []
    for step in order:
        plan.append([(knot, sorted({other // 2 for other in near[knot]})) for knot in step])
        for knot in step:
            assert not near[knot] & set(step)
            for other in near[knot]:
                near[other] = (near[other] | near[knot]) - {other, knot}
    return plan


PLAN = plan_of(ORDER)


def block_rows(entry, lines):
    scale = 1.0 / (entry[0, 0] * entry[1, 1] - entry[0, 1] * entry[0, 1])
    low, mid, high = entry[0, 0] * scale, entry[0, 1] * scale, entry[1, 1] * scale
    turned = {}
    for column in (2, 3):
        turned[0, column] = high * entry[0, column] - mid * entry[1, column]
        turned[1, column] = low * entry[1, column] - mid * entry[0, column]
    rest = {}
    for row, column in ((2, 2), (2, 3), (3, 3)):
        taken = entry[0, row] * turned[0, column] + entry[1, row] * turned[1, column]
        rest[row, column] = entry[row, column] - taken
    upper = [high * lines[0] - mid * lines[1], low * lines[1] - mid * lines[0]]
    lower = [
        lines[row] - (entry[0, row] * upper[0] + entry[1, row] * upper[1]) for row in (2, 3)
    ]
    scale = 1.0 / (rest[2, 2] * rest[3, 3] - rest[2, 3] * rest[2, 3])
    third = (rest[3, 3] * scale) * lower[0] - (rest[2, 3] * scale) * lower[1]
    fourth = (rest[2, 2] * scale) * lower[1] - (rest[2, 3] * scale) * lower[0]
    return [
        upper[0] - (turned[0, 2] * third + turned[0, 3] * fourth),
        upper[1] - (turned[1, 2] * third + turned[1, 3] * fourth),
        third,
        fourth,
    ]


def eliminate(matrix, right, lines_out):
    shape = (8, WIDTH)
    tiles = [matrix[8 * tile : 8 * tile + 8] for tile in range(WIDTH // 8)]
    lane = iota(shape, 1)
    for step in PLAN:
        held = list(tiles)
        border = right
        for knot, reach in step:
            at, sub, first = knot // 2, 4 * (knot % 2), 4 * knot
            inside = lane // 4 == knot
            columns = {
                tile: [
                    jnp.broadcast_to(held[tile][:, first + index : first + index + 1], shape)
                    for index in range(4)
                ]
                for tile in sorted({at, *reach})
            }
            entry = {
                (one, two): jnp.broadcast_to(columns[at][two][sub + one : sub + one + 1], shape)
                for one in range(4)
                for two in range(one, 4)
            }
            lines = [
                jnp.where(
                    inside,
                    jnp.where(lane == first + index, -1.0, 0.0),
                    jnp.broadcast_to(held[at][sub + index : sub + index + 1], shape),
                )
                for index in range(4)
            ]
            lines = block_rows(entry, lines)
            for index in range(4):
                lines_out[first + index : first + index + 1] = lines[index][0:1]
            for tile in reach:
                factors = columns[tile]
                taken = factors[0] * lines[0] + factors[1] * lines[1]
                taken = taken + (factors[2] * lines[2] + factors[3] * lines[3])
                tiles[tile] = jnp.where(inside, 0.0, tiles[tile]) - taken
            right = swept(right, border, knot, [line[0:1] for line in lines])
        yield
    return right


def swept(right, border, knot, lines):
    first = 4 * knot
    right = jnp.where(iota(right.shape, 1) // 4 == knot, 0.0, right)
    factors = [border[:, first + index : first + index + 1] for index in range(4)]
    taken = factors[0] * lines[0] + factors[1] * lines[1]
    return right - (taken + (factors[2] * lines[2] + factors[3] * lines[3]))


def substitute(right, lines):
    for step in PLAN:
        border = right
        for knot, unused in step:
            kept = [lines[4 * knot + index : 4 * knot + index + 1] for index in range(4)]
            right = swept(right, border, knot, kept)
        yield
    return right


def small_factor(sums):
    factor = {}
    for member in range(5):
        for column in range(member + 1):
            running = sums[8 * member + column : 8 * member + column + 1]
            if member == column:
                running = running + 1.0
            for offset in range(column):
                running = running - factor[member, offset] * factor[column, offset]
            if member == column:
                factor[member, member] = jnp.sqrt(running)
            else:
                factor[member, column] = running * inverse_of[column]
        inverse_of = {} if member == 0 else inverse_of
        inverse_of[member] = 1.0 / factor[member, member]
    inverse = {}
    for column in range(5):
        inverse[column, column] = inverse_of[column]
        for member in range(column + 1, 5):
            running = factor[member, column] * inverse[column, column]
            for offset in range(column + 1, member):
                running = running + factor[member, offset] * inverse[offset, column]
            inverse[member, column] = -running * inverse_of[member]
    return inverse


PLACES = [(row_id, col_id) for row_id in range(5) for col_id in range(row_id + 1)]


def small_apply(inverse, sides):
    forward = []
    for member in range(5):
        running = inverse[member, 0] * sides[0]
        for column in range(1, member + 1):
            running = running + inverse[member, column] * sides[column]
        forward.append(running)
    result = []
    for column in range(5):
        running = inverse[column, column] * forward[column]
        for member in range(column + 1, 5):
            running = running + inverse[member, column] * forward[member]
        result.append(running)
    return result


PAIRS = [(row_id, col_id) for row_id in range(5) for col_id in range(row_id + 1)]


def spline_terms(phase, attitude_partials):
    other = 1.0 - phase
    square = phase * phase
    cube = square * phase
    basis = [
        other * other * other / 6.0,
        (3.0 * cube - 6.0 * square + 4.0) / 6.0,
        (-3.0 * cube + 3.0 * square + 3.0 * phase + 1.0) / 6.0,
        cube / 6.0,
    ]
    return jnp.stack(
        [
            basis[knot_step] * attitude_partials[channel]
            for knot_step in range(4)
            for channel in range(4)
        ]
    )


def attitude_model(local, terms, knot_base):
    coefficients = lax.all_gather(local, "tm", axis=0, tiled=True)
    blocks, slots = knot_base.shape
    table = coefficients.reshape(blocks, -1, 4)
    knots_count = table.shape[1]
    grid = lax.broadcasted_iota(jnp.int32, (1, knots_count, 1), 1)
    running = jnp.zeros(knot_base.shape, jnp.float32)
    for knot_step in range(4):
        hit = (grid == (knot_base + knot_step)[:, None, :]).astype(jnp.float32)
        picked = jnp.einsum(
            "bkc,bks->bcs",
            table,
            hit,
            precision=lax.Precision.HIGHEST,
            preferred_element_type=jnp.float32,
        )
        for channel in range(4):
            running = running + terms[4 * knot_step + channel] * picked[:, channel, :]
    return running


def small_solve(matrix, right_side):
    extent = len(right_side)
    factor = {}
    for member in range(extent):
        for column in range(member + 1):
            running = matrix[member][column]
            for offset in range(column):
                running = running - factor[member, offset] * factor[column, offset]
            if member == column:
                factor[member, member] = jnp.sqrt(running)
            else:
                factor[member, column] = running / factor[column, column]
    forward = []
    for member in range(extent):
        running = right_side[member]
        for offset in range(member):
            running = running - factor[member, offset] * forward[offset]
        forward.append(running / factor[member, member])
    result = [None] * extent
    for member in reversed(range(extent)):
        running = forward[member]
        for offset in range(member + 1, extent):
            running = running - factor[offset, member] * result[offset]
        result[member] = running / factor[member, member]
    return jnp.stack(result)


def source_solve(ids, count, weighted, source_partials, target):
    products = [
        weighted * source_partials[row_id] * source_partials[col_id] for row_id, col_id in PAIRS
    ]
    products = products + [weighted * source_partials[row_id] * target for row_id in range(5)]
    stacked = jnp.moveaxis(jnp.stack(products), 1, 0)
    owners = lax.broadcasted_iota(jnp.int32, (count, 1), 0)

    def accumulate(total, item):
        values, block_ids = item
        hit = (block_ids[None, :] == owners).astype(jnp.float32)
        added = lax.dot_general(
            values,
            hit,
            (((1,), (1,)), ((), ())),
            precision=lax.Precision.HIGHEST,
            preferred_element_type=jnp.float32,
        )
        return (total + added, None)

    sums, unused = lax.scan(
        accumulate, jnp.zeros((len(products), count), jnp.float32), (stacked, ids)
    )
    entries = {}
    for position, pair in enumerate(PAIRS):
        entry_value = sums[position] + (1.0 if pair[0] == pair[1] else 0.0)
        entries[pair[0], pair[1]] = entry_value
        entries[pair[1], pair[0]] = entry_value
    matrix = [[entries[row_id, col_id] for col_id in range(5)] for row_id in range(5)]
    return small_solve(matrix, [sums[15 + row_id] for row_id in range(5)])


def pick_params(params, ids):
    count = params.shape[1]
    owners = lax.broadcasted_iota(jnp.int32, (count, 1), 0)

    def pick_single(carry, block_ids):
        hit = (block_ids[None, :] == owners).astype(jnp.float32)
        return (
            carry,
            jnp.dot(
                params, hit, precision=lax.Precision.HIGHEST, preferred_element_type=jnp.float32
            ),
        )

    unused, picked = lax.scan(pick_single, 0, ids)
    return jnp.moveaxis(picked, 1, 0)


def spd_solve(matrix, right_side):
    eye = jnp.eye(matrix.shape[-1], dtype=jnp.float32)
    lower = jnp.linalg.cholesky(matrix + eye)
    middle = lax.linalg.triangular_solve(lower, right_side[..., None], left_side=True, lower=True)
    result = lax.linalg.triangular_solve(
        lower, middle, left_side=True, lower=True, transpose_a=True
    )
    return result[..., 0]


def block_normals(terms, knot_base, weighted, resid):
    blocks, slots = knot_base.shape
    spread = jnp.moveaxis(terms.reshape(4, 4, blocks, slots), 2, 0)

    def block_single(item):
        part, base, weights, values = item
        grid = lax.broadcasted_iota(jnp.int32, (KNOTS_DEV, slots), 0)
        design = jnp.zeros((KNOTS_DEV, 4, slots), jnp.float32)
        for knot_step in range(4):
            hit = (grid == base[None, :] + knot_step).astype(jnp.float32)
            design = design + hit[:, None, :] * part[knot_step][None, :, :]
        design = design.reshape(KNOTS_DEV * 4, slots)
        normal = lax.dot_general(
            design * weights[None, :],
            design,
            (((1,), (1,)), ((), ())),
            precision=lax.Precision.HIGHEST,
            preferred_element_type=jnp.float32,
        )
        right = jnp.dot(
            design,
            weights * values,
            precision=lax.Precision.HIGHEST,
            preferred_element_type=jnp.float32,
        )
        return (normal, right)

    return lax.map(block_single, (spread, knot_base, weighted, resid))


def plain_body(
    observed,
    weight_obs,
    present,
    source_partials,
    attitude_partials,
    phase,
    knot_base,
    source_id,
    cal_id,
    attitude,
    calibration,
):
    weighted = present.astype(jnp.float32) * weight_obs
    terms = spline_terms(phase, attitude_partials)
    flat_cal = cal_id.reshape(-1)
    local = attitude
    cal_now = calibration
    params = jnp.zeros((5, SRC_DEV), jnp.float32)
    for sweep in range(2):
        target = observed - attitude_model(local, terms, knot_base) - cal_now[cal_id]
        params = source_solve(source_id, SRC_DEV, weighted, source_partials, target)
        resid = target - jnp.sum(source_partials * pick_params(params, source_id), axis=0)
        normals, rights = block_normals(terms, knot_base, weighted, resid)
        normal, right = (
            lax.psum_scatter(normals, "tm", scatter_dimension=0, tiled=True),
            lax.psum_scatter(rights, "tm", scatter_dimension=0, tiled=True),
        )
        normal, right = lax.psum((normal[0], right[0]), "src")
        local = local + spd_solve(normal, right)
        numer = jax.ops.segment_sum((weighted * resid).reshape(-1), flat_cal, num_segments=CAL)
        denom = jax.ops.segment_sum(weighted.reshape(-1), flat_cal, num_segments=CAL)
        numer, denom = lax.psum((numer, denom), ("src", "tm"))
        cal_now = cal_now + numer / (denom + 1.0)
    final = observed - attitude_model(local, terms, knot_base) - cal_now[cal_id]
    final = final - jnp.sum(source_partials * pick_params(params, source_id), axis=0)
    return (params, local, cal_now, final)


BAND = 16
PIECE = 2


def fetch(pairs, sems):
    copies = [
        pltpu.make_async_copy(origin, held, sems.at[place])
        for place, (origin, held) in enumerate(pairs)
    ]
    for copy in copies:
        copy.start()
    for copy in copies:
        copy.wait()


def tile_of(value):
    return jnp.concatenate(
        [value[:, at : at + LANES] for at in range(0, value.shape[1], LANES)], axis=0
    )


def pick_from(table_t, ids, units, rows):
    found = dot(jnp.concatenate(split3(table_t), axis=0), units)
    found = found[:LANES] + found[LANES : 2 * LANES] + found[2 * LANES :]
    hit = iota(found.shape, 0) == ids % LANES
    return unflat(jnp.sum(jnp.where(hit, found, 0.0), axis=0, keepdims=True), rows)


def two_parts(line):
    first = line.astype(BF16).astype(F32)
    return first, (line - first).astype(BF16).astype(F32)


def model_of(line, parts):
    first, second = two_parts(line)
    left = jnp.concatenate([first, first], axis=1)
    right = jnp.concatenate([second, jnp.zeros_like(second)], axis=1)
    row = iota((SUB, 2 * WIDTH), 0)
    both = jnp.where(row == 0, left, jnp.where(row == 1, right, 0.0)).astype(BF16)
    return jnp.sum(dot(both, parts), axis=0, keepdims=True)


def side_of(values, parts):
    first, second = two_parts(values)
    row = iota((SUB, values.shape[1]), 0)
    both = jnp.where(row == 0, first, jnp.where(row == 1, second, 0.0)).astype(BF16)
    found = dot_t(both, parts)
    return found[0:1, :WIDTH] + found[1:2, :WIDTH] + found[0:1, WIDTH:]


def normals_kernel(
    observed_in, weight_in, present_in, source_in, attitude_in, phase_in, knot_in, id_in, cal_in,
    start_in,
    send_out, design_out, weighted_out, observed, source_id, cal_id, source_partials,
    weight_obs, present, attitude_partials, phase, knot_base, start, stacked, sems,
):
    fetch(
        [
            (observed_in, observed), (weight_in, weight_obs), (present_in, present),
            (source_in, source_partials), (attitude_in, attitude_partials), (phase_in, phase),
            (knot_in, knot_base), (id_in, source_id), (cal_in, cal_id), (start_in, start),
        ],
        sems,
    )
    rows, slots = observed.shape
    weighted = present[...].astype(F32) * weight_obs[...]
    weighted_out[...] = weighted
    u = phase[...]
    other = 1.0 - u
    square = u * u
    cube = square * u
    basis = [
        other * other * other / 6.0,
        (3.0 * cube - 6.0 * square + 4.0) / 6.0,
        (-3.0 * cube + 3.0 * square + 3.0 * u + 1.0) / 6.0,
        cube / 6.0,
    ]
    first, second = tile_of(cal_id[...].astype(F32)), tile_of(weighted)
    devices = send_out.shape[0]
    for device in range(devices):
        core = core_of(device, rows)
        for index in range(rows):
            at = rows * core + index
            send_out[device, PIECE + index] = first[at : at + 1]
            send_out[device, PIECE + rows + index] = second[at : at + 1]
        send_out[device, PIECE + 2 * rows] = start[...]
    for row in range(rows):
        at = slice(row, row + 1)
        for channel in range(4):
            lines = attitude_partials[channel, at]
            stacked[row, channel : channel + 1] = lines
            stacked[row, channel + 4 : channel + 5] = lines
        design = design_of(knot_base[at], [part[at] for part in basis], stacked[row])
        design_out[row] = design
        band = pack_band(exact_dot_t(design * weighted[at], design))
        half, place = divmod(row, rows // PIECE)
        for index in range(BAND):
            send_out[place * BAND + index, half] = band[index : index + 1]


def sources_kernel(
    observed, source_partials, source_id, cal_id, weighted, design, calibration,
    partials_out, factor_out, target_out, table_out, hits_out, units_out, parts_out, table, sem,
):
    copy = pltpu.make_async_copy(calibration, table, sem)
    copy.start()
    rows, slots = observed.shape
    matrix = jnp.zeros((40, SRC_DEV), F32)
    for row in range(rows):
        at = slice(row, row + 1)
        for index in range(5):
            partials_out[row, index : index + 1] = source_partials[index, at]
        partials_out[row, 5:] = jnp.zeros((SUB - 5, slots), F32)
        partials = partials_out[row]
        products = jnp.concatenate(
            [partials * (weighted[at] * partials[index : index + 1]) for index in range(5)], axis=0
        )
        hits_out[row] = one_hot(source_id[at], SRC_DEV)
        found = dot_t(jnp.concatenate(split3(products), axis=0), hits_out[row])
        matrix = matrix + found[:40] + found[40:80] + found[80:]
        first, second, unused = split3(design[row])
        parts_out[row, :WIDTH] = first
        parts_out[row, WIDTH:] = second
    ids = flat(cal_id[...])
    units_out[...] = one_hot(ids // LANES, HIGH)
    inverse = small_factor(matrix)
    for place, pair in enumerate(PLACES):
        factor_out[place : place + 1] = inverse[pair]
    factor_out[15:16] = jnp.zeros((1, SRC_DEV), F32)
    copy.wait()
    table_t = table[...].T
    table_out[...] = table_t
    for row, picked in enumerate(pick_from(table_t, ids, units_out[...], rows)):
        target_out[row : row + 1] = observed[row : row + 1] - picked


def core_of(device, line):
    return device // line % 2


def residual_step(targets, parts, partials, factor, weighted, hits, send_out):
    rows = len(targets)
    inverse = {pair: factor[place : place + 1] for place, pair in enumerate(PLACES)}
    sides = jnp.zeros((SUB, SRC_DEV), F32)
    for row in range(rows):
        products = partials[row] * (weighted[row : row + 1] * targets[row])
        found = dot_t(jnp.concatenate(split3(products), axis=0), hits[row])
        sides = sides + found[:SUB] + found[SUB : 2 * SUB] + found[2 * SUB :]
    params = small_apply(inverse, [sides[index : index + 1] for index in range(5)])
    table = jnp.concatenate(params + [jnp.zeros((3, SRC_DEV), F32)], axis=0)
    split = jnp.concatenate(split3(table), axis=0)
    explained, scaled, rights = [], [], []
    for row in range(rows):
        found = dot(split, hits[row])
        found = found[:SUB] + found[SUB : 2 * SUB] + found[2 * SUB :]
        explained.append(jnp.sum(found * partials[row], axis=0, keepdims=True))
    for row in range(rows):
        scaled.append(weighted[row : row + 1] * (targets[row] - explained[row]))
        rights.append(side_of(scaled[row], parts[row]))
    half = rows // PIECE
    for device in range(send_out.shape[0]):
        core = core_of(device, rows)
        lines = [line[:, core * LANES : (core + 1) * LANES] for line in scaled]
        for index, line in enumerate(lines + rights[half * core : half * core + half]):
            send_out[device, index] = line
    return params, explained


def first_kernel(received, target, parts, partials, factor, weighted, hits, send_out):
    rows = parts.shape[0]
    last = received.shape[1] - 1
    targets = [
        target[row : row + 1] - model_of(received[row, last], parts[row]) for row in range(rows)
    ]
    residual_step(targets, parts, partials, factor, weighted, hits, send_out)
    totals = [right_side(received, place) for place in range(PIECE)]
    for device in range(send_out.shape[0]):
        send_out[device, send_out.shape[1] - 1] = totals[core_of(device, rows)]


def wide(row, count):
    tile = jnp.broadcast_to(row, (16, LANES)).astype(BF16)
    return jnp.concatenate([tile] * (count // 16), axis=0)


def unit_sums(received, value_of, total):
    rows = (received.shape[1] - PIECE - 1) // 2
    low_row = iota((LANES, LANES), 0).astype(F32).astype(BF16)
    high_row = iota((HIGH, LANES), 0).astype(F32).astype(BF16)
    one, none = jnp.ones((), BF16), jnp.zeros((), BF16)
    for begin in range(0, received.shape[0], 2):
        lefts, rights = [], []
        for device in (begin, begin + 1):
            for index in range(rows):
                unit = received[device, PIECE + index]
                high = jnp.floor(unit * (1.0 / LANES))
                hit = low_row == wide(unit - LANES * high, LANES)
                value = value_of(device, index)
                first = value.astype(BF16).astype(F32)
                lefts.append(
                    jnp.concatenate(
                        [
                            jnp.where(hit, wide(first, LANES), none),
                            jnp.where(hit, wide(value - first, LANES), none),
                        ],
                        axis=0,
                    )
                )
                rights.append(jnp.where(high_row == wide(high, HIGH), one, none))
        found = dot_t(jnp.concatenate(lefts, axis=1), jnp.concatenate(rights, axis=1))
        if begin == 0:
            total[:LANES] = found[:LANES] + found[LANES:]
        else:
            total[:LANES] += found[:LANES] + found[LANES:]
        yield


def matrix_of(band):
    lower = unpack_band(band)
    diagonal = iota(lower.shape, 0) == iota(lower.shape, 1)
    return lower + jnp.where(diagonal, 1.0, lower.T)


def together(works):
    works = list(works)
    while works:
        for work in list(works):
            if next(work, works) is works:
                works.remove(work)


def weights_kernel(received, sums_out):
    rows = (received.shape[1] - PIECE - 1) // 2
    together(
        [
            unit_sums(
                received, lambda device, index: received[device, PIECE + rows + index], sums_out
            )
        ]
    )


def right_side(values, place):
    total = values[0, place]
    for device in range(1, values.shape[0]):
        total = total + values[device, place]
    return total


def core(axis):
    return lax.rem(lax.axis_index(axis), 2)


def coefficients(bundle, place):
    return bundle[LANES + place : LANES + place + 1, :WIDTH]


def put(bundle, place, line):
    bundle[LANES + place : LANES + place + 1] = jnp.concatenate([line, line], axis=1)


def solve_kernel(axis, values, received, bundle_out, lines_out, bands):
    half = lines_out.shape[0]
    rows = values.shape[1] - half - 1
    for device in range(values.shape[0]):
        bands[device : device + 1] = values[device, rows + half]
    bundle_out[LANES:] = jnp.zeros((SUB, HIGH), F32)

    def attitude(place):
        matrix = matrix_of(bands[BAND * place : BAND * (place + 1)])
        change = yield from eliminate(matrix, right_side(values, rows + place), lines_out.at[place])
        start = received[half * core(axis) + place, received.shape[1] - 1]
        put(bundle_out, place, start + change)
        yield

    together(
        [unit_sums(received, lambda device, index: values[device, index], bundle_out)]
        + [attitude(place) for place in range(half)]
    )


def both_halves(axis, own, other, half):
    first = core(axis) == 0
    pairs = [(coefficients(own, place), coefficients(other, place)) for place in range(half)]
    lines = [jnp.where(first, one, two) for one, two in pairs]
    return lines + [jnp.where(first, two, one) for one, two in pairs]


def second_kernel(
    axis, bundle, other, weights, other_weights, table, ids, units, observed, parts, partials, factor,
    weighted, hits,
    send_out, params_out, explained_out, table_out, scale_out,
):
    rows = parts.shape[0]
    scale = 1.0 / (weights[...] + other_weights[...] + 1.0)
    scale_out[...] = scale
    table_t = table[...] + (bundle[:LANES] + other[:LANES]) * scale
    table_out[...] = table_t
    picked = pick_from(table_t, flat(ids[...]), units[...], rows)
    lines = both_halves(axis, bundle, other, rows // PIECE)
    targets = [
        observed[row : row + 1] - model_of(lines[row], parts[row]) - picked[row]
        for row in range(rows)
    ]
    params, explained = residual_step(targets, parts, partials, factor, weighted, hits, send_out)
    for index in range(5):
        params_out[index : index + 1] = params[index]
    for row in range(rows):
        explained_out[row : row + 1] = explained[row]


def last_kernel(values, received, bundle, lines, bundle_out):
    half = lines.shape[0]
    rows = values.shape[1] - half
    bundle_out[LANES:] = jnp.zeros((SUB, HIGH), F32)

    def solve(place):
        change = yield from substitute(right_side(values, rows + place), lines.at[place])
        put(bundle_out, place, coefficients(bundle, place) + change)
        yield

    together(
        [unit_sums(received, lambda device, index: values[device, index], bundle_out)]
        + [solve(place) for place in range(half)]
    )


def final_kernel(
    axis, line, bundle, other, table, scale, ids, units, observed, parts, explained,
    cal_out, attitude_out, resid_out,
):
    rows = parts.shape[0]
    table_t = table[...] + (bundle[:LANES] + other[:LANES]) * scale[...]
    cal_out[...] = table_t.T
    picked = pick_from(table_t, flat(ids[...]), units[...], rows)
    me = lax.axis_index(line)
    lines = both_halves(axis, bundle, other, rows // PIECE)
    own = lines[0]
    for row in range(rows):
        own = jnp.where(me == row, lines[row], own)
        at = slice(row, row + 1)
        resid_out[at] = observed[at] - model_of(lines[row], parts[row]) - picked[row] - explained[at]
    attitude_out[...] = own


VMEM = pl.BlockSpec(memory_space=pltpu.VMEM)
ANY = pl.BlockSpec(memory_space=pltpu.HBM)


def call(kernel, outs, *args, away=0, scratch=()):
    near = args[: len(args) - away]
    far = [pltpu.with_memory_space_constraint(arg, pltpu.HBM) for arg in args[len(args) - away :]]
    return pl.pallas_call(
        kernel,
        out_shape=outs,
        in_specs=[VMEM] * len(near) + [ANY] * away,
        out_specs=[VMEM] * len(outs),
        scratch_shapes=scratch,
        compiler_params=pltpu.CompilerParams(vmem_limit_bytes=VMEM_BYTES),
    )(*near, *far)


def stay(*shape, dtype=F32):
    return pltpu.VMEM(shape, dtype)


def leave(*shape):
    return jax.ShapeDtypeStruct(shape, F32)


def swap(value):
    return lax.ppermute(value, "src", [(at, at ^ 1) for at in range(lax.axis_size("src"))])


def exchange(value):
    return lax.all_to_all(value, ("src", "tm"), 0, 0, tiled=True)


def body(
    observed, weight_obs, present, source_partials, attitude_partials, phase, knot_base, source_id,
    cal_id, attitude, calibration,
):
    rows, slots = observed.shape
    devices = lax.axis_size("src") * lax.axis_size("tm")
    half = rows // PIECE
    first_q = attitude.reshape(1, WIDTH)
    held = [weight_obs, present, attitude_partials, phase, knot_base, first_q]
    received, design, weighted, seen, source_id, cal_id, source_partials = call(
        normals_kernel,
        [
            leave(devices, PIECE + 2 * rows + 1, 1, LANES), stay(rows, WIDTH, slots),
            stay(rows, slots), stay(rows, slots), stay(rows, slots, dtype=jnp.int32),
            stay(rows, slots, dtype=jnp.int32), stay(*source_partials.shape),
        ],
        observed, weight_obs, present, source_partials, attitude_partials, phase, knot_base,
        source_id, cal_id, first_q,
        away=10,
        scratch=[pltpu.VMEM(each.shape, each.dtype) for each in held]
        + [pltpu.VMEM((rows, SUB, slots), F32), pltpu.SemaphoreType.DMA((10,))],
    )
    received = exchange(received)
    partials, factor, target, table, hits, units, parts = call(
        sources_kernel,
        [
            stay(rows, SUB, slots), stay(16, SRC_DEV), stay(rows, slots), stay(LANES, HIGH),
            stay(rows, SRC_DEV, slots, dtype=BF16), stay(HIGH, rows * slots, dtype=BF16),
            stay(rows, 2 * WIDTH, slots, dtype=BF16),
        ],
        seen, source_partials, source_id, cal_id, weighted, design, calibration.reshape(HIGH, LANES),
        away=1,
        scratch=[pltpu.VMEM((HIGH, LANES), F32), pltpu.SemaphoreType.DMA],
    )
    received, factor = lax.optimization_barrier((received, factor))
    (values,) = call(
        first_kernel, [leave(devices, rows + half + 1, 1, LANES)],
        received, target, parts, partials, factor, weighted, hits,
    )
    values, received = lax.optimization_barrier((values, received))
    values = exchange(values)
    (weights,) = call(weights_kernel, [leave(LANES, HIGH)], received)
    weights, received = lax.optimization_barrier((weights, received))
    other_weights = swap(weights)
    bundle, lines = call(
        functools.partial(solve_kernel, "src"),
        [leave(LANES + SUB, HIGH), stay(half, WIDTH, WIDTH)],
        values, received,
        scratch=[pltpu.VMEM((half * BAND, WIDTH), F32)],
    )
    values, params, explained, table, scale = call(
        functools.partial(second_kernel, "src"),
        [
            leave(devices, rows + half, 1, LANES), leave(5, SRC_DEV), stay(rows, slots),
            stay(LANES, HIGH), stay(LANES, HIGH),
        ],
        bundle, swap(bundle), weights, other_weights, table, cal_id, units, seen, parts, partials,
        factor, weighted, hits,
    )
    values = exchange(values)
    (bundle,) = call(
        last_kernel, [leave(LANES + SUB, HIGH)], values, received, bundle, lines
    )
    cal, now, final = call(
        functools.partial(final_kernel, "src", "tm"),
        [leave(HIGH, LANES), leave(1, WIDTH), leave(rows, slots)],
        bundle, swap(bundle), table, scale, cal_id, units, seen, parts, explained,
    )
    return (params, now.reshape(WIDTH), cal.reshape(CAL), final)


def solution(mesh):
    many = mesh.shape["src"] * mesh.shape["tm"]
    return jax.shard_map(
        body if many * PIECE == mesh.shape["tm"] * BAND else plain_body,
        mesh=mesh,
        in_specs=(
            P(None, ("src", "tm")),
            P(None, ("src", "tm")),
            P(None, ("src", "tm")),
            P(None, None, ("src", "tm")),
            P(None, None, ("src", "tm")),
            P(None, ("src", "tm")),
            P(None, ("src", "tm")),
            P(None, ("src", "tm")),
            P(None, ("src", "tm")),
            P("tm"),
            P(),
        ),
        out_specs=(P(None, ("src", "tm")), P("tm"), P(), P(None, ("src", "tm"))),
        check_vma=False,
    )
```

```python
import functools

import jax
import jax.numpy as jnp
from jax import lax
from jax.experimental import pallas as pl
from jax.experimental.pallas import tpu as pltpu
from jax.sharding import PartitionSpec as P

KNOTS_DEV = 32
WIDTH = 4 * KNOTS_DEV
SRC_DEV = 128
CAL = 32768
LANES = 128
HIGH = CAL // LANES
SUB = 8
VMEM_BYTES = 48 * 1024 * 1024

F32 = jnp.float32
BF16 = jnp.bfloat16
EXACT = lax.Precision.HIGHEST


def iota(shape, dim):
    return lax.broadcasted_iota(jnp.int32, shape, dim)


def split3(value):
    first = value.astype(BF16)
    rest = value - first.astype(F32)
    second = rest.astype(BF16)
    third = (rest - second.astype(F32)).astype(BF16)
    return first, second, third


def dot(left, right):
    return lax.dot_general(left, right, (((1,), (0,)), ((), ())), preferred_element_type=F32)


def dot_t(left, right):
    return lax.dot_general(left, right, (((1,), (1,)), ((), ())), preferred_element_type=F32)


def exact_dot(left, right):
    return lax.dot_general(
        left, right, (((1,), (0,)), ((), ())), precision=EXACT, preferred_element_type=F32
    )


def exact_dot_t(left, right):
    return lax.dot_general(
        left, right, (((1,), (1,)), ((), ())), precision=EXACT, preferred_element_type=F32
    )


def one_hot(ids, count):
    return jnp.where(iota((count, ids.shape[1]), 0) == ids, 1.0, 0.0).astype(BF16)


def flat(value):
    return jnp.concatenate([value[row : row + 1] for row in range(value.shape[0])], axis=1)


def unflat(value, rows):
    slots = value.shape[1] // rows
    return [value[:, row * slots : (row + 1) * slots] for row in range(rows)]


def cal_pick(table, ids):
    parts = jnp.concatenate(split3(table.T), axis=0)
    high = ids // LANES
    low = ids % LANES
    found = dot(parts, one_hot(high, HIGH))
    found = found[:LANES] + found[LANES : 2 * LANES] + found[2 * LANES :]
    return jnp.sum(jnp.where(iota(found.shape, 0) == low, found, 0.0), axis=0, keepdims=True)


def cal_sums(values, ids):
    high = one_hot(ids // LANES, HIGH)
    low = iota((LANES, ids.shape[1]), 0) == ids % LANES
    total = None
    for part in split3(values):
        spread = jnp.where(low, part.astype(F32), 0.0).astype(BF16)
        added = dot_t(high, spread)
        total = added if total is None else total + added
    return total


def design_of(base, basis, partials):
    slots = base.shape[1]
    knot = iota((WIDTH, slots), 0) // 4
    step = knot - base
    spread = jnp.zeros((WIDTH, slots), F32)
    for index in range(4):
        spread = jnp.where(step == index, basis[index], spread)
    return spread * jnp.concatenate([partials] * (WIDTH // 8), axis=0)


def band_shift(tile, knot):
    return ((tile % 8) * 16 - (8 * tile + 4 * knot - 12)) % WIDTH


def pack_band(normal):
    place = iota((8, WIDTH), 1) // 16
    upper = iota((8, WIDTH), 0) < 4
    groups = []
    for group in range(2):
        packed = jnp.zeros((8, WIDTH), F32)
        for tile in range(8 * group, 8 * group + 8):
            rows = normal[8 * tile : 8 * tile + 8]
            rolled = jnp.where(
                upper,
                pltpu.roll(rows, band_shift(tile, 0), 1),
                pltpu.roll(rows, band_shift(tile, 1), 1),
            )
            packed = jnp.where(place == tile % 8, rolled, packed)
        groups.append(packed)
    return jnp.concatenate(groups, axis=0)


def unpack_band(packed):
    place = iota((8, WIDTH), 1) // 16
    upper = iota((8, WIDTH), 0) < 4
    tiles = []
    for tile in range(16):
        group = tile // 8
        rows = jnp.where(place == tile % 8, packed[8 * group : 8 * group + 8], 0.0)
        tiles.append(
            jnp.where(
                upper,
                pltpu.roll(rows, (-band_shift(tile, 0)) % WIDTH, 1),
                pltpu.roll(rows, (-band_shift(tile, 1)) % WIDTH, 1),
            )
        )
    full = jnp.concatenate(tiles, axis=0)
    return jnp.where(iota(full.shape, 0) >= iota(full.shape, 1), full, 0.0)


ORDER = (
    (0, 8, 17, 31), (1, 9, 18, 30), (2, 10, 19, 29), (3, 11, 20, 28), (4, 12, 21, 27), (13, 22, 26),
    (5, 23), (6, 24), (7, 25), (14,), (15,), (16,),
)


def plan_of(order):
    near = {
        knot: {other for other in range(KNOTS_DEV) if 0 < abs(other - knot) <= 3}
        for knot in range(KNOTS_DEV)
    }
    plan = []
    for step in order:
        plan.append([(knot, sorted({other // 2 for other in near[knot]})) for knot in step])
        for knot in step:
            assert not near[knot] & set(step)
            for other in near[knot]:
                near[other] = (near[other] | near[knot]) - {other, knot}
    return plan


PLAN = plan_of(ORDER)


def reciprocal(value):
    found = pl.reciprocal(value, approx=True)
    found = found * (2.0 - value * found)
    return found * (2.0 - value * found)


def block_rows(entry, lines):
    scale = reciprocal(entry[0, 0] * entry[1, 1] - entry[0, 1] * entry[0, 1])
    low, mid, high = entry[0, 0] * scale, entry[0, 1] * scale, entry[1, 1] * scale
    turned = {}
    for column in (2, 3):
        turned[0, column] = high * entry[0, column] - mid * entry[1, column]
        turned[1, column] = low * entry[1, column] - mid * entry[0, column]
    rest = {}
    for row, column in ((2, 2), (2, 3), (3, 3)):
        taken = entry[0, row] * turned[0, column] + entry[1, row] * turned[1, column]
        rest[row, column] = entry[row, column] - taken
    upper = [high * lines[0] - mid * lines[1], low * lines[1] - mid * lines[0]]
    lower = [
        lines[row] - (entry[0, row] * upper[0] + entry[1, row] * upper[1]) for row in (2, 3)
    ]
    scale = reciprocal(rest[2, 2] * rest[3, 3] - rest[2, 3] * rest[2, 3])
    third = (rest[3, 3] * scale) * lower[0] - (rest[2, 3] * scale) * lower[1]
    fourth = (rest[2, 2] * scale) * lower[1] - (rest[2, 3] * scale) * lower[0]
    return [
        upper[0] - (turned[0, 2] * third + turned[0, 3] * fourth),
        upper[1] - (turned[1, 2] * third + turned[1, 3] * fourth),
        third,
        fourth,
    ]


def eliminate(matrix, right, lines_out):
    shape = (8, WIDTH)
    tiles = [matrix[8 * tile : 8 * tile + 8] for tile in range(WIDTH // 8)]
    lane = iota(shape, 1)
    for step in PLAN:
        held = list(tiles)
        border = right
        for knot, reach in step:
            at, sub, first = knot // 2, 4 * (knot % 2), 4 * knot
            inside = lane // 4 == knot
            columns = {
                tile: [
                    jnp.broadcast_to(held[tile][:, first + index : first + index + 1], shape)
                    for index in range(4)
                ]
                for tile in sorted({at, *reach})
            }
            entry = {
                (one, two): jnp.broadcast_to(columns[at][two][sub + one : sub + one + 1], shape)
                for one in range(4)
                for two in range(one, 4)
            }
            lines = [
                jnp.where(
                    inside,
                    jnp.where(lane == first + index, -1.0, 0.0),
                    jnp.broadcast_to(held[at][sub + index : sub + index + 1], shape),
                )
                for index in range(4)
            ]
            lines = block_rows(entry, lines)
            for index in range(4):
                lines_out[first + index : first + index + 1] = lines[index][0:1]
            for tile in reach:
                factors = columns[tile]
                taken = factors[0] * lines[0] + factors[1] * lines[1]
                taken = taken + (factors[2] * lines[2] + factors[3] * lines[3])
                tiles[tile] = jnp.where(inside, 0.0, tiles[tile]) - taken
            right = swept(right, border, knot, [line[0:1] for line in lines])
        yield
    return right


def swept(right, border, knot, lines):
    first = 4 * knot
    right = jnp.where(iota(right.shape, 1) // 4 == knot, 0.0, right)
    factors = [border[:, first + index : first + index + 1] for index in range(4)]
    taken = factors[0] * lines[0] + factors[1] * lines[1]
    return right - (taken + (factors[2] * lines[2] + factors[3] * lines[3]))


def substitute(right, lines):
    for step in PLAN:
        border = right
        for knot, unused in step:
            kept = [lines[4 * knot + index : 4 * knot + index + 1] for index in range(4)]
            right = swept(right, border, knot, kept)
        yield
    return right


def small_factor(sums):
    factor = {}
    for member in range(5):
        for column in range(member + 1):
            running = sums[8 * member + column : 8 * member + column + 1]
            if member == column:
                running = running + 1.0
            for offset in range(column):
                running = running - factor[member, offset] * factor[column, offset]
            if member == column:
                factor[member, member] = jnp.sqrt(running)
            else:
                factor[member, column] = running * inverse_of[column]
        inverse_of = {} if member == 0 else inverse_of
        inverse_of[member] = 1.0 / factor[member, member]
    inverse = {}
    for column in range(5):
        inverse[column, column] = inverse_of[column]
        for member in range(column + 1, 5):
            running = factor[member, column] * inverse[column, column]
            for offset in range(column + 1, member):
                running = running + factor[member, offset] * inverse[offset, column]
            inverse[member, column] = -running * inverse_of[member]
    return inverse


PLACES = [(row_id, col_id) for row_id in range(5) for col_id in range(row_id + 1)]


def small_apply(inverse, sides):
    forward = []
    for member in range(5):
        running = inverse[member, 0] * sides[0]
        for column in range(1, member + 1):
            running = running + inverse[member, column] * sides[column]
        forward.append(running)
    result = []
    for column in range(5):
        running = inverse[column, column] * forward[column]
        for member in range(column + 1, 5):
            running = running + inverse[member, column] * forward[member]
        result.append(running)
    return result


PAIRS = [(row_id, col_id) for row_id in range(5) for col_id in range(row_id + 1)]


def spline_terms(phase, attitude_partials):
    other = 1.0 - phase
    square = phase * phase
    cube = square * phase
    basis = [
        other * other * other / 6.0,
        (3.0 * cube - 6.0 * square + 4.0) / 6.0,
        (-3.0 * cube + 3.0 * square + 3.0 * phase + 1.0) / 6.0,
        cube / 6.0,
    ]
    return jnp.stack(
        [
            basis[knot_step] * attitude_partials[channel]
            for knot_step in range(4)
            for channel in range(4)
        ]
    )


def attitude_model(local, terms, knot_base):
    coefficients = lax.all_gather(local, "tm", axis=0, tiled=True)
    blocks, slots = knot_base.shape
    table = coefficients.reshape(blocks, -1, 4)
    knots_count = table.shape[1]
    grid = lax.broadcasted_iota(jnp.int32, (1, knots_count, 1), 1)
    running = jnp.zeros(knot_base.shape, jnp.float32)
    for knot_step in range(4):
        hit = (grid == (knot_base + knot_step)[:, None, :]).astype(jnp.float32)
        picked = jnp.einsum(
            "bkc,bks->bcs",
            table,
            hit,
            precision=lax.Precision.HIGHEST,
            preferred_element_type=jnp.float32,
        )
        for channel in range(4):
            running = running + terms[4 * knot_step + channel] * picked[:, channel, :]
    return running


def small_solve(matrix, right_side):
    extent = len(right_side)
    factor = {}
    for member in range(extent):
        for column in range(member + 1):
            running = matrix[member][column]
            for offset in range(column):
                running = running - factor[member, offset] * factor[column, offset]
            if member == column:
                factor[member, member] = jnp.sqrt(running)
            else:
                factor[member, column] = running / factor[column, column]
    forward = []
    for member in range(extent):
        running = right_side[member]
        for offset in range(member):
            running = running - factor[member, offset] * forward[offset]
        forward.append(running / factor[member, member])
    result = [None] * extent
    for member in reversed(range(extent)):
        running = forward[member]
        for offset in range(member + 1, extent):
            running = running - factor[offset, member] * result[offset]
        result[member] = running / factor[member, member]
    return jnp.stack(result)


def source_solve(ids, count, weighted, source_partials, target):
    products = [
        weighted * source_partials[row_id] * source_partials[col_id] for row_id, col_id in PAIRS
    ]
    products = products + [weighted * source_partials[row_id] * target for row_id in range(5)]
    stacked = jnp.moveaxis(jnp.stack(products), 1, 0)
    owners = lax.broadcasted_iota(jnp.int32, (count, 1), 0)

    def accumulate(total, item):
        values, block_ids = item
        hit = (block_ids[None, :] == owners).astype(jnp.float32)
        added = lax.dot_general(
            values,
            hit,
            (((1,), (1,)), ((), ())),
            precision=lax.Precision.HIGHEST,
            preferred_element_type=jnp.float32,
        )
        return (total + added, None)

    sums, unused = lax.scan(
        accumulate, jnp.zeros((len(products), count), jnp.float32), (stacked, ids)
    )
    entries = {}
    for position, pair in enumerate(PAIRS):
        entry_value = sums[position] + (1.0 if pair[0] == pair[1] else 0.0)
        entries[pair[0], pair[1]] = entry_value
        entries[pair[1], pair[0]] = entry_value
    matrix = [[entries[row_id, col_id] for col_id in range(5)] for row_id in range(5)]
    return small_solve(matrix, [sums[15 + row_id] for row_id in range(5)])


def pick_params(params, ids):
    count = params.shape[1]
    owners = lax.broadcasted_iota(jnp.int32, (count, 1), 0)

    def pick_single(carry, block_ids):
        hit = (block_ids[None, :] == owners).astype(jnp.float32)
        return (
            carry,
            jnp.dot(
                params, hit, precision=lax.Precision.HIGHEST, preferred_element_type=jnp.float32
            ),
        )

    unused, picked = lax.scan(pick_single, 0, ids)
    return jnp.moveaxis(picked, 1, 0)


def spd_solve(matrix, right_side):
    eye = jnp.eye(matrix.shape[-1], dtype=jnp.float32)
    lower = jnp.linalg.cholesky(matrix + eye)
    middle = lax.linalg.triangular_solve(lower, right_side[..., None], left_side=True, lower=True)
    result = lax.linalg.triangular_solve(
        lower, middle, left_side=True, lower=True, transpose_a=True
    )
    return result[..., 0]


def block_normals(terms, knot_base, weighted, resid):
    blocks, slots = knot_base.shape
    spread = jnp.moveaxis(terms.reshape(4, 4, blocks, slots), 2, 0)

    def block_single(item):
        part, base, weights, values = item
        grid = lax.broadcasted_iota(jnp.int32, (KNOTS_DEV, slots), 0)
        design = jnp.zeros((KNOTS_DEV, 4, slots), jnp.float32)
        for knot_step in range(4):
            hit = (grid == base[None, :] + knot_step).astype(jnp.float32)
            design = design + hit[:, None, :] * part[knot_step][None, :, :]
        design = design.reshape(KNOTS_DEV * 4, slots)
        normal = lax.dot_general(
            design * weights[None, :],
            design,
            (((1,), (1,)), ((), ())),
            precision=lax.Precision.HIGHEST,
            preferred_element_type=jnp.float32,
        )
        right = jnp.dot(
            design,
            weights * values,
            precision=lax.Precision.HIGHEST,
            preferred_element_type=jnp.float32,
        )
        return (normal, right)

    return lax.map(block_single, (spread, knot_base, weighted, resid))


def plain_body(
    observed,
    weight_obs,
    present,
    source_partials,
    attitude_partials,
    phase,
    knot_base,
    source_id,
    cal_id,
    attitude,
    calibration,
):
    weighted = present.astype(jnp.float32) * weight_obs
    terms = spline_terms(phase, attitude_partials)
    flat_cal = cal_id.reshape(-1)
    local = attitude
    cal_now = calibration
    params = jnp.zeros((5, SRC_DEV), jnp.float32)
    for sweep in range(2):
        target = observed - attitude_model(local, terms, knot_base) - cal_now[cal_id]
        params = source_solve(source_id, SRC_DEV, weighted, source_partials, target)
        resid = target - jnp.sum(source_partials * pick_params(params, source_id), axis=0)
        normals, rights = block_normals(terms, knot_base, weighted, resid)
        normal, right = (
            lax.psum_scatter(normals, "tm", scatter_dimension=0, tiled=True),
            lax.psum_scatter(rights, "tm", scatter_dimension=0, tiled=True),
        )
        normal, right = lax.psum((normal[0], right[0]), "src")
        local = local + spd_solve(normal, right)
        numer = jax.ops.segment_sum((weighted * resid).reshape(-1), flat_cal, num_segments=CAL)
        denom = jax.ops.segment_sum(weighted.reshape(-1), flat_cal, num_segments=CAL)
        numer, denom = lax.psum((numer, denom), ("src", "tm"))
        cal_now = cal_now + numer / (denom + 1.0)
    final = observed - attitude_model(local, terms, knot_base) - cal_now[cal_id]
    final = final - jnp.sum(source_partials * pick_params(params, source_id), axis=0)
    return (params, local, cal_now, final)


BAND = 16
PIECE = 2


def fetch(pairs, sems):
    copies = [
        pltpu.make_async_copy(origin, held, sems.at[place])
        for place, (origin, held) in enumerate(pairs)
    ]
    for copy in copies:
        copy.start()
    for copy in copies:
        copy.wait()


def tile_of(value):
    return jnp.concatenate(
        [value[:, at : at + LANES] for at in range(0, value.shape[1], LANES)], axis=0
    )


def pick_from(table_t, ids, units, rows):
    found = dot(jnp.concatenate(split3(table_t)[:2], axis=0), units)
    found = found[:LANES] + found[LANES:]
    hit = iota(found.shape, 0) == ids % LANES
    return unflat(jnp.sum(jnp.where(hit, found, 0.0), axis=0, keepdims=True), rows)


def two_parts(line):
    first = line.astype(BF16).astype(F32)
    return first, (line - first).astype(BF16).astype(F32)


def model_of(line, parts):
    first, second = two_parts(line)
    left = jnp.concatenate([first, first], axis=1)
    right = jnp.concatenate([second, jnp.zeros_like(second)], axis=1)
    row = iota((SUB, 2 * WIDTH), 0)
    both = jnp.where(row == 0, left, jnp.where(row == 1, right, 0.0)).astype(BF16)
    return jnp.sum(dot(both, parts), axis=0, keepdims=True)


def side_of(values, parts):
    first, second = two_parts(values)
    row = iota((SUB, values.shape[1]), 0)
    both = jnp.where(row == 0, first, jnp.where(row == 1, second, 0.0)).astype(BF16)
    found = dot_t(both, parts)
    return found[0:1, :WIDTH] + found[1:2, :WIDTH] + found[0:1, WIDTH:]


def normals_kernel(
    weight_in, present_in, attitude_in, phase_in, knot_in, cal_in, start_in,
    send_out, design_out, weighted_out, cal_id,
    weight_obs, present, attitude_partials, phase, knot_base, start, stacked, sems,
):
    fetch(
        [
            (phase_in, phase), (knot_in, knot_base), (attitude_in, attitude_partials),
            (weight_in, weight_obs), (present_in, present), (cal_in, cal_id), (start_in, start),
        ],
        sems,
    )
    rows = weight_obs.shape[0]
    weighted = present[...].astype(F32) * weight_obs[...]
    weighted_out[...] = weighted
    u = phase[...]
    other = 1.0 - u
    square = u * u
    cube = square * u
    basis = [
        other * other * other / 6.0,
        (3.0 * cube - 6.0 * square + 4.0) / 6.0,
        (-3.0 * cube + 3.0 * square + 3.0 * u + 1.0) / 6.0,
        cube / 6.0,
    ]
    first, second = tile_of(cal_id[...].astype(F32)), tile_of(weighted)
    devices = send_out.shape[0]
    for device in range(devices):
        core = core_of(device, rows)
        for index in range(rows):
            at = rows * core + index
            send_out[device, PIECE + index] = first[at : at + 1]
            send_out[device, PIECE + rows + index] = second[at : at + 1]
        send_out[device, PIECE + 2 * rows] = start[...]
    for row in range(rows):
        at = slice(row, row + 1)
        for channel in range(4):
            lines = attitude_partials[channel, at]
            stacked[row, channel : channel + 1] = lines
            stacked[row, channel + 4 : channel + 5] = lines
        design = design_of(knot_base[at], [part[at] for part in basis], stacked[row])
        design_out[row] = design
        band = pack_band(exact_dot_t(design * weighted[at], design))
        half, place = divmod(row, rows // PIECE)
        for index in range(BAND):
            send_out[place * BAND + index, half] = band[index : index + 1]


def sources_kernel(
    cal_id, weighted, design, observed_in, source_in, id_in, calibration_in,
    partials_out, factor_out, target_out, table_out, hits_out, units_out, parts_out, observed,
    source_partials, source_id, table, sems,
):
    fetch(
        [
            (observed_in, observed), (source_in, source_partials), (id_in, source_id),
            (calibration_in, table),
        ],
        sems,
    )
    rows, slots = observed.shape
    matrix = jnp.zeros((40, SRC_DEV), F32)
    for row in range(rows):
        at = slice(row, row + 1)
        for index in range(5):
            partials_out[row, index : index + 1] = source_partials[index, at]
        partials_out[row, 5:] = jnp.zeros((SUB - 5, slots), F32)
        partials = partials_out[row]
        products = jnp.concatenate(
            [partials * (weighted[at] * partials[index : index + 1]) for index in range(5)], axis=0
        )
        hits_out[row] = one_hot(source_id[at], SRC_DEV)
        found = dot_t(jnp.concatenate(split3(products), axis=0), hits_out[row])
        matrix = matrix + found[:40] + found[40:80] + found[80:]
        first, second, unused = split3(design[row])
        parts_out[row, :WIDTH] = first
        parts_out[row, WIDTH:] = second
    ids = flat(cal_id[...])
    units_out[...] = one_hot(ids // LANES, HIGH)
    inverse = small_factor(matrix)
    for place, pair in enumerate(PLACES):
        factor_out[place : place + 1] = inverse[pair]
    factor_out[15:16] = jnp.zeros((1, SRC_DEV), F32)
    table_t = table[...].T
    table_out[...] = table_t
    for row, picked in enumerate(pick_from(table_t, ids, units_out[...], rows)):
        target_out[row : row + 1] = observed[row : row + 1] - picked


def core_of(device, line):
    return device // line % 2


def residual_step(targets, parts, partials, factor, weighted, hits, send_out):
    rows = len(targets)
    inverse = {pair: factor[place : place + 1] for place, pair in enumerate(PLACES)}
    sides = jnp.zeros((SUB, SRC_DEV), F32)
    for row in range(rows):
        products = partials[row] * (weighted[row : row + 1] * targets[row])
        found = dot_t(jnp.concatenate(split3(products), axis=0), hits[row])
        sides = sides + found[:SUB] + found[SUB : 2 * SUB] + found[2 * SUB :]
    params = small_apply(inverse, [sides[index : index + 1] for index in range(5)])
    table = jnp.concatenate(params + [jnp.zeros((3, SRC_DEV), F32)], axis=0)
    split = jnp.concatenate(split3(table), axis=0)
    explained, scaled, rights = [], [], []
    for row in range(rows):
        found = dot(split, hits[row])
        found = found[:SUB] + found[SUB : 2 * SUB] + found[2 * SUB :]
        explained.append(jnp.sum(found * partials[row], axis=0, keepdims=True))
    for row in range(rows):
        scaled.append(weighted[row : row + 1] * (targets[row] - explained[row]))
        rights.append(side_of(scaled[row], parts[row]))
    half = rows // PIECE
    for device in range(send_out.shape[0]):
        core = core_of(device, rows)
        lines = [line[:, core * LANES : (core + 1) * LANES] for line in scaled]
        for index, line in enumerate(lines + rights[half * core : half * core + half]):
            send_out[device, index] = line
    return params, explained


def first_kernel(received, target, parts, partials, factor, weighted, hits, send_out):
    rows = parts.shape[0]
    last = received.shape[1] - 1
    targets = [
        target[row : row + 1] - model_of(received[row, last], parts[row]) for row in range(rows)
    ]
    residual_step(targets, parts, partials, factor, weighted, hits, send_out)
    totals = [right_side(received, place) for place in range(PIECE)]
    for device in range(send_out.shape[0]):
        send_out[device, send_out.shape[1] - 1] = totals[core_of(device, rows)]


def wide(row, count):
    tile = jnp.broadcast_to(row, (16, LANES)).astype(BF16)
    return jnp.concatenate([tile] * (count // 16), axis=0)


def unit_sums(received, value_of, total):
    rows = (received.shape[1] - PIECE - 1) // 2
    low_row = iota((LANES, LANES), 0).astype(F32).astype(BF16)
    high_row = iota((HIGH, LANES), 0).astype(F32).astype(BF16)
    one, none = jnp.ones((), BF16), jnp.zeros((), BF16)
    for begin in range(0, received.shape[0], 2):
        lefts, rights = [], []
        for device in (begin, begin + 1):
            for index in range(rows):
                unit = received[device, PIECE + index]
                high = jnp.floor(unit * (1.0 / LANES))
                hit = low_row == wide(unit - LANES * high, LANES)
                value = value_of(device, index)
                first = value.astype(BF16).astype(F32)
                lefts.append(
                    jnp.concatenate(
                        [
                            jnp.where(hit, wide(first, LANES), none),
                            jnp.where(hit, wide(value - first, LANES), none),
                        ],
                        axis=0,
                    )
                )
                rights.append(jnp.where(high_row == wide(high, HIGH), one, none))
        found = dot_t(jnp.concatenate(lefts, axis=1), jnp.concatenate(rights, axis=1))
        if begin == 0:
            total[:LANES] = found[:LANES] + found[LANES:]
        else:
            total[:LANES] += found[:LANES] + found[LANES:]
        yield


def matrix_of(band):
    lower = unpack_band(band)
    diagonal = iota(lower.shape, 0) == iota(lower.shape, 1)
    return lower + jnp.where(diagonal, 1.0, lower.T)


def together(works):
    works = list(works)
    while works:
        for work in list(works):
            if next(work, works) is works:
                works.remove(work)


def weights_kernel(received, sums_out):
    rows = (received.shape[1] - PIECE - 1) // 2
    together(
        [
            unit_sums(
                received, lambda device, index: received[device, PIECE + rows + index], sums_out
            )
        ]
    )


def right_side(values, place):
    total = values[0, place]
    for device in range(1, values.shape[0]):
        total = total + values[device, place]
    return total


def core(axis):
    return lax.rem(lax.axis_index(axis), 2)


def coefficients(bundle, place):
    return bundle[LANES + place : LANES + place + 1, :WIDTH]


def put(bundle, place, line):
    bundle[LANES + place : LANES + place + 1] = jnp.concatenate([line, line], axis=1)


def solve_kernel(axis, values, received, bundle_out, lines_out, bands):
    half = lines_out.shape[0]
    rows = values.shape[1] - half - 1
    for device in range(values.shape[0]):
        bands[device : device + 1] = values[device, rows + half]
    bundle_out[LANES:] = jnp.zeros((SUB, HIGH), F32)

    def attitude(place):
        matrix = matrix_of(bands[BAND * place : BAND * (place + 1)])
        change = yield from eliminate(matrix, right_side(values, rows + place), lines_out.at[place])
        start = received[half * core(axis) + place, received.shape[1] - 1]
        put(bundle_out, place, start + change)
        yield

    together(
        [unit_sums(received, lambda device, index: values[device, index], bundle_out)]
        + [attitude(place) for place in range(half)]
    )


def both_halves(axis, own, other, half):
    first = core(axis) == 0
    pairs = [(coefficients(own, place), coefficients(other, place)) for place in range(half)]
    lines = [jnp.where(first, one, two) for one, two in pairs]
    return lines + [jnp.where(first, two, one) for one, two in pairs]


def second_kernel(
    axis, bundle, other, weights, other_weights, table, ids, units, observed, parts, partials, factor,
    weighted, hits,
    send_out, params_out, explained_out, table_out, scale_out,
):
    rows = parts.shape[0]
    scale = 1.0 / (weights[...] + other_weights[...] + 1.0)
    scale_out[...] = scale
    table_t = table[...] + (bundle[:LANES] + other[:LANES]) * scale
    table_out[...] = table_t
    picked = pick_from(table_t, flat(ids[...]), units[...], rows)
    lines = both_halves(axis, bundle, other, rows // PIECE)
    targets = [
        observed[row : row + 1] - model_of(lines[row], parts[row]) - picked[row]
        for row in range(rows)
    ]
    params, explained = residual_step(targets, parts, partials, factor, weighted, hits, send_out)
    for index in range(5):
        params_out[index : index + 1] = params[index]
    for row in range(rows):
        explained_out[row : row + 1] = explained[row]


def last_kernel(values, received, bundle, lines, bundle_out):
    half = lines.shape[0]
    rows = values.shape[1] - half
    bundle_out[LANES:] = jnp.zeros((SUB, HIGH), F32)

    def solve(place):
        change = yield from substitute(right_side(values, rows + place), lines.at[place])
        put(bundle_out, place, coefficients(bundle, place) + change)
        yield

    together(
        [unit_sums(received, lambda device, index: values[device, index], bundle_out)]
        + [solve(place) for place in range(half)]
    )


def final_kernel(
    axis, line, bundle, other, table, scale, ids, units, observed, parts, explained,
    cal_out, attitude_out, resid_out, new_cal, sem,
):
    rows = parts.shape[0]
    table_t = table[...] + (bundle[:LANES] + other[:LANES]) * scale[...]
    new_cal[...] = table_t.T
    copy = pltpu.make_async_copy(new_cal, cal_out, sem)
    copy.start()
    picked = pick_from(table_t, flat(ids[...]), units[...], rows)
    me = lax.axis_index(line)
    lines = both_halves(axis, bundle, other, rows // PIECE)
    own = lines[0]
    for row in range(rows):
        own = jnp.where(me == row, lines[row], own)
        at = slice(row, row + 1)
        resid_out[at] = observed[at] - model_of(lines[row], parts[row]) - picked[row] - explained[at]
    attitude_out[...] = own
    copy.wait()


VMEM = pl.BlockSpec(memory_space=pltpu.VMEM)
ANY = pl.BlockSpec(memory_space=pltpu.HBM)


def call(kernel, outs, *args, away=0, scratch=(), specs=None):
    near = args[: len(args) - away]
    far = [pltpu.with_memory_space_constraint(arg, pltpu.HBM) for arg in args[len(args) - away :]]
    return pl.pallas_call(
        kernel,
        out_shape=outs,
        in_specs=[VMEM] * len(near) + [ANY] * away,
        out_specs=specs or [VMEM] * len(outs),
        scratch_shapes=scratch,
        compiler_params=pltpu.CompilerParams(vmem_limit_bytes=VMEM_BYTES),
    )(*near, *far)


def stay(*shape, dtype=F32):
    return pltpu.VMEM(shape, dtype)


def leave(*shape):
    return jax.ShapeDtypeStruct(shape, F32)


def swap(value):
    return lax.ppermute(value, "src", [(at, at ^ 1) for at in range(lax.axis_size("src"))])


def exchange(value):
    return lax.all_to_all(value, ("src", "tm"), 0, 0, tiled=True)


def body(
    observed, weight_obs, present, source_partials, attitude_partials, phase, knot_base, source_id,
    cal_id, attitude, calibration,
):
    rows, slots = observed.shape
    devices = lax.axis_size("src") * lax.axis_size("tm")
    half = rows // PIECE
    first_q = attitude.reshape(1, WIDTH)
    held = [weight_obs, present, attitude_partials, phase, knot_base, first_q]
    received, design, weighted, units_seen = call(
        normals_kernel,
        [
            leave(devices, PIECE + 2 * rows + 1, 1, LANES), stay(rows, WIDTH, slots),
            stay(rows, slots), stay(rows, slots, dtype=jnp.int32),
        ],
        weight_obs, present, attitude_partials, phase, knot_base, cal_id, first_q,
        away=7,
        scratch=[pltpu.VMEM(each.shape, each.dtype) for each in held]
        + [pltpu.VMEM((rows, SUB, slots), F32), pltpu.SemaphoreType.DMA((7,))],
    )
    received = exchange(received)
    cal_id = units_seen
    partials, factor, target, table, hits, units, parts, seen = call(
        sources_kernel,
        [
            stay(rows, SUB, slots), stay(16, SRC_DEV), stay(rows, slots), stay(LANES, HIGH),
            stay(rows, SRC_DEV, slots, dtype=BF16), stay(HIGH, rows * slots, dtype=BF16),
            stay(rows, 2 * WIDTH, slots, dtype=BF16), stay(rows, slots),
        ],
        cal_id, weighted, design, observed, source_partials, source_id,
        calibration.reshape(HIGH, LANES),
        away=4,
        scratch=[
            pltpu.VMEM(source_partials.shape, F32), pltpu.VMEM((rows, slots), jnp.int32),
            pltpu.VMEM((HIGH, LANES), F32), pltpu.SemaphoreType.DMA((4,)),
        ],
    )
    received, factor = lax.optimization_barrier((received, factor))
    (values,) = call(
        first_kernel, [leave(devices, rows + half + 1, 1, LANES)],
        received, target, parts, partials, factor, weighted, hits,
    )
    values, received = lax.optimization_barrier((values, received))
    values = exchange(values)
    (weights,) = call(weights_kernel, [leave(LANES, HIGH)], received)
    weights, received = lax.optimization_barrier((weights, received))
    other_weights = swap(weights)
    bundle, lines = call(
        functools.partial(solve_kernel, "src"),
        [leave(LANES + SUB, HIGH), stay(half, WIDTH, WIDTH)],
        values, received,
        scratch=[pltpu.VMEM((half * BAND, WIDTH), F32)],
    )
    values, params, explained, table, scale = call(
        functools.partial(second_kernel, "src"),
        [
            leave(devices, rows + half, 1, LANES), leave(5, SRC_DEV), stay(rows, slots),
            stay(LANES, HIGH), stay(LANES, HIGH),
        ],
        bundle, swap(bundle), weights, other_weights, table, cal_id, units, seen, parts, partials,
        factor, weighted, hits,
    )
    values = exchange(values)
    (bundle,) = call(
        last_kernel, [leave(LANES + SUB, HIGH)], values, received, bundle, lines
    )
    cal, now, final = call(
        functools.partial(final_kernel, "src", "tm"),
        [leave(HIGH, LANES), leave(1, WIDTH), leave(rows, slots)],
        bundle, swap(bundle), table, scale, cal_id, units, seen, parts, explained,
        scratch=[pltpu.VMEM((HIGH, LANES), F32), pltpu.SemaphoreType.DMA],
        specs=[ANY, VMEM, VMEM],
    )
    return (params, now.reshape(WIDTH), cal.reshape(CAL), final)


def solution(mesh):
    many = mesh.shape["src"] * mesh.shape["tm"]
    return jax.shard_map(
        body if many * PIECE == mesh.shape["tm"] * BAND else plain_body,
        mesh=mesh,
        in_specs=(
            P(None, ("src", "tm")),
            P(None, ("src", "tm")),
            P(None, ("src", "tm")),
            P(None, None, ("src", "tm")),
            P(None, None, ("src", "tm")),
            P(None, ("src", "tm")),
            P(None, ("src", "tm")),
            P(None, ("src", "tm")),
            P(None, ("src", "tm")),
            P("tm"),
            P(),
        ),
        out_specs=(P(None, ("src", "tm")), P("tm"), P(), P(None, ("src", "tm"))),
        check_vma=False,
    )
```

```python
import functools

import jax
import jax.numpy as jnp
from jax import lax
from jax.experimental import pallas as pl
from jax.experimental.pallas import tpu as pltpu
from jax.sharding import PartitionSpec as P

KNOTS_DEV = 32
WIDTH = 4 * KNOTS_DEV
SRC_DEV = 128
CAL = 32768
LANES = 128
HIGH = CAL // LANES
SUB = 8
VMEM_BYTES = 48 * 1024 * 1024

F32 = jnp.float32
BF16 = jnp.bfloat16
EXACT = lax.Precision.HIGHEST


def iota(shape, dim):
    return lax.broadcasted_iota(jnp.int32, shape, dim)


def split3(value):
    first = value.astype(BF16)
    rest = value - first.astype(F32)
    second = rest.astype(BF16)
    third = (rest - second.astype(F32)).astype(BF16)
    return first, second, third


def dot(left, right):
    return lax.dot_general(left, right, (((1,), (0,)), ((), ())), preferred_element_type=F32)


def dot_t(left, right):
    return lax.dot_general(left, right, (((1,), (1,)), ((), ())), preferred_element_type=F32)


def exact_dot(left, right):
    return lax.dot_general(
        left, right, (((1,), (0,)), ((), ())), precision=EXACT, preferred_element_type=F32
    )


def exact_dot_t(left, right):
    return lax.dot_general(
        left, right, (((1,), (1,)), ((), ())), precision=EXACT, preferred_element_type=F32
    )


def one_hot(ids, count):
    return jnp.where(iota((count, ids.shape[1]), 0) == ids, 1.0, 0.0).astype(BF16)


def flat(value):
    return jnp.concatenate([value[row : row + 1] for row in range(value.shape[0])], axis=1)


def unflat(value, rows):
    slots = value.shape[1] // rows
    return [value[:, row * slots : (row + 1) * slots] for row in range(rows)]


def cal_pick(table, ids):
    parts = jnp.concatenate(split3(table.T), axis=0)
    high = ids // LANES
    low = ids % LANES
    found = dot(parts, one_hot(high, HIGH))
    found = found[:LANES] + found[LANES : 2 * LANES] + found[2 * LANES :]
    return jnp.sum(jnp.where(iota(found.shape, 0) == low, found, 0.0), axis=0, keepdims=True)


def cal_sums(values, ids):
    high = one_hot(ids // LANES, HIGH)
    low = iota((LANES, ids.shape[1]), 0) == ids % LANES
    total = None
    for part in split3(values):
        spread = jnp.where(low, part.astype(F32), 0.0).astype(BF16)
        added = dot_t(high, spread)
        total = added if total is None else total + added
    return total


def design_of(base, basis, partials):
    slots = base.shape[1]
    knot = iota((WIDTH, slots), 0) // 4
    step = knot - base
    spread = jnp.zeros((WIDTH, slots), F32)
    for index in range(4):
        spread = jnp.where(step == index, basis[index], spread)
    return spread * jnp.concatenate([partials] * (WIDTH // 8), axis=0)


def band_shift(tile, knot):
    return ((tile % 8) * 16 - (8 * tile + 4 * knot - 12)) % WIDTH


def pack_band(normal):
    place = iota((8, WIDTH), 1) // 16
    upper = iota((8, WIDTH), 0) < 4
    groups = []
    for group in range(2):
        packed = jnp.zeros((8, WIDTH), F32)
        for tile in range(8 * group, 8 * group + 8):
            rows = normal[8 * tile : 8 * tile + 8]
            rolled = jnp.where(
                upper,
                pltpu.roll(rows, band_shift(tile, 0), 1),
                pltpu.roll(rows, band_shift(tile, 1), 1),
            )
            packed = jnp.where(place == tile % 8, rolled, packed)
        groups.append(packed)
    return jnp.concatenate(groups, axis=0)


def unpack_band(packed):
    place = iota((8, WIDTH), 1) // 16
    upper = iota((8, WIDTH), 0) < 4
    tiles = []
    for tile in range(16):
        group = tile // 8
        rows = jnp.where(place == tile % 8, packed[8 * group : 8 * group + 8], 0.0)
        tiles.append(
            jnp.where(
                upper,
                pltpu.roll(rows, (-band_shift(tile, 0)) % WIDTH, 1),
                pltpu.roll(rows, (-band_shift(tile, 1)) % WIDTH, 1),
            )
        )
    full = jnp.concatenate(tiles, axis=0)
    return jnp.where(iota(full.shape, 0) >= iota(full.shape, 1), full, 0.0)


ORDER = (
    (0, 8, 17, 31), (1, 9, 18, 30), (2, 10, 19, 29), (3, 11, 20, 28), (4, 12, 21, 27), (13, 22, 26),
    (5, 23), (6, 24), (7, 25), (14,), (15,), (16,),
)


def plan_of(order):
    near = {
        knot: {other for other in range(KNOTS_DEV) if 0 < abs(other - knot) <= 3}
        for knot in range(KNOTS_DEV)
    }
    plan = []
    for step in order:
        plan.append([(knot, sorted({other // 2 for other in near[knot]})) for knot in step])
        for knot in step:
            assert not near[knot] & set(step)
            for other in near[knot]:
                near[other] = (near[other] | near[knot]) - {other, knot}
    return plan


PLAN = plan_of(ORDER)


def block_rows(entry, lines):
    scale = 1.0 / (entry[0, 0] * entry[1, 1] - entry[0, 1] * entry[0, 1])
    low, mid, high = entry[0, 0] * scale, entry[0, 1] * scale, entry[1, 1] * scale
    turned = {}
    for column in (2, 3):
        turned[0, column] = high * entry[0, column] - mid * entry[1, column]
        turned[1, column] = low * entry[1, column] - mid * entry[0, column]
    rest = {}
    for row, column in ((2, 2), (2, 3), (3, 3)):
        taken = entry[0, row] * turned[0, column] + entry[1, row] * turned[1, column]
        rest[row, column] = entry[row, column] - taken
    upper = [high * lines[0] - mid * lines[1], low * lines[1] - mid * lines[0]]
    lower = [
        lines[row] - (entry[0, row] * upper[0] + entry[1, row] * upper[1]) for row in (2, 3)
    ]
    scale = 1.0 / (rest[2, 2] * rest[3, 3] - rest[2, 3] * rest[2, 3])
    third = (rest[3, 3] * scale) * lower[0] - (rest[2, 3] * scale) * lower[1]
    fourth = (rest[2, 2] * scale) * lower[1] - (rest[2, 3] * scale) * lower[0]
    return [
        upper[0] - (turned[0, 2] * third + turned[0, 3] * fourth),
        upper[1] - (turned[1, 2] * third + turned[1, 3] * fourth),
        third,
        fourth,
    ]


def eliminate(matrix, right, lines_out):
    shape = (8, WIDTH)
    tiles = [matrix[8 * tile : 8 * tile + 8] for tile in range(WIDTH // 8)]
    lane = iota(shape, 1)
    for step in PLAN:
        held = list(tiles)
        border = right
        for knot, reach in step:
            at, sub, first = knot // 2, 4 * (knot % 2), 4 * knot
            inside = lane // 4 == knot
            columns = {
                tile: [
                    jnp.broadcast_to(held[tile][:, first + index : first + index + 1], shape)
                    for index in range(4)
                ]
                for tile in sorted({at, *reach})
            }
            entry = {
                (one, two): jnp.broadcast_to(columns[at][two][sub + one : sub + one + 1], shape)
                for one in range(4)
                for two in range(one, 4)
            }
            lines = [
                jnp.where(
                    inside,
                    jnp.where(lane == first + index, -1.0, 0.0),
                    jnp.broadcast_to(held[at][sub + index : sub + index + 1], shape),
                )
                for index in range(4)
            ]
            lines = block_rows(entry, lines)
            for index in range(4):
                lines_out[first + index : first + index + 1] = lines[index][0:1]
            for tile in reach:
                factors = columns[tile]
                taken = factors[0] * lines[0] + factors[1] * lines[1]
                taken = taken + (factors[2] * lines[2] + factors[3] * lines[3])
                tiles[tile] = jnp.where(inside, 0.0, tiles[tile]) - taken
            right = swept(right, border, knot, [line[0:1] for line in lines])
        yield
    return right


def swept(right, border, knot, lines):
    first = 4 * knot
    right = jnp.where(iota(right.shape, 1) // 4 == knot, 0.0, right)
    factors = [border[:, first + index : first + index + 1] for index in range(4)]
    taken = factors[0] * lines[0] + factors[1] * lines[1]
    return right - (taken + (factors[2] * lines[2] + factors[3] * lines[3]))


def substitute(right, lines):
    for step in PLAN:
        border = right
        for knot, unused in step:
            kept = [lines[4 * knot + index : 4 * knot + index + 1] for index in range(4)]
            right = swept(right, border, knot, kept)
        yield
    return right


def small_factor(sums):
    factor = {}
    for member in range(5):
        for column in range(member + 1):
            running = sums[8 * member + column : 8 * member + column + 1]
            if member == column:
                running = running + 1.0
            for offset in range(column):
                running = running - factor[member, offset] * factor[column, offset]
            if member == column:
                factor[member, member] = jnp.sqrt(running)
            else:
                factor[member, column] = running * inverse_of[column]
        inverse_of = {} if member == 0 else inverse_of
        inverse_of[member] = 1.0 / factor[member, member]
    inverse = {}
    for column in range(5):
        inverse[column, column] = inverse_of[column]
        for member in range(column + 1, 5):
            running = factor[member, column] * inverse[column, column]
            for offset in range(column + 1, member):
                running = running + factor[member, offset] * inverse[offset, column]
            inverse[member, column] = -running * inverse_of[member]
    return inverse


PLACES = [(row_id, col_id) for row_id in range(5) for col_id in range(row_id + 1)]


def small_apply(inverse, sides):
    forward = []
    for member in range(5):
        running = inverse[member, 0] * sides[0]
        for column in range(1, member + 1):
            running = running + inverse[member, column] * sides[column]
        forward.append(running)
    result = []
    for column in range(5):
        running = inverse[column, column] * forward[column]
        for member in range(column + 1, 5):
            running = running + inverse[member, column] * forward[member]
        result.append(running)
    return result


PAIRS = [(row_id, col_id) for row_id in range(5) for col_id in range(row_id + 1)]


def spline_terms(phase, attitude_partials):
    other = 1.0 - phase
    square = phase * phase
    cube = square * phase
    basis = [
        other * other * other / 6.0,
        (3.0 * cube - 6.0 * square + 4.0) / 6.0,
        (-3.0 * cube + 3.0 * square + 3.0 * phase + 1.0) / 6.0,
        cube / 6.0,
    ]
    return jnp.stack(
        [
            basis[knot_step] * attitude_partials[channel]
            for knot_step in range(4)
            for channel in range(4)
        ]
    )


def attitude_model(local, terms, knot_base):
    coefficients = lax.all_gather(local, "tm", axis=0, tiled=True)
    blocks, slots = knot_base.shape
    table = coefficients.reshape(blocks, -1, 4)
    knots_count = table.shape[1]
    grid = lax.broadcasted_iota(jnp.int32, (1, knots_count, 1), 1)
    running = jnp.zeros(knot_base.shape, jnp.float32)
    for knot_step in range(4):
        hit = (grid == (knot_base + knot_step)[:, None, :]).astype(jnp.float32)
        picked = jnp.einsum(
            "bkc,bks->bcs",
            table,
            hit,
            precision=lax.Precision.HIGHEST,
            preferred_element_type=jnp.float32,
        )
        for channel in range(4):
            running = running + terms[4 * knot_step + channel] * picked[:, channel, :]
    return running


def small_solve(matrix, right_side):
    extent = len(right_side)
    factor = {}
    for member in range(extent):
        for column in range(member + 1):
            running = matrix[member][column]
            for offset in range(column):
                running = running - factor[member, offset] * factor[column, offset]
            if member == column:
                factor[member, member] = jnp.sqrt(running)
            else:
                factor[member, column] = running / factor[column, column]
    forward = []
    for member in range(extent):
        running = right_side[member]
        for offset in range(member):
            running = running - factor[member, offset] * forward[offset]
        forward.append(running / factor[member, member])
    result = [None] * extent
    for member in reversed(range(extent)):
        running = forward[member]
        for offset in range(member + 1, extent):
            running = running - factor[offset, member] * result[offset]
        result[member] = running / factor[member, member]
    return jnp.stack(result)


def source_solve(ids, count, weighted, source_partials, target):
    products = [
        weighted * source_partials[row_id] * source_partials[col_id] for row_id, col_id in PAIRS
    ]
    products = products + [weighted * source_partials[row_id] * target for row_id in range(5)]
    stacked = jnp.moveaxis(jnp.stack(products), 1, 0)
    owners = lax.broadcasted_iota(jnp.int32, (count, 1), 0)

    def accumulate(total, item):
        values, block_ids = item
        hit = (block_ids[None, :] == owners).astype(jnp.float32)
        added = lax.dot_general(
            values,
            hit,
            (((1,), (1,)), ((), ())),
            precision=lax.Precision.HIGHEST,
            preferred_element_type=jnp.float32,
        )
        return (total + added, None)

    sums, unused = lax.scan(
        accumulate, jnp.zeros((len(products), count), jnp.float32), (stacked, ids)
    )
    entries = {}
    for position, pair in enumerate(PAIRS):
        entry_value = sums[position] + (1.0 if pair[0] == pair[1] else 0.0)
        entries[pair[0], pair[1]] = entry_value
        entries[pair[1], pair[0]] = entry_value
    matrix = [[entries[row_id, col_id] for col_id in range(5)] for row_id in range(5)]
    return small_solve(matrix, [sums[15 + row_id] for row_id in range(5)])


def pick_params(params, ids):
    count = params.shape[1]
    owners = lax.broadcasted_iota(jnp.int32, (count, 1), 0)

    def pick_single(carry, block_ids):
        hit = (block_ids[None, :] == owners).astype(jnp.float32)
        return (
            carry,
            jnp.dot(
                params, hit, precision=lax.Precision.HIGHEST, preferred_element_type=jnp.float32
            ),
        )

    unused, picked = lax.scan(pick_single, 0, ids)
    return jnp.moveaxis(picked, 1, 0)


def spd_solve(matrix, right_side):
    eye = jnp.eye(matrix.shape[-1], dtype=jnp.float32)
    lower = jnp.linalg.cholesky(matrix + eye)
    middle = lax.linalg.triangular_solve(lower, right_side[..., None], left_side=True, lower=True)
    result = lax.linalg.triangular_solve(
        lower, middle, left_side=True, lower=True, transpose_a=True
    )
    return result[..., 0]


def block_normals(terms, knot_base, weighted, resid):
    blocks, slots = knot_base.shape
    spread = jnp.moveaxis(terms.reshape(4, 4, blocks, slots), 2, 0)

    def block_single(item):
        part, base, weights, values = item
        grid = lax.broadcasted_iota(jnp.int32, (KNOTS_DEV, slots), 0)
        design = jnp.zeros((KNOTS_DEV, 4, slots), jnp.float32)
        for knot_step in range(4):
            hit = (grid == base[None, :] + knot_step).astype(jnp.float32)
            design = design + hit[:, None, :] * part[knot_step][None, :, :]
        design = design.reshape(KNOTS_DEV * 4, slots)
        normal = lax.dot_general(
            design * weights[None, :],
            design,
            (((1,), (1,)), ((), ())),
            precision=lax.Precision.HIGHEST,
            preferred_element_type=jnp.float32,
        )
        right = jnp.dot(
            design,
            weights * values,
            precision=lax.Precision.HIGHEST,
            preferred_element_type=jnp.float32,
        )
        return (normal, right)

    return lax.map(block_single, (spread, knot_base, weighted, resid))


def plain_body(
    observed,
    weight_obs,
    present,
    source_partials,
    attitude_partials,
    phase,
    knot_base,
    source_id,
    cal_id,
    attitude,
    calibration,
):
    weighted = present.astype(jnp.float32) * weight_obs
    terms = spline_terms(phase, attitude_partials)
    flat_cal = cal_id.reshape(-1)
    local = attitude
    cal_now = calibration
    params = jnp.zeros((5, SRC_DEV), jnp.float32)
    for sweep in range(2):
        target = observed - attitude_model(local, terms, knot_base) - cal_now[cal_id]
        params = source_solve(source_id, SRC_DEV, weighted, source_partials, target)
        resid = target - jnp.sum(source_partials * pick_params(params, source_id), axis=0)
        normals, rights = block_normals(terms, knot_base, weighted, resid)
        normal, right = (
            lax.psum_scatter(normals, "tm", scatter_dimension=0, tiled=True),
            lax.psum_scatter(rights, "tm", scatter_dimension=0, tiled=True),
        )
        normal, right = lax.psum((normal[0], right[0]), "src")
        local = local + spd_solve(normal, right)
        numer = jax.ops.segment_sum((weighted * resid).reshape(-1), flat_cal, num_segments=CAL)
        denom = jax.ops.segment_sum(weighted.reshape(-1), flat_cal, num_segments=CAL)
        numer, denom = lax.psum((numer, denom), ("src", "tm"))
        cal_now = cal_now + numer / (denom + 1.0)
    final = observed - attitude_model(local, terms, knot_base) - cal_now[cal_id]
    final = final - jnp.sum(source_partials * pick_params(params, source_id), axis=0)
    return (params, local, cal_now, final)


BAND = 16
PIECE = 2


def begin(pairs, sems):
    copies = [
        pltpu.make_async_copy(origin, held, sems.at[place])
        for place, (origin, held) in enumerate(pairs)
    ]
    for copy in copies:
        copy.start()
    return copies


def finish(copies):
    for copy in copies:
        copy.wait()


def tile_of(value):
    return jnp.concatenate(
        [value[:, at : at + LANES] for at in range(0, value.shape[1], LANES)], axis=0
    )


def pick_from(table_t, ids, units, rows):
    found = dot(jnp.concatenate(split3(table_t)[:2], axis=0), units)
    found = found[:LANES] + found[LANES:]
    hit = iota(found.shape, 0) == ids % LANES
    return unflat(jnp.sum(jnp.where(hit, found, 0.0), axis=0, keepdims=True), rows)


def two_parts(line):
    first = line.astype(BF16).astype(F32)
    return first, (line - first).astype(BF16).astype(F32)


def model_of(line, parts):
    first, second = two_parts(line)
    left = jnp.concatenate([first, first], axis=1)
    right = jnp.concatenate([second, jnp.zeros_like(second)], axis=1)
    row = iota((SUB, 2 * WIDTH), 0)
    both = jnp.where(row == 0, left, jnp.where(row == 1, right, 0.0)).astype(BF16)
    return jnp.sum(dot(both, parts), axis=0, keepdims=True)


def side_of(values, parts):
    first, second = two_parts(values)
    row = iota((SUB, values.shape[1]), 0)
    both = jnp.where(row == 0, first, jnp.where(row == 1, second, 0.0)).astype(BF16)
    found = dot_t(both, parts)
    return found[0:1, :WIDTH] + found[1:2, :WIDTH] + found[0:1, WIDTH:]


def normals_kernel(
    weight_in, present_in, attitude_in, phase_in, knot_in, cal_in, start_in,
    send_out, design_out, weighted_out, cal_id,
    weight_obs, present, attitude_partials, phase, knot_base, start, stacked, sems,
):
    copies = begin(
        [
            (weight_in, weight_obs), (present_in, present), (cal_in, cal_id), (start_in, start),
            (phase_in, phase), (knot_in, knot_base), (attitude_in, attitude_partials),
        ],
        sems,
    )
    finish(copies[:4])
    rows = weight_obs.shape[0]
    weighted = present[...].astype(F32) * weight_obs[...]
    weighted_out[...] = weighted
    first, second = tile_of(cal_id[...].astype(F32)), tile_of(weighted)
    devices = send_out.shape[0]
    for device in range(devices):
        core = core_of(device, rows)
        for index in range(rows):
            at = rows * core + index
            send_out[device, PIECE + index] = first[at : at + 1]
            send_out[device, PIECE + rows + index] = second[at : at + 1]
        send_out[device, PIECE + 2 * rows] = start[...]
    finish(copies[4:])
    u = phase[...]
    other = 1.0 - u
    square = u * u
    cube = square * u
    basis = [
        other * other * other / 6.0,
        (3.0 * cube - 6.0 * square + 4.0) / 6.0,
        (-3.0 * cube + 3.0 * square + 3.0 * u + 1.0) / 6.0,
        cube / 6.0,
    ]
    for row in range(rows):
        at = slice(row, row + 1)
        for channel in range(4):
            lines = attitude_partials[channel, at]
            stacked[row, channel : channel + 1] = lines
            stacked[row, channel + 4 : channel + 5] = lines
        design = design_of(knot_base[at], [part[at] for part in basis], stacked[row])
        design_out[row] = design
        band = pack_band(exact_dot_t(design * weighted[at], design))
        half, place = divmod(row, rows // PIECE)
        for index in range(BAND):
            send_out[place * BAND + index, half] = band[index : index + 1]


def sources_kernel(
    cal_id, weighted, design, observed_in, source_in, id_in, calibration_in,
    partials_out, factor_out, target_out, table_out, hits_out, units_out, parts_out, observed,
    source_partials, source_id, table, sems,
):
    copies = begin(
        [
            (observed_in, observed), (source_in, source_partials), (id_in, source_id),
            (calibration_in, table),
        ],
        sems,
    )
    finish(copies)
    rows, slots = observed.shape
    matrix = jnp.zeros((40, SRC_DEV), F32)
    for row in range(rows):
        at = slice(row, row + 1)
        for index in range(5):
            partials_out[row, index : index + 1] = source_partials[index, at]
        partials_out[row, 5:] = jnp.zeros((SUB - 5, slots), F32)
        partials = partials_out[row]
        products = jnp.concatenate(
            [partials * (weighted[at] * partials[index : index + 1]) for index in range(5)], axis=0
        )
        hits_out[row] = one_hot(source_id[at], SRC_DEV)
        found = dot_t(jnp.concatenate(split3(products), axis=0), hits_out[row])
        matrix = matrix + found[:40] + found[40:80] + found[80:]
        first, second, unused = split3(design[row])
        parts_out[row, :WIDTH] = first
        parts_out[row, WIDTH:] = second
    ids = flat(cal_id[...])
    units_out[...] = one_hot(ids // LANES, HIGH)
    inverse = small_factor(matrix)
    for place, pair in enumerate(PLACES):
        factor_out[place : place + 1] = inverse[pair]
    factor_out[15:16] = jnp.zeros((1, SRC_DEV), F32)
    table_t = table[...].T
    table_out[...] = table_t
    for row, picked in enumerate(pick_from(table_t, ids, units_out[...], rows)):
        target_out[row : row + 1] = observed[row : row + 1] - picked


def core_of(device, line):
    return device // line % 2


def residual_step(targets, parts, partials, factor, weighted, hits, send_out):
    rows = len(targets)
    inverse = {pair: factor[place : place + 1] for place, pair in enumerate(PLACES)}
    sides = jnp.zeros((SUB, SRC_DEV), F32)
    for row in range(rows):
        products = partials[row] * (weighted[row : row + 1] * targets[row])
        found = dot_t(jnp.concatenate(split3(products), axis=0), hits[row])
        sides = sides + found[:SUB] + found[SUB : 2 * SUB] + found[2 * SUB :]
    params = small_apply(inverse, [sides[index : index + 1] for index in range(5)])
    table = jnp.concatenate(params + [jnp.zeros((3, SRC_DEV), F32)], axis=0)
    split = jnp.concatenate(split3(table), axis=0)
    explained, scaled, rights = [], [], []
    for row in range(rows):
        found = dot(split, hits[row])
        found = found[:SUB] + found[SUB : 2 * SUB] + found[2 * SUB :]
        explained.append(jnp.sum(found * partials[row], axis=0, keepdims=True))
    for row in range(rows):
        scaled.append(weighted[row : row + 1] * (targets[row] - explained[row]))
        rights.append(side_of(scaled[row], parts[row]))
    half = rows // PIECE
    for device in range(send_out.shape[0]):
        core = core_of(device, rows)
        lines = [line[:, core * LANES : (core + 1) * LANES] for line in scaled]
        for index, line in enumerate(lines + rights[half * core : half * core + half]):
            send_out[device, index] = line
    return params, explained


def first_kernel(received, target, parts, partials, factor, weighted, hits, send_out):
    rows = parts.shape[0]
    last = received.shape[1] - 1
    targets = [
        target[row : row + 1] - model_of(received[row, last], parts[row]) for row in range(rows)
    ]
    residual_step(targets, parts, partials, factor, weighted, hits, send_out)
    totals = [right_side(received, place) for place in range(PIECE)]
    for device in range(send_out.shape[0]):
        send_out[device, send_out.shape[1] - 1] = totals[core_of(device, rows)]


def wide(row, count):
    tile = jnp.broadcast_to(row, (16, LANES)).astype(BF16)
    return jnp.concatenate([tile] * (count // 16), axis=0)


def unit_sums(received, value_of, total):
    rows = (received.shape[1] - PIECE - 1) // 2
    low_row = iota((LANES, LANES), 0).astype(F32).astype(BF16)
    high_row = iota((HIGH, LANES), 0).astype(F32).astype(BF16)
    one, none = jnp.ones((), BF16), jnp.zeros((), BF16)
    for begin in range(0, received.shape[0], 2):
        lefts, rights = [], []
        for device in (begin, begin + 1):
            for index in range(rows):
                unit = received[device, PIECE + index]
                high = jnp.floor(unit * (1.0 / LANES))
                hit = low_row == wide(unit - LANES * high, LANES)
                value = value_of(device, index)
                first = value.astype(BF16).astype(F32)
                lefts.append(
                    jnp.concatenate(
                        [
                            jnp.where(hit, wide(first, LANES), none),
                            jnp.where(hit, wide(value - first, LANES), none),
                        ],
                        axis=0,
                    )
                )
                rights.append(jnp.where(high_row == wide(high, HIGH), one, none))
        found = dot_t(jnp.concatenate(lefts, axis=1), jnp.concatenate(rights, axis=1))
        if begin == 0:
            total[:LANES] = found[:LANES] + found[LANES:]
        else:
            total[:LANES] += found[:LANES] + found[LANES:]
        yield


def matrix_of(band):
    lower = unpack_band(band)
    diagonal = iota(lower.shape, 0) == iota(lower.shape, 1)
    return lower + jnp.where(diagonal, 1.0, lower.T)


def together(works):
    works = list(works)
    while works:
        for work in list(works):
            if next(work, works) is works:
                works.remove(work)


def weights_kernel(received, sums_out):
    rows = (received.shape[1] - PIECE - 1) // 2
    together(
        [
            unit_sums(
                received, lambda device, index: received[device, PIECE + rows + index], sums_out
            )
        ]
    )


def right_side(values, place):
    total = values[0, place]
    for device in range(1, values.shape[0]):
        total = total + values[device, place]
    return total


def core(axis):
    return lax.rem(lax.axis_index(axis), 2)


def coefficients(bundle, place):
    return bundle[LANES + place : LANES + place + 1, :WIDTH]


def put(bundle, place, line):
    bundle[LANES + place : LANES + place + 1] = jnp.concatenate([line, line], axis=1)


def solve_kernel(axis, values, received, bundle_out, lines_out, bands):
    half = lines_out.shape[0]
    rows = values.shape[1] - half - 1
    for device in range(values.shape[0]):
        bands[device : device + 1] = values[device, rows + half]
    bundle_out[LANES:] = jnp.zeros((SUB, HIGH), F32)

    def attitude(place):
        matrix = matrix_of(bands[BAND * place : BAND * (place + 1)])
        change = yield from eliminate(matrix, right_side(values, rows + place), lines_out.at[place])
        start = received[half * core(axis) + place, received.shape[1] - 1]
        put(bundle_out, place, start + change)
        yield

    together(
        [unit_sums(received, lambda device, index: values[device, index], bundle_out)]
        + [attitude(place) for place in range(half)]
    )


def both_halves(axis, own, other, half):
    first = core(axis) == 0
    pairs = [(coefficients(own, place), coefficients(other, place)) for place in range(half)]
    lines = [jnp.where(first, one, two) for one, two in pairs]
    return lines + [jnp.where(first, two, one) for one, two in pairs]


def second_kernel(
    axis, bundle, other, weights, other_weights, table, ids, units, observed, parts, partials, factor,
    weighted, hits,
    send_out, params_out, explained_out, table_out, scale_out,
):
    rows = parts.shape[0]
    scale = 1.0 / (weights[...] + other_weights[...] + 1.0)
    scale_out[...] = scale
    table_t = table[...] + (bundle[:LANES] + other[:LANES]) * scale
    table_out[...] = table_t
    picked = pick_from(table_t, flat(ids[...]), units[...], rows)
    lines = both_halves(axis, bundle, other, rows // PIECE)
    targets = [
        observed[row : row + 1] - model_of(lines[row], parts[row]) - picked[row]
        for row in range(rows)
    ]
    params, explained = residual_step(targets, parts, partials, factor, weighted, hits, send_out)
    for index in range(5):
        params_out[index : index + 1] = params[index]
    for row in range(rows):
        explained_out[row : row + 1] = explained[row]


def last_kernel(values, received, bundle, lines, bundle_out):
    half = lines.shape[0]
    rows = values.shape[1] - half
    bundle_out[LANES:] = jnp.zeros((SUB, HIGH), F32)

    def solve(place):
        change = yield from substitute(right_side(values, rows + place), lines.at[place])
        put(bundle_out, place, coefficients(bundle, place) + change)
        yield

    together(
        [unit_sums(received, lambda device, index: values[device, index], bundle_out)]
        + [solve(place) for place in range(half)]
    )


def final_kernel(
    axis, line, bundle, other, table, scale, ids, units, observed, parts, explained,
    cal_out, attitude_out, resid_out,
):
    rows = parts.shape[0]
    table_t = table[...] + (bundle[:LANES] + other[:LANES]) * scale[...]
    cal_out[...] = table_t.T
    picked = pick_from(table_t, flat(ids[...]), units[...], rows)
    me = lax.axis_index(line)
    lines = both_halves(axis, bundle, other, rows // PIECE)
    own = lines[0]
    for row in range(rows):
        own = jnp.where(me == row, lines[row], own)
        at = slice(row, row + 1)
        resid_out[at] = observed[at] - model_of(lines[row], parts[row]) - picked[row] - explained[at]
    attitude_out[...] = own


VMEM = pl.BlockSpec(memory_space=pltpu.VMEM)
ANY = pl.BlockSpec(memory_space=pltpu.HBM)


def call(kernel, outs, *args, away=0, scratch=()):
    near = args[: len(args) - away]
    far = [pltpu.with_memory_space_constraint(arg, pltpu.HBM) for arg in args[len(args) - away :]]
    return pl.pallas_call(
        kernel,
        out_shape=outs,
        in_specs=[VMEM] * len(near) + [ANY] * away,
        out_specs=[VMEM] * len(outs),
        scratch_shapes=scratch,
        compiler_params=pltpu.CompilerParams(vmem_limit_bytes=VMEM_BYTES),
    )(*near, *far)


def stay(*shape, dtype=F32):
    return pltpu.VMEM(shape, dtype)


def leave(*shape):
    return jax.ShapeDtypeStruct(shape, F32)


def swap(value):
    return lax.ppermute(value, "src", [(at, at ^ 1) for at in range(lax.axis_size("src"))])


def exchange(value):
    return lax.all_to_all(value, ("src", "tm"), 0, 0, tiled=True)


def body(
    observed, weight_obs, present, source_partials, attitude_partials, phase, knot_base, source_id,
    cal_id, attitude, calibration,
):
    rows, slots = observed.shape
    devices = lax.axis_size("src") * lax.axis_size("tm")
    half = rows // PIECE
    first_q = attitude.reshape(1, WIDTH)
    held = [weight_obs, present, attitude_partials, phase, knot_base, first_q]
    received, design, weighted, units_seen = call(
        normals_kernel,
        [
            leave(devices, PIECE + 2 * rows + 1, 1, LANES), stay(rows, WIDTH, slots),
            stay(rows, slots), stay(rows, slots, dtype=jnp.int32),
        ],
        weight_obs, present, attitude_partials, phase, knot_base, cal_id, first_q,
        away=7,
        scratch=[pltpu.VMEM(each.shape, each.dtype) for each in held]
        + [pltpu.VMEM((rows, SUB, slots), F32), pltpu.SemaphoreType.DMA((7,))],
    )
    received = exchange(received)
    cal_id = units_seen
    partials, factor, target, table, hits, units, parts, seen = call(
        sources_kernel,
        [
            stay(rows, SUB, slots), stay(16, SRC_DEV), stay(rows, slots), stay(LANES, HIGH),
            stay(rows, SRC_DEV, slots, dtype=BF16), stay(HIGH, rows * slots, dtype=BF16),
            stay(rows, 2 * WIDTH, slots, dtype=BF16), stay(rows, slots),
        ],
        cal_id, weighted, design, observed, source_partials, source_id,
        calibration.reshape(HIGH, LANES),
        away=4,
        scratch=[
            pltpu.VMEM(source_partials.shape, F32), pltpu.VMEM((rows, slots), jnp.int32),
            pltpu.VMEM((HIGH, LANES), F32), pltpu.SemaphoreType.DMA((4,)),
        ],
    )
    received, factor = lax.optimization_barrier((received, factor))
    (values,) = call(
        first_kernel, [leave(devices, rows + half + 1, 1, LANES)],
        received, target, parts, partials, factor, weighted, hits,
    )
    values, received = lax.optimization_barrier((values, received))
    values = exchange(values)
    (weights,) = call(weights_kernel, [leave(LANES, HIGH)], received)
    other_weights, received = lax.optimization_barrier((swap(weights), received))
    bundle, lines = call(
        functools.partial(solve_kernel, "src"),
        [leave(LANES + SUB, HIGH), stay(half, WIDTH, WIDTH)],
        values, received,
        scratch=[pltpu.VMEM((half * BAND, WIDTH), F32)],
    )
    values, params, explained, table, scale = call(
        functools.partial(second_kernel, "src"),
        [
            leave(devices, rows + half, 1, LANES), leave(5, SRC_DEV), stay(rows, slots),
            stay(LANES, HIGH), stay(LANES, HIGH),
        ],
        bundle, swap(bundle), weights, other_weights, table, cal_id, units, seen, parts, partials,
        factor, weighted, hits,
    )
    values = exchange(values)
    (bundle,) = call(
        last_kernel, [leave(LANES + SUB, HIGH)], values, received, bundle, lines
    )
    cal, now, final = call(
        functools.partial(final_kernel, "src", "tm"),
        [leave(HIGH, LANES), leave(1, WIDTH), leave(rows, slots)],
        bundle, swap(bundle), table, scale, cal_id, units, seen, parts, explained,
    )
    return (params, now.reshape(WIDTH), cal.reshape(CAL), final)


def solution(mesh):
    many = mesh.shape["src"] * mesh.shape["tm"]
    return jax.shard_map(
        body if many * PIECE == mesh.shape["tm"] * BAND else plain_body,
        mesh=mesh,
        in_specs=(
            P(None, ("src", "tm")),
            P(None, ("src", "tm")),
            P(None, ("src", "tm")),
            P(None, None, ("src", "tm")),
            P(None, None, ("src", "tm")),
            P(None, ("src", "tm")),
            P(None, ("src", "tm")),
            P(None, ("src", "tm")),
            P(None, ("src", "tm")),
            P("tm"),
            P(),
        ),
        out_specs=(P(None, ("src", "tm")), P("tm"), P(), P(None, ("src", "tm"))),
        check_vma=False,
    )
```

```python
import functools

import jax
import jax.numpy as jnp
from jax import lax
from jax.experimental import pallas as pl
from jax.experimental.pallas import tpu as pltpu
from jax.sharding import PartitionSpec as P

KNOTS_DEV = 32
WIDTH = 4 * KNOTS_DEV
SRC_DEV = 128
CAL = 32768
LANES = 128
HIGH = CAL // LANES
SUB = 8
VMEM_BYTES = 48 * 1024 * 1024

F32 = jnp.float32
BF16 = jnp.bfloat16
EXACT = lax.Precision.HIGHEST


def iota(shape, dim):
    return lax.broadcasted_iota(jnp.int32, shape, dim)


def split3(value):
    first = value.astype(BF16)
    rest = value - first.astype(F32)
    second = rest.astype(BF16)
    third = (rest - second.astype(F32)).astype(BF16)
    return first, second, third


def dot(left, right):
    return lax.dot_general(left, right, (((1,), (0,)), ((), ())), preferred_element_type=F32)


def dot_t(left, right):
    return lax.dot_general(left, right, (((1,), (1,)), ((), ())), preferred_element_type=F32)


def exact_dot(left, right):
    return lax.dot_general(
        left, right, (((1,), (0,)), ((), ())), precision=EXACT, preferred_element_type=F32
    )


def exact_dot_t(left, right):
    return lax.dot_general(
        left, right, (((1,), (1,)), ((), ())), precision=EXACT, preferred_element_type=F32
    )


def one_hot(ids, count):
    return jnp.where(iota((count, ids.shape[1]), 0) == ids, 1.0, 0.0).astype(BF16)


def flat(value):
    return jnp.concatenate([value[row : row + 1] for row in range(value.shape[0])], axis=1)


def unflat(value, rows):
    slots = value.shape[1] // rows
    return [value[:, row * slots : (row + 1) * slots] for row in range(rows)]


def cal_pick(table, ids):
    parts = jnp.concatenate(split3(table.T), axis=0)
    high = ids // LANES
    low = ids % LANES
    found = dot(parts, one_hot(high, HIGH))
    found = found[:LANES] + found[LANES : 2 * LANES] + found[2 * LANES :]
    return jnp.sum(jnp.where(iota(found.shape, 0) == low, found, 0.0), axis=0, keepdims=True)


def cal_sums(values, ids):
    high = one_hot(ids // LANES, HIGH)
    low = iota((LANES, ids.shape[1]), 0) == ids % LANES
    total = None
    for part in split3(values):
        spread = jnp.where(low, part.astype(F32), 0.0).astype(BF16)
        added = dot_t(high, spread)
        total = added if total is None else total + added
    return total


def design_of(base, basis, partials):
    slots = base.shape[1]
    knot = iota((WIDTH, slots), 0) // 4
    step = knot - base
    spread = jnp.zeros((WIDTH, slots), F32)
    for index in range(4):
        spread = jnp.where(step == index, basis[index], spread)
    return spread * jnp.concatenate([partials] * (WIDTH // 8), axis=0)


def band_shift(tile, knot):
    return ((tile % 8) * 16 - (8 * tile + 4 * knot - 12)) % WIDTH


def pack_band(normal):
    place = iota((8, WIDTH), 1) // 16
    upper = iota((8, WIDTH), 0) < 4
    groups = []
    for group in range(2):
        packed = jnp.zeros((8, WIDTH), F32)
        for tile in range(8 * group, 8 * group + 8):
            rows = normal[8 * tile : 8 * tile + 8]
            rolled = jnp.where(
                upper,
                pltpu.roll(rows, band_shift(tile, 0), 1),
                pltpu.roll(rows, band_shift(tile, 1), 1),
            )
            packed = jnp.where(place == tile % 8, rolled, packed)
        groups.append(packed)
    return jnp.concatenate(groups, axis=0)


def unpack_band(packed):
    place = iota((8, WIDTH), 1) // 16
    upper = iota((8, WIDTH), 0) < 4
    tiles = []
    for tile in range(16):
        group = tile // 8
        rows = jnp.where(place == tile % 8, packed[8 * group : 8 * group + 8], 0.0)
        tiles.append(
            jnp.where(
                upper,
                pltpu.roll(rows, (-band_shift(tile, 0)) % WIDTH, 1),
                pltpu.roll(rows, (-band_shift(tile, 1)) % WIDTH, 1),
            )
        )
    full = jnp.concatenate(tiles, axis=0)
    return jnp.where(iota(full.shape, 0) >= iota(full.shape, 1), full, 0.0)


ORDER = (
    (0, 8, 17, 31), (1, 9, 18, 30), (2, 10, 19, 29), (3, 11, 20, 28), (4, 12, 21, 27), (13, 22, 26),
    (5, 23), (6, 24), (7, 25), (14,), (15,), (16,),
)


def plan_of(order):
    near = {
        knot: {other for other in range(KNOTS_DEV) if 0 < abs(other - knot) <= 3}
        for knot in range(KNOTS_DEV)
    }
    plan = []
    for step in order:
        plan.append([(knot, sorted({other // 2 for other in near[knot]})) for knot in step])
        for knot in step:
            assert not near[knot] & set(step)
            for other in near[knot]:
                near[other] = (near[other] | near[knot]) - {other, knot}
    return plan


PLAN = plan_of(ORDER)


def block_rows(entry, lines):
    scale = 1.0 / (entry[0, 0] * entry[1, 1] - entry[0, 1] * entry[0, 1])
    low, mid, high = entry[0, 0] * scale, entry[0, 1] * scale, entry[1, 1] * scale
    turned = {}
    for column in (2, 3):
        turned[0, column] = high * entry[0, column] - mid * entry[1, column]
        turned[1, column] = low * entry[1, column] - mid * entry[0, column]
    rest = {}
    for row, column in ((2, 2), (2, 3), (3, 3)):
        taken = entry[0, row] * turned[0, column] + entry[1, row] * turned[1, column]
        rest[row, column] = entry[row, column] - taken
    upper = [high * lines[0] - mid * lines[1], low * lines[1] - mid * lines[0]]
    lower = [
        lines[row] - (entry[0, row] * upper[0] + entry[1, row] * upper[1]) for row in (2, 3)
    ]
    scale = 1.0 / (rest[2, 2] * rest[3, 3] - rest[2, 3] * rest[2, 3])
    third = (rest[3, 3] * scale) * lower[0] - (rest[2, 3] * scale) * lower[1]
    fourth = (rest[2, 2] * scale) * lower[1] - (rest[2, 3] * scale) * lower[0]
    return [
        upper[0] - (turned[0, 2] * third + turned[0, 3] * fourth),
        upper[1] - (turned[1, 2] * third + turned[1, 3] * fourth),
        third,
        fourth,
    ]


def eliminate(state, entries, right, lines_out):
    shape = (8, WIDTH)
    lane = iota(shape, 1)
    for step in PLAN:
        works = []
        for slot, (knot, reach) in enumerate(step):
            at, sub, first = knot // 2, 4 * (knot % 2), 4 * knot
            inside = lane // 4 == knot
            columns = {}
            for tile in sorted({at, *reach}):
                held = state[8 * tile : 8 * tile + 8]
                columns[tile] = [
                    jnp.broadcast_to(held[:, first + index : first + index + 1], shape)
                    for index in range(4)
                ]
            for index in range(4):
                entries[slot, index] = columns[at][index]
            entry = {
                (one, two): jnp.broadcast_to(entries[slot, two, sub + one : sub + one + 1], shape)
                for one in range(4)
                for two in range(one, 4)
            }
            lines = [
                jnp.where(
                    inside,
                    jnp.where(lane == first + index, -1.0, 0.0),
                    jnp.broadcast_to(state[first + index : first + index + 1], shape),
                )
                for index in range(4)
            ]
            works.append((knot, reach, inside, columns, block_rows(entry, lines)))
        border = right
        for knot, reach, inside, columns, lines in works:
            for index in range(4):
                lines_out[4 * knot + index : 4 * knot + index + 1] = lines[index][0:1]
            for tile in reach:
                factors = columns[tile]
                taken = factors[0] * lines[0] + factors[1] * lines[1]
                taken = taken + (factors[2] * lines[2] + factors[3] * lines[3])
                rows = slice(8 * tile, 8 * tile + 8)
                state[rows] = jnp.where(inside, 0.0, state[rows]) - taken
            right = swept(right, border, knot, [line[0:1] for line in lines])
        yield
    return right


def swept(right, border, knot, lines):
    first = 4 * knot
    right = jnp.where(iota(right.shape, 1) // 4 == knot, 0.0, right)
    factors = [border[:, first + index : first + index + 1] for index in range(4)]
    taken = factors[0] * lines[0] + factors[1] * lines[1]
    return right - (taken + (factors[2] * lines[2] + factors[3] * lines[3]))


def substitute(right, lines):
    for step in PLAN:
        border = right
        for knot, unused in step:
            kept = [lines[4 * knot + index : 4 * knot + index + 1] for index in range(4)]
            right = swept(right, border, knot, kept)
        yield
    return right


def small_factor(sums):
    factor = {}
    for member in range(5):
        for column in range(member + 1):
            running = sums[8 * member + column : 8 * member + column + 1]
            if member == column:
                running = running + 1.0
            for offset in range(column):
                running = running - factor[member, offset] * factor[column, offset]
            if member == column:
                factor[member, member] = jnp.sqrt(running)
            else:
                factor[member, column] = running * inverse_of[column]
        inverse_of = {} if member == 0 else inverse_of
        inverse_of[member] = 1.0 / factor[member, member]
    inverse = {}
    for column in range(5):
        inverse[column, column] = inverse_of[column]
        for member in range(column + 1, 5):
            running = factor[member, column] * inverse[column, column]
            for offset in range(column + 1, member):
                running = running + factor[member, offset] * inverse[offset, column]
            inverse[member, column] = -running * inverse_of[member]
    return inverse


PLACES = [(row_id, col_id) for row_id in range(5) for col_id in range(row_id + 1)]


def small_apply(inverse, sides):
    forward = []
    for member in range(5):
        running = inverse[member, 0] * sides[0]
        for column in range(1, member + 1):
            running = running + inverse[member, column] * sides[column]
        forward.append(running)
    result = []
    for column in range(5):
        running = inverse[column, column] * forward[column]
        for member in range(column + 1, 5):
            running = running + inverse[member, column] * forward[member]
        result.append(running)
    return result


PAIRS = [(row_id, col_id) for row_id in range(5) for col_id in range(row_id + 1)]


def spline_terms(phase, attitude_partials):
    other = 1.0 - phase
    square = phase * phase
    cube = square * phase
    basis = [
        other * other * other / 6.0,
        (3.0 * cube - 6.0 * square + 4.0) / 6.0,
        (-3.0 * cube + 3.0 * square + 3.0 * phase + 1.0) / 6.0,
        cube / 6.0,
    ]
    return jnp.stack(
        [
            basis[knot_step] * attitude_partials[channel]
            for knot_step in range(4)
            for channel in range(4)
        ]
    )


def attitude_model(local, terms, knot_base):
    coefficients = lax.all_gather(local, "tm", axis=0, tiled=True)
    blocks, slots = knot_base.shape
    table = coefficients.reshape(blocks, -1, 4)
    knots_count = table.shape[1]
    grid = lax.broadcasted_iota(jnp.int32, (1, knots_count, 1), 1)
    running = jnp.zeros(knot_base.shape, jnp.float32)
    for knot_step in range(4):
        hit = (grid == (knot_base + knot_step)[:, None, :]).astype(jnp.float32)
        picked = jnp.einsum(
            "bkc,bks->bcs",
            table,
            hit,
            precision=lax.Precision.HIGHEST,
            preferred_element_type=jnp.float32,
        )
        for channel in range(4):
            running = running + terms[4 * knot_step + channel] * picked[:, channel, :]
    return running


def small_solve(matrix, right_side):
    extent = len(right_side)
    factor = {}
    for member in range(extent):
        for column in range(member + 1):
            running = matrix[member][column]
            for offset in range(column):
                running = running - factor[member, offset] * factor[column, offset]
            if member == column:
                factor[member, member] = jnp.sqrt(running)
            else:
                factor[member, column] = running / factor[column, column]
    forward = []
    for member in range(extent):
        running = right_side[member]
        for offset in range(member):
            running = running - factor[member, offset] * forward[offset]
        forward.append(running / factor[member, member])
    result = [None] * extent
    for member in reversed(range(extent)):
        running = forward[member]
        for offset in range(member + 1, extent):
            running = running - factor[offset, member] * result[offset]
        result[member] = running / factor[member, member]
    return jnp.stack(result)


def source_solve(ids, count, weighted, source_partials, target):
    products = [
        weighted * source_partials[row_id] * source_partials[col_id] for row_id, col_id in PAIRS
    ]
    products = products + [weighted * source_partials[row_id] * target for row_id in range(5)]
    stacked = jnp.moveaxis(jnp.stack(products), 1, 0)
    owners = lax.broadcasted_iota(jnp.int32, (count, 1), 0)

    def accumulate(total, item):
        values, block_ids = item
        hit = (block_ids[None, :] == owners).astype(jnp.float32)
        added = lax.dot_general(
            values,
            hit,
            (((1,), (1,)), ((), ())),
            precision=lax.Precision.HIGHEST,
            preferred_element_type=jnp.float32,
        )
        return (total + added, None)

    sums, unused = lax.scan(
        accumulate, jnp.zeros((len(products), count), jnp.float32), (stacked, ids)
    )
    entries = {}
    for position, pair in enumerate(PAIRS):
        entry_value = sums[position] + (1.0 if pair[0] == pair[1] else 0.0)
        entries[pair[0], pair[1]] = entry_value
        entries[pair[1], pair[0]] = entry_value
    matrix = [[entries[row_id, col_id] for col_id in range(5)] for row_id in range(5)]
    return small_solve(matrix, [sums[15 + row_id] for row_id in range(5)])


def pick_params(params, ids):
    count = params.shape[1]
    owners = lax.broadcasted_iota(jnp.int32, (count, 1), 0)

    def pick_single(carry, block_ids):
        hit = (block_ids[None, :] == owners).astype(jnp.float32)
        return (
            carry,
            jnp.dot(
                params, hit, precision=lax.Precision.HIGHEST, preferred_element_type=jnp.float32
            ),
        )

    unused, picked = lax.scan(pick_single, 0, ids)
    return jnp.moveaxis(picked, 1, 0)


def spd_solve(matrix, right_side):
    eye = jnp.eye(matrix.shape[-1], dtype=jnp.float32)
    lower = jnp.linalg.cholesky(matrix + eye)
    middle = lax.linalg.triangular_solve(lower, right_side[..., None], left_side=True, lower=True)
    result = lax.linalg.triangular_solve(
        lower, middle, left_side=True, lower=True, transpose_a=True
    )
    return result[..., 0]


def block_normals(terms, knot_base, weighted, resid):
    blocks, slots = knot_base.shape
    spread = jnp.moveaxis(terms.reshape(4, 4, blocks, slots), 2, 0)

    def block_single(item):
        part, base, weights, values = item
        grid = lax.broadcasted_iota(jnp.int32, (KNOTS_DEV, slots), 0)
        design = jnp.zeros((KNOTS_DEV, 4, slots), jnp.float32)
        for knot_step in range(4):
            hit = (grid == base[None, :] + knot_step).astype(jnp.float32)
            design = design + hit[:, None, :] * part[knot_step][None, :, :]
        design = design.reshape(KNOTS_DEV * 4, slots)
        normal = lax.dot_general(
            design * weights[None, :],
            design,
            (((1,), (1,)), ((), ())),
            precision=lax.Precision.HIGHEST,
            preferred_element_type=jnp.float32,
        )
        right = jnp.dot(
            design,
            weights * values,
            precision=lax.Precision.HIGHEST,
            preferred_element_type=jnp.float32,
        )
        return (normal, right)

    return lax.map(block_single, (spread, knot_base, weighted, resid))


def plain_body(
    observed,
    weight_obs,
    present,
    source_partials,
    attitude_partials,
    phase,
    knot_base,
    source_id,
    cal_id,
    attitude,
    calibration,
):
    weighted = present.astype(jnp.float32) * weight_obs
    terms = spline_terms(phase, attitude_partials)
    flat_cal = cal_id.reshape(-1)
    local = attitude
    cal_now = calibration
    params = jnp.zeros((5, SRC_DEV), jnp.float32)
    for sweep in range(2):
        target = observed - attitude_model(local, terms, knot_base) - cal_now[cal_id]
        params = source_solve(source_id, SRC_DEV, weighted, source_partials, target)
        resid = target - jnp.sum(source_partials * pick_params(params, source_id), axis=0)
        normals, rights = block_normals(terms, knot_base, weighted, resid)
        normal, right = (
            lax.psum_scatter(normals, "tm", scatter_dimension=0, tiled=True),
            lax.psum_scatter(rights, "tm", scatter_dimension=0, tiled=True),
        )
        normal, right = lax.psum((normal[0], right[0]), "src")
        local = local + spd_solve(normal, right)
        numer = jax.ops.segment_sum((weighted * resid).reshape(-1), flat_cal, num_segments=CAL)
        denom = jax.ops.segment_sum(weighted.reshape(-1), flat_cal, num_segments=CAL)
        numer, denom = lax.psum((numer, denom), ("src", "tm"))
        cal_now = cal_now + numer / (denom + 1.0)
    final = observed - attitude_model(local, terms, knot_base) - cal_now[cal_id]
    final = final - jnp.sum(source_partials * pick_params(params, source_id), axis=0)
    return (params, local, cal_now, final)


BAND = 16
PIECE = 2


def begin(pairs, sems):
    copies = [
        pltpu.make_async_copy(origin, held, sems.at[place])
        for place, (origin, held) in enumerate(pairs)
    ]
    for copy in copies:
        copy.start()
    return copies


def finish(copies):
    for copy in copies:
        copy.wait()


def tile_of(value):
    return jnp.concatenate(
        [value[:, at : at + LANES] for at in range(0, value.shape[1], LANES)], axis=0
    )


def pick_from(table_t, ids, units, rows):
    found = dot(jnp.concatenate(split3(table_t)[:2], axis=0), units)
    found = found[:LANES] + found[LANES:]
    hit = iota(found.shape, 0) == ids % LANES
    return unflat(jnp.sum(jnp.where(hit, found, 0.0), axis=0, keepdims=True), rows)


def two_parts(line):
    first = line.astype(BF16).astype(F32)
    return first, (line - first).astype(BF16).astype(F32)


def model_of(line, parts):
    first, second = two_parts(line)
    left = jnp.concatenate([first, first], axis=1)
    right = jnp.concatenate([second, jnp.zeros_like(second)], axis=1)
    row = iota((SUB, 2 * WIDTH), 0)
    both = jnp.where(row == 0, left, jnp.where(row == 1, right, 0.0)).astype(BF16)
    return jnp.sum(dot(both, parts), axis=0, keepdims=True)


def side_of(values, parts):
    first, second = two_parts(values)
    row = iota((SUB, values.shape[1]), 0)
    both = jnp.where(row == 0, first, jnp.where(row == 1, second, 0.0)).astype(BF16)
    found = dot_t(both, parts)
    return found[0:1, :WIDTH] + found[1:2, :WIDTH] + found[0:1, WIDTH:]


def normals_kernel(
    weight_in, present_in, attitude_in, phase_in, knot_in, cal_in, start_in,
    send_out, design_out, weighted_out, cal_id,
    weight_obs, present, attitude_partials, phase, knot_base, start, stacked, sems,
):
    copies = begin(
        [
            (weight_in, weight_obs), (present_in, present), (cal_in, cal_id), (start_in, start),
            (phase_in, phase), (knot_in, knot_base), (attitude_in, attitude_partials),
        ],
        sems,
    )
    finish(copies[:4])
    rows = weight_obs.shape[0]
    weighted = present[...].astype(F32) * weight_obs[...]
    weighted_out[...] = weighted
    first, second = tile_of(cal_id[...].astype(F32)), tile_of(weighted)
    devices = send_out.shape[0]
    for device in range(devices):
        core = core_of(device, rows)
        for index in range(rows):
            at = rows * core + index
            send_out[device, PIECE + index] = first[at : at + 1]
            send_out[device, PIECE + rows + index] = second[at : at + 1]
        send_out[device, PIECE + 2 * rows] = start[...]
    finish(copies[4:])
    u = phase[...]
    other = 1.0 - u
    square = u * u
    cube = square * u
    basis = [
        other * other * other / 6.0,
        (3.0 * cube - 6.0 * square + 4.0) / 6.0,
        (-3.0 * cube + 3.0 * square + 3.0 * u + 1.0) / 6.0,
        cube / 6.0,
    ]
    for row in range(rows):
        at = slice(row, row + 1)
        for channel in range(4):
            lines = attitude_partials[channel, at]
            stacked[row, channel : channel + 1] = lines
            stacked[row, channel + 4 : channel + 5] = lines
        design = design_of(knot_base[at], [part[at] for part in basis], stacked[row])
        design_out[row] = design
        band = pack_band(exact_dot_t(design * weighted[at], design))
        half, place = divmod(row, rows // PIECE)
        for index in range(BAND):
            send_out[place * BAND + index, half] = band[index : index + 1]


def sources_kernel(
    cal_id, weighted, design, observed_in, source_in, id_in, calibration_in,
    partials_out, factor_out, target_out, table_out, hits_out, units_out, parts_out, observed,
    source_partials, source_id, table, sems,
):
    copies = begin(
        [
            (observed_in, observed), (source_in, source_partials), (id_in, source_id),
            (calibration_in, table),
        ],
        sems,
    )
    finish(copies)
    rows, slots = observed.shape
    matrix = jnp.zeros((40, SRC_DEV), F32)
    for row in range(rows):
        at = slice(row, row + 1)
        for index in range(5):
            partials_out[row, index : index + 1] = source_partials[index, at]
        partials_out[row, 5:] = jnp.zeros((SUB - 5, slots), F32)
        partials = partials_out[row]
        products = jnp.concatenate(
            [partials * (weighted[at] * partials[index : index + 1]) for index in range(5)], axis=0
        )
        hits_out[row] = one_hot(source_id[at], SRC_DEV)
        found = dot_t(jnp.concatenate(split3(products), axis=0), hits_out[row])
        matrix = matrix + found[:40] + found[40:80] + found[80:]
        first, second, unused = split3(design[row])
        parts_out[row, :WIDTH] = first
        parts_out[row, WIDTH:] = second
    ids = flat(cal_id[...])
    units_out[...] = one_hot(ids // LANES, HIGH)
    inverse = small_factor(matrix)
    for place, pair in enumerate(PLACES):
        factor_out[place : place + 1] = inverse[pair]
    factor_out[15:16] = jnp.zeros((1, SRC_DEV), F32)
    table_t = table[...].T
    table_out[...] = table_t
    for row, picked in enumerate(pick_from(table_t, ids, units_out[...], rows)):
        target_out[row : row + 1] = observed[row : row + 1] - picked


def core_of(device, line):
    return device // line % 2


def residual_step(targets, parts, partials, factor, weighted, hits, send_out):
    rows = len(targets)
    inverse = {pair: factor[place : place + 1] for place, pair in enumerate(PLACES)}
    sides = jnp.zeros((SUB, SRC_DEV), F32)
    for row in range(rows):
        products = partials[row] * (weighted[row : row + 1] * targets[row])
        found = dot_t(jnp.concatenate(split3(products), axis=0), hits[row])
        sides = sides + found[:SUB] + found[SUB : 2 * SUB] + found[2 * SUB :]
    params = small_apply(inverse, [sides[index : index + 1] for index in range(5)])
    table = jnp.concatenate(params + [jnp.zeros((3, SRC_DEV), F32)], axis=0)
    split = jnp.concatenate(split3(table), axis=0)
    explained, scaled, rights = [], [], []
    for row in range(rows):
        found = dot(split, hits[row])
        found = found[:SUB] + found[SUB : 2 * SUB] + found[2 * SUB :]
        explained.append(jnp.sum(found * partials[row], axis=0, keepdims=True))
    for row in range(rows):
        scaled.append(weighted[row : row + 1] * (targets[row] - explained[row]))
        rights.append(side_of(scaled[row], parts[row]))
    half = rows // PIECE
    for device in range(send_out.shape[0]):
        core = core_of(device, rows)
        lines = [line[:, core * LANES : (core + 1) * LANES] for line in scaled]
        for index, line in enumerate(lines + rights[half * core : half * core + half]):
            send_out[device, index] = line
    return params, explained


def first_kernel(received, target, parts, partials, factor, weighted, hits, send_out):
    rows = parts.shape[0]
    last = received.shape[1] - 1
    targets = [
        target[row : row + 1] - model_of(received[row, last], parts[row]) for row in range(rows)
    ]
    residual_step(targets, parts, partials, factor, weighted, hits, send_out)
    totals = [right_side(received, place) for place in range(PIECE)]
    for device in range(send_out.shape[0]):
        send_out[device, send_out.shape[1] - 1] = totals[core_of(device, rows)]


def wide(row, count):
    tile = jnp.broadcast_to(row, (16, LANES)).astype(BF16)
    return jnp.concatenate([tile] * (count // 16), axis=0)


def unit_sums(received, value_of, total):
    rows = (received.shape[1] - PIECE - 1) // 2
    low_row = iota((LANES, LANES), 0).astype(F32).astype(BF16)
    high_row = iota((HIGH, LANES), 0).astype(F32).astype(BF16)
    one, none = jnp.ones((), BF16), jnp.zeros((), BF16)
    for begin in range(0, received.shape[0], 2):
        lefts, rights = [], []
        for device in (begin, begin + 1):
            for index in range(rows):
                unit = received[device, PIECE + index]
                high = jnp.floor(unit * (1.0 / LANES))
                hit = low_row == wide(unit - LANES * high, LANES)
                value = value_of(device, index)
                first = value.astype(BF16).astype(F32)
                lefts.append(
                    jnp.concatenate(
                        [
                            jnp.where(hit, wide(first, LANES), none),
                            jnp.where(hit, wide(value - first, LANES), none),
                        ],
                        axis=0,
                    )
                )
                rights.append(jnp.where(high_row == wide(high, HIGH), one, none))
        found = dot_t(jnp.concatenate(lefts, axis=1), jnp.concatenate(rights, axis=1))
        if begin == 0:
            total[:LANES] = found[:LANES] + found[LANES:]
        else:
            total[:LANES] += found[:LANES] + found[LANES:]
        yield


def matrix_of(band):
    lower = unpack_band(band)
    diagonal = iota(lower.shape, 0) == iota(lower.shape, 1)
    return lower + jnp.where(diagonal, 1.0, lower.T)


def together(works):
    works = list(works)
    while works:
        for work in list(works):
            if next(work, works) is works:
                works.remove(work)


def weights_kernel(received, sums_out):
    rows = (received.shape[1] - PIECE - 1) // 2
    together(
        [
            unit_sums(
                received, lambda device, index: received[device, PIECE + rows + index], sums_out
            )
        ]
    )


def right_side(values, place):
    total = values[0, place]
    for device in range(1, values.shape[0]):
        total = total + values[device, place]
    return total


def core(axis):
    return lax.rem(lax.axis_index(axis), 2)


def coefficients(bundle, place):
    return bundle[LANES + place : LANES + place + 1, :WIDTH]


def put(bundle, place, line):
    bundle[LANES + place : LANES + place + 1] = jnp.concatenate([line, line], axis=1)


def solve_kernel(axis, values, received, bundle_out, lines_out, bands, states, entries):
    half = lines_out.shape[0]
    rows = values.shape[1] - half - 1
    for device in range(values.shape[0]):
        bands[device : device + 1] = values[device, rows + half]
    bundle_out[LANES:] = jnp.zeros((SUB, HIGH), F32)

    def attitude(place):
        states[place] = matrix_of(bands[BAND * place : BAND * (place + 1)])
        change = yield from eliminate(
            states.at[place],
            entries.at[place],
            right_side(values, rows + place),
            lines_out.at[place],
        )
        start = received[half * core(axis) + place, received.shape[1] - 1]
        put(bundle_out, place, start + change)
        yield

    together(
        [unit_sums(received, lambda device, index: values[device, index], bundle_out)]
        + [attitude(place) for place in range(half)]
    )


def both_halves(axis, own, other, half):
    first = core(axis) == 0
    pairs = [(coefficients(own, place), coefficients(other, place)) for place in range(half)]
    lines = [jnp.where(first, one, two) for one, two in pairs]
    return lines + [jnp.where(first, two, one) for one, two in pairs]


def second_kernel(
    axis, bundle, other, weights, other_weights, table, ids, units, observed, parts, partials, factor,
    weighted, hits,
    send_out, params_out, explained_out, table_out, scale_out,
):
    rows = parts.shape[0]
    scale = 1.0 / (weights[...] + other_weights[...] + 1.0)
    scale_out[...] = scale
    table_t = table[...] + (bundle[:LANES] + other[:LANES]) * scale
    table_out[...] = table_t
    picked = pick_from(table_t, flat(ids[...]), units[...], rows)
    lines = both_halves(axis, bundle, other, rows // PIECE)
    targets = [
        observed[row : row + 1] - model_of(lines[row], parts[row]) - picked[row]
        for row in range(rows)
    ]
    params, explained = residual_step(targets, parts, partials, factor, weighted, hits, send_out)
    for index in range(5):
        params_out[index : index + 1] = params[index]
    for row in range(rows):
        explained_out[row : row + 1] = explained[row]


def last_kernel(values, received, bundle, lines, bundle_out):
    half = lines.shape[0]
    rows = values.shape[1] - half
    bundle_out[LANES:] = jnp.zeros((SUB, HIGH), F32)

    def solve(place):
        change = yield from substitute(right_side(values, rows + place), lines.at[place])
        put(bundle_out, place, coefficients(bundle, place) + change)
        yield

    together(
        [unit_sums(received, lambda device, index: values[device, index], bundle_out)]
        + [solve(place) for place in range(half)]
    )


def final_kernel(
    axis, line, bundle, other, table, scale, ids, units, observed, parts, explained,
    cal_out, attitude_out, resid_out,
):
    rows = parts.shape[0]
    table_t = table[...] + (bundle[:LANES] + other[:LANES]) * scale[...]
    cal_out[...] = table_t.T
    picked = pick_from(table_t, flat(ids[...]), units[...], rows)
    me = lax.axis_index(line)
    lines = both_halves(axis, bundle, other, rows // PIECE)
    own = lines[0]
    for row in range(rows):
        own = jnp.where(me == row, lines[row], own)
        at = slice(row, row + 1)
        resid_out[at] = observed[at] - model_of(lines[row], parts[row]) - picked[row] - explained[at]
    attitude_out[...] = own


VMEM = pl.BlockSpec(memory_space=pltpu.VMEM)
ANY = pl.BlockSpec(memory_space=pltpu.HBM)


def call(kernel, outs, *args, away=0, scratch=()):
    near = args[: len(args) - away]
    far = [pltpu.with_memory_space_constraint(arg, pltpu.HBM) for arg in args[len(args) - away :]]
    return pl.pallas_call(
        kernel,
        out_shape=outs,
        in_specs=[VMEM] * len(near) + [ANY] * away,
        out_specs=[VMEM] * len(outs),
        scratch_shapes=scratch,
        compiler_params=pltpu.CompilerParams(vmem_limit_bytes=VMEM_BYTES),
    )(*near, *far)


def stay(*shape, dtype=F32):
    return pltpu.VMEM(shape, dtype)


def leave(*shape):
    return jax.ShapeDtypeStruct(shape, F32)


def swap(value):
    return lax.ppermute(value, "src", [(at, at ^ 1) for at in range(lax.axis_size("src"))])


def exchange(value):
    return lax.all_to_all(value, ("src", "tm"), 0, 0, tiled=True)


def body(
    observed, weight_obs, present, source_partials, attitude_partials, phase, knot_base, source_id,
    cal_id, attitude, calibration,
):
    rows, slots = observed.shape
    devices = lax.axis_size("src") * lax.axis_size("tm")
    half = rows // PIECE
    first_q = attitude.reshape(1, WIDTH)
    held = [weight_obs, present, attitude_partials, phase, knot_base, first_q]
    received, design, weighted, units_seen = call(
        normals_kernel,
        [
            leave(devices, PIECE + 2 * rows + 1, 1, LANES), stay(rows, WIDTH, slots),
            stay(rows, slots), stay(rows, slots, dtype=jnp.int32),
        ],
        weight_obs, present, attitude_partials, phase, knot_base, cal_id, first_q,
        away=7,
        scratch=[pltpu.VMEM(each.shape, each.dtype) for each in held]
        + [pltpu.VMEM((rows, SUB, slots), F32), pltpu.SemaphoreType.DMA((7,))],
    )
    received = exchange(received)
    cal_id = units_seen
    partials, factor, target, table, hits, units, parts, seen = call(
        sources_kernel,
        [
            stay(rows, SUB, slots), stay(16, SRC_DEV), stay(rows, slots), stay(LANES, HIGH),
            stay(rows, SRC_DEV, slots, dtype=BF16), stay(HIGH, rows * slots, dtype=BF16),
            stay(rows, 2 * WIDTH, slots, dtype=BF16), stay(rows, slots),
        ],
        cal_id, weighted, design, observed, source_partials, source_id,
        calibration.reshape(HIGH, LANES),
        away=4,
        scratch=[
            pltpu.VMEM(source_partials.shape, F32), pltpu.VMEM((rows, slots), jnp.int32),
            pltpu.VMEM((HIGH, LANES), F32), pltpu.SemaphoreType.DMA((4,)),
        ],
    )
    received, factor = lax.optimization_barrier((received, factor))
    (values,) = call(
        first_kernel, [leave(devices, rows + half + 1, 1, LANES)],
        received, target, parts, partials, factor, weighted, hits,
    )
    values, received = lax.optimization_barrier((values, received))
    values = exchange(values)
    (weights,) = call(weights_kernel, [leave(LANES, HIGH)], received)
    other_weights, received = lax.optimization_barrier((swap(weights), received))
    bundle, lines = call(
        functools.partial(solve_kernel, "src"),
        [leave(LANES + SUB, HIGH), stay(half, WIDTH, WIDTH)],
        values, received,
        scratch=[
            pltpu.VMEM((half * BAND, WIDTH), F32), pltpu.VMEM((half, WIDTH, WIDTH), F32),
            pltpu.VMEM((half, len(PLAN[0]), 4, 8, WIDTH), F32),
        ],
    )
    values, params, explained, table, scale = call(
        functools.partial(second_kernel, "src"),
        [
            leave(devices, rows + half, 1, LANES), leave(5, SRC_DEV), stay(rows, slots),
            stay(LANES, HIGH), stay(LANES, HIGH),
        ],
        bundle, swap(bundle), weights, other_weights, table, cal_id, units, seen, parts, partials,
        factor, weighted, hits,
    )
    values = exchange(values)
    (bundle,) = call(
        last_kernel, [leave(LANES + SUB, HIGH)], values, received, bundle, lines
    )
    cal, now, final = call(
        functools.partial(final_kernel, "src", "tm"),
        [leave(HIGH, LANES), leave(1, WIDTH), leave(rows, slots)],
        bundle, swap(bundle), table, scale, cal_id, units, seen, parts, explained,
    )
    return (params, now.reshape(WIDTH), cal.reshape(CAL), final)


def solution(mesh):
    many = mesh.shape["src"] * mesh.shape["tm"]
    return jax.shard_map(
        body if many * PIECE == mesh.shape["tm"] * BAND else plain_body,
        mesh=mesh,
        in_specs=(
            P(None, ("src", "tm")),
            P(None, ("src", "tm")),
            P(None, ("src", "tm")),
            P(None, None, ("src", "tm")),
            P(None, None, ("src", "tm")),
            P(None, ("src", "tm")),
            P(None, ("src", "tm")),
            P(None, ("src", "tm")),
            P(None, ("src", "tm")),
            P("tm"),
            P(),
        ),
        out_specs=(P(None, ("src", "tm")), P("tm"), P(), P(None, ("src", "tm"))),
        check_vma=False,
    )
```

```python
import functools

import jax
import jax.numpy as jnp
from jax import lax
from jax.experimental import pallas as pl
from jax.experimental.pallas import tpu as pltpu
from jax.sharding import PartitionSpec as P

KNOTS_DEV = 32
WIDTH = 4 * KNOTS_DEV
SRC_DEV = 128
CAL = 32768
LANES = 128
HIGH = CAL // LANES
SUB = 8
VMEM_BYTES = 48 * 1024 * 1024

F32 = jnp.float32
BF16 = jnp.bfloat16
EXACT = lax.Precision.HIGHEST


def iota(shape, dim):
    return lax.broadcasted_iota(jnp.int32, shape, dim)


def split3(value):
    first = value.astype(BF16)
    rest = value - first.astype(F32)
    second = rest.astype(BF16)
    third = (rest - second.astype(F32)).astype(BF16)
    return first, second, third


def dot(left, right):
    return lax.dot_general(left, right, (((1,), (0,)), ((), ())), preferred_element_type=F32)


def dot_t(left, right):
    return lax.dot_general(left, right, (((1,), (1,)), ((), ())), preferred_element_type=F32)


def exact_dot(left, right):
    return lax.dot_general(
        left, right, (((1,), (0,)), ((), ())), precision=EXACT, preferred_element_type=F32
    )


def exact_dot_t(left, right):
    return lax.dot_general(
        left, right, (((1,), (1,)), ((), ())), precision=EXACT, preferred_element_type=F32
    )


def one_hot(ids, count):
    return jnp.where(iota((count, ids.shape[1]), 0) == ids, 1.0, 0.0).astype(BF16)


def flat(value):
    return jnp.concatenate([value[row : row + 1] for row in range(value.shape[0])], axis=1)


def unflat(value, rows):
    slots = value.shape[1] // rows
    return [value[:, row * slots : (row + 1) * slots] for row in range(rows)]


def cal_pick(table, ids):
    parts = jnp.concatenate(split3(table.T), axis=0)
    high = ids // LANES
    low = ids % LANES
    found = dot(parts, one_hot(high, HIGH))
    found = found[:LANES] + found[LANES : 2 * LANES] + found[2 * LANES :]
    return jnp.sum(jnp.where(iota(found.shape, 0) == low, found, 0.0), axis=0, keepdims=True)


def cal_sums(values, ids):
    high = one_hot(ids // LANES, HIGH)
    low = iota((LANES, ids.shape[1]), 0) == ids % LANES
    total = None
    for part in split3(values):
        spread = jnp.where(low, part.astype(F32), 0.0).astype(BF16)
        added = dot_t(high, spread)
        total = added if total is None else total + added
    return total


def design_of(base, basis, partials):
    slots = base.shape[1]
    knot = iota((WIDTH, slots), 0) // 4
    step = knot - base
    spread = jnp.zeros((WIDTH, slots), F32)
    for index in range(4):
        spread = jnp.where(step == index, basis[index], spread)
    return spread * jnp.concatenate([partials] * (WIDTH // 8), axis=0)


def band_shift(tile, knot):
    return ((tile % 8) * 16 - (8 * tile + 4 * knot - 12)) % WIDTH


def pack_band(normal):
    place = iota((8, WIDTH), 1) // 16
    upper = iota((8, WIDTH), 0) < 4
    groups = []
    for group in range(2):
        packed = jnp.zeros((8, WIDTH), F32)
        for tile in range(8 * group, 8 * group + 8):
            rows = normal[8 * tile : 8 * tile + 8]
            rolled = jnp.where(
                upper,
                pltpu.roll(rows, band_shift(tile, 0), 1),
                pltpu.roll(rows, band_shift(tile, 1), 1),
            )
            packed = jnp.where(place == tile % 8, rolled, packed)
        groups.append(packed)
    return jnp.concatenate(groups, axis=0)


def unpack_band(packed):
    place = iota((8, WIDTH), 1) // 16
    upper = iota((8, WIDTH), 0) < 4
    tiles = []
    for tile in range(16):
        group = tile // 8
        rows = jnp.where(place == tile % 8, packed[8 * group : 8 * group + 8], 0.0)
        tiles.append(
            jnp.where(
                upper,
                pltpu.roll(rows, (-band_shift(tile, 0)) % WIDTH, 1),
                pltpu.roll(rows, (-band_shift(tile, 1)) % WIDTH, 1),
            )
        )
    full = jnp.concatenate(tiles, axis=0)
    return jnp.where(iota(full.shape, 0) >= iota(full.shape, 1), full, 0.0)


ORDER = (
    (0, 8, 17, 31), (1, 9, 18, 30), (2, 10, 19, 29), (3, 11, 20, 28), (4, 12, 21, 27), (13, 22, 26),
    (5, 23), (6, 24), (7, 25), (14,), (15,), (16,),
)


def plan_of(order):
    near = {
        knot: {other for other in range(KNOTS_DEV) if 0 < abs(other - knot) <= 3}
        for knot in range(KNOTS_DEV)
    }
    plan = []
    for step in order:
        plan.append([(knot, sorted({other // 2 for other in near[knot]})) for knot in step])
        for knot in step:
            assert not near[knot] & set(step)
            for other in near[knot]:
                near[other] = (near[other] | near[knot]) - {other, knot}
    return plan


PLAN = plan_of(ORDER)


def block_rows(entry, lines):
    scale = 1.0 / (entry[0, 0] * entry[1, 1] - entry[0, 1] * entry[0, 1])
    low, mid, high = entry[0, 0] * scale, entry[0, 1] * scale, entry[1, 1] * scale
    turned = {}
    for column in (2, 3):
        turned[0, column] = high * entry[0, column] - mid * entry[1, column]
        turned[1, column] = low * entry[1, column] - mid * entry[0, column]
    rest = {}
    for row, column in ((2, 2), (2, 3), (3, 3)):
        taken = entry[0, row] * turned[0, column] + entry[1, row] * turned[1, column]
        rest[row, column] = entry[row, column] - taken
    upper = [high * lines[0] - mid * lines[1], low * lines[1] - mid * lines[0]]
    lower = [
        lines[row] - (entry[0, row] * upper[0] + entry[1, row] * upper[1]) for row in (2, 3)
    ]
    scale = 1.0 / (rest[2, 2] * rest[3, 3] - rest[2, 3] * rest[2, 3])
    third = (rest[3, 3] * scale) * lower[0] - (rest[2, 3] * scale) * lower[1]
    fourth = (rest[2, 2] * scale) * lower[1] - (rest[2, 3] * scale) * lower[0]
    return [
        upper[0] - (turned[0, 2] * third + turned[0, 3] * fourth),
        upper[1] - (turned[1, 2] * third + turned[1, 3] * fourth),
        third,
        fourth,
    ]


def eliminate(state, entries, right, lines_out):
    shape = (8, WIDTH)
    lane = iota(shape, 1)
    for step in PLAN:
        works = []
        for slot, (knot, reach) in enumerate(step):
            at, sub, first = knot // 2, 4 * (knot % 2), 4 * knot
            inside = lane // 4 == knot
            columns = {}
            for tile in sorted({at, *reach}):
                held = state[8 * tile : 8 * tile + 8]
                columns[tile] = [
                    jnp.broadcast_to(held[:, first + index : first + index + 1], shape)
                    for index in range(4)
                ]
            for index in range(4):
                entries[slot, index] = columns[at][index]
            entry = {
                (one, two): jnp.broadcast_to(entries[slot, two, sub + one : sub + one + 1], shape)
                for one in range(4)
                for two in range(one, 4)
            }
            lines = [
                jnp.where(
                    inside,
                    jnp.where(lane == first + index, -1.0, 0.0),
                    jnp.broadcast_to(state[first + index : first + index + 1], shape),
                )
                for index in range(4)
            ]
            works.append((knot, reach, inside, columns, block_rows(entry, lines)))
        border = right
        for knot, reach, inside, columns, lines in works:
            for index in range(4):
                lines_out[4 * knot + index : 4 * knot + index + 1] = lines[index][0:1]
            for tile in reach:
                factors = columns[tile]
                taken = factors[0] * lines[0] + factors[1] * lines[1]
                taken = taken + (factors[2] * lines[2] + factors[3] * lines[3])
                rows = slice(8 * tile, 8 * tile + 8)
                state[rows] = jnp.where(inside, 0.0, state[rows]) - taken
            right = swept(right, border, knot, [line[0:1] for line in lines])
        yield
    return right


def swept(right, border, knot, lines):
    first = 4 * knot
    right = jnp.where(iota(right.shape, 1) // 4 == knot, 0.0, right)
    factors = [border[:, first + index : first + index + 1] for index in range(4)]
    taken = factors[0] * lines[0] + factors[1] * lines[1]
    return right - (taken + (factors[2] * lines[2] + factors[3] * lines[3]))


def substitute(right, lines):
    for step in PLAN:
        border = right
        for knot, unused in step:
            kept = [lines[4 * knot + index : 4 * knot + index + 1] for index in range(4)]
            right = swept(right, border, knot, kept)
        yield
    return right


def small_factor(sums):
    factor = {}
    for member in range(5):
        for column in range(member + 1):
            running = sums[8 * member + column : 8 * member + column + 1]
            if member == column:
                running = running + 1.0
            for offset in range(column):
                running = running - factor[member, offset] * factor[column, offset]
            if member == column:
                factor[member, member] = jnp.sqrt(running)
            else:
                factor[member, column] = running * inverse_of[column]
        inverse_of = {} if member == 0 else inverse_of
        inverse_of[member] = 1.0 / factor[member, member]
    inverse = {}
    for column in range(5):
        inverse[column, column] = inverse_of[column]
        for member in range(column + 1, 5):
            running = factor[member, column] * inverse[column, column]
            for offset in range(column + 1, member):
                running = running + factor[member, offset] * inverse[offset, column]
            inverse[member, column] = -running * inverse_of[member]
    return inverse


PLACES = [(row_id, col_id) for row_id in range(5) for col_id in range(row_id + 1)]


def small_apply(inverse, sides):
    forward = []
    for member in range(5):
        running = inverse[member, 0] * sides[0]
        for column in range(1, member + 1):
            running = running + inverse[member, column] * sides[column]
        forward.append(running)
    result = []
    for column in range(5):
        running = inverse[column, column] * forward[column]
        for member in range(column + 1, 5):
            running = running + inverse[member, column] * forward[member]
        result.append(running)
    return result


PAIRS = [(row_id, col_id) for row_id in range(5) for col_id in range(row_id + 1)]


def spline_terms(phase, attitude_partials):
    other = 1.0 - phase
    square = phase * phase
    cube = square * phase
    basis = [
        other * other * other / 6.0,
        (3.0 * cube - 6.0 * square + 4.0) / 6.0,
        (-3.0 * cube + 3.0 * square + 3.0 * phase + 1.0) / 6.0,
        cube / 6.0,
    ]
    return jnp.stack(
        [
            basis[knot_step] * attitude_partials[channel]
            for knot_step in range(4)
            for channel in range(4)
        ]
    )


def attitude_model(local, terms, knot_base):
    coefficients = lax.all_gather(local, "tm", axis=0, tiled=True)
    blocks, slots = knot_base.shape
    table = coefficients.reshape(blocks, -1, 4)
    knots_count = table.shape[1]
    grid = lax.broadcasted_iota(jnp.int32, (1, knots_count, 1), 1)
    running = jnp.zeros(knot_base.shape, jnp.float32)
    for knot_step in range(4):
        hit = (grid == (knot_base + knot_step)[:, None, :]).astype(jnp.float32)
        picked = jnp.einsum(
            "bkc,bks->bcs",
            table,
            hit,
            precision=lax.Precision.HIGHEST,
            preferred_element_type=jnp.float32,
        )
        for channel in range(4):
            running = running + terms[4 * knot_step + channel] * picked[:, channel, :]
    return running


def small_solve(matrix, right_side):
    extent = len(right_side)
    factor = {}
    for member in range(extent):
        for column in range(member + 1):
            running = matrix[member][column]
            for offset in range(column):
                running = running - factor[member, offset] * factor[column, offset]
            if member == column:
                factor[member, member] = jnp.sqrt(running)
            else:
                factor[member, column] = running / factor[column, column]
    forward = []
    for member in range(extent):
        running = right_side[member]
        for offset in range(member):
            running = running - factor[member, offset] * forward[offset]
        forward.append(running / factor[member, member])
    result = [None] * extent
    for member in reversed(range(extent)):
        running = forward[member]
        for offset in range(member + 1, extent):
            running = running - factor[offset, member] * result[offset]
        result[member] = running / factor[member, member]
    return jnp.stack(result)


def source_solve(ids, count, weighted, source_partials, target):
    products = [
        weighted * source_partials[row_id] * source_partials[col_id] for row_id, col_id in PAIRS
    ]
    products = products + [weighted * source_partials[row_id] * target for row_id in range(5)]
    stacked = jnp.moveaxis(jnp.stack(products), 1, 0)
    owners = lax.broadcasted_iota(jnp.int32, (count, 1), 0)

    def accumulate(total, item):
        values, block_ids = item
        hit = (block_ids[None, :] == owners).astype(jnp.float32)
        added = lax.dot_general(
            values,
            hit,
            (((1,), (1,)), ((), ())),
            precision=lax.Precision.HIGHEST,
            preferred_element_type=jnp.float32,
        )
        return (total + added, None)

    sums, unused = lax.scan(
        accumulate, jnp.zeros((len(products), count), jnp.float32), (stacked, ids)
    )
    entries = {}
    for position, pair in enumerate(PAIRS):
        entry_value = sums[position] + (1.0 if pair[0] == pair[1] else 0.0)
        entries[pair[0], pair[1]] = entry_value
        entries[pair[1], pair[0]] = entry_value
    matrix = [[entries[row_id, col_id] for col_id in range(5)] for row_id in range(5)]
    return small_solve(matrix, [sums[15 + row_id] for row_id in range(5)])


def pick_params(params, ids):
    count = params.shape[1]
    owners = lax.broadcasted_iota(jnp.int32, (count, 1), 0)

    def pick_single(carry, block_ids):
        hit = (block_ids[None, :] == owners).astype(jnp.float32)
        return (
            carry,
            jnp.dot(
                params, hit, precision=lax.Precision.HIGHEST, preferred_element_type=jnp.float32
            ),
        )

    unused, picked = lax.scan(pick_single, 0, ids)
    return jnp.moveaxis(picked, 1, 0)


def spd_solve(matrix, right_side):
    eye = jnp.eye(matrix.shape[-1], dtype=jnp.float32)
    lower = jnp.linalg.cholesky(matrix + eye)
    middle = lax.linalg.triangular_solve(lower, right_side[..., None], left_side=True, lower=True)
    result = lax.linalg.triangular_solve(
        lower, middle, left_side=True, lower=True, transpose_a=True
    )
    return result[..., 0]


def block_normals(terms, knot_base, weighted, resid):
    blocks, slots = knot_base.shape
    spread = jnp.moveaxis(terms.reshape(4, 4, blocks, slots), 2, 0)

    def block_single(item):
        part, base, weights, values = item
        grid = lax.broadcasted_iota(jnp.int32, (KNOTS_DEV, slots), 0)
        design = jnp.zeros((KNOTS_DEV, 4, slots), jnp.float32)
        for knot_step in range(4):
            hit = (grid == base[None, :] + knot_step).astype(jnp.float32)
            design = design + hit[:, None, :] * part[knot_step][None, :, :]
        design = design.reshape(KNOTS_DEV * 4, slots)
        normal = lax.dot_general(
            design * weights[None, :],
            design,
            (((1,), (1,)), ((), ())),
            precision=lax.Precision.HIGHEST,
            preferred_element_type=jnp.float32,
        )
        right = jnp.dot(
            design,
            weights * values,
            precision=lax.Precision.HIGHEST,
            preferred_element_type=jnp.float32,
        )
        return (normal, right)

    return lax.map(block_single, (spread, knot_base, weighted, resid))


def plain_body(
    observed,
    weight_obs,
    present,
    source_partials,
    attitude_partials,
    phase,
    knot_base,
    source_id,
    cal_id,
    attitude,
    calibration,
):
    weighted = present.astype(jnp.float32) * weight_obs
    terms = spline_terms(phase, attitude_partials)
    flat_cal = cal_id.reshape(-1)
    local = attitude
    cal_now = calibration
    params = jnp.zeros((5, SRC_DEV), jnp.float32)
    for sweep in range(2):
        target = observed - attitude_model(local, terms, knot_base) - cal_now[cal_id]
        params = source_solve(source_id, SRC_DEV, weighted, source_partials, target)
        resid = target - jnp.sum(source_partials * pick_params(params, source_id), axis=0)
        normals, rights = block_normals(terms, knot_base, weighted, resid)
        normal, right = (
            lax.psum_scatter(normals, "tm", scatter_dimension=0, tiled=True),
            lax.psum_scatter(rights, "tm", scatter_dimension=0, tiled=True),
        )
        normal, right = lax.psum((normal[0], right[0]), "src")
        local = local + spd_solve(normal, right)
        numer = jax.ops.segment_sum((weighted * resid).reshape(-1), flat_cal, num_segments=CAL)
        denom = jax.ops.segment_sum(weighted.reshape(-1), flat_cal, num_segments=CAL)
        numer, denom = lax.psum((numer, denom), ("src", "tm"))
        cal_now = cal_now + numer / (denom + 1.0)
    final = observed - attitude_model(local, terms, knot_base) - cal_now[cal_id]
    final = final - jnp.sum(source_partials * pick_params(params, source_id), axis=0)
    return (params, local, cal_now, final)


BAND = 16
PIECE = 2


def begin(pairs, sems):
    copies = [
        pltpu.make_async_copy(origin, held, sems.at[place])
        for place, (origin, held) in enumerate(pairs)
    ]
    for copy in copies:
        copy.start()
    return copies


def finish(copies):
    for copy in copies:
        copy.wait()


def tile_of(value):
    return jnp.concatenate(
        [value[:, at : at + LANES] for at in range(0, value.shape[1], LANES)], axis=0
    )


def pick_from(table_t, ids, units, rows):
    found = dot(jnp.concatenate(split3(table_t)[:2], axis=0), units)
    found = found[:LANES] + found[LANES:]
    hit = iota(found.shape, 0) == ids % LANES
    return unflat(jnp.sum(jnp.where(hit, found, 0.0), axis=0, keepdims=True), rows)


def two_parts(line):
    first = line.astype(BF16).astype(F32)
    return first, (line - first).astype(BF16).astype(F32)


def model_of(line, parts):
    first, second = two_parts(line)
    left = jnp.concatenate([first, first], axis=1)
    right = jnp.concatenate([second, jnp.zeros_like(second)], axis=1)
    row = iota((SUB, 2 * WIDTH), 0)
    both = jnp.where(row == 0, left, jnp.where(row == 1, right, 0.0)).astype(BF16)
    return jnp.sum(dot(both, parts), axis=0, keepdims=True)


def side_of(values, parts):
    first, second = two_parts(values)
    row = iota((SUB, values.shape[1]), 0)
    both = jnp.where(row == 0, first, jnp.where(row == 1, second, 0.0)).astype(BF16)
    found = dot_t(both, parts)
    return found[0:1, :WIDTH] + found[1:2, :WIDTH] + found[0:1, WIDTH:]


def normals_kernel(
    weight_in, present_in, attitude_in, phase_in, knot_in, cal_in, start_in,
    send_out, design_out, weighted_out, cal_id,
    weight_obs, present, attitude_partials, phase, knot_base, start, stacked, sems,
):
    copies = begin(
        [
            (weight_in, weight_obs), (present_in, present), (cal_in, cal_id), (start_in, start),
            (phase_in, phase), (knot_in, knot_base), (attitude_in, attitude_partials),
        ],
        sems,
    )
    finish(copies[:4])
    rows = weight_obs.shape[0]
    weighted = present[...].astype(F32) * weight_obs[...]
    weighted_out[...] = weighted
    first, second = tile_of(cal_id[...].astype(F32)), tile_of(weighted)
    devices = send_out.shape[0]
    for device in range(devices):
        core = core_of(device, rows)
        for index in range(rows):
            at = rows * core + index
            send_out[device, PIECE + index] = first[at : at + 1]
            send_out[device, PIECE + rows + index] = second[at : at + 1]
        send_out[device, PIECE + 2 * rows] = start[...]
    finish(copies[4:])
    u = phase[...]
    other = 1.0 - u
    square = u * u
    cube = square * u
    basis = [
        other * other * other / 6.0,
        (3.0 * cube - 6.0 * square + 4.0) / 6.0,
        (-3.0 * cube + 3.0 * square + 3.0 * u + 1.0) / 6.0,
        cube / 6.0,
    ]
    for row in range(rows):
        at = slice(row, row + 1)
        for channel in range(4):
            lines = attitude_partials[channel, at]
            stacked[row, channel : channel + 1] = lines
            stacked[row, channel + 4 : channel + 5] = lines
        design = design_of(knot_base[at], [part[at] for part in basis], stacked[row])
        design_out[row] = design
        band = pack_band(exact_dot_t(design * weighted[at], design))
        half, place = divmod(row, rows // PIECE)
        for index in range(BAND):
            send_out[place * BAND + index, half] = band[index : index + 1]


def sources_kernel(
    cal_id, weighted, design, observed_in, source_in, id_in, calibration_in,
    partials_out, factor_out, target_out, table_out, hits_out, units_out, parts_out, observed,
    source_partials, source_id, table, sems,
):
    copies = begin(
        [
            (observed_in, observed), (source_in, source_partials), (id_in, source_id),
            (calibration_in, table),
        ],
        sems,
    )
    finish(copies)
    rows, slots = observed.shape
    matrix = jnp.zeros((40, SRC_DEV), F32)
    for row in range(rows):
        at = slice(row, row + 1)
        for index in range(5):
            partials_out[row, index : index + 1] = source_partials[index, at]
        partials_out[row, 5:] = jnp.zeros((SUB - 5, slots), F32)
        partials = partials_out[row]
        products = jnp.concatenate(
            [partials * (weighted[at] * partials[index : index + 1]) for index in range(5)], axis=0
        )
        hits_out[row] = one_hot(source_id[at], SRC_DEV)
        found = dot_t(jnp.concatenate(split3(products), axis=0), hits_out[row])
        matrix = matrix + found[:40] + found[40:80] + found[80:]
        first, second, unused = split3(design[row])
        parts_out[row, :WIDTH] = first
        parts_out[row, WIDTH:] = second
    ids = flat(cal_id[...])
    units_out[...] = one_hot(ids // LANES, HIGH)
    inverse = small_factor(matrix)
    for place, pair in enumerate(PLACES):
        factor_out[place : place + 1] = inverse[pair]
    factor_out[15:16] = jnp.zeros((1, SRC_DEV), F32)
    table_t = table[...].T
    table_out[...] = table_t
    for row, picked in enumerate(pick_from(table_t, ids, units_out[...], rows)):
        target_out[row : row + 1] = observed[row : row + 1] - picked


def core_of(device, line):
    return device // line % 2


def residual_step(targets, parts, partials, factor, weighted, hits, send_out):
    rows = len(targets)
    inverse = {pair: factor[place : place + 1] for place, pair in enumerate(PLACES)}
    sides = jnp.zeros((SUB, SRC_DEV), F32)
    for row in range(rows):
        products = partials[row] * (weighted[row : row + 1] * targets[row])
        found = dot_t(jnp.concatenate(split3(products), axis=0), hits[row])
        sides = sides + found[:SUB] + found[SUB : 2 * SUB] + found[2 * SUB :]
    params = small_apply(inverse, [sides[index : index + 1] for index in range(5)])
    table = jnp.concatenate(params + [jnp.zeros((3, SRC_DEV), F32)], axis=0)
    split = jnp.concatenate(split3(table), axis=0)
    explained, scaled, rights = [], [], []
    for row in range(rows):
        found = dot(split, hits[row])
        found = found[:SUB] + found[SUB : 2 * SUB] + found[2 * SUB :]
        explained.append(jnp.sum(found * partials[row], axis=0, keepdims=True))
    for row in range(rows):
        scaled.append(weighted[row : row + 1] * (targets[row] - explained[row]))
        rights.append(side_of(scaled[row], parts[row]))
    half = rows // PIECE
    for device in range(send_out.shape[0]):
        core = core_of(device, rows)
        lines = [line[:, core * LANES : (core + 1) * LANES] for line in scaled]
        for index, line in enumerate(lines + rights[half * core : half * core + half]):
            send_out[device, index] = line
    return params, explained


def first_kernel(received, target, parts, partials, factor, weighted, hits, send_out):
    rows = parts.shape[0]
    last = received.shape[1] - 1
    targets = [
        target[row : row + 1] - model_of(received[row, last], parts[row]) for row in range(rows)
    ]
    residual_step(targets, parts, partials, factor, weighted, hits, send_out)
    totals = [right_side(received, place) for place in range(PIECE)]
    for device in range(send_out.shape[0]):
        send_out[device, send_out.shape[1] - 1] = totals[core_of(device, rows)]


def spread(line):
    return jnp.broadcast_to(line, (SUB, LANES))


def wide(tile, count):
    tile = jnp.concatenate([tile, tile], axis=0).astype(BF16)
    return jnp.concatenate([tile] * (count // 16), axis=0)


def unit_sums(received, value_of, total):
    rows = (received.shape[1] - PIECE - 1) // 2
    low_row = iota((LANES, LANES), 0).astype(F32).astype(BF16)
    high_row = iota((HIGH, LANES), 0).astype(F32).astype(BF16)
    one, none = jnp.ones((), BF16), jnp.zeros((), BF16)
    for begin in range(0, received.shape[0], 2):
        lefts, rights = [], []
        for device in (begin, begin + 1):
            for index in range(rows):
                unit = spread(received[device, PIECE + index])
                high = jnp.floor(unit * (1.0 / LANES))
                hit = low_row == wide(unit - LANES * high, LANES)
                value = spread(value_of(device, index))
                first = value.astype(BF16).astype(F32)
                lefts.append(
                    jnp.concatenate(
                        [
                            jnp.where(hit, wide(first, LANES), none),
                            jnp.where(hit, wide(value - first, LANES), none),
                        ],
                        axis=0,
                    )
                )
                rights.append(jnp.where(high_row == wide(high, HIGH), one, none))
        found = dot_t(jnp.concatenate(lefts, axis=1), jnp.concatenate(rights, axis=1))
        if begin == 0:
            total[:LANES] = found[:LANES] + found[LANES:]
        else:
            total[:LANES] += found[:LANES] + found[LANES:]
        yield


def matrix_of(band):
    lower = unpack_band(band)
    diagonal = iota(lower.shape, 0) == iota(lower.shape, 1)
    return lower + jnp.where(diagonal, 1.0, lower.T)


def together(works):
    works = list(works)
    while works:
        for work in list(works):
            if next(work, works) is works:
                works.remove(work)


def weights_kernel(received, sums_out):
    rows = (received.shape[1] - PIECE - 1) // 2
    together(
        [
            unit_sums(
                received, lambda device, index: received[device, PIECE + rows + index], sums_out
            )
        ]
    )


def right_side(values, place):
    total = values[0, place]
    for device in range(1, values.shape[0]):
        total = total + values[device, place]
    return total


def core(axis):
    return lax.rem(lax.axis_index(axis), 2)


def coefficients(bundle, place):
    return bundle[LANES + place : LANES + place + 1, :WIDTH]


def put(bundle, place, line):
    bundle[LANES + place : LANES + place + 1] = jnp.concatenate([line, line], axis=1)


def solve_kernel(axis, values, received, bundle_out, lines_out, bands, states, entries):
    half = lines_out.shape[0]
    rows = values.shape[1] - half - 1
    for device in range(values.shape[0]):
        bands[device : device + 1] = values[device, rows + half]
    bundle_out[LANES:] = jnp.zeros((SUB, HIGH), F32)

    def attitude(place):
        states[place] = matrix_of(bands[BAND * place : BAND * (place + 1)])
        change = yield from eliminate(
            states.at[place],
            entries.at[place],
            right_side(values, rows + place),
            lines_out.at[place],
        )
        start = received[half * core(axis) + place, received.shape[1] - 1]
        put(bundle_out, place, start + change)
        yield

    together(
        [unit_sums(received, lambda device, index: values[device, index], bundle_out)]
        + [attitude(place) for place in range(half)]
    )


def both_halves(axis, own, other, half):
    first = core(axis) == 0
    pairs = [(coefficients(own, place), coefficients(other, place)) for place in range(half)]
    lines = [jnp.where(first, one, two) for one, two in pairs]
    return lines + [jnp.where(first, two, one) for one, two in pairs]


def second_kernel(
    axis, bundle, other, weights, other_weights, table, ids, units, observed, parts, partials, factor,
    weighted, hits,
    send_out, params_out, explained_out, table_out, scale_out,
):
    rows = parts.shape[0]
    scale = 1.0 / (weights[...] + other_weights[...] + 1.0)
    scale_out[...] = scale
    table_t = table[...] + (bundle[:LANES] + other[:LANES]) * scale
    table_out[...] = table_t
    picked = pick_from(table_t, flat(ids[...]), units[...], rows)
    lines = both_halves(axis, bundle, other, rows // PIECE)
    targets = [
        observed[row : row + 1] - model_of(lines[row], parts[row]) - picked[row]
        for row in range(rows)
    ]
    params, explained = residual_step(targets, parts, partials, factor, weighted, hits, send_out)
    for index in range(5):
        params_out[index : index + 1] = params[index]
    for row in range(rows):
        explained_out[row : row + 1] = explained[row]


def last_kernel(values, received, bundle, lines, bundle_out):
    half = lines.shape[0]
    rows = values.shape[1] - half
    bundle_out[LANES:] = jnp.zeros((SUB, HIGH), F32)

    def solve(place):
        change = yield from substitute(right_side(values, rows + place), lines.at[place])
        put(bundle_out, place, coefficients(bundle, place) + change)
        yield

    together(
        [unit_sums(received, lambda device, index: values[device, index], bundle_out)]
        + [solve(place) for place in range(half)]
    )


def final_kernel(
    axis, line, bundle, other, table, scale, ids, units, observed, parts, explained,
    cal_out, attitude_out, resid_out,
):
    rows = parts.shape[0]
    table_t = table[...] + (bundle[:LANES] + other[:LANES]) * scale[...]
    cal_out[...] = table_t.T
    picked = pick_from(table_t, flat(ids[...]), units[...], rows)
    me = lax.axis_index(line)
    lines = both_halves(axis, bundle, other, rows // PIECE)
    own = lines[0]
    for row in range(rows):
        own = jnp.where(me == row, lines[row], own)
        at = slice(row, row + 1)
        resid_out[at] = observed[at] - model_of(lines[row], parts[row]) - picked[row] - explained[at]
    attitude_out[...] = own


VMEM = pl.BlockSpec(memory_space=pltpu.VMEM)
ANY = pl.BlockSpec(memory_space=pltpu.HBM)


def call(kernel, outs, *args, away=0, scratch=()):
    near = args[: len(args) - away]
    far = [pltpu.with_memory_space_constraint(arg, pltpu.HBM) for arg in args[len(args) - away :]]
    return pl.pallas_call(
        kernel,
        out_shape=outs,
        in_specs=[VMEM] * len(near) + [ANY] * away,
        out_specs=[VMEM] * len(outs),
        scratch_shapes=scratch,
        compiler_params=pltpu.CompilerParams(vmem_limit_bytes=VMEM_BYTES),
    )(*near, *far)


def stay(*shape, dtype=F32):
    return pltpu.VMEM(shape, dtype)


def leave(*shape):
    return jax.ShapeDtypeStruct(shape, F32)


def swap(value):
    return lax.ppermute(value, "src", [(at, at ^ 1) for at in range(lax.axis_size("src"))])


def exchange(value):
    return lax.all_to_all(value, ("src", "tm"), 0, 0, tiled=True)


def body(
    observed, weight_obs, present, source_partials, attitude_partials, phase, knot_base, source_id,
    cal_id, attitude, calibration,
):
    rows, slots = observed.shape
    devices = lax.axis_size("src") * lax.axis_size("tm")
    half = rows // PIECE
    first_q = attitude.reshape(1, WIDTH)
    held = [weight_obs, present, attitude_partials, phase, knot_base, first_q]
    received, design, weighted, units_seen = call(
        normals_kernel,
        [
            leave(devices, PIECE + 2 * rows + 1, 1, LANES), stay(rows, WIDTH, slots),
            stay(rows, slots), stay(rows, slots, dtype=jnp.int32),
        ],
        weight_obs, present, attitude_partials, phase, knot_base, cal_id, first_q,
        away=7,
        scratch=[pltpu.VMEM(each.shape, each.dtype) for each in held]
        + [pltpu.VMEM((rows, SUB, slots), F32), pltpu.SemaphoreType.DMA((7,))],
    )
    received = exchange(received)
    cal_id = units_seen
    partials, factor, target, table, hits, units, parts, seen = call(
        sources_kernel,
        [
            stay(rows, SUB, slots), stay(16, SRC_DEV), stay(rows, slots), stay(LANES, HIGH),
            stay(rows, SRC_DEV, slots, dtype=BF16), stay(HIGH, rows * slots, dtype=BF16),
            stay(rows, 2 * WIDTH, slots, dtype=BF16), stay(rows, slots),
        ],
        cal_id, weighted, design, observed, source_partials, source_id,
        calibration.reshape(HIGH, LANES),
        away=4,
        scratch=[
            pltpu.VMEM(source_partials.shape, F32), pltpu.VMEM((rows, slots), jnp.int32),
            pltpu.VMEM((HIGH, LANES), F32), pltpu.SemaphoreType.DMA((4,)),
        ],
    )
    received, factor = lax.optimization_barrier((received, factor))
    (values,) = call(
        first_kernel, [leave(devices, rows + half + 1, 1, LANES)],
        received, target, parts, partials, factor, weighted, hits,
    )
    values, received = lax.optimization_barrier((values, received))
    values = exchange(values)
    (weights,) = call(weights_kernel, [leave(LANES, HIGH)], received)
    other_weights, received = lax.optimization_barrier((swap(weights), received))
    bundle, lines = call(
        functools.partial(solve_kernel, "src"),
        [leave(LANES + SUB, HIGH), stay(half, WIDTH, WIDTH)],
        values, received,
        scratch=[
            pltpu.VMEM((half * BAND, WIDTH), F32), pltpu.VMEM((half, WIDTH, WIDTH), F32),
            pltpu.VMEM((half, len(PLAN[0]), 4, 8, WIDTH), F32),
        ],
    )
    values, params, explained, table, scale = call(
        functools.partial(second_kernel, "src"),
        [
            leave(devices, rows + half, 1, LANES), leave(5, SRC_DEV), stay(rows, slots),
            stay(LANES, HIGH), stay(LANES, HIGH),
        ],
        bundle, swap(bundle), weights, other_weights, table, cal_id, units, seen, parts, partials,
        factor, weighted, hits,
    )
    values = exchange(values)
    (bundle,) = call(
        last_kernel, [leave(LANES + SUB, HIGH)], values, received, bundle, lines
    )
    cal, now, final = call(
        functools.partial(final_kernel, "src", "tm"),
        [leave(HIGH, LANES), leave(1, WIDTH), leave(rows, slots)],
        bundle, swap(bundle), table, scale, cal_id, units, seen, parts, explained,
    )
    return (params, now.reshape(WIDTH), cal.reshape(CAL), final)


def solution(mesh):
    many = mesh.shape["src"] * mesh.shape["tm"]
    return jax.shard_map(
        body if many * PIECE == mesh.shape["tm"] * BAND else plain_body,
        mesh=mesh,
        in_specs=(
            P(None, ("src", "tm")),
            P(None, ("src", "tm")),
            P(None, ("src", "tm")),
            P(None, None, ("src", "tm")),
            P(None, None, ("src", "tm")),
            P(None, ("src", "tm")),
            P(None, ("src", "tm")),
            P(None, ("src", "tm")),
            P(None, ("src", "tm")),
            P("tm"),
            P(),
        ),
        out_specs=(P(None, ("src", "tm")), P("tm"), P(), P(None, ("src", "tm"))),
        check_vma=False,
    )
```

```python
import functools

import jax
import jax.numpy as jnp
from jax import lax
from jax.experimental import pallas as pl
from jax.experimental.pallas import tpu as pltpu
from jax.sharding import PartitionSpec as P

KNOTS_DEV = 32
WIDTH = 4 * KNOTS_DEV
SRC_DEV = 128
CAL = 32768
LANES = 128
HIGH = CAL // LANES
SUB = 8
VMEM_BYTES = 48 * 1024 * 1024

F32 = jnp.float32
BF16 = jnp.bfloat16
EXACT = lax.Precision.HIGHEST


def iota(shape, dim):
    return lax.broadcasted_iota(jnp.int32, shape, dim)


def split3(value):
    first = value.astype(BF16)
    rest = value - first.astype(F32)
    second = rest.astype(BF16)
    third = (rest - second.astype(F32)).astype(BF16)
    return first, second, third


def dot(left, right):
    return lax.dot_general(left, right, (((1,), (0,)), ((), ())), preferred_element_type=F32)


def dot_t(left, right):
    return lax.dot_general(left, right, (((1,), (1,)), ((), ())), preferred_element_type=F32)


def exact_dot(left, right):
    return lax.dot_general(
        left, right, (((1,), (0,)), ((), ())), precision=EXACT, preferred_element_type=F32
    )


def exact_dot_t(left, right):
    return lax.dot_general(
        left, right, (((1,), (1,)), ((), ())), precision=EXACT, preferred_element_type=F32
    )


def one_hot(ids, count):
    return jnp.where(iota((count, ids.shape[1]), 0) == ids, 1.0, 0.0).astype(BF16)


def flat(value):
    return jnp.concatenate([value[row : row + 1] for row in range(value.shape[0])], axis=1)


def unflat(value, rows):
    slots = value.shape[1] // rows
    return [value[:, row * slots : (row + 1) * slots] for row in range(rows)]


def cal_pick(table, ids):
    parts = jnp.concatenate(split3(table.T), axis=0)
    high = ids // LANES
    low = ids % LANES
    found = dot(parts, one_hot(high, HIGH))
    found = found[:LANES] + found[LANES : 2 * LANES] + found[2 * LANES :]
    return jnp.sum(jnp.where(iota(found.shape, 0) == low, found, 0.0), axis=0, keepdims=True)


def cal_sums(values, ids):
    high = one_hot(ids // LANES, HIGH)
    low = iota((LANES, ids.shape[1]), 0) == ids % LANES
    total = None
    for part in split3(values):
        spread = jnp.where(low, part.astype(F32), 0.0).astype(BF16)
        added = dot_t(high, spread)
        total = added if total is None else total + added
    return total


def design_of(base, basis, partials):
    slots = base.shape[1]
    knot = iota((WIDTH, slots), 0) // 4
    step = knot - base
    spread = jnp.zeros((WIDTH, slots), F32)
    for index in range(4):
        spread = jnp.where(step == index, basis[index], spread)
    return spread * jnp.concatenate([partials] * (WIDTH // 8), axis=0)


def band_shift(tile, knot):
    return ((tile % 8) * 16 - (8 * tile + 4 * knot - 12)) % WIDTH


def pack_band(normal):
    place = iota((8, WIDTH), 1) // 16
    upper = iota((8, WIDTH), 0) < 4
    groups = []
    for group in range(2):
        packed = jnp.zeros((8, WIDTH), F32)
        for tile in range(8 * group, 8 * group + 8):
            rows = normal[8 * tile : 8 * tile + 8]
            rolled = jnp.where(
                upper,
                pltpu.roll(rows, band_shift(tile, 0), 1),
                pltpu.roll(rows, band_shift(tile, 1), 1),
            )
            packed = jnp.where(place == tile % 8, rolled, packed)
        groups.append(packed)
    return jnp.concatenate(groups, axis=0)


def unpack_band(packed):
    place = iota((8, WIDTH), 1) // 16
    upper = iota((8, WIDTH), 0) < 4
    tiles = []
    for tile in range(16):
        group = tile // 8
        rows = jnp.where(place == tile % 8, packed[8 * group : 8 * group + 8], 0.0)
        tiles.append(
            jnp.where(
                upper,
                pltpu.roll(rows, (-band_shift(tile, 0)) % WIDTH, 1),
                pltpu.roll(rows, (-band_shift(tile, 1)) % WIDTH, 1),
            )
        )
    full = jnp.concatenate(tiles, axis=0)
    return jnp.where(iota(full.shape, 0) >= iota(full.shape, 1), full, 0.0)


ORDER = (
    (0, 8, 17, 31), (1, 9, 18, 30), (2, 10, 19, 29), (3, 11, 20, 28), (4, 12, 21, 27), (13, 22, 26),
    (5, 23), (6, 24), (7, 25), (14,), (15,), (16,),
)


def plan_of(order):
    near = {
        knot: {other for other in range(KNOTS_DEV) if 0 < abs(other - knot) <= 3}
        for knot in range(KNOTS_DEV)
    }
    plan = []
    for step in order:
        plan.append([(knot, sorted({other // 2 for other in near[knot]})) for knot in step])
        for knot in step:
            assert not near[knot] & set(step)
            for other in near[knot]:
                near[other] = (near[other] | near[knot]) - {other, knot}
    return plan


PLAN = plan_of(ORDER)


def block_rows(entry, lines):
    scale = 1.0 / (entry[0, 0] * entry[1, 1] - entry[0, 1] * entry[0, 1])
    low, mid, high = entry[0, 0] * scale, entry[0, 1] * scale, entry[1, 1] * scale
    turned = {}
    for column in (2, 3):
        turned[0, column] = high * entry[0, column] - mid * entry[1, column]
        turned[1, column] = low * entry[1, column] - mid * entry[0, column]
    rest = {}
    for row, column in ((2, 2), (2, 3), (3, 3)):
        taken = entry[0, row] * turned[0, column] + entry[1, row] * turned[1, column]
        rest[row, column] = entry[row, column] - taken
    upper = [high * lines[0] - mid * lines[1], low * lines[1] - mid * lines[0]]
    lower = [
        lines[row] - (entry[0, row] * upper[0] + entry[1, row] * upper[1]) for row in (2, 3)
    ]
    scale = 1.0 / (rest[2, 2] * rest[3, 3] - rest[2, 3] * rest[2, 3])
    third = (rest[3, 3] * scale) * lower[0] - (rest[2, 3] * scale) * lower[1]
    fourth = (rest[2, 2] * scale) * lower[1] - (rest[2, 3] * scale) * lower[0]
    return [
        upper[0] - (turned[0, 2] * third + turned[0, 3] * fourth),
        upper[1] - (turned[1, 2] * third + turned[1, 3] * fourth),
        third,
        fourth,
    ]


def eliminate(state, entries, right, lines_out):
    shape = (8, WIDTH)
    lane = iota(shape, 1)
    for step in PLAN:
        works = []
        for slot, (knot, reach) in enumerate(step):
            at, sub, first = knot // 2, 4 * (knot % 2), 4 * knot
            inside = lane // 4 == knot
            columns = {}
            for tile in sorted({at, *reach}):
                held = state[8 * tile : 8 * tile + 8]
                columns[tile] = [
                    jnp.broadcast_to(held[:, first + index : first + index + 1], shape)
                    for index in range(4)
                ]
            for index in range(4):
                entries[slot, index] = columns[at][index]
            entry = {
                (one, two): jnp.broadcast_to(entries[slot, two, sub + one : sub + one + 1], shape)
                for one in range(4)
                for two in range(one, 4)
            }
            lines = [
                jnp.where(
                    inside,
                    jnp.where(lane == first + index, -1.0, 0.0),
                    jnp.broadcast_to(state[first + index : first + index + 1], shape),
                )
                for index in range(4)
            ]
            works.append((knot, reach, inside, columns, block_rows(entry, lines)))
        border = right
        for knot, reach, inside, columns, lines in works:
            for index in range(4):
                lines_out[4 * knot + index : 4 * knot + index + 1] = lines[index][0:1]
            for tile in reach:
                factors = columns[tile]
                taken = factors[0] * lines[0] + factors[1] * lines[1]
                taken = taken + (factors[2] * lines[2] + factors[3] * lines[3])
                rows = slice(8 * tile, 8 * tile + 8)
                state[rows] = jnp.where(inside, 0.0, state[rows]) - taken
            right = swept(right, border, knot, [line[0:1] for line in lines])
        yield
    return right


def swept(right, border, knot, lines):
    first = 4 * knot
    right = jnp.where(iota(right.shape, 1) // 4 == knot, 0.0, right)
    factors = [border[:, first + index : first + index + 1] for index in range(4)]
    taken = factors[0] * lines[0] + factors[1] * lines[1]
    return right - (taken + (factors[2] * lines[2] + factors[3] * lines[3]))


def substitute(right, lines):
    for step in PLAN:
        border = right
        for knot, unused in step:
            kept = [lines[4 * knot + index : 4 * knot + index + 1] for index in range(4)]
            right = swept(right, border, knot, kept)
        yield
    return right


def small_factor(sums):
    factor = {}
    for member in range(5):
        for column in range(member + 1):
            running = sums[8 * member + column : 8 * member + column + 1]
            if member == column:
                running = running + 1.0
            for offset in range(column):
                running = running - factor[member, offset] * factor[column, offset]
            if member == column:
                factor[member, member] = jnp.sqrt(running)
            else:
                factor[member, column] = running * inverse_of[column]
        inverse_of = {} if member == 0 else inverse_of
        inverse_of[member] = 1.0 / factor[member, member]
    inverse = {}
    for column in range(5):
        inverse[column, column] = inverse_of[column]
        for member in range(column + 1, 5):
            running = factor[member, column] * inverse[column, column]
            for offset in range(column + 1, member):
                running = running + factor[member, offset] * inverse[offset, column]
            inverse[member, column] = -running * inverse_of[member]
    return inverse


PLACES = [(row_id, col_id) for row_id in range(5) for col_id in range(row_id + 1)]


def small_apply(inverse, sides):
    forward = []
    for member in range(5):
        running = inverse[member, 0] * sides[0]
        for column in range(1, member + 1):
            running = running + inverse[member, column] * sides[column]
        forward.append(running)
    result = []
    for column in range(5):
        running = inverse[column, column] * forward[column]
        for member in range(column + 1, 5):
            running = running + inverse[member, column] * forward[member]
        result.append(running)
    return result


PAIRS = [(row_id, col_id) for row_id in range(5) for col_id in range(row_id + 1)]


def spline_terms(phase, attitude_partials):
    other = 1.0 - phase
    square = phase * phase
    cube = square * phase
    basis = [
        other * other * other / 6.0,
        (3.0 * cube - 6.0 * square + 4.0) / 6.0,
        (-3.0 * cube + 3.0 * square + 3.0 * phase + 1.0) / 6.0,
        cube / 6.0,
    ]
    return jnp.stack(
        [
            basis[knot_step] * attitude_partials[channel]
            for knot_step in range(4)
            for channel in range(4)
        ]
    )


def attitude_model(local, terms, knot_base):
    coefficients = lax.all_gather(local, "tm", axis=0, tiled=True)
    blocks, slots = knot_base.shape
    table = coefficients.reshape(blocks, -1, 4)
    knots_count = table.shape[1]
    grid = lax.broadcasted_iota(jnp.int32, (1, knots_count, 1), 1)
    running = jnp.zeros(knot_base.shape, jnp.float32)
    for knot_step in range(4):
        hit = (grid == (knot_base + knot_step)[:, None, :]).astype(jnp.float32)
        picked = jnp.einsum(
            "bkc,bks->bcs",
            table,
            hit,
            precision=lax.Precision.HIGHEST,
            preferred_element_type=jnp.float32,
        )
        for channel in range(4):
            running = running + terms[4 * knot_step + channel] * picked[:, channel, :]
    return running


def small_solve(matrix, right_side):
    extent = len(right_side)
    factor = {}
    for member in range(extent):
        for column in range(member + 1):
            running = matrix[member][column]
            for offset in range(column):
                running = running - factor[member, offset] * factor[column, offset]
            if member == column:
                factor[member, member] = jnp.sqrt(running)
            else:
                factor[member, column] = running / factor[column, column]
    forward = []
    for member in range(extent):
        running = right_side[member]
        for offset in range(member):
            running = running - factor[member, offset] * forward[offset]
        forward.append(running / factor[member, member])
    result = [None] * extent
    for member in reversed(range(extent)):
        running = forward[member]
        for offset in range(member + 1, extent):
            running = running - factor[offset, member] * result[offset]
        result[member] = running / factor[member, member]
    return jnp.stack(result)


def source_solve(ids, count, weighted, source_partials, target):
    products = [
        weighted * source_partials[row_id] * source_partials[col_id] for row_id, col_id in PAIRS
    ]
    products = products + [weighted * source_partials[row_id] * target for row_id in range(5)]
    stacked = jnp.moveaxis(jnp.stack(products), 1, 0)
    owners = lax.broadcasted_iota(jnp.int32, (count, 1), 0)

    def accumulate(total, item):
        values, block_ids = item
        hit = (block_ids[None, :] == owners).astype(jnp.float32)
        added = lax.dot_general(
            values,
            hit,
            (((1,), (1,)), ((), ())),
            precision=lax.Precision.HIGHEST,
            preferred_element_type=jnp.float32,
        )
        return (total + added, None)

    sums, unused = lax.scan(
        accumulate, jnp.zeros((len(products), count), jnp.float32), (stacked, ids)
    )
    entries = {}
    for position, pair in enumerate(PAIRS):
        entry_value = sums[position] + (1.0 if pair[0] == pair[1] else 0.0)
        entries[pair[0], pair[1]] = entry_value
        entries[pair[1], pair[0]] = entry_value
    matrix = [[entries[row_id, col_id] for col_id in range(5)] for row_id in range(5)]
    return small_solve(matrix, [sums[15 + row_id] for row_id in range(5)])


def pick_params(params, ids):
    count = params.shape[1]
    owners = lax.broadcasted_iota(jnp.int32, (count, 1), 0)

    def pick_single(carry, block_ids):
        hit = (block_ids[None, :] == owners).astype(jnp.float32)
        return (
            carry,
            jnp.dot(
                params, hit, precision=lax.Precision.HIGHEST, preferred_element_type=jnp.float32
            ),
        )

    unused, picked = lax.scan(pick_single, 0, ids)
    return jnp.moveaxis(picked, 1, 0)


def spd_solve(matrix, right_side):
    eye = jnp.eye(matrix.shape[-1], dtype=jnp.float32)
    lower = jnp.linalg.cholesky(matrix + eye)
    middle = lax.linalg.triangular_solve(lower, right_side[..., None], left_side=True, lower=True)
    result = lax.linalg.triangular_solve(
        lower, middle, left_side=True, lower=True, transpose_a=True
    )
    return result[..., 0]


def block_normals(terms, knot_base, weighted, resid):
    blocks, slots = knot_base.shape
    spread = jnp.moveaxis(terms.reshape(4, 4, blocks, slots), 2, 0)

    def block_single(item):
        part, base, weights, values = item
        grid = lax.broadcasted_iota(jnp.int32, (KNOTS_DEV, slots), 0)
        design = jnp.zeros((KNOTS_DEV, 4, slots), jnp.float32)
        for knot_step in range(4):
            hit = (grid == base[None, :] + knot_step).astype(jnp.float32)
            design = design + hit[:, None, :] * part[knot_step][None, :, :]
        design = design.reshape(KNOTS_DEV * 4, slots)
        normal = lax.dot_general(
            design * weights[None, :],
            design,
            (((1,), (1,)), ((), ())),
            precision=lax.Precision.HIGHEST,
            preferred_element_type=jnp.float32,
        )
        right = jnp.dot(
            design,
            weights * values,
            precision=lax.Precision.HIGHEST,
            preferred_element_type=jnp.float32,
        )
        return (normal, right)

    return lax.map(block_single, (spread, knot_base, weighted, resid))


def plain_body(
    observed,
    weight_obs,
    present,
    source_partials,
    attitude_partials,
    phase,
    knot_base,
    source_id,
    cal_id,
    attitude,
    calibration,
):
    weighted = present.astype(jnp.float32) * weight_obs
    terms = spline_terms(phase, attitude_partials)
    flat_cal = cal_id.reshape(-1)
    local = attitude
    cal_now = calibration
    params = jnp.zeros((5, SRC_DEV), jnp.float32)
    for sweep in range(2):
        target = observed - attitude_model(local, terms, knot_base) - cal_now[cal_id]
        params = source_solve(source_id, SRC_DEV, weighted, source_partials, target)
        resid = target - jnp.sum(source_partials * pick_params(params, source_id), axis=0)
        normals, rights = block_normals(terms, knot_base, weighted, resid)
        normal, right = (
            lax.psum_scatter(normals, "tm", scatter_dimension=0, tiled=True),
            lax.psum_scatter(rights, "tm", scatter_dimension=0, tiled=True),
        )
        normal, right = lax.psum((normal[0], right[0]), "src")
        local = local + spd_solve(normal, right)
        numer = jax.ops.segment_sum((weighted * resid).reshape(-1), flat_cal, num_segments=CAL)
        denom = jax.ops.segment_sum(weighted.reshape(-1), flat_cal, num_segments=CAL)
        numer, denom = lax.psum((numer, denom), ("src", "tm"))
        cal_now = cal_now + numer / (denom + 1.0)
    final = observed - attitude_model(local, terms, knot_base) - cal_now[cal_id]
    final = final - jnp.sum(source_partials * pick_params(params, source_id), axis=0)
    return (params, local, cal_now, final)


BAND = 16
PIECE = 2


def begin(pairs, sems):
    copies = [
        pltpu.make_async_copy(origin, held, sems.at[place])
        for place, (origin, held) in enumerate(pairs)
    ]
    for copy in copies:
        copy.start()
    return copies


def finish(copies):
    for copy in copies:
        copy.wait()


def tile_of(value):
    return jnp.concatenate(
        [value[:, at : at + LANES] for at in range(0, value.shape[1], LANES)], axis=0
    )


def pick_from(table_t, ids, units, rows):
    found = dot(jnp.concatenate(split3(table_t)[:2], axis=0), units)
    found = found[:LANES] + found[LANES:]
    hit = iota(found.shape, 0) == ids % LANES
    return unflat(jnp.sum(jnp.where(hit, found, 0.0), axis=0, keepdims=True), rows)


def two_parts(line):
    first = line.astype(BF16).astype(F32)
    return first, (line - first).astype(BF16).astype(F32)


def model_of(line, parts):
    first, second = two_parts(line)
    left = jnp.concatenate([first, first], axis=1)
    right = jnp.concatenate([second, jnp.zeros_like(second)], axis=1)
    row = iota((SUB, 2 * WIDTH), 0)
    both = jnp.where(row == 0, left, jnp.where(row == 1, right, 0.0)).astype(BF16)
    return jnp.sum(dot(both, parts), axis=0, keepdims=True)


def side_of(values, parts):
    first, second = two_parts(values)
    row = iota((SUB, values.shape[1]), 0)
    both = jnp.where(row == 0, first, jnp.where(row == 1, second, 0.0)).astype(BF16)
    found = dot_t(both, parts)
    return found[0:1, :WIDTH] + found[1:2, :WIDTH] + found[0:1, WIDTH:]


def normals_kernel(
    weight_in, present_in, attitude_in, phase_in, knot_in, cal_in, start_in,
    send_out, design_out, weighted_out, cal_id,
    weight_obs, present, attitude_partials, phase, knot_base, start, stacked, sems,
):
    copies = begin(
        [
            (weight_in, weight_obs), (present_in, present), (cal_in, cal_id), (start_in, start),
            (phase_in, phase), (knot_in, knot_base), (attitude_in, attitude_partials),
        ],
        sems,
    )
    finish(copies[:4])
    rows = weight_obs.shape[0]
    weighted = present[...].astype(F32) * weight_obs[...]
    weighted_out[...] = weighted
    first, second = tile_of(cal_id[...].astype(F32)), tile_of(weighted)
    devices = send_out.shape[0]
    for device in range(devices):
        core = core_of(device, rows)
        for index in range(rows):
            at = rows * core + index
            send_out[device, PIECE + index] = first[at : at + 1]
            send_out[device, PIECE + rows + index] = second[at : at + 1]
        send_out[device, PIECE + 2 * rows] = start[...]
    finish(copies[4:])
    u = phase[...]
    other = 1.0 - u
    square = u * u
    cube = square * u
    basis = [
        other * other * other / 6.0,
        (3.0 * cube - 6.0 * square + 4.0) / 6.0,
        (-3.0 * cube + 3.0 * square + 3.0 * u + 1.0) / 6.0,
        cube / 6.0,
    ]
    for row in range(rows):
        at = slice(row, row + 1)
        for channel in range(4):
            lines = attitude_partials[channel, at]
            stacked[row, channel : channel + 1] = lines
            stacked[row, channel + 4 : channel + 5] = lines
        design = design_of(knot_base[at], [part[at] for part in basis], stacked[row])
        design_out[row] = design
        band = pack_band(exact_dot_t(design * weighted[at], design))
        half, place = divmod(row, rows // PIECE)
        for index in range(BAND):
            send_out[place * BAND + index, half] = band[index : index + 1]


def sources_kernel(
    cal_id, weighted, design, observed_in, source_in, id_in, calibration_in,
    partials_out, factor_out, target_out, table_out, hits_out, units_out, parts_out, observed,
    source_partials, source_id, table, sems,
):
    copies = begin(
        [
            (observed_in, observed), (source_in, source_partials), (id_in, source_id),
            (calibration_in, table),
        ],
        sems,
    )
    finish(copies)
    rows, slots = observed.shape
    matrix = jnp.zeros((40, SRC_DEV), F32)
    for row in range(rows):
        at = slice(row, row + 1)
        for index in range(5):
            partials_out[row, index : index + 1] = source_partials[index, at]
        partials_out[row, 5:] = jnp.zeros((SUB - 5, slots), F32)
        partials = partials_out[row]
        products = jnp.concatenate(
            [partials * (weighted[at] * partials[index : index + 1]) for index in range(5)], axis=0
        )
        hits_out[row] = one_hot(source_id[at], SRC_DEV)
        found = dot_t(jnp.concatenate(split3(products), axis=0), hits_out[row])
        matrix = matrix + found[:40] + found[40:80] + found[80:]
        first, second, unused = split3(design[row])
        parts_out[row, :WIDTH] = first
        parts_out[row, WIDTH:] = second
    ids = flat(cal_id[...])
    units_out[...] = one_hot(ids // LANES, HIGH)
    inverse = small_factor(matrix)
    for place, pair in enumerate(PLACES):
        factor_out[place : place + 1] = inverse[pair]
    factor_out[15:16] = jnp.zeros((1, SRC_DEV), F32)
    table_t = table[...].T
    table_out[...] = table_t
    for row, picked in enumerate(pick_from(table_t, ids, units_out[...], rows)):
        target_out[row : row + 1] = observed[row : row + 1] - picked


def core_of(device, line):
    return device // line % 2


def residual_step(targets, parts, partials, factor, weighted, hits, send_out):
    rows = len(targets)
    inverse = {pair: factor[place : place + 1] for place, pair in enumerate(PLACES)}
    sides = jnp.zeros((SUB, SRC_DEV), F32)
    for row in range(rows):
        products = partials[row] * (weighted[row : row + 1] * targets[row])
        found = dot_t(jnp.concatenate(split3(products), axis=0), hits[row])
        sides = sides + found[:SUB] + found[SUB : 2 * SUB] + found[2 * SUB :]
    params = small_apply(inverse, [sides[index : index + 1] for index in range(5)])
    table = jnp.concatenate(params + [jnp.zeros((3, SRC_DEV), F32)], axis=0)
    split = jnp.concatenate(split3(table), axis=0)
    explained, scaled, rights = [], [], []
    for row in range(rows):
        found = dot(split, hits[row])
        found = found[:SUB] + found[SUB : 2 * SUB] + found[2 * SUB :]
        explained.append(jnp.sum(found * partials[row], axis=0, keepdims=True))
    for row in range(rows):
        scaled.append(weighted[row : row + 1] * (targets[row] - explained[row]))
        rights.append(side_of(scaled[row], parts[row]))
    half = rows // PIECE
    for device in range(send_out.shape[0]):
        core = core_of(device, rows)
        lines = [line[:, core * LANES : (core + 1) * LANES] for line in scaled]
        for index, line in enumerate(lines + rights[half * core : half * core + half]):
            send_out[device, index] = line
    return params, explained


def first_kernel(received, target, parts, partials, factor, weighted, hits, send_out):
    rows = parts.shape[0]
    last = received.shape[1] - 1
    targets = [
        target[row : row + 1] - model_of(received[row, last], parts[row]) for row in range(rows)
    ]
    residual_step(targets, parts, partials, factor, weighted, hits, send_out)
    totals = [right_side(received, place) for place in range(PIECE)]
    for device in range(send_out.shape[0]):
        send_out[device, send_out.shape[1] - 1] = totals[core_of(device, rows)]


def spread(line):
    return jnp.broadcast_to(line, (SUB, LANES))


def wide(tile, count):
    tile = jnp.concatenate([tile, tile], axis=0).astype(BF16)
    return jnp.concatenate([tile] * (count // 16), axis=0)


def unit_sums(received, value_of, total):
    rows = (received.shape[1] - PIECE - 1) // 2
    low_row = iota((LANES, LANES), 0).astype(F32).astype(BF16)
    high_row = iota((HIGH, LANES), 0).astype(F32).astype(BF16)
    one, none = jnp.ones((), BF16), jnp.zeros((), BF16)
    for begin in range(0, received.shape[0], 4):
        lefts, rights = [], []
        for device in range(begin, begin + 4):
            for index in range(rows):
                unit = spread(received[device, PIECE + index])
                high = jnp.floor(unit * (1.0 / LANES))
                hit = low_row == wide(unit - LANES * high, LANES)
                value = spread(value_of(device, index))
                first = value.astype(BF16).astype(F32)
                lefts.append(
                    jnp.concatenate(
                        [
                            jnp.where(hit, wide(first, LANES), none),
                            jnp.where(hit, wide(value - first, LANES), none),
                        ],
                        axis=0,
                    )
                )
                rights.append(jnp.where(high_row == wide(high, HIGH), one, none))
        found = dot_t(jnp.concatenate(lefts, axis=1), jnp.concatenate(rights, axis=1))
        if begin == 0:
            total[:LANES] = found[:LANES] + found[LANES:]
        else:
            total[:LANES] += found[:LANES] + found[LANES:]
        yield


def matrix_of(band):
    lower = unpack_band(band)
    diagonal = iota(lower.shape, 0) == iota(lower.shape, 1)
    return lower + jnp.where(diagonal, 1.0, lower.T)


def together(works):
    works = list(works)
    while works:
        for work in list(works):
            if next(work, works) is works:
                works.remove(work)


def weights_kernel(received, sums_out):
    rows = (received.shape[1] - PIECE - 1) // 2
    together(
        [
            unit_sums(
                received, lambda device, index: received[device, PIECE + rows + index], sums_out
            )
        ]
    )


def right_side(values, place):
    total = values[0, place]
    for device in range(1, values.shape[0]):
        total = total + values[device, place]
    return total


def core(axis):
    return lax.rem(lax.axis_index(axis), 2)


def coefficients(bundle, place):
    return bundle[LANES + place : LANES + place + 1, :WIDTH]


def put(bundle, place, line):
    bundle[LANES + place : LANES + place + 1] = jnp.concatenate([line, line], axis=1)


def solve_kernel(axis, values, received, bundle_out, lines_out, bands, states, entries):
    half = lines_out.shape[0]
    rows = values.shape[1] - half - 1
    for device in range(values.shape[0]):
        bands[device : device + 1] = values[device, rows + half]
    bundle_out[LANES:] = jnp.zeros((SUB, HIGH), F32)

    def attitude(place):
        states[place] = matrix_of(bands[BAND * place : BAND * (place + 1)])
        change = yield from eliminate(
            states.at[place],
            entries.at[place],
            right_side(values, rows + place),
            lines_out.at[place],
        )
        start = received[half * core(axis) + place, received.shape[1] - 1]
        put(bundle_out, place, start + change)
        yield

    together(
        [unit_sums(received, lambda device, index: values[device, index], bundle_out)]
        + [attitude(place) for place in range(half)]
    )


def both_halves(axis, own, other, half):
    first = core(axis) == 0
    pairs = [(coefficients(own, place), coefficients(other, place)) for place in range(half)]
    lines = [jnp.where(first, one, two) for one, two in pairs]
    return lines + [jnp.where(first, two, one) for one, two in pairs]


def second_kernel(
    axis, bundle, other, weights, other_weights, table, ids, units, observed, parts, partials, factor,
    weighted, hits,
    send_out, params_out, explained_out, table_out, scale_out,
):
    rows = parts.shape[0]
    scale = 1.0 / (weights[...] + other_weights[...] + 1.0)
    scale_out[...] = scale
    table_t = table[...] + (bundle[:LANES] + other[:LANES]) * scale
    table_out[...] = table_t
    picked = pick_from(table_t, flat(ids[...]), units[...], rows)
    lines = both_halves(axis, bundle, other, rows // PIECE)
    targets = [
        observed[row : row + 1] - model_of(lines[row], parts[row]) - picked[row]
        for row in range(rows)
    ]
    params, explained = residual_step(targets, parts, partials, factor, weighted, hits, send_out)
    for index in range(5):
        params_out[index : index + 1] = params[index]
    for row in range(rows):
        explained_out[row : row + 1] = explained[row]


def last_kernel(values, received, bundle, lines, bundle_out):
    half = lines.shape[0]
    rows = values.shape[1] - half
    bundle_out[LANES:] = jnp.zeros((SUB, HIGH), F32)

    def solve(place):
        change = yield from substitute(right_side(values, rows + place), lines.at[place])
        put(bundle_out, place, coefficients(bundle, place) + change)
        yield

    together(
        [unit_sums(received, lambda device, index: values[device, index], bundle_out)]
        + [solve(place) for place in range(half)]
    )


def final_kernel(
    axis, line, bundle, other, table, scale, ids, units, observed, parts, explained,
    cal_out, attitude_out, resid_out,
):
    rows = parts.shape[0]
    table_t = table[...] + (bundle[:LANES] + other[:LANES]) * scale[...]
    cal_out[...] = table_t.T
    picked = pick_from(table_t, flat(ids[...]), units[...], rows)
    me = lax.axis_index(line)
    lines = both_halves(axis, bundle, other, rows // PIECE)
    own = lines[0]
    for row in range(rows):
        own = jnp.where(me == row, lines[row], own)
        at = slice(row, row + 1)
        resid_out[at] = observed[at] - model_of(lines[row], parts[row]) - picked[row] - explained[at]
    attitude_out[...] = own


VMEM = pl.BlockSpec(memory_space=pltpu.VMEM)
ANY = pl.BlockSpec(memory_space=pltpu.HBM)


def call(kernel, outs, *args, away=0, scratch=()):
    near = args[: len(args) - away]
    far = [pltpu.with_memory_space_constraint(arg, pltpu.HBM) for arg in args[len(args) - away :]]
    return pl.pallas_call(
        kernel,
        out_shape=outs,
        in_specs=[VMEM] * len(near) + [ANY] * away,
        out_specs=[VMEM] * len(outs),
        scratch_shapes=scratch,
        compiler_params=pltpu.CompilerParams(vmem_limit_bytes=VMEM_BYTES),
    )(*near, *far)


def stay(*shape, dtype=F32):
    return pltpu.VMEM(shape, dtype)


def leave(*shape):
    return jax.ShapeDtypeStruct(shape, F32)


def swap(value):
    return lax.ppermute(value, "src", [(at, at ^ 1) for at in range(lax.axis_size("src"))])


def exchange(value):
    return lax.all_to_all(value, ("src", "tm"), 0, 0, tiled=True)


def body(
    observed, weight_obs, present, source_partials, attitude_partials, phase, knot_base, source_id,
    cal_id, attitude, calibration,
):
    rows, slots = observed.shape
    devices = lax.axis_size("src") * lax.axis_size("tm")
    half = rows // PIECE
    first_q = attitude.reshape(1, WIDTH)
    held = [weight_obs, present, attitude_partials, phase, knot_base, first_q]
    received, design, weighted, units_seen = call(
        normals_kernel,
        [
            stay(devices, PIECE + 2 * rows + 1, 1, LANES), stay(rows, WIDTH, slots),
            stay(rows, slots), stay(rows, slots, dtype=jnp.int32),
        ],
        weight_obs, present, attitude_partials, phase, knot_base, cal_id, first_q,
        away=7,
        scratch=[pltpu.VMEM(each.shape, each.dtype) for each in held]
        + [pltpu.VMEM((rows, SUB, slots), F32), pltpu.SemaphoreType.DMA((7,))],
    )
    received = exchange(received)
    cal_id = units_seen
    partials, factor, target, table, hits, units, parts, seen = call(
        sources_kernel,
        [
            stay(rows, SUB, slots), stay(16, SRC_DEV), stay(rows, slots), stay(LANES, HIGH),
            stay(rows, SRC_DEV, slots, dtype=BF16), stay(HIGH, rows * slots, dtype=BF16),
            stay(rows, 2 * WIDTH, slots, dtype=BF16), stay(rows, slots),
        ],
        cal_id, weighted, design, observed, source_partials, source_id,
        calibration.reshape(HIGH, LANES),
        away=4,
        scratch=[
            pltpu.VMEM(source_partials.shape, F32), pltpu.VMEM((rows, slots), jnp.int32),
            pltpu.VMEM((HIGH, LANES), F32), pltpu.SemaphoreType.DMA((4,)),
        ],
    )
    received, factor = lax.optimization_barrier((received, factor))
    (values,) = call(
        first_kernel, [stay(devices, rows + half + 1, 1, LANES)],
        received, target, parts, partials, factor, weighted, hits,
    )
    values, received = lax.optimization_barrier((values, received))
    values = exchange(values)
    (weights,) = call(weights_kernel, [leave(LANES, HIGH)], received)
    other_weights, received = lax.optimization_barrier((swap(weights), received))
    bundle, lines = call(
        functools.partial(solve_kernel, "src"),
        [leave(LANES + SUB, HIGH), stay(half, WIDTH, WIDTH)],
        values, received,
        scratch=[
            pltpu.VMEM((half * BAND, WIDTH), F32), pltpu.VMEM((half, WIDTH, WIDTH), F32),
            pltpu.VMEM((half, len(PLAN[0]), 4, 8, WIDTH), F32),
        ],
    )
    values, params, explained, table, scale = call(
        functools.partial(second_kernel, "src"),
        [
            leave(devices, rows + half, 1, LANES), leave(5, SRC_DEV), stay(rows, slots),
            stay(LANES, HIGH), stay(LANES, HIGH),
        ],
        bundle, swap(bundle), weights, other_weights, table, cal_id, units, seen, parts, partials,
        factor, weighted, hits,
    )
    values = exchange(values)
    (bundle,) = call(
        last_kernel, [leave(LANES + SUB, HIGH)], values, received, bundle, lines
    )
    cal, now, final = call(
        functools.partial(final_kernel, "src", "tm"),
        [leave(HIGH, LANES), leave(1, WIDTH), leave(rows, slots)],
        bundle, swap(bundle), table, scale, cal_id, units, seen, parts, explained,
    )
    return (params, now.reshape(WIDTH), cal.reshape(CAL), final)


def solution(mesh):
    many = mesh.shape["src"] * mesh.shape["tm"]
    return jax.shard_map(
        body if many * PIECE == mesh.shape["tm"] * BAND else plain_body,
        mesh=mesh,
        in_specs=(
            P(None, ("src", "tm")),
            P(None, ("src", "tm")),
            P(None, ("src", "tm")),
            P(None, None, ("src", "tm")),
            P(None, None, ("src", "tm")),
            P(None, ("src", "tm")),
            P(None, ("src", "tm")),
            P(None, ("src", "tm")),
            P(None, ("src", "tm")),
            P("tm"),
            P(),
        ),
        out_specs=(P(None, ("src", "tm")), P("tm"), P(), P(None, ("src", "tm"))),
        check_vma=False,
    )
```

```python
import functools

import jax
import jax.numpy as jnp
from jax import lax
from jax.experimental import pallas as pl
from jax.experimental.pallas import tpu as pltpu
from jax.sharding import PartitionSpec as P

KNOTS_DEV = 32
WIDTH = 4 * KNOTS_DEV
SRC_DEV = 128
CAL = 32768
LANES = 128
HIGH = CAL // LANES
SUB = 8
VMEM_BYTES = 48 * 1024 * 1024

F32 = jnp.float32
BF16 = jnp.bfloat16
EXACT = lax.Precision.HIGHEST


def iota(shape, dim):
    return lax.broadcasted_iota(jnp.int32, shape, dim)


def split3(value):
    first = value.astype(BF16)
    rest = value - first.astype(F32)
    second = rest.astype(BF16)
    third = (rest - second.astype(F32)).astype(BF16)
    return first, second, third


def dot(left, right):
    return lax.dot_general(left, right, (((1,), (0,)), ((), ())), preferred_element_type=F32)


def dot_t(left, right):
    return lax.dot_general(left, right, (((1,), (1,)), ((), ())), preferred_element_type=F32)


def exact_dot(left, right):
    return lax.dot_general(
        left, right, (((1,), (0,)), ((), ())), precision=EXACT, preferred_element_type=F32
    )


def exact_dot_t(left, right):
    return lax.dot_general(
        left, right, (((1,), (1,)), ((), ())), precision=EXACT, preferred_element_type=F32
    )


def one_hot(ids, count):
    return jnp.where(iota((count, ids.shape[1]), 0) == ids, 1.0, 0.0).astype(BF16)


def flat(value):
    return jnp.concatenate([value[row : row + 1] for row in range(value.shape[0])], axis=1)


def unflat(value, rows):
    slots = value.shape[1] // rows
    return [value[:, row * slots : (row + 1) * slots] for row in range(rows)]


def cal_pick(table, ids):
    parts = jnp.concatenate(split3(table.T), axis=0)
    high = ids // LANES
    low = ids % LANES
    found = dot(parts, one_hot(high, HIGH))
    found = found[:LANES] + found[LANES : 2 * LANES] + found[2 * LANES :]
    return jnp.sum(jnp.where(iota(found.shape, 0) == low, found, 0.0), axis=0, keepdims=True)


def cal_sums(values, ids):
    high = one_hot(ids // LANES, HIGH)
    low = iota((LANES, ids.shape[1]), 0) == ids % LANES
    total = None
    for part in split3(values):
        spread = jnp.where(low, part.astype(F32), 0.0).astype(BF16)
        added = dot_t(high, spread)
        total = added if total is None else total + added
    return total


def design_of(base, basis, partials):
    slots = base.shape[1]
    knot = iota((WIDTH, slots), 0) // 4
    step = knot - base
    spread = jnp.zeros((WIDTH, slots), F32)
    for index in range(4):
        spread = jnp.where(step == index, basis[index], spread)
    return spread * jnp.concatenate([partials] * (WIDTH // 8), axis=0)


def band_shift(tile, knot):
    return ((tile % 8) * 16 - (8 * tile + 4 * knot - 12)) % WIDTH


def pack_band(normal):
    place = iota((8, WIDTH), 1) // 16
    upper = iota((8, WIDTH), 0) < 4
    groups = []
    for group in range(2):
        packed = jnp.zeros((8, WIDTH), F32)
        for tile in range(8 * group, 8 * group + 8):
            rows = normal[8 * tile : 8 * tile + 8]
            rolled = jnp.where(
                upper,
                pltpu.roll(rows, band_shift(tile, 0), 1),
                pltpu.roll(rows, band_shift(tile, 1), 1),
            )
            packed = jnp.where(place == tile % 8, rolled, packed)
        groups.append(packed)
    return jnp.concatenate(groups, axis=0)


def unpack_band(packed):
    place = iota((8, WIDTH), 1) // 16
    upper = iota((8, WIDTH), 0) < 4
    tiles = []
    for tile in range(16):
        group = tile // 8
        rows = jnp.where(place == tile % 8, packed[8 * group : 8 * group + 8], 0.0)
        tiles.append(
            jnp.where(
                upper,
                pltpu.roll(rows, (-band_shift(tile, 0)) % WIDTH, 1),
                pltpu.roll(rows, (-band_shift(tile, 1)) % WIDTH, 1),
            )
        )
    full = jnp.concatenate(tiles, axis=0)
    return jnp.where(iota(full.shape, 0) >= iota(full.shape, 1), full, 0.0)


ORDER = (
    (0, 8, 17, 31), (1, 9, 18, 30), (2, 10, 19, 29), (3, 11, 20, 28), (4, 12, 21, 27), (13, 22, 26),
    (5, 23), (6, 24), (7, 25), (14,), (15,), (16,),
)


def plan_of(order):
    near = {
        knot: {other for other in range(KNOTS_DEV) if 0 < abs(other - knot) <= 3}
        for knot in range(KNOTS_DEV)
    }
    plan = []
    for step in order:
        plan.append([(knot, sorted({other // 2 for other in near[knot]})) for knot in step])
        for knot in step:
            assert not near[knot] & set(step)
            for other in near[knot]:
                near[other] = (near[other] | near[knot]) - {other, knot}
    return plan


PLAN = plan_of(ORDER)


def block_rows(entry, lines):
    scale = 1.0 / (entry[0, 0] * entry[1, 1] - entry[0, 1] * entry[0, 1])
    low, mid, high = entry[0, 0] * scale, entry[0, 1] * scale, entry[1, 1] * scale
    turned = {}
    for column in (2, 3):
        turned[0, column] = high * entry[0, column] - mid * entry[1, column]
        turned[1, column] = low * entry[1, column] - mid * entry[0, column]
    rest = {}
    for row, column in ((2, 2), (2, 3), (3, 3)):
        taken = entry[0, row] * turned[0, column] + entry[1, row] * turned[1, column]
        rest[row, column] = entry[row, column] - taken
    upper = [high * lines[0] - mid * lines[1], low * lines[1] - mid * lines[0]]
    lower = [
        lines[row] - (entry[0, row] * upper[0] + entry[1, row] * upper[1]) for row in (2, 3)
    ]
    scale = 1.0 / (rest[2, 2] * rest[3, 3] - rest[2, 3] * rest[2, 3])
    third = (rest[3, 3] * scale) * lower[0] - (rest[2, 3] * scale) * lower[1]
    fourth = (rest[2, 2] * scale) * lower[1] - (rest[2, 3] * scale) * lower[0]
    return [
        upper[0] - (turned[0, 2] * third + turned[0, 3] * fourth),
        upper[1] - (turned[1, 2] * third + turned[1, 3] * fourth),
        third,
        fourth,
    ]


def eliminate(state, entries, right, lines_out):
    shape = (8, WIDTH)
    lane = iota(shape, 1)
    for step in PLAN:
        works = []
        for slot, (knot, reach) in enumerate(step):
            at, sub, first = knot // 2, 4 * (knot % 2), 4 * knot
            inside = lane // 4 == knot
            columns = {}
            for tile in sorted({at, *reach}):
                held = state[8 * tile : 8 * tile + 8]
                columns[tile] = [
                    jnp.broadcast_to(held[:, first + index : first + index + 1], shape)
                    for index in range(4)
                ]
            for index in range(4):
                entries[slot, index] = columns[at][index]
            entry = {
                (one, two): jnp.broadcast_to(entries[slot, two, sub + one : sub + one + 1], shape)
                for one in range(4)
                for two in range(one, 4)
            }
            lines = [
                jnp.where(
                    inside,
                    jnp.where(lane == first + index, -1.0, 0.0),
                    jnp.broadcast_to(state[first + index : first + index + 1], shape),
                )
                for index in range(4)
            ]
            works.append((knot, reach, inside, columns, block_rows(entry, lines)))
        border = right
        for knot, reach, inside, columns, lines in works:
            for index in range(4):
                lines_out[4 * knot + index : 4 * knot + index + 1] = lines[index][0:1]
            for tile in reach:
                factors = columns[tile]
                taken = factors[0] * lines[0] + factors[1] * lines[1]
                taken = taken + (factors[2] * lines[2] + factors[3] * lines[3])
                rows = slice(8 * tile, 8 * tile + 8)
                state[rows] = jnp.where(inside, 0.0, state[rows]) - taken
            right = swept(right, border, knot, [line[0:1] for line in lines])
        yield
    return right


def swept(right, border, knot, lines):
    first = 4 * knot
    right = jnp.where(iota(right.shape, 1) // 4 == knot, 0.0, right)
    factors = [border[:, first + index : first + index + 1] for index in range(4)]
    taken = factors[0] * lines[0] + factors[1] * lines[1]
    return right - (taken + (factors[2] * lines[2] + factors[3] * lines[3]))


def substitute(right, lines):
    for step in PLAN:
        border = right
        for knot, unused in step:
            kept = [lines[4 * knot + index : 4 * knot + index + 1] for index in range(4)]
            right = swept(right, border, knot, kept)
        yield
    return right


def small_factor(sums):
    factor = {}
    for member in range(5):
        for column in range(member + 1):
            running = sums[8 * member + column : 8 * member + column + 1]
            if member == column:
                running = running + 1.0
            for offset in range(column):
                running = running - factor[member, offset] * factor[column, offset]
            if member == column:
                factor[member, member] = jnp.sqrt(running)
            else:
                factor[member, column] = running * inverse_of[column]
        inverse_of = {} if member == 0 else inverse_of
        inverse_of[member] = 1.0 / factor[member, member]
    inverse = {}
    for column in range(5):
        inverse[column, column] = inverse_of[column]
        for member in range(column + 1, 5):
            running = factor[member, column] * inverse[column, column]
            for offset in range(column + 1, member):
                running = running + factor[member, offset] * inverse[offset, column]
            inverse[member, column] = -running * inverse_of[member]
    return inverse


PLACES = [(row_id, col_id) for row_id in range(5) for col_id in range(row_id + 1)]


def small_apply(inverse, sides):
    forward = []
    for member in range(5):
        running = inverse[member, 0] * sides[0]
        for column in range(1, member + 1):
            running = running + inverse[member, column] * sides[column]
        forward.append(running)
    result = []
    for column in range(5):
        running = inverse[column, column] * forward[column]
        for member in range(column + 1, 5):
            running = running + inverse[member, column] * forward[member]
        result.append(running)
    return result


PAIRS = [(row_id, col_id) for row_id in range(5) for col_id in range(row_id + 1)]


def spline_terms(phase, attitude_partials):
    other = 1.0 - phase
    square = phase * phase
    cube = square * phase
    basis = [
        other * other * other / 6.0,
        (3.0 * cube - 6.0 * square + 4.0) / 6.0,
        (-3.0 * cube + 3.0 * square + 3.0 * phase + 1.0) / 6.0,
        cube / 6.0,
    ]
    return jnp.stack(
        [
            basis[knot_step] * attitude_partials[channel]
            for knot_step in range(4)
            for channel in range(4)
        ]
    )


def attitude_model(local, terms, knot_base):
    coefficients = lax.all_gather(local, "tm", axis=0, tiled=True)
    blocks, slots = knot_base.shape
    table = coefficients.reshape(blocks, -1, 4)
    knots_count = table.shape[1]
    grid = lax.broadcasted_iota(jnp.int32, (1, knots_count, 1), 1)
    running = jnp.zeros(knot_base.shape, jnp.float32)
    for knot_step in range(4):
        hit = (grid == (knot_base + knot_step)[:, None, :]).astype(jnp.float32)
        picked = jnp.einsum(
            "bkc,bks->bcs",
            table,
            hit,
            precision=lax.Precision.HIGHEST,
            preferred_element_type=jnp.float32,
        )
        for channel in range(4):
            running = running + terms[4 * knot_step + channel] * picked[:, channel, :]
    return running


def small_solve(matrix, right_side):
    extent = len(right_side)
    factor = {}
    for member in range(extent):
        for column in range(member + 1):
            running = matrix[member][column]
            for offset in range(column):
                running = running - factor[member, offset] * factor[column, offset]
            if member == column:
                factor[member, member] = jnp.sqrt(running)
            else:
                factor[member, column] = running / factor[column, column]
    forward = []
    for member in range(extent):
        running = right_side[member]
        for offset in range(member):
            running = running - factor[member, offset] * forward[offset]
        forward.append(running / factor[member, member])
    result = [None] * extent
    for member in reversed(range(extent)):
        running = forward[member]
        for offset in range(member + 1, extent):
            running = running - factor[offset, member] * result[offset]
        result[member] = running / factor[member, member]
    return jnp.stack(result)


def source_solve(ids, count, weighted, source_partials, target):
    products = [
        weighted * source_partials[row_id] * source_partials[col_id] for row_id, col_id in PAIRS
    ]
    products = products + [weighted * source_partials[row_id] * target for row_id in range(5)]
    stacked = jnp.moveaxis(jnp.stack(products), 1, 0)
    owners = lax.broadcasted_iota(jnp.int32, (count, 1), 0)

    def accumulate(total, item):
        values, block_ids = item
        hit = (block_ids[None, :] == owners).astype(jnp.float32)
        added = lax.dot_general(
            values,
            hit,
            (((1,), (1,)), ((), ())),
            precision=lax.Precision.HIGHEST,
            preferred_element_type=jnp.float32,
        )
        return (total + added, None)

    sums, unused = lax.scan(
        accumulate, jnp.zeros((len(products), count), jnp.float32), (stacked, ids)
    )
    entries = {}
    for position, pair in enumerate(PAIRS):
        entry_value = sums[position] + (1.0 if pair[0] == pair[1] else 0.0)
        entries[pair[0], pair[1]] = entry_value
        entries[pair[1], pair[0]] = entry_value
    matrix = [[entries[row_id, col_id] for col_id in range(5)] for row_id in range(5)]
    return small_solve(matrix, [sums[15 + row_id] for row_id in range(5)])


def pick_params(params, ids):
    count = params.shape[1]
    owners = lax.broadcasted_iota(jnp.int32, (count, 1), 0)

    def pick_single(carry, block_ids):
        hit = (block_ids[None, :] == owners).astype(jnp.float32)
        return (
            carry,
            jnp.dot(
                params, hit, precision=lax.Precision.HIGHEST, preferred_element_type=jnp.float32
            ),
        )

    unused, picked = lax.scan(pick_single, 0, ids)
    return jnp.moveaxis(picked, 1, 0)


def spd_solve(matrix, right_side):
    eye = jnp.eye(matrix.shape[-1], dtype=jnp.float32)
    lower = jnp.linalg.cholesky(matrix + eye)
    middle = lax.linalg.triangular_solve(lower, right_side[..., None], left_side=True, lower=True)
    result = lax.linalg.triangular_solve(
        lower, middle, left_side=True, lower=True, transpose_a=True
    )
    return result[..., 0]


def block_normals(terms, knot_base, weighted, resid):
    blocks, slots = knot_base.shape
    spread = jnp.moveaxis(terms.reshape(4, 4, blocks, slots), 2, 0)

    def block_single(item):
        part, base, weights, values = item
        grid = lax.broadcasted_iota(jnp.int32, (KNOTS_DEV, slots), 0)
        design = jnp.zeros((KNOTS_DEV, 4, slots), jnp.float32)
        for knot_step in range(4):
            hit = (grid == base[None, :] + knot_step).astype(jnp.float32)
            design = design + hit[:, None, :] * part[knot_step][None, :, :]
        design = design.reshape(KNOTS_DEV * 4, slots)
        normal = lax.dot_general(
            design * weights[None, :],
            design,
            (((1,), (1,)), ((), ())),
            precision=lax.Precision.HIGHEST,
            preferred_element_type=jnp.float32,
        )
        right = jnp.dot(
            design,
            weights * values,
            precision=lax.Precision.HIGHEST,
            preferred_element_type=jnp.float32,
        )
        return (normal, right)

    return lax.map(block_single, (spread, knot_base, weighted, resid))


def plain_body(
    observed,
    weight_obs,
    present,
    source_partials,
    attitude_partials,
    phase,
    knot_base,
    source_id,
    cal_id,
    attitude,
    calibration,
):
    weighted = present.astype(jnp.float32) * weight_obs
    terms = spline_terms(phase, attitude_partials)
    flat_cal = cal_id.reshape(-1)
    local = attitude
    cal_now = calibration
    params = jnp.zeros((5, SRC_DEV), jnp.float32)
    for sweep in range(2):
        target = observed - attitude_model(local, terms, knot_base) - cal_now[cal_id]
        params = source_solve(source_id, SRC_DEV, weighted, source_partials, target)
        resid = target - jnp.sum(source_partials * pick_params(params, source_id), axis=0)
        normals, rights = block_normals(terms, knot_base, weighted, resid)
        normal, right = (
            lax.psum_scatter(normals, "tm", scatter_dimension=0, tiled=True),
            lax.psum_scatter(rights, "tm", scatter_dimension=0, tiled=True),
        )
        normal, right = lax.psum((normal[0], right[0]), "src")
        local = local + spd_solve(normal, right)
        numer = jax.ops.segment_sum((weighted * resid).reshape(-1), flat_cal, num_segments=CAL)
        denom = jax.ops.segment_sum(weighted.reshape(-1), flat_cal, num_segments=CAL)
        numer, denom = lax.psum((numer, denom), ("src", "tm"))
        cal_now = cal_now + numer / (denom + 1.0)
    final = observed - attitude_model(local, terms, knot_base) - cal_now[cal_id]
    final = final - jnp.sum(source_partials * pick_params(params, source_id), axis=0)
    return (params, local, cal_now, final)


BAND = 16
PIECE = 2


def begin(pairs, sems):
    copies = [
        pltpu.make_async_copy(origin, held, sems.at[place])
        for place, (origin, held) in enumerate(pairs)
    ]
    for copy in copies:
        copy.start()
    return copies


def finish(copies):
    for copy in copies:
        copy.wait()


def tile_of(value):
    return jnp.concatenate(
        [value[:, at : at + LANES] for at in range(0, value.shape[1], LANES)], axis=0
    )


def pick_from(table_t, ids, units, rows):
    found = dot(jnp.concatenate(split3(table_t)[:2], axis=0), units)
    found = found[:LANES] + found[LANES:]
    hit = iota(found.shape, 0) == ids % LANES
    return unflat(jnp.sum(jnp.where(hit, found, 0.0), axis=0, keepdims=True), rows)


def two_parts(line):
    first = line.astype(BF16).astype(F32)
    return first, (line - first).astype(BF16).astype(F32)


def model_of(line, parts):
    first, second = two_parts(line)
    left = jnp.concatenate([first, first], axis=1)
    right = jnp.concatenate([second, jnp.zeros_like(second)], axis=1)
    row = iota((SUB, 2 * WIDTH), 0)
    both = jnp.where(row == 0, left, jnp.where(row == 1, right, 0.0)).astype(BF16)
    return jnp.sum(dot(both, parts), axis=0, keepdims=True)


def side_of(values, parts):
    first, second = two_parts(values)
    row = iota((SUB, values.shape[1]), 0)
    both = jnp.where(row == 0, first, jnp.where(row == 1, second, 0.0)).astype(BF16)
    found = dot_t(both, parts)
    return found[0:1, :WIDTH] + found[1:2, :WIDTH] + found[0:1, WIDTH:]


def normals_kernel(
    weight_in, present_in, attitude_in, phase_in, knot_in, cal_in, start_in,
    send_out, parts_out, weighted_out, cal_id,
    weight_obs, present, attitude_partials, phase, knot_base, start, stacked, sems,
):
    copies = begin(
        [
            (weight_in, weight_obs), (present_in, present), (cal_in, cal_id), (start_in, start),
            (phase_in, phase), (knot_in, knot_base), (attitude_in, attitude_partials),
        ],
        sems,
    )
    finish(copies[:4])
    rows = weight_obs.shape[0]
    weighted = present[...].astype(F32) * weight_obs[...]
    weighted_out[...] = weighted
    first, second = tile_of(cal_id[...].astype(F32)), tile_of(weighted)
    devices = send_out.shape[0]
    for device in range(devices):
        core = core_of(device, rows)
        for index in range(rows):
            at = rows * core + index
            send_out[device, PIECE + index] = first[at : at + 1]
            send_out[device, PIECE + rows + index] = second[at : at + 1]
        send_out[device, PIECE + 2 * rows] = start[...]
    finish(copies[4:])
    u = phase[...]
    other = 1.0 - u
    square = u * u
    cube = square * u
    basis = [
        other * other * other / 6.0,
        (3.0 * cube - 6.0 * square + 4.0) / 6.0,
        (-3.0 * cube + 3.0 * square + 3.0 * u + 1.0) / 6.0,
        cube / 6.0,
    ]
    for row in range(rows):
        at = slice(row, row + 1)
        for channel in range(4):
            lines = attitude_partials[channel, at]
            stacked[row, channel : channel + 1] = lines
            stacked[row, channel + 4 : channel + 5] = lines
        design = design_of(knot_base[at], [part[at] for part in basis], stacked[row])
        one, two, three = split3(design)
        parts_out[row, :WIDTH] = one
        parts_out[row, WIDTH:] = two
        high, middle, low = split3(design * weighted[at])
        most = dot_t(jnp.concatenate([high, middle], axis=0), jnp.concatenate([one, two], axis=0))
        rest = dot_t(jnp.concatenate([high, low], axis=0), jnp.concatenate([three, one], axis=0))
        small = most[WIDTH:, WIDTH:] + (rest[:WIDTH, :WIDTH] + rest[WIDTH:, WIDTH:])
        small = small + (most[:WIDTH, WIDTH:] + most[WIDTH:, :WIDTH])
        band = pack_band(most[:WIDTH, :WIDTH] + small)
        half, place = divmod(row, rows // PIECE)
        for index in range(BAND):
            send_out[place * BAND + index, half] = band[index : index + 1]


def sources_kernel(
    cal_id, weighted, observed_in, source_in, id_in, calibration_in,
    partials_out, factor_out, target_out, table_out, hits_out, units_out, observed,
    source_partials, source_id, table, sems,
):
    copies = begin(
        [
            (observed_in, observed), (source_in, source_partials), (id_in, source_id),
            (calibration_in, table),
        ],
        sems,
    )
    finish(copies)
    rows, slots = observed.shape
    matrix = jnp.zeros((40, SRC_DEV), F32)
    for row in range(rows):
        at = slice(row, row + 1)
        for index in range(5):
            partials_out[row, index : index + 1] = source_partials[index, at]
        partials_out[row, 5:] = jnp.zeros((SUB - 5, slots), F32)
        partials = partials_out[row]
        products = jnp.concatenate(
            [partials * (weighted[at] * partials[index : index + 1]) for index in range(5)], axis=0
        )
        hits_out[row] = one_hot(source_id[at], SRC_DEV)
        found = dot_t(jnp.concatenate(split3(products), axis=0), hits_out[row])
        matrix = matrix + found[:40] + found[40:80] + found[80:]
    ids = flat(cal_id[...])
    units_out[...] = one_hot(ids // LANES, HIGH)
    inverse = small_factor(matrix)
    for place, pair in enumerate(PLACES):
        factor_out[place : place + 1] = inverse[pair]
    factor_out[15:16] = jnp.zeros((1, SRC_DEV), F32)
    table_t = table[...].T
    table_out[...] = table_t
    for row, picked in enumerate(pick_from(table_t, ids, units_out[...], rows)):
        target_out[row : row + 1] = observed[row : row + 1] - picked


def core_of(device, line):
    return device // line % 2


def residual_step(targets, parts, partials, factor, weighted, hits, send_out):
    rows = len(targets)
    inverse = {pair: factor[place : place + 1] for place, pair in enumerate(PLACES)}
    sides = jnp.zeros((SUB, SRC_DEV), F32)
    for row in range(rows):
        products = partials[row] * (weighted[row : row + 1] * targets[row])
        found = dot_t(jnp.concatenate(split3(products), axis=0), hits[row])
        sides = sides + found[:SUB] + found[SUB : 2 * SUB] + found[2 * SUB :]
    params = small_apply(inverse, [sides[index : index + 1] for index in range(5)])
    table = jnp.concatenate(params + [jnp.zeros((3, SRC_DEV), F32)], axis=0)
    split = jnp.concatenate(split3(table), axis=0)
    explained, scaled, rights = [], [], []
    for row in range(rows):
        found = dot(split, hits[row])
        found = found[:SUB] + found[SUB : 2 * SUB] + found[2 * SUB :]
        explained.append(jnp.sum(found * partials[row], axis=0, keepdims=True))
    for row in range(rows):
        scaled.append(weighted[row : row + 1] * (targets[row] - explained[row]))
        rights.append(side_of(scaled[row], parts[row]))
    half = rows // PIECE
    for device in range(send_out.shape[0]):
        core = core_of(device, rows)
        lines = [line[:, core * LANES : (core + 1) * LANES] for line in scaled]
        for index, line in enumerate(lines + rights[half * core : half * core + half]):
            send_out[device, index] = line
    return params, explained


def first_kernel(received, target, parts, partials, factor, weighted, hits, send_out):
    rows = parts.shape[0]
    last = received.shape[1] - 1
    targets = [
        target[row : row + 1] - model_of(received[row, last], parts[row]) for row in range(rows)
    ]
    residual_step(targets, parts, partials, factor, weighted, hits, send_out)
    totals = [right_side(received, place) for place in range(PIECE)]
    for device in range(send_out.shape[0]):
        send_out[device, send_out.shape[1] - 1] = totals[core_of(device, rows)]


def spread(line):
    return jnp.broadcast_to(line, (SUB, LANES))


def wide(tile, count):
    tile = jnp.concatenate([tile, tile], axis=0).astype(BF16)
    return jnp.concatenate([tile] * (count // 16), axis=0)


def unit_sums(received, value_of, total):
    rows = (received.shape[1] - PIECE - 1) // 2
    low_row = iota((LANES, LANES), 0).astype(F32).astype(BF16)
    high_row = iota((HIGH, LANES), 0).astype(F32).astype(BF16)
    one, none = jnp.ones((), BF16), jnp.zeros((), BF16)
    for begin in range(0, received.shape[0], 2):
        lefts, rights = [], []
        for device in (begin, begin + 1):
            for index in range(rows):
                unit = spread(received[device, PIECE + index])
                high = jnp.floor(unit * (1.0 / LANES))
                hit = low_row == wide(unit - LANES * high, LANES)
                value = spread(value_of(device, index))
                first = value.astype(BF16).astype(F32)
                lefts.append(
                    jnp.concatenate(
                        [
                            jnp.where(hit, wide(first, LANES), none),
                            jnp.where(hit, wide(value - first, LANES), none),
                        ],
                        axis=0,
                    )
                )
                rights.append(jnp.where(high_row == wide(high, HIGH), one, none))
        found = dot_t(jnp.concatenate(lefts, axis=1), jnp.concatenate(rights, axis=1))
        if begin == 0:
            total[:LANES] = found[:LANES] + found[LANES:]
        else:
            total[:LANES] += found[:LANES] + found[LANES:]
        yield


def matrix_of(band):
    lower = unpack_band(band)
    diagonal = iota(lower.shape, 0) == iota(lower.shape, 1)
    return lower + jnp.where(diagonal, 1.0, lower.T)


def together(works):
    works = list(works)
    while works:
        for work in list(works):
            if next(work, works) is works:
                works.remove(work)


def weights_kernel(received, sums_out):
    rows = (received.shape[1] - PIECE - 1) // 2
    together(
        [
            unit_sums(
                received, lambda device, index: received[device, PIECE + rows + index], sums_out
            )
        ]
    )


def right_side(values, place):
    total = values[0, place]
    for device in range(1, values.shape[0]):
        total = total + values[device, place]
    return total


def core(axis):
    return lax.rem(lax.axis_index(axis), 2)


def coefficients(bundle, place):
    return bundle[LANES + place : LANES + place + 1, :WIDTH]


def put(bundle, place, line):
    bundle[LANES + place : LANES + place + 1] = jnp.concatenate([line, line], axis=1)


def solve_kernel(axis, values, received, bundle_out, lines_out, bands, states, entries):
    half = lines_out.shape[0]
    rows = values.shape[1] - half - 1
    for device in range(values.shape[0]):
        bands[device : device + 1] = values[device, rows + half]
    bundle_out[LANES:] = jnp.zeros((SUB, HIGH), F32)

    def attitude(place):
        states[place] = matrix_of(bands[BAND * place : BAND * (place + 1)])
        change = yield from eliminate(
            states.at[place],
            entries.at[place],
            right_side(values, rows + place),
            lines_out.at[place],
        )
        start = received[half * core(axis) + place, received.shape[1] - 1]
        put(bundle_out, place, start + change)
        yield

    together(
        [unit_sums(received, lambda device, index: values[device, index], bundle_out)]
        + [attitude(place) for place in range(half)]
    )


def both_halves(axis, own, other, half):
    first = core(axis) == 0
    pairs = [(coefficients(own, place), coefficients(other, place)) for place in range(half)]
    lines = [jnp.where(first, one, two) for one, two in pairs]
    return lines + [jnp.where(first, two, one) for one, two in pairs]


def second_kernel(
    axis, bundle, other, weights, other_weights, table, ids, units, observed, parts, partials, factor,
    weighted, hits,
    send_out, params_out, explained_out, table_out, scale_out,
):
    rows = parts.shape[0]
    scale = 1.0 / (weights[...] + other_weights[...] + 1.0)
    scale_out[...] = scale
    table_t = table[...] + (bundle[:LANES] + other[:LANES]) * scale
    table_out[...] = table_t
    picked = pick_from(table_t, flat(ids[...]), units[...], rows)
    lines = both_halves(axis, bundle, other, rows // PIECE)
    targets = [
        observed[row : row + 1] - model_of(lines[row], parts[row]) - picked[row]
        for row in range(rows)
    ]
    params, explained = residual_step(targets, parts, partials, factor, weighted, hits, send_out)
    for index in range(5):
        params_out[index : index + 1] = params[index]
    for row in range(rows):
        explained_out[row : row + 1] = explained[row]


def last_kernel(values, received, bundle, lines, bundle_out):
    half = lines.shape[0]
    rows = values.shape[1] - half
    bundle_out[LANES:] = jnp.zeros((SUB, HIGH), F32)

    def solve(place):
        change = yield from substitute(right_side(values, rows + place), lines.at[place])
        put(bundle_out, place, coefficients(bundle, place) + change)
        yield

    together(
        [unit_sums(received, lambda device, index: values[device, index], bundle_out)]
        + [solve(place) for place in range(half)]
    )


def final_kernel(
    axis, line, bundle, other, table, scale, ids, units, observed, parts, explained,
    cal_out, attitude_out, resid_out,
):
    rows = parts.shape[0]
    table_t = table[...] + (bundle[:LANES] + other[:LANES]) * scale[...]
    cal_out[...] = table_t.T
    picked = pick_from(table_t, flat(ids[...]), units[...], rows)
    me = lax.axis_index(line)
    lines = both_halves(axis, bundle, other, rows // PIECE)
    own = lines[0]
    for row in range(rows):
        own = jnp.where(me == row, lines[row], own)
        at = slice(row, row + 1)
        resid_out[at] = observed[at] - model_of(lines[row], parts[row]) - picked[row] - explained[at]
    attitude_out[...] = own


VMEM = pl.BlockSpec(memory_space=pltpu.VMEM)
ANY = pl.BlockSpec(memory_space=pltpu.HBM)


def call(kernel, outs, *args, away=0, scratch=()):
    near = args[: len(args) - away]
    far = [pltpu.with_memory_space_constraint(arg, pltpu.HBM) for arg in args[len(args) - away :]]
    return pl.pallas_call(
        kernel,
        out_shape=outs,
        in_specs=[VMEM] * len(near) + [ANY] * away,
        out_specs=[VMEM] * len(outs),
        scratch_shapes=scratch,
        compiler_params=pltpu.CompilerParams(vmem_limit_bytes=VMEM_BYTES),
    )(*near, *far)


def stay(*shape, dtype=F32):
    return pltpu.VMEM(shape, dtype)


def leave(*shape):
    return jax.ShapeDtypeStruct(shape, F32)


def swap(value):
    return lax.ppermute(value, "src", [(at, at ^ 1) for at in range(lax.axis_size("src"))])


def exchange(value):
    return lax.all_to_all(value, ("src", "tm"), 0, 0, tiled=True)


def body(
    observed, weight_obs, present, source_partials, attitude_partials, phase, knot_base, source_id,
    cal_id, attitude, calibration,
):
    rows, slots = observed.shape
    devices = lax.axis_size("src") * lax.axis_size("tm")
    half = rows // PIECE
    first_q = attitude.reshape(1, WIDTH)
    held = [weight_obs, present, attitude_partials, phase, knot_base, first_q]
    received, parts, weighted, units_seen = call(
        normals_kernel,
        [
            leave(devices, PIECE + 2 * rows + 1, 1, LANES),
            stay(rows, 2 * WIDTH, slots, dtype=BF16),
            stay(rows, slots), stay(rows, slots, dtype=jnp.int32),
        ],
        weight_obs, present, attitude_partials, phase, knot_base, cal_id, first_q,
        away=7,
        scratch=[pltpu.VMEM(each.shape, each.dtype) for each in held]
        + [pltpu.VMEM((rows, SUB, slots), F32), pltpu.SemaphoreType.DMA((7,))],
    )
    received = exchange(received)
    cal_id = units_seen
    partials, factor, target, table, hits, units, seen = call(
        sources_kernel,
        [
            stay(rows, SUB, slots), stay(16, SRC_DEV), stay(rows, slots), stay(LANES, HIGH),
            stay(rows, SRC_DEV, slots, dtype=BF16), stay(HIGH, rows * slots, dtype=BF16),
            stay(rows, slots),
        ],
        cal_id, weighted, observed, source_partials, source_id,
        calibration.reshape(HIGH, LANES),
        away=4,
        scratch=[
            pltpu.VMEM(source_partials.shape, F32), pltpu.VMEM((rows, slots), jnp.int32),
            pltpu.VMEM((HIGH, LANES), F32), pltpu.SemaphoreType.DMA((4,)),
        ],
    )
    received, factor = lax.optimization_barrier((received, factor))
    (values,) = call(
        first_kernel, [leave(devices, rows + half + 1, 1, LANES)],
        received, target, parts, partials, factor, weighted, hits,
    )
    values, received = lax.optimization_barrier((values, received))
    values = exchange(values)
    (weights,) = call(weights_kernel, [leave(LANES, HIGH)], received)
    other_weights, received = lax.optimization_barrier((swap(weights), received))
    bundle, lines = call(
        functools.partial(solve_kernel, "src"),
        [leave(LANES + SUB, HIGH), stay(half, WIDTH, WIDTH)],
        values, received,
        scratch=[
            pltpu.VMEM((half * BAND, WIDTH), F32), pltpu.VMEM((half, WIDTH, WIDTH), F32),
            pltpu.VMEM((half, len(PLAN[0]), 4, 8, WIDTH), F32),
        ],
    )
    values, params, explained, table, scale = call(
        functools.partial(second_kernel, "src"),
        [
            leave(devices, rows + half, 1, LANES), leave(5, SRC_DEV), stay(rows, slots),
            stay(LANES, HIGH), stay(LANES, HIGH),
        ],
        bundle, swap(bundle), weights, other_weights, table, cal_id, units, seen, parts, partials,
        factor, weighted, hits,
    )
    values = exchange(values)
    (bundle,) = call(
        last_kernel, [leave(LANES + SUB, HIGH)], values, received, bundle, lines
    )
    cal, now, final = call(
        functools.partial(final_kernel, "src", "tm"),
        [leave(HIGH, LANES), leave(1, WIDTH), leave(rows, slots)],
        bundle, swap(bundle), table, scale, cal_id, units, seen, parts, explained,
    )
    return (params, now.reshape(WIDTH), cal.reshape(CAL), final)


def solution(mesh):
    many = mesh.shape["src"] * mesh.shape["tm"]
    return jax.shard_map(
        body if many * PIECE == mesh.shape["tm"] * BAND else plain_body,
        mesh=mesh,
        in_specs=(
            P(None, ("src", "tm")),
            P(None, ("src", "tm")),
            P(None, ("src", "tm")),
            P(None, None, ("src", "tm")),
            P(None, None, ("src", "tm")),
            P(None, ("src", "tm")),
            P(None, ("src", "tm")),
            P(None, ("src", "tm")),
            P(None, ("src", "tm")),
            P("tm"),
            P(),
        ),
        out_specs=(P(None, ("src", "tm")), P("tm"), P(), P(None, ("src", "tm"))),
        check_vma=False,
    )
```

```python
import functools

import jax
import jax.numpy as jnp
from jax import lax
from jax.experimental import pallas as pl
from jax.experimental.pallas import tpu as pltpu
from jax.sharding import PartitionSpec as P

KNOTS_DEV = 32
WIDTH = 4 * KNOTS_DEV
SRC_DEV = 128
CAL = 32768
LANES = 128
HIGH = CAL // LANES
SUB = 8
VMEM_BYTES = 48 * 1024 * 1024

F32 = jnp.float32
BF16 = jnp.bfloat16
EXACT = lax.Precision.HIGHEST


def iota(shape, dim):
    return lax.broadcasted_iota(jnp.int32, shape, dim)


def split3(value):
    first = value.astype(BF16)
    rest = value - first.astype(F32)
    second = rest.astype(BF16)
    third = (rest - second.astype(F32)).astype(BF16)
    return first, second, third


def dot(left, right):
    return lax.dot_general(left, right, (((1,), (0,)), ((), ())), preferred_element_type=F32)


def dot_t(left, right):
    return lax.dot_general(left, right, (((1,), (1,)), ((), ())), preferred_element_type=F32)


def exact_dot(left, right):
    return lax.dot_general(
        left, right, (((1,), (0,)), ((), ())), precision=EXACT, preferred_element_type=F32
    )


def exact_dot_t(left, right):
    return lax.dot_general(
        left, right, (((1,), (1,)), ((), ())), precision=EXACT, preferred_element_type=F32
    )


def one_hot(ids, count):
    return jnp.where(iota((count, ids.shape[1]), 0) == ids, 1.0, 0.0).astype(BF16)


def flat(value):
    return jnp.concatenate([value[row : row + 1] for row in range(value.shape[0])], axis=1)


def unflat(value, rows):
    slots = value.shape[1] // rows
    return [value[:, row * slots : (row + 1) * slots] for row in range(rows)]


def cal_pick(table, ids):
    parts = jnp.concatenate(split3(table.T), axis=0)
    high = ids // LANES
    low = ids % LANES
    found = dot(parts, one_hot(high, HIGH))
    found = found[:LANES] + found[LANES : 2 * LANES] + found[2 * LANES :]
    return jnp.sum(jnp.where(iota(found.shape, 0) == low, found, 0.0), axis=0, keepdims=True)


def cal_sums(values, ids):
    high = one_hot(ids // LANES, HIGH)
    low = iota((LANES, ids.shape[1]), 0) == ids % LANES
    total = None
    for part in split3(values):
        spread = jnp.where(low, part.astype(F32), 0.0).astype(BF16)
        added = dot_t(high, spread)
        total = added if total is None else total + added
    return total


def design_of(base, basis, partials):
    slots = base.shape[1]
    knot = iota((WIDTH, slots), 0) // 4
    step = knot - base
    spread = jnp.zeros((WIDTH, slots), F32)
    for index in range(4):
        spread = jnp.where(step == index, basis[index], spread)
    return spread * jnp.concatenate([partials] * (WIDTH // 8), axis=0)


def band_shift(tile, knot):
    return ((tile % 8) * 16 - (8 * tile + 4 * knot - 12)) % WIDTH


def pack_band(normal):
    place = iota((8, WIDTH), 1) // 16
    upper = iota((8, WIDTH), 0) < 4
    groups = []
    for group in range(2):
        packed = jnp.zeros((8, WIDTH), F32)
        for tile in range(8 * group, 8 * group + 8):
            rows = normal[8 * tile : 8 * tile + 8]
            rolled = jnp.where(
                upper,
                pltpu.roll(rows, band_shift(tile, 0), 1),
                pltpu.roll(rows, band_shift(tile, 1), 1),
            )
            packed = jnp.where(place == tile % 8, rolled, packed)
        groups.append(packed)
    return jnp.concatenate(groups, axis=0)


def unpack_band(packed):
    place = iota((8, WIDTH), 1) // 16
    upper = iota((8, WIDTH), 0) < 4
    tiles = []
    for tile in range(16):
        group = tile // 8
        rows = jnp.where(place == tile % 8, packed[8 * group : 8 * group + 8], 0.0)
        tiles.append(
            jnp.where(
                upper,
                pltpu.roll(rows, (-band_shift(tile, 0)) % WIDTH, 1),
                pltpu.roll(rows, (-band_shift(tile, 1)) % WIDTH, 1),
            )
        )
    full = jnp.concatenate(tiles, axis=0)
    return jnp.where(iota(full.shape, 0) >= iota(full.shape, 1), full, 0.0)


ORDER = (
    (0, 8, 17, 31), (1, 9, 18, 30), (2, 10, 19, 29), (3, 11, 20, 28), (4, 12, 21, 27), (13, 22, 26),
    (5, 23), (6, 24), (7, 25), (14,), (15,), (16,),
)


def plan_of(order):
    near = {
        knot: {other for other in range(KNOTS_DEV) if 0 < abs(other - knot) <= 3}
        for knot in range(KNOTS_DEV)
    }
    plan = []
    for step in order:
        plan.append([(knot, sorted({other // 2 for other in near[knot]})) for knot in step])
        for knot in step:
            assert not near[knot] & set(step)
            for other in near[knot]:
                near[other] = (near[other] | near[knot]) - {other, knot}
    return plan


PLAN = plan_of(ORDER)


def block_rows(entry, lines):
    scale = 1.0 / (entry[0, 0] * entry[1, 1] - entry[0, 1] * entry[0, 1])
    low, mid, high = entry[0, 0] * scale, entry[0, 1] * scale, entry[1, 1] * scale
    turned = {}
    for column in (2, 3):
        turned[0, column] = high * entry[0, column] - mid * entry[1, column]
        turned[1, column] = low * entry[1, column] - mid * entry[0, column]
    rest = {}
    for row, column in ((2, 2), (2, 3), (3, 3)):
        taken = entry[0, row] * turned[0, column] + entry[1, row] * turned[1, column]
        rest[row, column] = entry[row, column] - taken
    upper = [high * lines[0] - mid * lines[1], low * lines[1] - mid * lines[0]]
    lower = [
        lines[row] - (entry[0, row] * upper[0] + entry[1, row] * upper[1]) for row in (2, 3)
    ]
    scale = 1.0 / (rest[2, 2] * rest[3, 3] - rest[2, 3] * rest[2, 3])
    third = (rest[3, 3] * scale) * lower[0] - (rest[2, 3] * scale) * lower[1]
    fourth = (rest[2, 2] * scale) * lower[1] - (rest[2, 3] * scale) * lower[0]
    return [
        upper[0] - (turned[0, 2] * third + turned[0, 3] * fourth),
        upper[1] - (turned[1, 2] * third + turned[1, 3] * fourth),
        third,
        fourth,
    ]


def eliminate(state, entries, right, lines_out):
    shape = (8, WIDTH)
    lane = iota(shape, 1)
    for step in PLAN:
        works = []
        for slot, (knot, reach) in enumerate(step):
            at, sub, first = knot // 2, 4 * (knot % 2), 4 * knot
            inside = lane // 4 == knot
            columns = {}
            for tile in sorted({at, *reach}):
                held = state[8 * tile : 8 * tile + 8]
                columns[tile] = [
                    jnp.broadcast_to(held[:, first + index : first + index + 1], shape)
                    for index in range(4)
                ]
            for index in range(4):
                entries[slot, index] = columns[at][index]
            entry = {
                (one, two): jnp.broadcast_to(entries[slot, two, sub + one : sub + one + 1], shape)
                for one in range(4)
                for two in range(one, 4)
            }
            lines = [
                jnp.where(
                    inside,
                    jnp.where(lane == first + index, -1.0, 0.0),
                    jnp.broadcast_to(state[first + index : first + index + 1], shape),
                )
                for index in range(4)
            ]
            works.append((knot, reach, inside, columns, block_rows(entry, lines)))
        border = right
        for knot, reach, inside, columns, lines in works:
            for index in range(4):
                lines_out[4 * knot + index : 4 * knot + index + 1] = lines[index][0:1]
            for tile in reach:
                factors = columns[tile]
                taken = factors[0] * lines[0] + factors[1] * lines[1]
                taken = taken + (factors[2] * lines[2] + factors[3] * lines[3])
                rows = slice(8 * tile, 8 * tile + 8)
                state[rows] = jnp.where(inside, 0.0, state[rows]) - taken
            right = swept(right, border, knot, [line[0:1] for line in lines])
        yield
    return right


def swept(right, border, knot, lines):
    first = 4 * knot
    right = jnp.where(iota(right.shape, 1) // 4 == knot, 0.0, right)
    factors = [border[:, first + index : first + index + 1] for index in range(4)]
    taken = factors[0] * lines[0] + factors[1] * lines[1]
    return right - (taken + (factors[2] * lines[2] + factors[3] * lines[3]))


def substitute(right, lines):
    for step in PLAN:
        border = right
        for knot, unused in step:
            kept = [lines[4 * knot + index : 4 * knot + index + 1] for index in range(4)]
            right = swept(right, border, knot, kept)
        yield
    return right


def small_factor(sums):
    factor = {}
    for member in range(5):
        for column in range(member + 1):
            running = sums[8 * member + column : 8 * member + column + 1]
            if member == column:
                running = running + 1.0
            for offset in range(column):
                running = running - factor[member, offset] * factor[column, offset]
            if member == column:
                factor[member, member] = jnp.sqrt(running)
            else:
                factor[member, column] = running * inverse_of[column]
        inverse_of = {} if member == 0 else inverse_of
        inverse_of[member] = 1.0 / factor[member, member]
    inverse = {}
    for column in range(5):
        inverse[column, column] = inverse_of[column]
        for member in range(column + 1, 5):
            running = factor[member, column] * inverse[column, column]
            for offset in range(column + 1, member):
                running = running + factor[member, offset] * inverse[offset, column]
            inverse[member, column] = -running * inverse_of[member]
    return inverse


PLACES = [(row_id, col_id) for row_id in range(5) for col_id in range(row_id + 1)]


def small_apply(inverse, sides):
    forward = []
    for member in range(5):
        running = inverse[member, 0] * sides[0]
        for column in range(1, member + 1):
            running = running + inverse[member, column] * sides[column]
        forward.append(running)
    result = []
    for column in range(5):
        running = inverse[column, column] * forward[column]
        for member in range(column + 1, 5):
            running = running + inverse[member, column] * forward[member]
        result.append(running)
    return result


PAIRS = [(row_id, col_id) for row_id in range(5) for col_id in range(row_id + 1)]


def spline_terms(phase, attitude_partials):
    other = 1.0 - phase
    square = phase * phase
    cube = square * phase
    basis = [
        other * other * other / 6.0,
        (3.0 * cube - 6.0 * square + 4.0) / 6.0,
        (-3.0 * cube + 3.0 * square + 3.0 * phase + 1.0) / 6.0,
        cube / 6.0,
    ]
    return jnp.stack(
        [
            basis[knot_step] * attitude_partials[channel]
            for knot_step in range(4)
            for channel in range(4)
        ]
    )


def attitude_model(local, terms, knot_base):
    coefficients = lax.all_gather(local, "tm", axis=0, tiled=True)
    blocks, slots = knot_base.shape
    table = coefficients.reshape(blocks, -1, 4)
    knots_count = table.shape[1]
    grid = lax.broadcasted_iota(jnp.int32, (1, knots_count, 1), 1)
    running = jnp.zeros(knot_base.shape, jnp.float32)
    for knot_step in range(4):
        hit = (grid == (knot_base + knot_step)[:, None, :]).astype(jnp.float32)
        picked = jnp.einsum(
            "bkc,bks->bcs",
            table,
            hit,
            precision=lax.Precision.HIGHEST,
            preferred_element_type=jnp.float32,
        )
        for channel in range(4):
            running = running + terms[4 * knot_step + channel] * picked[:, channel, :]
    return running


def small_solve(matrix, right_side):
    extent = len(right_side)
    factor = {}
    for member in range(extent):
        for column in range(member + 1):
            running = matrix[member][column]
            for offset in range(column):
                running = running - factor[member, offset] * factor[column, offset]
            if member == column:
                factor[member, member] = jnp.sqrt(running)
            else:
                factor[member, column] = running / factor[column, column]
    forward = []
    for member in range(extent):
        running = right_side[member]
        for offset in range(member):
            running = running - factor[member, offset] * forward[offset]
        forward.append(running / factor[member, member])
    result = [None] * extent
    for member in reversed(range(extent)):
        running = forward[member]
        for offset in range(member + 1, extent):
            running = running - factor[offset, member] * result[offset]
        result[member] = running / factor[member, member]
    return jnp.stack(result)


def source_solve(ids, count, weighted, source_partials, target):
    products = [
        weighted * source_partials[row_id] * source_partials[col_id] for row_id, col_id in PAIRS
    ]
    products = products + [weighted * source_partials[row_id] * target for row_id in range(5)]
    stacked = jnp.moveaxis(jnp.stack(products), 1, 0)
    owners = lax.broadcasted_iota(jnp.int32, (count, 1), 0)

    def accumulate(total, item):
        values, block_ids = item
        hit = (block_ids[None, :] == owners).astype(jnp.float32)
        added = lax.dot_general(
            values,
            hit,
            (((1,), (1,)), ((), ())),
            precision=lax.Precision.HIGHEST,
            preferred_element_type=jnp.float32,
        )
        return (total + added, None)

    sums, unused = lax.scan(
        accumulate, jnp.zeros((len(products), count), jnp.float32), (stacked, ids)
    )
    entries = {}
    for position, pair in enumerate(PAIRS):
        entry_value = sums[position] + (1.0 if pair[0] == pair[1] else 0.0)
        entries[pair[0], pair[1]] = entry_value
        entries[pair[1], pair[0]] = entry_value
    matrix = [[entries[row_id, col_id] for col_id in range(5)] for row_id in range(5)]
    return small_solve(matrix, [sums[15 + row_id] for row_id in range(5)])


def pick_params(params, ids):
    count = params.shape[1]
    owners = lax.broadcasted_iota(jnp.int32, (count, 1), 0)

    def pick_single(carry, block_ids):
        hit = (block_ids[None, :] == owners).astype(jnp.float32)
        return (
            carry,
            jnp.dot(
                params, hit, precision=lax.Precision.HIGHEST, preferred_element_type=jnp.float32
            ),
        )

    unused, picked = lax.scan(pick_single, 0, ids)
    return jnp.moveaxis(picked, 1, 0)


def spd_solve(matrix, right_side):
    eye = jnp.eye(matrix.shape[-1], dtype=jnp.float32)
    lower = jnp.linalg.cholesky(matrix + eye)
    middle = lax.linalg.triangular_solve(lower, right_side[..., None], left_side=True, lower=True)
    result = lax.linalg.triangular_solve(
        lower, middle, left_side=True, lower=True, transpose_a=True
    )
    return result[..., 0]


def block_normals(terms, knot_base, weighted, resid):
    blocks, slots = knot_base.shape
    spread = jnp.moveaxis(terms.reshape(4, 4, blocks, slots), 2, 0)

    def block_single(item):
        part, base, weights, values = item
        grid = lax.broadcasted_iota(jnp.int32, (KNOTS_DEV, slots), 0)
        design = jnp.zeros((KNOTS_DEV, 4, slots), jnp.float32)
        for knot_step in range(4):
            hit = (grid == base[None, :] + knot_step).astype(jnp.float32)
            design = design + hit[:, None, :] * part[knot_step][None, :, :]
        design = design.reshape(KNOTS_DEV * 4, slots)
        normal = lax.dot_general(
            design * weights[None, :],
            design,
            (((1,), (1,)), ((), ())),
            precision=lax.Precision.HIGHEST,
            preferred_element_type=jnp.float32,
        )
        right = jnp.dot(
            design,
            weights * values,
            precision=lax.Precision.HIGHEST,
            preferred_element_type=jnp.float32,
        )
        return (normal, right)

    return lax.map(block_single, (spread, knot_base, weighted, resid))


def plain_body(
    observed,
    weight_obs,
    present,
    source_partials,
    attitude_partials,
    phase,
    knot_base,
    source_id,
    cal_id,
    attitude,
    calibration,
):
    weighted = present.astype(jnp.float32) * weight_obs
    terms = spline_terms(phase, attitude_partials)
    flat_cal = cal_id.reshape(-1)
    local = attitude
    cal_now = calibration
    params = jnp.zeros((5, SRC_DEV), jnp.float32)
    for sweep in range(2):
        target = observed - attitude_model(local, terms, knot_base) - cal_now[cal_id]
        params = source_solve(source_id, SRC_DEV, weighted, source_partials, target)
        resid = target - jnp.sum(source_partials * pick_params(params, source_id), axis=0)
        normals, rights = block_normals(terms, knot_base, weighted, resid)
        normal, right = (
            lax.psum_scatter(normals, "tm", scatter_dimension=0, tiled=True),
            lax.psum_scatter(rights, "tm", scatter_dimension=0, tiled=True),
        )
        normal, right = lax.psum((normal[0], right[0]), "src")
        local = local + spd_solve(normal, right)
        numer = jax.ops.segment_sum((weighted * resid).reshape(-1), flat_cal, num_segments=CAL)
        denom = jax.ops.segment_sum(weighted.reshape(-1), flat_cal, num_segments=CAL)
        numer, denom = lax.psum((numer, denom), ("src", "tm"))
        cal_now = cal_now + numer / (denom + 1.0)
    final = observed - attitude_model(local, terms, knot_base) - cal_now[cal_id]
    final = final - jnp.sum(source_partials * pick_params(params, source_id), axis=0)
    return (params, local, cal_now, final)


BAND = 16
PIECE = 2


def begin(pairs, sems):
    copies = [
        pltpu.make_async_copy(origin, held, sems.at[place])
        for place, (origin, held) in enumerate(pairs)
    ]
    for copy in copies:
        copy.start()
    return copies


def finish(copies):
    for copy in copies:
        copy.wait()


def tile_of(value):
    return jnp.concatenate(
        [value[:, at : at + LANES] for at in range(0, value.shape[1], LANES)], axis=0
    )


def pick_from(table_t, ids, units, rows):
    found = dot(jnp.concatenate(split3(table_t)[:2], axis=0), units)
    found = found[:LANES] + found[LANES:]
    hit = iota(found.shape, 0) == ids % LANES
    return unflat(jnp.sum(jnp.where(hit, found, 0.0), axis=0, keepdims=True), rows)


def two_parts(line):
    first = line.astype(BF16).astype(F32)
    return first, (line - first).astype(BF16).astype(F32)


def model_of(line, parts):
    first, second = two_parts(line)
    left = jnp.concatenate([first, first], axis=1)
    right = jnp.concatenate([second, jnp.zeros_like(second)], axis=1)
    row = iota((SUB, 2 * WIDTH), 0)
    both = jnp.where(row == 0, left, jnp.where(row == 1, right, 0.0)).astype(BF16)
    return jnp.sum(dot(both, parts), axis=0, keepdims=True)


def side_of(values, parts):
    first, second = two_parts(values)
    row = iota((SUB, values.shape[1]), 0)
    both = jnp.where(row == 0, first, jnp.where(row == 1, second, 0.0)).astype(BF16)
    found = dot_t(both, parts)
    return found[0:1, :WIDTH] + found[1:2, :WIDTH] + found[0:1, WIDTH:]


def normals_kernel(
    weight_in, present_in, attitude_in, phase_in, knot_in, cal_in, start_in,
    send_out, parts_out, weighted_out, cal_id,
    weight_obs, present, attitude_partials, phase, knot_base, start, stacked, sems,
):
    copies = begin(
        [
            (weight_in, weight_obs), (present_in, present), (cal_in, cal_id), (start_in, start),
            (phase_in, phase), (knot_in, knot_base), (attitude_in, attitude_partials),
        ],
        sems,
    )
    finish(copies[:4])
    rows = weight_obs.shape[0]
    weighted = present[...].astype(F32) * weight_obs[...]
    weighted_out[...] = weighted
    first, second = tile_of(cal_id[...].astype(F32)), tile_of(weighted)
    devices = send_out.shape[0]
    for device in range(devices):
        core = core_of(device, rows)
        for index in range(rows):
            at = rows * core + index
            send_out[device, PIECE + index] = first[at : at + 1]
            send_out[device, PIECE + rows + index] = second[at : at + 1]
        send_out[device, PIECE + 2 * rows] = start[...]
    finish(copies[4:])
    u = phase[...]
    other = 1.0 - u
    square = u * u
    cube = square * u
    basis = [
        other * other * other / 6.0,
        (3.0 * cube - 6.0 * square + 4.0) / 6.0,
        (-3.0 * cube + 3.0 * square + 3.0 * u + 1.0) / 6.0,
        cube / 6.0,
    ]
    for row in range(rows):
        at = slice(row, row + 1)
        for channel in range(4):
            lines = attitude_partials[channel, at]
            stacked[row, channel : channel + 1] = lines
            stacked[row, channel + 4 : channel + 5] = lines
        design = design_of(knot_base[at], [part[at] for part in basis], stacked[row])
        one, two, three = split3(design)
        parts_out[row, :WIDTH] = one
        parts_out[row, WIDTH:] = two
        high, middle, low = split3(design * weighted[at])
        most = dot_t(jnp.concatenate([high, middle], axis=0), jnp.concatenate([one, two], axis=0))
        rest = dot_t(jnp.concatenate([high, low], axis=0), jnp.concatenate([three, one], axis=0))
        small = most[WIDTH:, WIDTH:] + (rest[:WIDTH, :WIDTH] + rest[WIDTH:, WIDTH:])
        small = small + (most[:WIDTH, WIDTH:] + most[WIDTH:, :WIDTH])
        band = pack_band(most[:WIDTH, :WIDTH] + small)
        half, place = divmod(row, rows // PIECE)
        for index in range(BAND):
            send_out[place * BAND + index, half] = band[index : index + 1]


def sources_kernel(
    cal_id, weighted, observed_in, source_in, id_in, calibration_in,
    partials_out, factor_out, target_out, table_out, hits_out, units_out, observed,
    source_partials, source_id, table, sems,
):
    copies = begin(
        [
            (observed_in, observed), (source_in, source_partials), (id_in, source_id),
            (calibration_in, table),
        ],
        sems,
    )
    finish(copies)
    rows, slots = observed.shape
    matrix = jnp.zeros((40, SRC_DEV), F32)
    for row in range(rows):
        at = slice(row, row + 1)
        for index in range(5):
            partials_out[row, index : index + 1] = source_partials[index, at]
        partials_out[row, 5:] = jnp.zeros((SUB - 5, slots), F32)
        partials = partials_out[row]
        products = jnp.concatenate(
            [partials * (weighted[at] * partials[index : index + 1]) for index in range(5)], axis=0
        )
        hits_out[row] = one_hot(source_id[at], SRC_DEV)
        found = dot_t(jnp.concatenate(split3(products), axis=0), hits_out[row])
        matrix = matrix + found[:40] + found[40:80] + found[80:]
    ids = flat(cal_id[...])
    units_out[...] = one_hot(ids // LANES, HIGH)
    inverse = small_factor(matrix)
    for place, pair in enumerate(PLACES):
        factor_out[place : place + 1] = inverse[pair]
    factor_out[15:16] = jnp.zeros((1, SRC_DEV), F32)
    table_t = table[...].T
    table_out[...] = table_t
    for row, picked in enumerate(pick_from(table_t, ids, units_out[...], rows)):
        target_out[row : row + 1] = observed[row : row + 1] - picked


def core_of(device, line):
    return device // line % 2


def residual_step(targets, parts, partials, factor, weighted, hits, send_out):
    rows = len(targets)
    inverse = {pair: factor[place : place + 1] for place, pair in enumerate(PLACES)}
    sides = jnp.zeros((SUB, SRC_DEV), F32)
    for row in range(rows):
        products = partials[row] * (weighted[row : row + 1] * targets[row])
        found = dot_t(jnp.concatenate(split3(products)[:2], axis=0), hits[row])
        sides = sides + found[:SUB] + found[SUB:]
    params = small_apply(inverse, [sides[index : index + 1] for index in range(5)])
    table = jnp.concatenate(params + [jnp.zeros((3, SRC_DEV), F32)], axis=0)
    split = jnp.concatenate(split3(table)[:2], axis=0)
    explained, scaled, rights = [], [], []
    for row in range(rows):
        found = dot(split, hits[row])
        found = found[:SUB] + found[SUB:]
        explained.append(jnp.sum(found * partials[row], axis=0, keepdims=True))
    for row in range(rows):
        scaled.append(weighted[row : row + 1] * (targets[row] - explained[row]))
        rights.append(side_of(scaled[row], parts[row]))
    half = rows // PIECE
    for device in range(send_out.shape[0]):
        core = core_of(device, rows)
        lines = [line[:, core * LANES : (core + 1) * LANES] for line in scaled]
        for index, line in enumerate(lines + rights[half * core : half * core + half]):
            send_out[device, index] = line
    return params, explained


def first_kernel(received, target, parts, partials, factor, weighted, hits, send_out):
    rows = parts.shape[0]
    last = received.shape[1] - 1
    targets = [
        target[row : row + 1] - model_of(received[row, last], parts[row]) for row in range(rows)
    ]
    residual_step(targets, parts, partials, factor, weighted, hits, send_out)
    totals = [right_side(received, place) for place in range(PIECE)]
    for device in range(send_out.shape[0]):
        send_out[device, send_out.shape[1] - 1] = totals[core_of(device, rows)]


def spread(line):
    return jnp.broadcast_to(line, (SUB, LANES))


def wide(tile, count):
    tile = jnp.concatenate([tile, tile], axis=0).astype(BF16)
    return jnp.concatenate([tile] * (count // 16), axis=0)


def unit_sums(received, value_of, total):
    rows = (received.shape[1] - PIECE - 1) // 2
    low_row = iota((LANES, LANES), 0).astype(F32).astype(BF16)
    high_row = iota((HIGH, LANES), 0).astype(F32).astype(BF16)
    one, none = jnp.ones((), BF16), jnp.zeros((), BF16)
    for begin in range(0, received.shape[0], 2):
        lefts, rights = [], []
        for device in (begin, begin + 1):
            for index in range(rows):
                unit = spread(received[device, PIECE + index])
                high = jnp.floor(unit * (1.0 / LANES))
                hit = low_row == wide(unit - LANES * high, LANES)
                value = spread(value_of(device, index))
                first = value.astype(BF16).astype(F32)
                lefts.append(
                    jnp.concatenate(
                        [
                            jnp.where(hit, wide(first, LANES), none),
                            jnp.where(hit, wide(value - first, LANES), none),
                        ],
                        axis=0,
                    )
                )
                rights.append(jnp.where(high_row == wide(high, HIGH), one, none))
        found = dot_t(jnp.concatenate(lefts, axis=1), jnp.concatenate(rights, axis=1))
        if begin == 0:
            total[:LANES] = found[:LANES] + found[LANES:]
        else:
            total[:LANES] += found[:LANES] + found[LANES:]
        yield


def matrix_of(band):
    lower = unpack_band(band)
    diagonal = iota(lower.shape, 0) == iota(lower.shape, 1)
    return lower + jnp.where(diagonal, 1.0, lower.T)


def together(works):
    works = list(works)
    while works:
        for work in list(works):
            if next(work, works) is works:
                works.remove(work)


def weights_kernel(received, sums_out):
    rows = (received.shape[1] - PIECE - 1) // 2
    together(
        [
            unit_sums(
                received, lambda device, index: received[device, PIECE + rows + index], sums_out
            )
        ]
    )


def right_side(values, place):
    total = values[0, place]
    for device in range(1, values.shape[0]):
        total = total + values[device, place]
    return total


def core(axis):
    return lax.rem(lax.axis_index(axis), 2)


def coefficients(bundle, place):
    return bundle[LANES + place : LANES + place + 1, :WIDTH]


def put(bundle, place, line):
    bundle[LANES + place : LANES + place + 1] = jnp.concatenate([line, line], axis=1)


def solve_kernel(axis, values, received, bundle_out, lines_out, bands, states, entries):
    half = lines_out.shape[0]
    rows = values.shape[1] - half - 1
    for device in range(values.shape[0]):
        bands[device : device + 1] = values[device, rows + half]
    bundle_out[LANES:] = jnp.zeros((SUB, HIGH), F32)

    def attitude(place):
        states[place] = matrix_of(bands[BAND * place : BAND * (place + 1)])
        change = yield from eliminate(
            states.at[place],
            entries.at[place],
            right_side(values, rows + place),
            lines_out.at[place],
        )
        start = received[half * core(axis) + place, received.shape[1] - 1]
        put(bundle_out, place, start + change)
        yield

    together(
        [unit_sums(received, lambda device, index: values[device, index], bundle_out)]
        + [attitude(place) for place in range(half)]
    )


def both_halves(axis, own, other, half):
    first = core(axis) == 0
    pairs = [(coefficients(own, place), coefficients(other, place)) for place in range(half)]
    lines = [jnp.where(first, one, two) for one, two in pairs]
    return lines + [jnp.where(first, two, one) for one, two in pairs]


def second_kernel(
    axis, bundle, other, weights, other_weights, table, ids, units, observed, parts, partials, factor,
    weighted, hits,
    send_out, params_out, explained_out, table_out, scale_out,
):
    rows = parts.shape[0]
    scale = 1.0 / (weights[...] + other_weights[...] + 1.0)
    scale_out[...] = scale
    table_t = table[...] + (bundle[:LANES] + other[:LANES]) * scale
    table_out[...] = table_t
    picked = pick_from(table_t, flat(ids[...]), units[...], rows)
    lines = both_halves(axis, bundle, other, rows // PIECE)
    targets = [
        observed[row : row + 1] - model_of(lines[row], parts[row]) - picked[row]
        for row in range(rows)
    ]
    params, explained = residual_step(targets, parts, partials, factor, weighted, hits, send_out)
    for index in range(5):
        params_out[index : index + 1] = params[index]
    for row in range(rows):
        explained_out[row : row + 1] = explained[row]


def last_kernel(values, received, bundle, lines, bundle_out):
    half = lines.shape[0]
    rows = values.shape[1] - half
    bundle_out[LANES:] = jnp.zeros((SUB, HIGH), F32)

    def solve(place):
        change = yield from substitute(right_side(values, rows + place), lines.at[place])
        put(bundle_out, place, coefficients(bundle, place) + change)
        yield

    together(
        [unit_sums(received, lambda device, index: values[device, index], bundle_out)]
        + [solve(place) for place in range(half)]
    )


def final_kernel(
    axis, line, bundle, other, table, scale, ids, units, observed, parts, explained,
    cal_out, attitude_out, resid_out,
):
    rows = parts.shape[0]
    table_t = table[...] + (bundle[:LANES] + other[:LANES]) * scale[...]
    cal_out[...] = table_t.T
    picked = pick_from(table_t, flat(ids[...]), units[...], rows)
    me = lax.axis_index(line)
    lines = both_halves(axis, bundle, other, rows // PIECE)
    own = lines[0]
    for row in range(rows):
        own = jnp.where(me == row, lines[row], own)
        at = slice(row, row + 1)
        resid_out[at] = observed[at] - model_of(lines[row], parts[row]) - picked[row] - explained[at]
    attitude_out[...] = own


VMEM = pl.BlockSpec(memory_space=pltpu.VMEM)
ANY = pl.BlockSpec(memory_space=pltpu.HBM)


def call(kernel, outs, *args, away=0, scratch=()):
    near = args[: len(args) - away]
    far = [pltpu.with_memory_space_constraint(arg, pltpu.HBM) for arg in args[len(args) - away :]]
    return pl.pallas_call(
        kernel,
        out_shape=outs,
        in_specs=[VMEM] * len(near) + [ANY] * away,
        out_specs=[VMEM] * len(outs),
        scratch_shapes=scratch,
        compiler_params=pltpu.CompilerParams(vmem_limit_bytes=VMEM_BYTES),
    )(*near, *far)


def stay(*shape, dtype=F32):
    return pltpu.VMEM(shape, dtype)


def leave(*shape):
    return jax.ShapeDtypeStruct(shape, F32)


def swap(value):
    return lax.ppermute(value, "src", [(at, at ^ 1) for at in range(lax.axis_size("src"))])


def exchange(value):
    return lax.all_to_all(value, ("src", "tm"), 0, 0, tiled=True)


def body(
    observed, weight_obs, present, source_partials, attitude_partials, phase, knot_base, source_id,
    cal_id, attitude, calibration,
):
    rows, slots = observed.shape
    devices = lax.axis_size("src") * lax.axis_size("tm")
    half = rows // PIECE
    first_q = attitude.reshape(1, WIDTH)
    held = [weight_obs, present, attitude_partials, phase, knot_base, first_q]
    received, parts, weighted, units_seen = call(
        normals_kernel,
        [
            leave(devices, PIECE + 2 * rows + 1, 1, LANES),
            stay(rows, 2 * WIDTH, slots, dtype=BF16),
            stay(rows, slots), stay(rows, slots, dtype=jnp.int32),
        ],
        weight_obs, present, attitude_partials, phase, knot_base, cal_id, first_q,
        away=7,
        scratch=[pltpu.VMEM(each.shape, each.dtype) for each in held]
        + [pltpu.VMEM((rows, SUB, slots), F32), pltpu.SemaphoreType.DMA((7,))],
    )
    received = exchange(received)
    cal_id = units_seen
    partials, factor, target, table, hits, units, seen = call(
        sources_kernel,
        [
            stay(rows, SUB, slots), stay(16, SRC_DEV), stay(rows, slots), stay(LANES, HIGH),
            stay(rows, SRC_DEV, slots, dtype=BF16), stay(HIGH, rows * slots, dtype=BF16),
            stay(rows, slots),
        ],
        cal_id, weighted, observed, source_partials, source_id,
        calibration.reshape(HIGH, LANES),
        away=4,
        scratch=[
            pltpu.VMEM(source_partials.shape, F32), pltpu.VMEM((rows, slots), jnp.int32),
            pltpu.VMEM((HIGH, LANES), F32), pltpu.SemaphoreType.DMA((4,)),
        ],
    )
    received, factor = lax.optimization_barrier((received, factor))
    (values,) = call(
        first_kernel, [leave(devices, rows + half + 1, 1, LANES)],
        received, target, parts, partials, factor, weighted, hits,
    )
    values, received = lax.optimization_barrier((values, received))
    values = exchange(values)
    (weights,) = call(weights_kernel, [leave(LANES, HIGH)], received)
    other_weights, received = lax.optimization_barrier((swap(weights), received))
    bundle, lines = call(
        functools.partial(solve_kernel, "src"),
        [leave(LANES + SUB, HIGH), stay(half, WIDTH, WIDTH)],
        values, received,
        scratch=[
            pltpu.VMEM((half * BAND, WIDTH), F32), pltpu.VMEM((half, WIDTH, WIDTH), F32),
            pltpu.VMEM((half, len(PLAN[0]), 4, 8, WIDTH), F32),
        ],
    )
    values, params, explained, table, scale = call(
        functools.partial(second_kernel, "src"),
        [
            leave(devices, rows + half, 1, LANES), leave(5, SRC_DEV), stay(rows, slots),
            stay(LANES, HIGH), stay(LANES, HIGH),
        ],
        bundle, swap(bundle), weights, other_weights, table, cal_id, units, seen, parts, partials,
        factor, weighted, hits,
    )
    values = exchange(values)
    (bundle,) = call(
        last_kernel, [leave(LANES + SUB, HIGH)], values, received, bundle, lines
    )
    cal, now, final = call(
        functools.partial(final_kernel, "src", "tm"),
        [leave(HIGH, LANES), leave(1, WIDTH), leave(rows, slots)],
        bundle, swap(bundle), table, scale, cal_id, units, seen, parts, explained,
    )
    return (params, now.reshape(WIDTH), cal.reshape(CAL), final)


def solution(mesh):
    many = mesh.shape["src"] * mesh.shape["tm"]
    return jax.shard_map(
        body if many * PIECE == mesh.shape["tm"] * BAND else plain_body,
        mesh=mesh,
        in_specs=(
            P(None, ("src", "tm")),
            P(None, ("src", "tm")),
            P(None, ("src", "tm")),
            P(None, None, ("src", "tm")),
            P(None, None, ("src", "tm")),
            P(None, ("src", "tm")),
            P(None, ("src", "tm")),
            P(None, ("src", "tm")),
            P(None, ("src", "tm")),
            P("tm"),
            P(),
        ),
        out_specs=(P(None, ("src", "tm")), P("tm"), P(), P(None, ("src", "tm"))),
        check_vma=False,
    )
```
